32 devices in a mesh: rows: 8 (over z, y), blk: 4 (over x, core).
Axes of the slice: x: 2, y: 2, z: 4, core: 2. Of those that a mesh axis runs over, the one named last changes fastest.
Arguments:
- inputs: bfloat16 [8, 1792, 768], P('rows', 'blk'), may hold values from -6 to 6
- encoded: bfloat16 [8, 1536, 768], P('rows', 'blk'), may hold values from -6 to 6
- cotangent: bfloat16 [8, 1792, 768], P('rows', 'blk'), may hold values from -6 to 6
- dec_seg: int32 [8, 1792], P('rows', 'blk'), may hold values from 0 to 2, as said below
- pass_doc: int32 [8, 4], P('rows', 'blk'), may hold values from 0 to 2, as said below
- enc_mask: int32 [8, 1536], P('rows', 'blk'), may hold values from 0 to 1, as said below
- self_query: bfloat16 [768, 768], replicated, may hold values from -0.21875 to 0.21875
- self_key: bfloat16 [768, 768], replicated, may hold values from -0.21875 to 0.21875
- self_value: bfloat16 [768, 768], replicated, may hold values from -0.21875 to 0.21875
- self_output: bfloat16 [768, 768], replicated, may hold values from -3 to 3
- cross_query: bfloat16 [768, 768], replicated, may hold values from -0.21875 to 0.21875
- cross_key: bfloat16 [768, 768], replicated, may hold values from -0.21875 to 0.21875
- cross_value: bfloat16 [768, 768], replicated, may hold values from -0.21875 to 0.21875
- cross_output: bfloat16 [768, 768], replicated, may hold values from -6 to 6
- feed_in: bfloat16 [768, 3072], replicated, may hold values from -0.21875 to 0.21875
- feed_out: bfloat16 [3072, 768], replicated, may hold values from -0.109375 to 0.109375
- gain_self: float32 [768], replicated, may hold values from 0.1 to 1.9
- gain_cross: float32 [768], replicated, may hold values from 0.1 to 1.9
- gain_ff: float32 [768], replicated, may hold values from 0.1 to 1.9
Outputs:
- output: bfloat16 [8, 1792, 768], P('rows', 'blk')
- input_grad: float32 [8, 1792, 768], P('rows', 'blk')
- encoded_grad: float32 [8, 1536, 768], P('rows', 'blk')
- grad_self_query: float32 [768, 768], P('rows', 'blk')
- grad_self_key: float32 [768, 768], P('rows', 'blk')
- grad_self_value: float32 [768, 768], P('rows', 'blk')
- grad_self_output: float32 [768, 768], P('rows', 'blk')
- grad_cross_query: float32 [768, 768], P('rows', 'blk')
- grad_cross_key: float32 [768, 768], P('rows', 'blk')
- grad_cross_value: float32 [768, 768], P('rows', 'blk')
- grad_cross_output: float32 [768, 768], P('rows', 'blk')
- grad_feed_in: float32 [768, 3072], P('rows', 'blk')
- grad_feed_out: float32 [3072, 768], P('rows', 'blk')
- grad_gain_self: float32 [768], P('rows')
- grad_gain_cross: float32 [768], P('rows')
- grad_gain_ff: float32 [768], P('rows')
The draws below stay inside these ranges and needn't reach their ends.
Inputs may be any that keep to these rules, and one draw needn't show every extreme that they name: `dec_seg`: each row holds three documents of consecutive decoder tokens, numbered 0, 1, 2 in order; document 1 begins within the row's first 448 tokens and ends within its last 448. `pass_doc`: every document of a row is served by one passage or more; the first and the last passage of each row serve document 1. `enc_mask`: the live tokens of each passage are a prefix of 336 to 384 tokens; the first passage of every row is wholly live.
All inputs are finite; a program needn't handle non-finite values.
Results may differ from the reference program's by a relative error of at most 0.025.
Values may be sent and summed in bfloat16 or wider, within the bound.
No kernel may reach another device: no remote copies, remote signals or barrier semaphores. Data moves between devices by JAX's collectives and lax.ppermute only.
A program may use at most 320 MiB of HBM per device.

```python
import jax
import jax.numpy as jnp
from jax import lax

D = 768
FF = 3072
HEADS = 12
HEAD_DIM = 64
PLEN = 384
LENGTH = 1792
DEC_DEV = 448
PASSAGES = 4
ENC_LEN = 1536
ROWS = 8


def draw_dec_seg(key, part):
    key = jax.random.fold_in(key, 11)
    key_first, key_last = jax.random.split(key)
    first_edge = jax.random.randint(key_first, (ROWS, 1), 1, DEC_DEV)
    last_edge = jax.random.randint(key_last, (ROWS, 1), LENGTH - DEC_DEV + 1, LENGTH)
    places = jnp.arange(LENGTH)[None, :]
    return (places >= first_edge).astype(jnp.int32) + (places >= last_edge).astype(jnp.int32)


def draw_pass_doc(key, part):
    key = jax.random.fold_in(key, 12)
    key_first, key_second, key_rest = jax.random.split(key, 3)
    middle = PASSAGES - 2
    first_spot = jax.random.randint(key_first, (ROWS, 1), 1, PASSAGES - 1)
    step_size = jax.random.randint(key_second, (ROWS, 1), 1, middle)
    second_spot = 1 + (first_spot - 1 + step_size) % middle
    others = jax.random.randint(key_rest, (ROWS, PASSAGES), 0, 3)
    places = jnp.arange(PASSAGES)[None, :]
    docs = jnp.where((places == 0) | (places == PASSAGES - 1), 1, others)
    docs = jnp.where(places == first_spot, 0, docs)
    docs = jnp.where(places == second_spot, 2, docs)
    return docs.astype(jnp.int32)


def draw_enc_mask(key, part):
    key = jax.random.fold_in(key, 13)
    live = jax.random.randint(key, (ROWS, PASSAGES, 1), PLEN - PLEN // 8, PLEN + 1)
    live = jnp.where(jnp.arange(PASSAGES)[None, :, None] == 0, PLEN, live)
    places = jnp.arange(PLEN)[None, None, :]
    return (places < live).astype(jnp.int32).reshape(ROWS, PASSAGES * PLEN)


def levels(stream_key, shape, pieces, least, largest):
    level = 1.0
    for axis_at, blocks in pieces:
        steps = jax.random.uniform(jax.random.fold_in(jax.random.fold_in(stream_key, 6), axis_at), (blocks,), jnp.float32, least / len(pieces), largest / len(pieces))
        level = level * jnp.repeat(jnp.exp(steps), shape[axis_at] // blocks).reshape((-1,) + (1,) * (len(shape) - 1 - axis_at))
    return level


def scatter_about(stream_key, extent, deviation, reach, pieces=(), dtype=jnp.bfloat16):
    entries = deviation * jax.random.normal(stream_key, extent, jnp.float32)
    if pieces:
        entries = entries * levels(stream_key, extent, pieces, -0.22, 0.18)
    return jnp.clip(entries, -reach, reach).astype(dtype)


def setup_inputs(seed: int = 0) -> dict:
    key_list = jax.random.split(jax.random.key(seed), 20)
    inputs = scatter_about(key_list[0], (ROWS, LENGTH, D), 1.0, 6.0, ((0, 8), (1, 4)))
    encoded = scatter_about(key_list[1], (ROWS, ENC_LEN, D), 1.0, 6.0, ((0, 8), (1, 4)))
    cotangent = scatter_about(key_list[2], (ROWS, LENGTH, D), 1.0, 6.0, ((0, 8), (1, 4)))
    dec_seg = draw_dec_seg(jax.random.fold_in(key_list[19], 71), 0)
    pass_doc = draw_pass_doc(jax.random.fold_in(key_list[19], 71), 0)
    enc_mask = draw_enc_mask(jax.random.fold_in(key_list[19], 71), 0)
    self_query = scatter_about(key_list[6], (D, D), D ** -0.5, 0.21875)
    self_key = scatter_about(key_list[7], (D, D), D ** -0.5, 0.21875)
    self_value = scatter_about(key_list[8], (D, D), D ** -0.5, 0.21875)
    self_output = scatter_about(key_list[9], (D, D), 4 ** -0.5, 3.0)
    cross_query = scatter_about(key_list[10], (D, D), D ** -0.5, 0.21875)
    cross_key = scatter_about(key_list[11], (D, D), D ** -0.5, 0.21875)
    cross_value = scatter_about(key_list[12], (D, D), D ** -0.5, 0.21875)
    cross_output = scatter_about(key_list[13], (D, D), 1 ** -0.5, 6.0)
    feed_in = scatter_about(key_list[14], (D, FF), D ** -0.5, 0.21875)
    feed_out = scatter_about(key_list[15], (FF, D), FF ** -0.5, 0.109375)
    gain_self = jnp.clip(1.0 + 0.18 * jax.random.normal(key_list[16], (D,), jnp.float32), 0.1, 1.9)
    gain_cross = jnp.clip(1.0 + 0.18 * jax.random.normal(key_list[17], (D,), jnp.float32), 0.1, 1.9)
    gain_ff = jnp.clip(1.0 + 0.18 * jax.random.normal(key_list[18], (D,), jnp.float32), 0.1, 1.9)
    return {"inputs": inputs, "encoded": encoded, "cotangent": cotangent, "dec_seg": dec_seg, "pass_doc": pass_doc, "enc_mask": enc_mask, "self_query": self_query, "self_key": self_key, "self_value": self_value, "self_output": self_output, "cross_query": cross_query, "cross_key": cross_key, "cross_value": cross_value, "cross_output": cross_output, "feed_in": feed_in, "feed_out": feed_out, "gain_self": gain_self, "gain_cross": gain_cross, "gain_ff": gain_ff}


@jax.custom_vjp
def low(v):
    return lax.optimization_barrier(v.astype(jnp.bfloat16)).astype(jnp.float32)

@jax.custom_vjp
def low_back(v):
    return v

def low_keep(v):
    return (low(v), None)

def low_pass(kept, grad):
    return (grad,)

def back_keep(v):
    return (v, None)

def back_low(kept, grad):
    return (low(grad),)
low.defvjp(low_keep, low_pass)
low_back.defvjp(back_keep, back_low)

def multiply(left, right):
    return jnp.dot(left, right, precision=lax.Precision.HIGHEST)

def rms_norm(values, gain_vec):
    return values * lax.rsqrt(lax.optimization_barrier(jnp.mean(values * values, axis=-1, keepdims=True)) + 1e-06) * gain_vec

def to_heads(matrix):
    return matrix.reshape(matrix.shape[0], HEADS, HEAD_DIM).transpose(1, 0, 2)

def attend(queries, keys, values, allowed):

    def one_head(operands):
        query_head, key_head, value_head = operands
        scores = low_back(multiply(query_head, key_head.T) * 0.125)
        scores = jnp.where(allowed, scores, -1e+30)
        weights = jax.nn.softmax(scores, axis=-1)
        return multiply(low(weights), value_head)
    merged = lax.map(jax.checkpoint(one_head), (to_heads(queries), to_heads(keys), to_heads(values)))
    return merged.transpose(1, 0, 2).reshape(queries.shape[0], HEADS * HEAD_DIM)

def layer(inputs, encoded, params, segments, key_docs):
    self_query, self_key, self_value, self_output, cross_query, cross_key, cross_value, cross_output, feed_in, feed_out, gain_self, gain_cross, gain_ff = params
    places = jnp.arange(inputs.shape[0])
    self_allowed = (segments[:, None] == segments[None, :]) & (places[None, :] <= places[:, None])
    cross_allowed = segments[:, None] == key_docs[None, :]
    normed = low(rms_norm(inputs, gain_self))
    queries = low_back(low(multiply(normed, self_query)))
    keys = low_back(low(multiply(normed, self_key)))
    values = low_back(low(multiply(normed, self_value)))
    context = low_back(low(attend(queries, keys, values, self_allowed)))
    after_self = inputs + low_back(multiply(context, self_output))
    normed = low(rms_norm(after_self, gain_cross))
    queries = low_back(low(multiply(normed, cross_query)))
    keys = low_back(low(multiply(encoded, cross_key)))
    values = low_back(low(multiply(encoded, cross_value)))
    context = low_back(low(attend(queries, keys, values, cross_allowed)))
    after_cross = after_self + low_back(multiply(context, cross_output))
    normed = low(rms_norm(after_cross, gain_ff))
    before = low_back(multiply(normed, feed_in))
    hidden = low(jax.nn.gelu(before))
    return after_cross + low_back(multiply(hidden, feed_out))

def reference(inputs, encoded, cotangent, dec_seg, pass_doc, enc_mask, self_query, self_key, self_value, self_output, cross_query, cross_key, cross_value, cross_output, feed_in, feed_out, gain_self, gain_cross, gain_ff):
    params = tuple((weight.astype(jnp.float32) for weight in (self_query, self_key, self_value, self_output, cross_query, cross_key, cross_value, cross_output, feed_in, feed_out, gain_self, gain_cross, gain_ff)))
    key_docs = jnp.where(enc_mask == 1, jnp.repeat(pass_doc, PLEN, axis=1), -1).astype(jnp.int32)

    def one_row(totals, operands):
        row_inputs, row_encoded, row_cotangent, row_segments, row_docs = operands

        def forward(layer_in, layer_enc, layer_params):
            return layer(layer_in, layer_enc, layer_params, row_segments, row_docs)
        result, pullback = jax.vjp(forward, row_inputs.astype(jnp.float32), row_encoded.astype(jnp.float32), params)
        grad_in, grad_enc, grad_params = pullback(row_cotangent.astype(jnp.float32))
        totals = tuple((running + update for running, update in zip(totals, grad_params)))
        return (totals, (result.astype(jnp.bfloat16), grad_in, grad_enc))
    start_totals = tuple((jnp.zeros_like(param) for param in params))
    totals, stacked = lax.scan(one_row, start_totals, (inputs, encoded, cotangent, dec_seg, key_docs))
    return (stacked[0], stacked[1], stacked[2], totals[0], totals[1], totals[2], totals[3], totals[4], totals[5], totals[6], totals[7], totals[8], totals[9], totals[10], totals[11], totals[12])
```

```python
import jax
import jax.numpy as jnp
from jax import lax
from jax.experimental import pallas as pl
from jax.experimental.pallas import tpu as pltpu
from jax.sharding import PartitionSpec as P

HEADS = 12
HEAD_DIM = 64
PLEN = 384


NEG_FILL = -1e30
SCALE = 0.125


def split_heads(matrix):
    return matrix.reshape(matrix.shape[0], matrix.shape[1], HEADS, HEAD_DIM)


def join_heads(tensor):
    return jnp.transpose(tensor, (0, 2, 1, 3)).reshape(
        tensor.shape[0], tensor.shape[2], HEADS * HEAD_DIM
    )


def rms_norm(values, gain_vec):
    return values * lax.rsqrt(jnp.mean(values * values, axis=-1, keepdims=True) + 1e-06) * gain_vec


def norm_back(values, gain_vec, grad_out):
    _, pullback = jax.vjp(rms_norm, values, gain_vec)
    return pullback(grad_out)


def project(left, weight):
    return jnp.einsum("rqd,df->rqf", left, weight, preferred_element_type=jnp.float32)


def back_project(grad_out, weight):
    return jnp.einsum("rqf,df->rqd", grad_out, weight, preferred_element_type=jnp.float32)


def weight_grad(left, grad_out):
    return jnp.einsum("rqd,rqf->df", left, grad_out, preferred_element_type=jnp.float32)


def head_scores(queries, keys):
    return (
        jnp.einsum(
            "rqhe,rkhe->rhqk",
            split_heads(queries),
            split_heads(keys),
            preferred_element_type=jnp.float32,
        )
        * SCALE
    )


def empty_state(row_count, query_count):
    return (
        jnp.full((row_count, HEADS, query_count), NEG_FILL, jnp.float32),
        jnp.zeros((row_count, HEADS, query_count), jnp.float32),
        jnp.zeros((row_count, HEADS, query_count, HEAD_DIM), jnp.float32),
    )


def online_block(state, queries, keys, values, allowed):
    run_max, run_sum, run_acc = state
    scores = head_scores(queries, keys)
    allowed = allowed[:, None]
    new_max = jnp.maximum(run_max, jnp.max(jnp.where(allowed, scores, NEG_FILL), axis=-1))
    weights = jnp.where(allowed, jnp.exp(scores - new_max[..., None]), 0.0)
    new_sum = jnp.sum(weights, axis=-1)
    new_acc = jnp.einsum(
        "rhqk,rkhe->rhqe",
        weights.astype(jnp.bfloat16),
        split_heads(values),
        preferred_element_type=jnp.float32,
    )
    return (new_max, new_sum, new_acc)


def finish(state):
    run_max, run_sum, run_acc = state
    return (run_acc / run_sum[..., None], run_max + jnp.log(run_sum))


def grad_pair(queries, grad_ctx, log_sum, delta, keys, values, allowed):
    scores = head_scores(queries, keys)
    probs_now = jnp.where(allowed[:, None], jnp.exp(scores - log_sum[..., None]), 0.0)
    grad_probs = jnp.einsum(
        "rqhe,rkhe->rhqk",
        split_heads(grad_ctx),
        split_heads(values),
        preferred_element_type=jnp.float32,
    )
    grad_scores = (probs_now * (grad_probs - delta[..., None])).astype(jnp.bfloat16)
    grad_query = (
        jnp.einsum(
            "rhqk,rkhe->rqhe", grad_scores, split_heads(keys), preferred_element_type=jnp.float32
        )
        * SCALE
    )
    grad_key = (
        jnp.einsum(
            "rhqk,rqhe->rkhe", grad_scores, split_heads(queries), preferred_element_type=jnp.float32
        )
        * SCALE
    )
    grad_value = jnp.einsum(
        "rhqk,rqhe->rkhe",
        probs_now.astype(jnp.bfloat16),
        split_heads(grad_ctx),
        preferred_element_type=jnp.float32,
    )
    row_count = keys.shape[0]
    key_count = keys.shape[1]
    joined = jnp.concatenate(
        (grad_key.reshape(row_count, key_count, -1), grad_value.reshape(row_count, key_count, -1)),
        axis=-1,
    )
    return (grad_query.reshape(row_count, queries.shape[1], -1), joined)


def head_delta(grad_ctx, attended):
    return jnp.einsum("rqhe,rhqe->rhq", split_heads(grad_ctx).astype(jnp.float32), attended)


def spread_matrix(matrix, row_split, block_count):
    first, second = matrix.shape
    tiles = matrix.reshape(row_split, first // row_split, block_count, second // block_count)
    return jnp.transpose(tiles, (0, 2, 1, 3)).reshape(
        row_split * block_count, first // row_split, second // block_count
    )


def spread_gain(vector, row_split, block_count):
    tiles = vector.reshape(row_split, 1, vector.shape[0] // row_split)
    return jnp.broadcast_to(tiles, (row_split, block_count, vector.shape[0] // row_split)).reshape(
        row_split * block_count, vector.shape[0] // row_split
    )


def local_any(
    inputs,
    encoded,
    cotangent,
    dec_seg,
    pass_doc,
    enc_mask,
    self_query,
    self_key,
    self_value,
    self_output,
    cross_query,
    cross_key,
    cross_value,
    cross_output,
    feed_in,
    feed_out,
    gain_self,
    gain_cross,
    gain_ff,
):
    row_count, tok_shard, width = inputs.shape
    enc_shard = encoded.shape[1]
    block_count = lax.axis_size("blk")
    row_split = lax.axis_size("rows")
    block_ids = jnp.arange(block_count)
    query_places = lax.axis_index("blk") * tok_shard + jnp.arange(tok_shard)
    start_state = empty_state(row_count, tok_shard)
    residual = inputs.astype(jnp.float32)
    normed_self = rms_norm(residual, gain_self).astype(jnp.bfloat16)
    self_queries = project(normed_self, self_query).astype(jnp.bfloat16)
    self_keys = project(normed_self, self_key).astype(jnp.bfloat16)
    self_values = project(normed_self, self_value).astype(jnp.bfloat16)
    piece_keys = lax.all_gather(self_keys, "blk", axis=1, tiled=True)
    piece_values = lax.all_gather(self_values, "blk", axis=1, tiled=True)
    piece_segs = lax.all_gather(dec_seg, "blk", axis=1, tiled=True)
    key_places = jnp.arange(piece_keys.shape[1])
    allowed = (dec_seg[:, :, None] == piece_segs[:, None, :]) & (
        key_places[None, None, :] <= query_places[None, :, None]
    )
    self_attn, self_lse = finish(
        online_block(start_state, self_queries, piece_keys, piece_values, allowed)
    )
    self_context = join_heads(self_attn).astype(jnp.bfloat16)
    after_self = residual + project(self_context, self_output)
    normed_cross = rms_norm(after_self, gain_cross).astype(jnp.bfloat16)
    cross_queries = project(normed_cross, cross_query).astype(jnp.bfloat16)
    cross_keys = project(encoded, cross_key).astype(jnp.bfloat16)
    cross_values = project(encoded, cross_value).astype(jnp.bfloat16)
    key_docs = jnp.where(enc_mask == 1, jnp.repeat(pass_doc, PLEN, axis=1), -1)
    piece_keys = lax.all_gather(cross_keys, "blk", axis=1, tiled=True)
    piece_values = lax.all_gather(cross_values, "blk", axis=1, tiled=True)
    piece_docs = lax.all_gather(key_docs, "blk", axis=1, tiled=True)
    allowed = dec_seg[:, :, None] == piece_docs[:, None, :]
    cross_attn, cross_lse = finish(
        online_block(start_state, cross_queries, piece_keys, piece_values, allowed)
    )
    cross_context = join_heads(cross_attn).astype(jnp.bfloat16)
    after_cross = after_self + project(cross_context, cross_output)
    normed_ff = rms_norm(after_cross, gain_ff).astype(jnp.bfloat16)
    before_act = project(normed_ff, feed_in)
    hidden = jax.nn.gelu(before_act).astype(jnp.bfloat16)
    output = (after_cross + project(hidden, feed_out)).astype(jnp.bfloat16)
    grad_feed_out = weight_grad(hidden, cotangent)
    grad_hidden = back_project(cotangent, feed_out)
    _, gelu_back = jax.vjp(jax.nn.gelu, before_act)
    grad_before = gelu_back(grad_hidden)[0].astype(jnp.bfloat16)
    grad_feed_in = weight_grad(normed_ff, grad_before)
    grad_cross_res, grad_gain_ff = norm_back(
        after_cross, gain_ff, back_project(grad_before, feed_in)
    )
    grad_cross_res = cotangent.astype(jnp.float32) + grad_cross_res
    cross_branch = grad_cross_res.astype(jnp.bfloat16)
    grad_cross_output = weight_grad(cross_context, cross_branch)
    grad_cross_ctx = back_project(cross_branch, cross_output).astype(jnp.bfloat16)
    cross_delta = head_delta(grad_cross_ctx, cross_attn)
    all_keys, all_values, all_docs = (
        lax.all_gather(cross_keys, "blk", axis=1, tiled=True),
        lax.all_gather(cross_values, "blk", axis=1, tiled=True),
        lax.all_gather(key_docs, "blk", axis=1, tiled=True),
    )

    def passage_step(running, block_index):
        offset = block_index * enc_shard
        piece_keys = lax.dynamic_slice_in_dim(all_keys, offset, enc_shard, 1)
        piece_values = lax.dynamic_slice_in_dim(all_values, offset, enc_shard, 1)
        piece_docs = lax.dynamic_slice_in_dim(all_docs, offset, enc_shard, 1)
        allowed = dec_seg[:, :, None] == piece_docs[:, None, :]
        grad_query, grad_kv = grad_pair(
            cross_queries, grad_cross_ctx, cross_lse, cross_delta, piece_keys, piece_values, allowed
        )
        return (running + grad_query, grad_kv)

    grad_cross_q, key_terms = lax.scan(
        passage_step, jnp.zeros((row_count, tok_shard, width), jnp.float32), block_ids
    )
    grad_cross_kv = lax.psum_scatter(
        key_terms.astype(jnp.bfloat16), "blk", scatter_dimension=0, tiled=True
    ).astype(jnp.float32)[0]
    low_cross_q = grad_cross_q.astype(jnp.bfloat16)
    low_cross_k = grad_cross_kv[..., :width].astype(jnp.bfloat16)
    low_cross_v = grad_cross_kv[..., width:].astype(jnp.bfloat16)
    grad_cross_query = weight_grad(normed_cross, low_cross_q)
    grad_cross_key = weight_grad(encoded, low_cross_k)
    grad_cross_value = weight_grad(encoded, low_cross_v)
    encoded_grad = back_project(low_cross_k, cross_key) + back_project(low_cross_v, cross_value)
    grad_self_res, grad_gain_cross = norm_back(
        after_self, gain_cross, back_project(low_cross_q, cross_query)
    )
    grad_self_res = grad_cross_res + grad_self_res
    self_branch = grad_self_res.astype(jnp.bfloat16)
    grad_self_output = weight_grad(self_context, self_branch)
    grad_self_ctx = back_project(self_branch, self_output).astype(jnp.bfloat16)
    self_delta = head_delta(grad_self_ctx, self_attn)
    all_self_keys, all_self_values, all_self_segs = (
        lax.all_gather(self_keys, "blk", axis=1, tiled=True),
        lax.all_gather(self_values, "blk", axis=1, tiled=True),
        lax.all_gather(dec_seg, "blk", axis=1, tiled=True),
    )

    def self_step(running, block_index):
        offset = block_index * tok_shard
        piece_keys = lax.dynamic_slice_in_dim(all_self_keys, offset, tok_shard, 1)
        piece_values = lax.dynamic_slice_in_dim(all_self_values, offset, tok_shard, 1)
        piece_segs = lax.dynamic_slice_in_dim(all_self_segs, offset, tok_shard, 1)
        key_places = offset + jnp.arange(tok_shard)
        allowed = (dec_seg[:, :, None] == piece_segs[:, None, :]) & (
            key_places[None, None, :] <= query_places[None, :, None]
        )
        grad_query, grad_kv = grad_pair(
            self_queries, grad_self_ctx, self_lse, self_delta, piece_keys, piece_values, allowed
        )
        return (running + grad_query, grad_kv)

    grad_self_q, self_terms = lax.scan(
        self_step, jnp.zeros((row_count, tok_shard, width), jnp.float32), block_ids
    )
    grad_self_kv = lax.psum_scatter(
        self_terms.astype(jnp.bfloat16), "blk", scatter_dimension=0, tiled=True
    ).astype(jnp.float32)[0]
    low_self_q = grad_self_q.astype(jnp.bfloat16)
    low_self_k = grad_self_kv[..., :width].astype(jnp.bfloat16)
    low_self_v = grad_self_kv[..., width:].astype(jnp.bfloat16)
    grad_self_query = weight_grad(normed_self, low_self_q)
    grad_self_key = weight_grad(normed_self, low_self_k)
    grad_self_value = weight_grad(normed_self, low_self_v)
    grad_normed = (
        back_project(low_self_q, self_query)
        + back_project(low_self_k, self_key)
        + back_project(low_self_v, self_value)
    )
    grad_first, grad_gain_self = norm_back(residual, gain_self, grad_normed)
    input_grad = grad_self_res + grad_first
    matrices = (
        grad_self_query,
        grad_self_key,
        grad_self_value,
        grad_self_output,
        grad_cross_query,
        grad_cross_key,
        grad_cross_value,
        grad_cross_output,
        grad_feed_in,
        grad_feed_out,
    )
    spread_mats = tuple((spread_matrix(matrix, row_split, block_count) for matrix in matrices))
    spread_gains = tuple(
        (
            spread_gain(vector, row_split, block_count)
            for vector in (grad_gain_self, grad_gain_cross, grad_gain_ff)
        )
    )
    summed = (
        lax.psum_scatter(spread_mats[0], ("rows", "blk"), scatter_dimension=0, tiled=True),
        lax.psum_scatter(spread_mats[1], ("rows", "blk"), scatter_dimension=0, tiled=True),
        lax.psum_scatter(spread_mats[2], ("rows", "blk"), scatter_dimension=0, tiled=True),
        lax.psum_scatter(spread_mats[3], ("rows", "blk"), scatter_dimension=0, tiled=True),
        lax.psum_scatter(spread_mats[4], ("rows", "blk"), scatter_dimension=0, tiled=True),
        lax.psum_scatter(spread_mats[5], ("rows", "blk"), scatter_dimension=0, tiled=True),
        lax.psum_scatter(spread_mats[6], ("rows", "blk"), scatter_dimension=0, tiled=True),
        lax.psum_scatter(spread_mats[7], ("rows", "blk"), scatter_dimension=0, tiled=True),
        lax.psum_scatter(spread_mats[8], ("rows", "blk"), scatter_dimension=0, tiled=True),
        lax.psum_scatter(spread_mats[9], ("rows", "blk"), scatter_dimension=0, tiled=True),
        lax.psum_scatter(spread_gains[0], ("rows", "blk"), scatter_dimension=0, tiled=True),
        lax.psum_scatter(spread_gains[1], ("rows", "blk"), scatter_dimension=0, tiled=True),
        lax.psum_scatter(spread_gains[2], ("rows", "blk"), scatter_dimension=0, tiled=True),
    )
    return (
        output,
        input_grad,
        encoded_grad,
        summed[0][0],
        summed[1][0],
        summed[2][0],
        summed[3][0],
        summed[4][0],
        summed[5][0],
        summed[6][0],
        summed[7][0],
        summed[8][0],
        summed[9][0],
        summed[10][0],
        summed[11][0],
        summed[12][0],
    )


BF16 = jnp.bfloat16
F32 = jnp.float32
LANES = 128
HALF = 2 * LANES + LANES
CORE_SWAP = ((0, 1), (1, 0), (2, 3), (3, 2))
CHIP_SWAP = ((0, 2), (2, 0), (1, 3), (3, 1))


def dot_nn(left, right):
    return jnp.dot(left, right, preferred_element_type=F32)


def dot_nt(left, right):
    return lax.dot_general(left, right, (((1,), (1,)), ((), ())), preferred_element_type=F32)


def dot_tn(left, right):
    return lax.dot_general(left, right, (((0,), (0,)), ((), ())), preferred_element_type=F32)


def whole(array):
    rank = len(array.shape)
    return pl.BlockSpec(array.shape, lambda *_: (0,) * rank)


def struct(shape, dtype):
    return jax.ShapeDtypeStruct(shape, dtype)


def run_kernel(name, body, scalars, args, in_specs, outs, out_specs, grid=(1,), scratch=(), flops=0):
    moved = sum(a.size * a.dtype.itemsize for a in args)
    moved += sum(o.size * o.dtype.itemsize for o in outs)
    return pl.pallas_call(
        body,
        grid_spec=pltpu.PrefetchScalarGridSpec(
            num_scalar_prefetch=1,
            grid=grid,
            in_specs=list(in_specs),
            out_specs=list(out_specs),
            scratch_shapes=list(scratch),
        ),
        out_shape=list(outs),
        compiler_params=pltpu.CompilerParams(vmem_limit_bytes=58 << 20),
        cost_estimate=pl.CostEstimate(flops=int(flops), bytes_accessed=int(moved), transcendentals=0),
        name=name,
    )(scalars, *args)


def unit_norm(values):
    scale = lax.rsqrt(jnp.mean(values * values, axis=-1, keepdims=True) + 1e-06)
    return (values * scale, scale)


def norm_pull(values, gain_vec, grad_out):
    normal, scale = unit_norm(values)
    scaled = grad_out * gain_vec
    inner = jnp.mean(scaled * normal, axis=-1, keepdims=True)
    return (scale * (scaled - normal * inner), jnp.sum(grad_out * normal, axis=0, keepdims=True))


def projections(name, place, mine, other, gain_vec, weights, scales):
    tok, width = mine.shape
    count = len(weights)

    def body(s, mine_ref, other_ref, gain_ref, *refs):
        weight_refs, normed_ref, out_refs = refs[:count], refs[count], refs[count + 1 :]
        for source, part in ((mine_ref, s[0]), (other_ref, 1 - s[0])):
            rows = pl.ds(pl.multiple_of(part * tok, tok), tok)
            normed = (unit_norm(source[...].astype(F32))[0] * gain_ref[...]).astype(BF16)
            normed_ref[rows, :] = normed
            for weight_ref, out_ref, scale in zip(weight_refs, out_refs, scales):
                out_ref[rows, :] = (dot_nn(normed, weight_ref[...]) * scale).astype(BF16)

    columns = pl.BlockSpec((width, HALF), lambda _, s: (0, s[0]))
    outs = [struct((2 * tok, width), BF16)] + [struct((2 * tok, HALF), BF16)] * count
    return run_kernel(
        name,
        body,
        place,
        (mine, other, gain_vec, *weights),
        [whole(mine), whole(other), whole(gain_vec)] + [columns] * count,
        outs,
        [whole(o) for o in outs],
        flops=4 * tok * width * HALF * count,
    )


def passage_pair(place, first, second, key_weight, value_weight):
    enc, width = first.shape

    def body(s, first_ref, second_ref, key_w_ref, value_w_ref, key_ref, value_ref):
        for at, source in enumerate((first_ref, second_ref)):
            rows = pl.ds(at * enc, enc)
            key_ref[rows, :] = dot_nn(source[...], key_w_ref[...]).astype(BF16)
            value_ref[rows, :] = dot_nn(source[...], value_w_ref[...]).astype(BF16)

    args = (first, second, key_weight, value_weight)
    outs = [struct((2 * enc, width), BF16)] * 2
    return run_kernel(
        "passage_pair",
        body,
        place,
        args,
        [whole(a) for a in args],
        outs,
        [whole(o) for o in outs],
        flops=8 * enc * width * width,
    )


def head_lanes():
    lane = lax.broadcasted_iota(jnp.int32, (1, LANES), 1)
    return (lane, (lane < HEAD_DIM, lane >= HEAD_DIM))


def only(keep, values):
    return jnp.where(keep, values, jnp.zeros_like(values))


def soft_block(queries, marks, keys, values, causal):
    lane, masks = head_lanes()
    rows, cols = queries.shape[0], keys.shape[0]
    attended, sums = ([], [])
    for keep in masks:
        scores = dot_nt(jnp.concatenate([only(keep, queries), marks], axis=1), keys)
        if causal:
            at_row = lax.broadcasted_iota(jnp.int32, (rows, rows), 0)
            at_col = lax.broadcasted_iota(jnp.int32, (rows, rows), 1)
            last = jnp.where(at_col <= at_row, scores[:, cols - rows :], NEG_FILL)
            scores = last if cols == rows else jnp.concatenate([scores[:, : cols - rows], last], axis=1)
        top = jnp.max(scores, axis=1, keepdims=True)
        weights = jnp.exp(scores - top)
        total = jnp.sum(weights, axis=1, keepdims=True)
        attended.append(dot_nn(weights.astype(BF16), values) / total)
        sums.append(top + jnp.log(total))
    return (jnp.where(masks[0], *attended), jnp.where(masks[0], *sums))


def three_parts(lane, column, base):
    high = column.astype(BF16)
    rest = column - high.astype(F32)
    middle = rest.astype(BF16)
    low = (rest - middle.astype(F32)).astype(BF16)
    out = jnp.where(lane == 3, -high, base)
    out = jnp.where(lane == 4, -middle, out)
    return jnp.where(lane == 5, -low, out)


def pull_block(queries, marks, keys, key_marks, values, grads, attended, sums, causal):
    lane, masks = head_lanes()
    rows, cols = queries.shape[0], keys.shape[0]
    wide_keys = jnp.concatenate([keys, key_marks], axis=1)
    ones = jnp.where((lane >= 3) & (lane < 6), 1.0, 0.0).astype(BF16)
    wide_values = jnp.concatenate([values, jnp.broadcast_to(ones, (cols, LANES))], axis=1)
    product = grads.astype(F32) * attended
    flipped = keys.T
    grad_queries = []
    grad_keys = grad_values = None
    for at, keep in enumerate(masks):
        query, grad = (only(keep, queries), only(keep, grads))
        delta = jnp.sum(jnp.where(keep, product, 0.0), axis=1, keepdims=True)
        log_sum = sums[:, HEAD_DIM * at : HEAD_DIM * at + 1]
        wide_query = jnp.concatenate([query, three_parts(lane, log_sum, marks)], axis=1)
        wide_grad = jnp.concatenate([grad, three_parts(lane, delta, jnp.zeros_like(marks))], axis=1)
        probs = jnp.exp(dot_nt(wide_keys, wide_query))
        if causal:
            at_row = lax.broadcasted_iota(jnp.int32, (rows, rows), 0)
            at_col = lax.broadcasted_iota(jnp.int32, (rows, rows), 1)
            last = jnp.where(at_row <= at_col, probs[cols - rows :, :], 0.0)
            probs = last if cols == rows else jnp.concatenate([probs[: cols - rows, :], last], axis=0)
        grad_scores = (probs * dot_nt(wide_values, wide_grad)).astype(BF16)
        grad_queries.append(dot_nn(flipped, grad_scores))
        key_part = dot_nn(grad_scores, query)
        value_part = dot_nn(probs.astype(BF16), grad)
        grad_keys = key_part if at == 0 else grad_keys + key_part
        grad_values = value_part if at == 0 else grad_values + value_part
    sub = lax.broadcasted_iota(jnp.int32, (LANES, 1), 0)
    return (jnp.where(sub < HEAD_DIM, *grad_queries).T * SCALE, grad_keys, grad_values)


def pair_columns(array):
    return pl.BlockSpec((array.shape[0], LANES), lambda p, _: (0, p))


def near_attention(place, queries, keys, values, marks, key_marks):
    both, width = queries.shape
    tok = both // 2

    def body(s, q_ref, k_ref, v_ref, m_ref, km_ref, out_ref, sum_ref):
        for at in (0, 1):
            rows, seen = (pl.ds(at * tok, tok), pl.ds(0, (at + 1) * tok))
            wide = jnp.concatenate([k_ref[seen, :], km_ref[seen, :]], axis=1)
            out_ref[rows, :], sum_ref[rows, :] = soft_block(q_ref[rows, :], m_ref[rows, :], wide, v_ref[seen, :], True)

    args = (queries, keys, values, marks, key_marks)
    outs = [struct((both, width), F32)] * 2
    return run_kernel(
        "near_attention",
        body,
        place,
        args,
        [pair_columns(a) for a in args[:3]] + [whole(a) for a in args[3:]],
        outs,
        [pair_columns(o) for o in outs],
        grid=(width // LANES,),
        flops=both * both * 0.75 * 8 * 2 * width,
    )


def far_attention(place, queries, keys, values, marks, key_marks, near_out, near_sum):
    both, width = queries.shape
    tok = both // 2

    def body(s, q_ref, k_ref, v_ref, m_ref, km_ref, no_ref, ns_ref, out_ref, sum_ref, keep_ref, send_ref):
        def write(at, out, log_sum):
            rows = pl.ds(at * tok, tok)
            out_ref[rows, :] = out
            sum_ref[rows, :] = log_sum

            @pl.when(s[0] == at)
            def _():
                keep_ref[...] = out.astype(BF16)

            @pl.when(s[0] != at)
            def _():
                send_ref[...] = out.astype(BF16)

        @pl.when(s[1] == 0)
        def _():
            for at in (0, 1):
                rows = pl.ds(at * tok, tok)
                write(at, no_ref[rows, :], ns_ref[rows, :])

        @pl.when(s[1] != 0)
        def _():
            wide = jnp.concatenate([k_ref[...], km_ref[...]], axis=1)
            for at in (0, 1):
                rows = pl.ds(at * tok, tok)
                out, log_sum = soft_block(q_ref[rows, :], m_ref[rows, :], wide, v_ref[...], False)
                near_log = ns_ref[rows, :]
                top = jnp.maximum(near_log, log_sum)
                near_part, far_part = (jnp.exp(near_log - top), jnp.exp(log_sum - top))
                total = near_part + far_part
                write(at, (no_ref[rows, :] * near_part + out * far_part) / total, top + jnp.log(total))

    args = (queries, keys, values, marks, key_marks, near_out, near_sum)
    outs = [struct((both, width), F32)] * 2 + [struct((tok, width), BF16)] * 2
    columns = [pair_columns(a) for a in args]
    columns[3], columns[4] = whole(marks), whole(key_marks)
    return run_kernel(
        "far_attention",
        body,
        place,
        args,
        columns,
        outs,
        [pair_columns(o) for o in outs],
        grid=(width // LANES,),
        flops=both * both * 8 * 2 * width,
    )


def self_pull(name, place, near, queries, keys, values, marks, key_marks, grad_keep, grad_recv, attended, sums, carried):
    both, width = queries.shape
    tok = both // 2

    def body(s, q_ref, k_ref, v_ref, m_ref, km_ref, gk_ref, gr_ref, at_ref, ls_ref, ca_ref, dq_ref, dk_ref, dv_ref, sum_k, sum_v):
        def work():
            for at in (0, 1):
                rows = pl.ds(at * tok, tok)
                count = (at + 1) * tok if near else both
                seen = pl.ds(0, count)
                grads = jnp.where(s[0] == at, gk_ref[...], gr_ref[...])
                grad_q, grad_k, grad_v = pull_block(
                    q_ref[rows, :], m_ref[rows, :], k_ref[seen, :], km_ref[seen, :], v_ref[seen, :], grads,
                    at_ref[rows, :], ls_ref[rows, :], near,
                )
                if near:
                    dq_ref[rows, :] = (grad_q + ca_ref[rows, :]).astype(BF16)
                else:
                    dq_ref[rows, :] = grad_q
                if at == 0:
                    sum_k[seen, :] = grad_k
                    sum_v[seen, :] = grad_v
                    if count < both:
                        sum_k[pl.ds(count, both - count), :] = jnp.zeros((both - count, LANES), F32)
                        sum_v[pl.ds(count, both - count), :] = jnp.zeros((both - count, LANES), F32)
                else:
                    dk_ref[...] = (sum_k[...] + grad_k).astype(BF16)
                    dv_ref[...] = (sum_v[...] + grad_v).astype(BF16)

        if near:
            work()
        else:
            pl.when(s[1] != 0)(work)

            @pl.when(s[1] == 0)
            def _():
                for ref in (dq_ref, dk_ref, dv_ref):
                    ref[...] = jnp.zeros_like(ref)

    args = (queries, keys, values, marks, key_marks, grad_keep, grad_recv, attended, sums, carried)
    specs = [pair_columns(a) for a in args]
    specs[3], specs[4] = whole(marks), whole(key_marks)
    if not near:
        specs[9] = whole(carried)
    outs = [struct((both, width), BF16 if near else F32)] + [struct((both, width), BF16)] * 2
    return run_kernel(
        name,
        body,
        place,
        args,
        specs,
        outs,
        [pair_columns(o) for o in outs],
        grid=(width // LANES,),
        scratch=[pltpu.VMEM((both, LANES), F32)] * 2,
        flops=both * both * (0.75 if near else 1.0) * 20 * 2 * width,
    )


def gather_slots(s, enc, target, first_ref, second_ref):
    for at in range(4):
        slot = s[at]
        rows = pl.ds(at * enc, enc)

        @pl.when(slot < 2)
        def _():
            target[rows, :] = first_ref[pl.ds(pl.multiple_of(slot * enc, enc), enc), :]

        @pl.when(slot >= 2)
        def _():
            target[rows, :] = second_ref[pl.ds(pl.multiple_of((slot - 2) * enc, enc), enc), :]


def by_count(s, work):
    pl.when(s[4] <= 2)(lambda: work(2))
    pl.when(s[4] == 3)(lambda: work(3))
    pl.when(s[4] >= 4)(lambda: work(4))


def cross_attention(needed, queries, keys, values, marks, key_marks):
    tok, width = queries.shape
    enc = keys[0].shape[0] // 2

    def body(s, q_ref, k0_ref, k1_ref, v0_ref, v1_ref, m_ref, km0_ref, km1_ref, ctx_ref, out_ref, sum_ref, all_k, all_v):
        keep = pl.ds(0, LANES)
        gather_slots(s, enc, all_k.at[:, keep], k0_ref, k1_ref)
        gather_slots(s, enc, all_v, v0_ref, v1_ref)

        @pl.when(pl.program_id(0) == 0)
        def _():
            gather_slots(s, enc, all_k.at[:, pl.ds(LANES, LANES)], km0_ref, km1_ref)

        def work(count):
            seen = pl.ds(0, count * enc)
            out, log_sum = soft_block(q_ref[...], m_ref[...], all_k[seen, :], all_v[seen, :], False)
            ctx_ref[...] = out.astype(BF16)
            out_ref[...] = out
            sum_ref[...] = log_sum

        by_count(s, work)

    args = (queries, *keys, *values, marks, *key_marks)
    outs = [struct((tok, width), BF16)] + [struct((tok, width), F32)] * 2
    return run_kernel(
        "cross_attention",
        body,
        needed,
        args,
        [pair_columns(a) for a in args[:5]] + [whole(a) for a in args[5:]],
        outs,
        [pair_columns(o) for o in outs],
        grid=(width // LANES,),
        scratch=[pltpu.VMEM((4 * enc, 2 * LANES), BF16), pltpu.VMEM((4 * enc, LANES), BF16)],
        flops=tok * 2.5 * enc * 8 * 2 * width,
    )


def cross_pull(needed, queries, keys, values, marks, key_marks, grads, attended, sums):
    tok, width = queries.shape
    enc = keys[0].shape[0] // 2

    def body(s, q_ref, k0_ref, k1_ref, v0_ref, v1_ref, m_ref, km0_ref, km1_ref, g_ref, at_ref, ls_ref, dq_ref, dk_ref, dv_ref, all_k, all_v, all_m):
        gather_slots(s, enc, all_k, k0_ref, k1_ref)
        gather_slots(s, enc, all_v, v0_ref, v1_ref)

        @pl.when(pl.program_id(0) == 0)
        def _():
            gather_slots(s, enc, all_m, km0_ref, km1_ref)

        def work(count):
            seen = pl.ds(0, count * enc)
            grad_q, grad_k, grad_v = pull_block(
                q_ref[...], m_ref[...], all_k[seen, :], all_m[seen, :], all_v[seen, :], g_ref[...], at_ref[...],
                ls_ref[...], False,
            )
            dq_ref[...] = grad_q.astype(BF16)
            low_k, low_v = (grad_k.astype(BF16), grad_v.astype(BF16))
            for at in range(4):
                rows = pl.ds(pl.multiple_of(s[at] * enc, enc), enc)
                if at < count:
                    dk_ref[rows, :] = low_k[at * enc : (at + 1) * enc, :]
                    dv_ref[rows, :] = low_v[at * enc : (at + 1) * enc, :]
                else:
                    dk_ref[rows, :] = jnp.zeros((enc, LANES), BF16)
                    dv_ref[rows, :] = jnp.zeros((enc, LANES), BF16)

        by_count(s, work)

    args = (queries, *keys, *values, marks, *key_marks, grads, attended, sums)
    specs = [pair_columns(a) for a in args]
    for at in (5, 6, 7):
        specs[at] = whole(args[at])
    outs = [struct((tok, width), BF16)] + [struct((4 * enc, width), BF16)] * 2
    return run_kernel(
        "cross_pull",
        body,
        needed,
        args,
        specs,
        outs,
        [pair_columns(o) for o in outs],
        grid=(width // LANES,),
        scratch=[pltpu.VMEM((4 * enc, LANES), BF16)] * 3,
        flops=tok * 2.5 * enc * 20 * 2 * width,
    )


def after_self_attention(place, inputs, ctx_keep, ctx_recv, out_weight, gain_vec, query_weight):
    tok, width = inputs.shape

    def body(s, in_ref, keep_ref, recv_ref, wk_ref, wr_ref, gain_ref, wq_ref, x_ref, h_ref, q_ref, ctx_ref):
        total = dot_nn(keep_ref[...], wk_ref[...]) + dot_nn(recv_ref[...], wr_ref[...])
        residual = in_ref[...].astype(F32) + total
        x_ref[...] = residual
        normed = (unit_norm(residual)[0] * gain_ref[...]).astype(BF16)
        h_ref[...] = normed
        q_ref[...] = (dot_nn(normed, wq_ref[...]) * SCALE).astype(BF16)
        ctx_ref[:, pl.ds(pl.multiple_of(s[0] * HALF, LANES), HALF)] = keep_ref[...]
        ctx_ref[:, pl.ds(pl.multiple_of((1 - s[0]) * HALF, LANES), HALF)] = recv_ref[...]

    args = (inputs, ctx_keep, ctx_recv, out_weight, out_weight, gain_vec, query_weight)
    specs = [whole(a) for a in args]
    specs[3] = pl.BlockSpec((HALF, width), lambda _, s: (s[0], 0))
    specs[4] = pl.BlockSpec((HALF, width), lambda _, s: (1 - s[0], 0))
    outs = [struct((tok, width), F32)] + [struct((tok, width), BF16)] * 3
    return run_kernel(
        "after_self_attention", body, place, args, specs, outs, [whole(o) for o in outs], flops=4 * tok * width * width
    )


def split_rows(total, s, keep_ref, send_ref, write, groups, rows):
    for at in range(groups):
        for target, half in ((keep_ref, s[0]), (send_ref, 1 - s[0])):
            first = pl.multiple_of(at * 2 * rows + half * rows, 16)
            write(target, at, total[pl.ds(first, rows), :].astype(BF16))


def feed_forward(place, residual, context, out_weight, gain_vec, feed_in, feed_out, cotangent):
    tok, width = residual.shape
    hidden_width = feed_in.shape[1]
    steps = 4
    chunk = hidden_width // steps
    rows_in = width // 16
    rows_out = hidden_width // 16

    def body(
        s, x1_ref, ctx_ref, wo_ref, gain_ref, w1_ref, w2_ref, g_ref,
        out_ref, dx_ref, low_ref, dctx_ref, gain_grad_ref, keep1, send1, keep2, send2,
        x2, normed, sum_out, sum_norm, total,
    ):
        step = pl.program_id(0)

        @pl.when(step == 0)
        def _():
            x2[...] = x1_ref[...] + dot_nn(ctx_ref[...], wo_ref[...])
            normed[...] = (unit_norm(x2[...])[0] * gain_ref[...]).astype(BF16)
            sum_out[...] = jnp.zeros_like(sum_out)
            sum_norm[...] = jnp.zeros_like(sum_norm)

        w1, w2, grad = (w1_ref[...], w2_ref[...], g_ref[...])
        pre = dot_nn(normed[...], w1)
        root = 0.7978845608028654
        bend = 0.044715
        square = pre * pre
        swing = jnp.tanh(root * (pre + bend * pre * square))
        hidden = (0.5 * pre * (1.0 + swing)).astype(BF16)
        sum_out[...] += dot_nn(hidden, w2)
        slope = 0.5 * (1.0 + swing) + 0.5 * pre * (1.0 - swing * swing) * (root * (1.0 + 3.0 * bend * square))
        grad_pre = (dot_nt(grad, w2) * slope).astype(BF16)
        sum_norm[...] += dot_nt(grad_pre, w1)
        total[...] = dot_tn(normed[...], grad_pre)

        def write_in(target, at, values):
            deep, far = (at // 2, at % 2)
            for unit in range(2):
                target[0, far, deep % 2, deep // 2, unit] = values[:, unit * HALF : (unit + 1) * HALF]

        split_rows(total, s, keep1, send1, write_in, 8, rows_in)
        total[...] = dot_tn(hidden, grad)

        def write_out(target, at, values):
            for side in range(2):
                target[at, 0, 0, side] = values[:, side * HALF : (side + 1) * HALF]

        split_rows(total, s, keep2, send2, write_out, 2, rows_out)

        @pl.when(step == steps - 1)
        def _():
            out_ref[...] = (x2[...] + sum_out[...]).astype(BF16)
            back, gain_grad_ref[...] = norm_pull(x2[...], gain_ref[...], sum_norm[...])
            grad_x = grad.astype(F32) + back
            dx_ref[...] = grad_x
            low = grad_x.astype(BF16)
            low_ref[...] = low
            dctx_ref[...] = dot_nt(low, wo_ref[...]).astype(BF16)

    args = (residual, context, out_weight, gain_vec, feed_in, feed_out, cotangent)
    specs = [whole(a) for a in args]
    specs[4] = pl.BlockSpec((width, chunk), lambda c, _: (0, c))
    specs[5] = pl.BlockSpec((chunk, width), lambda c, _: (c, 0))
    outs = [
        struct((tok, width), BF16),
        struct((tok, width), F32),
        struct((tok, width), BF16),
        struct((tok, width), BF16),
        struct((1, width), F32),
        struct((2, 2, 2, 2, 4, rows_in, HALF), BF16),
        struct((2, 2, 2, 2, 4, rows_in, HALF), BF16),
        struct((2, 2, 2, 2, rows_out, HALF), BF16),
        struct((2, 2, 2, 2, rows_out, HALF), BF16),
    ]
    out_specs = [whole(o) for o in outs]
    in_block = pl.BlockSpec((1, 2, 2, 2, 2, rows_in, HALF), lambda c, _: (c // 2, 0, 0, 0, c % 2, 0, 0))
    out_block = pl.BlockSpec((2, 1, 1, 2, rows_out, HALF), lambda c, _: (0, c % 2, c // 2, 0, 0, 0))
    out_specs[5] = out_specs[6] = in_block
    out_specs[7] = out_specs[8] = out_block
    return run_kernel(
        "feed_forward",
        body,
        place,
        args,
        specs,
        outs,
        out_specs,
        grid=(steps,),
        scratch=[
            pltpu.VMEM((tok, width), F32),
            pltpu.VMEM((tok, width), BF16),
            pltpu.VMEM((tok, width), F32),
            pltpu.VMEM((tok, width), F32),
            pltpu.VMEM((width, width), F32),
        ],
        flops=12 * tok * width * hidden_width + 4 * tok * width * width,
    )


def after_cross_pull(place, residual, grad_res, grad_query, query_weight, gain_vec, out_weight):
    tok, width = residual.shape

    def body(s, x_ref, dx_ref, dq_ref, wq_ref, gain_ref, wk_ref, wr_ref, dx1_ref, low_ref, gain_grad_ref, keep_ref, send_ref):
        back, gain_grad_ref[...] = norm_pull(x_ref[...], gain_ref[...], dot_nt(dq_ref[...], wq_ref[...]))
        grad_x = dx_ref[...] + back
        dx1_ref[...] = grad_x
        low = grad_x.astype(BF16)
        low_ref[...] = low
        keep_ref[...] = dot_nt(low, wk_ref[...]).astype(BF16)
        send_ref[...] = dot_nt(low, wr_ref[...]).astype(BF16)

    args = (residual, grad_res, grad_query, query_weight, gain_vec, out_weight, out_weight)
    specs = [whole(a) for a in args]
    specs[5] = pl.BlockSpec((HALF, width), lambda _, s: (s[0], 0))
    specs[6] = pl.BlockSpec((HALF, width), lambda _, s: (1 - s[0], 0))
    outs = [struct((tok, width), F32), struct((tok, width), BF16), struct((1, width), F32)]
    outs += [struct((tok, HALF), BF16)] * 2
    return run_kernel(
        "after_cross_pull", body, place, args, specs, outs, [whole(o) for o in outs], flops=4 * tok * width * width
    )


def square_grads(name, place, pairs, columns, extra=None):
    width = pairs[0][0][0].shape[1]
    rows = width // 16
    sides = columns // HALF
    count = len(pairs)
    extra_rows = 0 if extra is None else 16
    lefts = [part for left, _ in pairs for part in left]
    rights = [part for _, right in pairs for part in right]
    at_left = [sum(len(left) for left, _ in pairs[:m]) for m in range(count)]
    at_right = [sum(len(right) for _, right in pairs[:m]) for m in range(count)]

    def body(s, *refs):
        left_refs, right_refs = refs[: len(lefts)], refs[len(lefts) : len(lefts) + len(rights)]
        rest = refs[len(lefts) + len(rights) :]
        if extra is not None:
            extra_ref, rest = rest[0], rest[1:]
        keep, send, total = rest
        for m, (left, right) in enumerate(pairs):
            value = None
            for a in range(len(left)):
                left_part = left_refs[at_left[m] + a][...]
                if len(right) == len(left):
                    right_part = right_refs[at_right[m] + a][...]
                else:
                    right_part = right_refs[at_right[m]][pl.ds(a * left_part.shape[0], left_part.shape[0]), :]
                part = dot_tn(left_part, right_part)
                value = part if value is None else value + part
            total[...] = value

            def write(target, at, values, m=m):
                deep, far = (at // 2, at % 2)
                for side in range(sides):
                    target[far, side, deep % 2, deep // 2, pl.ds(m * rows, rows), :] = values[
                        :, side * HALF : (side + 1) * HALF
                    ]

            split_rows(total, s, keep, send, write, 8, rows)
        if extra is not None:
            for at in range(8):
                deep, far = (at // 2, at % 2)
                row = lax.broadcasted_iota(jnp.int32, (extra_rows, 1), 0)
                value = jnp.where(row == 0, extra_ref[at : at + 1, :], 0.0).astype(BF16)
                for target in (keep, send):
                    for side in range(sides):
                        target[far, side, deep % 2, deep // 2, pl.ds(count * rows, extra_rows), :] = value

    args = (*lefts, *rights) + (() if extra is None else (extra,))
    outs = [struct((2, sides, 2, 2, count * rows + extra_rows, HALF), BF16)] * 2
    return run_kernel(
        name,
        body,
        place,
        args,
        [whole(a) for a in args],
        outs,
        [whole(o) for o in outs],
        scratch=[pltpu.VMEM((width, columns), F32)],
        flops=sum(2 * sum(p.shape[0] for p in left) * width * columns for left, _ in pairs),
    )


def passage_grads(place, grad_keys, grad_values, key_weight, value_weight):
    keys4, width = grad_keys.shape
    enc = keys4 // 4

    def body(s, dk_ref, dv_ref, wk_ref, wv_ref, keep_ref, send_ref):
        for slot in range(4):
            rows = pl.ds(slot * enc, enc)
            value = dot_nt(dk_ref[rows, :], wk_ref[...]) + dot_nt(dv_ref[rows, :], wv_ref[...])
            if slot % 2 == 0:
                keep_ref[slot // 2] = value
            else:
                send_ref[slot // 2] = value.astype(BF16)

    args = (grad_keys, grad_values, key_weight, value_weight)
    outs = [struct((2, enc, width), F32), struct((2, enc, width), BF16)]
    return run_kernel(
        "passage_grads", body, place, args, [whole(a) for a in args], outs, [whole(o) for o in outs],
        flops=4 * keys4 * width * width,
    )


def normed_grads(name, place, normed, gain_vec, grads, weights):
    both, width = normed.shape
    tok = both // 2
    count = len(grads)

    def body(s, h_ref, gain_ref, *refs):
        grad_refs, weight_refs = refs[:count], refs[count : 2 * count]
        keep_ref, send_ref, gain_grad_ref = refs[2 * count :]
        running = None
        for target, part in ((keep_ref, s[0]), (send_ref, 1 - s[0])):
            rows = pl.ds(pl.multiple_of(part * tok, tok), tok)
            value = None
            for grad_ref, weight_ref in zip(grad_refs, weight_refs):
                piece = dot_nt(grad_ref[rows, :], weight_ref[...])
                value = piece if value is None else value + piece
            target[...] = value.astype(BF16)
            inner = jnp.sum(value * h_ref[rows, :].astype(F32), axis=0, keepdims=True)
            running = inner if running is None else running + inner
        gain_grad_ref[...] = running / gain_ref[...]

    columns = pl.BlockSpec((width, HALF), lambda _, s: (0, s[0]))
    args = (normed, gain_vec, *grads, *weights)
    outs = [struct((tok, width), BF16)] * 2 + [struct((1, width), F32)]
    return run_kernel(
        name, body, place, args, [whole(a) for a in args[: 2 + count]] + [columns] * count, outs,
        [whole(o) for o in outs], flops=4 * tok * width * HALF * count,
    )


def last_pull(place, inputs, gain_vec, grad_res, parts):
    tok, width = inputs.shape

    def body(s, in_ref, gain_ref, dx_ref, *refs):
        part_refs, out_ref = refs[:-1], refs[-1]
        total = part_refs[0][...].astype(F32)
        for ref in part_refs[1:]:
            total = total + ref[...].astype(F32)
        out_ref[...] = dx_ref[...] + norm_pull(in_ref[...].astype(F32), gain_ref[...], total)[0]

    args = (inputs, gain_vec, grad_res, *parts)
    outs = [struct((tok, width), F32)]
    return run_kernel(
        "last_pull", body, place, args, [whole(a) for a in args], outs, [whole(outs[0])], flops=20 * tok * width
    )[0]


def add_split(half, keep, recv):
    rows = keep.shape[1]
    steps = 1
    while rows // steps > 512 and rows % (steps * 2) == 0 and (rows // (steps * 2)) % 16 == 0:
        steps *= 2
    tile = rows // steps

    def body(s, km_ref, rm_ref, ko_ref, ro_ref, keep_ref, send_ref):
        keep_ref[...] = (km_ref[0].astype(F32) + rm_ref[0].astype(F32)).astype(BF16)
        send_ref[...] = (ko_ref[0].astype(F32) + ro_ref[0].astype(F32)).astype(BF16)

    mine = pl.BlockSpec((1, tile, HALF), lambda i, s: (s[0], i, 0))
    other = pl.BlockSpec((1, tile, HALF), lambda i, s: (1 - s[0], i, 0))
    outs = [struct((rows, HALF), BF16)] * 2
    flat = pl.BlockSpec((tile, HALF), lambda i, s: (i, 0))
    return run_kernel(
        "add_split", body, half, (keep, recv, keep, recv), [mine, mine, other, other], outs, [flat, flat], grid=(steps,),
        flops=4 * rows * HALF,
    )


def sum_over(keep, recv, steps):
    for half, axis, pairs in steps:
        kept, send = add_split(half, keep.reshape(2, -1, HALF), recv.reshape(2, -1, HALF))
        keep, recv = (kept, lax.ppermute(send, axis, pairs))
    return keep.astype(F32) + recv.astype(F32)


def local_paired(
    inputs,
    encoded,
    cotangent,
    dec_seg,
    pass_doc,
    enc_mask,
    self_query,
    self_key,
    self_value,
    self_output,
    cross_query,
    cross_key,
    cross_value,
    cross_output,
    feed_in,
    feed_out,
    gain_self,
    gain_cross,
    gain_ff,
):
    inputs, encoded, cotangent = (inputs[0], encoded[0], cotangent[0])
    tok, width = inputs.shape
    enc = encoded.shape[0]
    blk, row = (lax.axis_index("blk"), lax.axis_index("rows"))
    core, chip = (blk % 2, blk // 2)
    y_at, z_low, z_high = (row % 2, (row // 2) % 2, row // 4)
    place = jnp.stack([core, chip]).astype(jnp.int32)
    gain_self, gain_cross, gain_ff = (g.reshape(1, width) for g in (gain_self, gain_cross, gain_ff))
    to_core = lambda array: lax.ppermute(array, "blk", CORE_SWAP)
    to_chip = lambda array: lax.ppermute(array, "blk", CHIP_SWAP)
    in_order = lambda mine, other: jnp.where(core == 0, jnp.concatenate([mine, other]), jnp.concatenate([other, mine]))

    def swap(distance):
        return tuple((at, at ^ distance) for at in range(8))

    one = lambda value: value.astype(jnp.int32).reshape(1)
    over_x = (one(chip), "blk", CHIP_SWAP)
    over_y = (one(y_at), "rows", swap(1))
    over_z = ((one(z_low), "rows", swap(2)), (one(z_high), "rows", swap(4)))

    docs = jnp.where(enc_mask[0] == 1, jnp.broadcast_to(pass_doc[0], (enc,)), -1)
    spare = 8 * LANES - tok - enc - 1
    labels = jnp.concatenate([dec_seg[0], docs, pass_doc[0], jnp.zeros((spare,), jnp.int32)]).reshape(8, LANES)
    labels_x = to_chip(labels)
    inputs_x = to_chip(inputs)
    encoded_x = to_chip(encoded)
    labels = jnp.concatenate([labels, labels_x])
    labels = jnp.concatenate([labels, to_core(labels)]).reshape(4, 8 * LANES)
    inputs_c = to_core(inputs)
    encoded_c = to_core(encoded)
    seg_own, seg_x, seg_c, seg_d = (labels[at, :tok] for at in range(4))
    docs_own, docs_x, docs_c, docs_d = (labels[at, tok : tok + enc] for at in range(4))

    lanes = jnp.arange(LANES)[None, :]
    query_marks = lambda seg: (seg[:, None] == lanes).astype(BF16)

    def key_marks(seg):
        closed = jnp.where(seg[:, None] != lanes, NEG_FILL, 0.0)
        return jnp.where(lanes < 3, closed, jnp.where(lanes < 6, 1.0, 0.0)).astype(BF16)

    seg_near, seg_far = (in_order(seg_own, seg_c), in_order(seg_x, seg_d))
    near_marks, near_keys_marks, far_keys_marks = (query_marks(seg_near), key_marks(seg_near), key_marks(seg_far))
    own_marks = query_marks(seg_own)
    doc_marks = (key_marks(jnp.concatenate([docs_own, docs_c])), key_marks(jnp.concatenate([docs_x, docs_d])))
    slot_docs = jnp.stack([labels[at, tok + enc] for at in (0, 2, 1, 3)])
    wanted = jnp.any(slot_docs[:, None] == seg_own[None, :], axis=1)
    count = jnp.sum(wanted.astype(jnp.int32))
    order = jnp.arange(4)
    ahead = (order[None, :] < order[:, None]).astype(jnp.int32)
    before = jnp.sum(ahead * wanted[None, :].astype(jnp.int32), axis=1)
    spot = jnp.where(wanted, before, count + order - before)
    listed = jnp.sum(jnp.where(spot[None, :] == order[:, None], order[None, :], 0), axis=1)
    needed = jnp.concatenate([listed, count[None]]).astype(jnp.int32)

    h1, sq, sk, sv = projections(
        "near_projections", place, inputs, inputs_c, gain_self, (self_query, self_key, self_value), (SCALE, 1.0, 1.0)
    )
    near_out, near_sum = near_attention(place, sq, sk, sv, near_marks, near_keys_marks)
    ck0, cv0 = passage_pair(place, encoded, encoded_c, cross_key, cross_value)
    inputs_d = to_core(inputs_x)
    encoded_d = to_core(encoded_x)
    h1_far, fk, fv = projections(
        "far_projections", place, inputs_x, inputs_d, gain_self, (self_key, self_value), (1.0, 1.0)
    )
    self_out, self_sum, ctx_keep, ctx_send = far_attention(
        place, sq, fk, fv, near_marks, far_keys_marks, near_out, near_sum
    )
    ck1, cv1 = passage_pair(place, encoded_x, encoded_d, cross_key, cross_value)
    x1, h2, cq, self_context = after_self_attention(
        place, inputs, ctx_keep, to_core(ctx_send), self_output, gain_cross, cross_query
    )
    cross_context, cross_out, cross_sum = cross_attention(needed, cq, (ck0, ck1), (cv0, cv1), own_marks, doc_marks)
    output, dx2, e2, d_cross, grad_gain_ff, keep1, send1, keep2, send2 = feed_forward(
        place, x1, cross_context, cross_output, gain_ff, feed_in, feed_out, cotangent
    )
    recv1, recv2 = (to_core(send1), to_core(send2))
    dcq, dck, dcv = cross_pull(
        needed, cq, (ck0, ck1), (cv0, cv1), own_marks, doc_marks, d_cross, cross_out, cross_sum
    )
    total1 = sum_over(keep1, recv1, (over_x, over_y) + over_z)
    total2 = sum_over(keep2, recv2, (over_y,) + over_z + (over_x,))
    dx1, e1, grad_gain_cross, ds_keep, ds_send = after_cross_pull(
        place, x1, dx2, dcq, cross_query, gain_cross, self_output
    )
    ds_recv = to_core(ds_send)
    dq_far, dk_far, dv_far = self_pull(
        "far_pull", place, False, sq, fk, fv, near_marks, far_keys_marks, ds_keep, ds_recv, self_out, self_sum,
        jnp.zeros((8, LANES), F32),
    )
    far_keep, far_send, gain_far = normed_grads(
        "far_normed_grads", place, h1_far, gain_self, (dk_far, dv_far), (self_key, self_value)
    )
    far_here = (far_keep.astype(F32) + to_core(far_send).astype(F32)).astype(BF16)
    from_far = to_chip(far_here)
    enc_keep, enc_send = passage_grads(place, dck, dcv, cross_key, cross_value)
    enc_sum = enc_keep + to_core(enc_send).astype(F32)
    encoded_grad = enc_sum[0] + to_chip(enc_sum[1].astype(BF16)).astype(F32)
    passages = (encoded, encoded_c, encoded_x, encoded_d)
    keep3, send3 = square_grads(
        "cross_grads",
        place,
        (
            ((cross_context,), (e2,)),
            ((h2,), (dcq,)),
            (passages, (dck,)),
            (passages, (dcv,)),
            ((self_context,), (e1,)),
        ),
        width,
    )
    total3 = sum_over(keep3, to_core(send3), (over_y, over_x) + over_z)
    dq, dk, dv = self_pull(
        "near_pull", place, True, sq, sk, sv, near_marks, near_keys_marks, ds_keep, ds_recv, self_out, self_sum, dq_far
    )
    near_keep, near_send, gain_near = normed_grads(
        "near_normed_grads", place, h1, gain_self, (dq, dk, dv), (self_query, self_key, self_value)
    )
    input_grad = last_pull(place, inputs, gain_self, dx1, (near_keep, to_core(near_send), from_far))
    gains = jnp.concatenate([gain_far + gain_near, grad_gain_cross, grad_gain_ff])
    gains = gains + to_core(gains)
    gains = jnp.transpose(gains.reshape(3, 8, width // 8), (1, 0, 2)).reshape(8, 3 * (width // 8))
    gains = jnp.pad(gains, ((0, 0), (0, HALF - gains.shape[1])))
    keep4, send4 = square_grads(
        "self_grads",
        place,
        (((h1,), (dq,)), ((h1, h1_far), (dk, dk_far)), ((h1, h1_far), (dv, dv_far))),
        HALF,
        gains,
    )
    recv4 = to_core(send4)
    here = chip == core
    keep4, send4 = (jnp.where(here, keep4, recv4), jnp.where(here, recv4, keep4))
    total4 = sum_over(keep4, to_chip(send4), (over_y,) + over_z)

    wide = total1.reshape(4, width // 16, HALF)
    wide_keep = lax.dynamic_slice_in_dim(wide, 2 * core, 2)
    wide_recv = to_core(lax.dynamic_slice_in_dim(wide, 2 * (1 - core), 2))
    side = HALF // 2
    rows = width // 16
    tall = total2.shape[0]
    rest = jnp.concatenate([total2, total3, total4[: 3 * rows]])
    rest_keep = jnp.where(core == 0, rest[:, :side], rest[:, side:])
    rest_recv = to_core(jnp.where(core == 0, rest[:, side:], rest[:, :side]))
    join = lambda array: jnp.transpose(array, (1, 0, 2)).reshape(rows, 2 * HALF)
    grad_feed_in = in_order(join(wide_keep), join(wide_recv))
    grad_feed_out = in_order(rest_keep[:tall], rest_recv[:tall])
    squares = []
    for at in range(8):
        part = slice(tall + at * rows, tall + (at + 1) * rows)
        squares.append(in_order(rest_keep[part], rest_recv[part]))
    cross_o, cross_q, cross_k, cross_v, self_o, self_q, self_k, self_v = squares
    gain_row = total4[3 * rows]
    piece = width // 8
    return (
        output[None],
        input_grad[None],
        encoded_grad[None],
        self_q,
        self_k,
        self_v,
        self_o,
        cross_q,
        cross_k,
        cross_v,
        cross_o,
        grad_feed_in,
        grad_feed_out,
        gain_row[:piece],
        gain_row[piece : 2 * piece],
        gain_row[2 * piece : 3 * piece],
    )


def solution(mesh):
    paired = mesh.shape["blk"] == 4 and mesh.shape["rows"] == 8
    body = local_paired if paired else local_any
    in_specs = (
        P("rows", "blk", None),
        P("rows", "blk", None),
        P("rows", "blk", None),
        P("rows", "blk"),
        P("rows", "blk"),
        P("rows", "blk"),
        P(),
        P(),
        P(),
        P(),
        P(),
        P(),
        P(),
        P(),
        P(),
        P(),
        P(),
        P(),
        P(),
    )
    out_specs = (
        P("rows", "blk", None),
        P("rows", "blk", None),
        P("rows", "blk", None),
        P("rows", "blk"),
        P("rows", "blk"),
        P("rows", "blk"),
        P("rows", "blk"),
        P("rows", "blk"),
        P("rows", "blk"),
        P("rows", "blk"),
        P("rows", "blk"),
        P("rows", "blk"),
        P("rows", "blk"),
        P("rows"),
        P("rows"),
        P("rows"),
    )
    return jax.shard_map(body, mesh=mesh, in_specs=in_specs, out_specs=out_specs, check_vma=False)
```

```python
import jax
import jax.numpy as jnp
from jax import lax
from jax.experimental import pallas as pl
from jax.experimental.pallas import tpu as pltpu
from jax.sharding import PartitionSpec as P

HEADS = 12
HEAD_DIM = 64
PLEN = 384


NEG_FILL = -1e30
SCALE = 0.125


def split_heads(matrix):
    return matrix.reshape(matrix.shape[0], matrix.shape[1], HEADS, HEAD_DIM)


def join_heads(tensor):
    return jnp.transpose(tensor, (0, 2, 1, 3)).reshape(
        tensor.shape[0], tensor.shape[2], HEADS * HEAD_DIM
    )


def rms_norm(values, gain_vec):
    return values * lax.rsqrt(jnp.mean(values * values, axis=-1, keepdims=True) + 1e-06) * gain_vec


def norm_back(values, gain_vec, grad_out):
    _, pullback = jax.vjp(rms_norm, values, gain_vec)
    return pullback(grad_out)


def project(left, weight):
    return jnp.einsum("rqd,df->rqf", left, weight, preferred_element_type=jnp.float32)


def back_project(grad_out, weight):
    return jnp.einsum("rqf,df->rqd", grad_out, weight, preferred_element_type=jnp.float32)


def weight_grad(left, grad_out):
    return jnp.einsum("rqd,rqf->df", left, grad_out, preferred_element_type=jnp.float32)


def head_scores(queries, keys):
    return (
        jnp.einsum(
            "rqhe,rkhe->rhqk",
            split_heads(queries),
            split_heads(keys),
            preferred_element_type=jnp.float32,
        )
        * SCALE
    )


def empty_state(row_count, query_count):
    return (
        jnp.full((row_count, HEADS, query_count), NEG_FILL, jnp.float32),
        jnp.zeros((row_count, HEADS, query_count), jnp.float32),
        jnp.zeros((row_count, HEADS, query_count, HEAD_DIM), jnp.float32),
    )


def online_block(state, queries, keys, values, allowed):
    run_max, run_sum, run_acc = state
    scores = head_scores(queries, keys)
    allowed = allowed[:, None]
    new_max = jnp.maximum(run_max, jnp.max(jnp.where(allowed, scores, NEG_FILL), axis=-1))
    weights = jnp.where(allowed, jnp.exp(scores - new_max[..., None]), 0.0)
    new_sum = jnp.sum(weights, axis=-1)
    new_acc = jnp.einsum(
        "rhqk,rkhe->rhqe",
        weights.astype(jnp.bfloat16),
        split_heads(values),
        preferred_element_type=jnp.float32,
    )
    return (new_max, new_sum, new_acc)


def finish(state):
    run_max, run_sum, run_acc = state
    return (run_acc / run_sum[..., None], run_max + jnp.log(run_sum))


def grad_pair(queries, grad_ctx, log_sum, delta, keys, values, allowed):
    scores = head_scores(queries, keys)
    probs_now = jnp.where(allowed[:, None], jnp.exp(scores - log_sum[..., None]), 0.0)
    grad_probs = jnp.einsum(
        "rqhe,rkhe->rhqk",
        split_heads(grad_ctx),
        split_heads(values),
        preferred_element_type=jnp.float32,
    )
    grad_scores = (probs_now * (grad_probs - delta[..., None])).astype(jnp.bfloat16)
    grad_query = (
        jnp.einsum(
            "rhqk,rkhe->rqhe", grad_scores, split_heads(keys), preferred_element_type=jnp.float32
        )
        * SCALE
    )
    grad_key = (
        jnp.einsum(
            "rhqk,rqhe->rkhe", grad_scores, split_heads(queries), preferred_element_type=jnp.float32
        )
        * SCALE
    )
    grad_value = jnp.einsum(
        "rhqk,rqhe->rkhe",
        probs_now.astype(jnp.bfloat16),
        split_heads(grad_ctx),
        preferred_element_type=jnp.float32,
    )
    row_count = keys.shape[0]
    key_count = keys.shape[1]
    joined = jnp.concatenate(
        (grad_key.reshape(row_count, key_count, -1), grad_value.reshape(row_count, key_count, -1)),
        axis=-1,
    )
    return (grad_query.reshape(row_count, queries.shape[1], -1), joined)


def head_delta(grad_ctx, attended):
    return jnp.einsum("rqhe,rhqe->rhq", split_heads(grad_ctx).astype(jnp.float32), attended)


def spread_matrix(matrix, row_split, block_count):
    first, second = matrix.shape
    tiles = matrix.reshape(row_split, first // row_split, block_count, second // block_count)
    return jnp.transpose(tiles, (0, 2, 1, 3)).reshape(
        row_split * block_count, first // row_split, second // block_count
    )


def spread_gain(vector, row_split, block_count):
    tiles = vector.reshape(row_split, 1, vector.shape[0] // row_split)
    return jnp.broadcast_to(tiles, (row_split, block_count, vector.shape[0] // row_split)).reshape(
        row_split * block_count, vector.shape[0] // row_split
    )


def local_any(
    inputs,
    encoded,
    cotangent,
    dec_seg,
    pass_doc,
    enc_mask,
    self_query,
    self_key,
    self_value,
    self_output,
    cross_query,
    cross_key,
    cross_value,
    cross_output,
    feed_in,
    feed_out,
    gain_self,
    gain_cross,
    gain_ff,
):
    row_count, tok_shard, width = inputs.shape
    enc_shard = encoded.shape[1]
    block_count = lax.axis_size("blk")
    row_split = lax.axis_size("rows")
    block_ids = jnp.arange(block_count)
    query_places = lax.axis_index("blk") * tok_shard + jnp.arange(tok_shard)
    start_state = empty_state(row_count, tok_shard)
    residual = inputs.astype(jnp.float32)
    normed_self = rms_norm(residual, gain_self).astype(jnp.bfloat16)
    self_queries = project(normed_self, self_query).astype(jnp.bfloat16)
    self_keys = project(normed_self, self_key).astype(jnp.bfloat16)
    self_values = project(normed_self, self_value).astype(jnp.bfloat16)
    piece_keys = lax.all_gather(self_keys, "blk", axis=1, tiled=True)
    piece_values = lax.all_gather(self_values, "blk", axis=1, tiled=True)
    piece_segs = lax.all_gather(dec_seg, "blk", axis=1, tiled=True)
    key_places = jnp.arange(piece_keys.shape[1])
    allowed = (dec_seg[:, :, None] == piece_segs[:, None, :]) & (
        key_places[None, None, :] <= query_places[None, :, None]
    )
    self_attn, self_lse = finish(
        online_block(start_state, self_queries, piece_keys, piece_values, allowed)
    )
    self_context = join_heads(self_attn).astype(jnp.bfloat16)
    after_self = residual + project(self_context, self_output)
    normed_cross = rms_norm(after_self, gain_cross).astype(jnp.bfloat16)
    cross_queries = project(normed_cross, cross_query).astype(jnp.bfloat16)
    cross_keys = project(encoded, cross_key).astype(jnp.bfloat16)
    cross_values = project(encoded, cross_value).astype(jnp.bfloat16)
    key_docs = jnp.where(enc_mask == 1, jnp.repeat(pass_doc, PLEN, axis=1), -1)
    piece_keys = lax.all_gather(cross_keys, "blk", axis=1, tiled=True)
    piece_values = lax.all_gather(cross_values, "blk", axis=1, tiled=True)
    piece_docs = lax.all_gather(key_docs, "blk", axis=1, tiled=True)
    allowed = dec_seg[:, :, None] == piece_docs[:, None, :]
    cross_attn, cross_lse = finish(
        online_block(start_state, cross_queries, piece_keys, piece_values, allowed)
    )
    cross_context = join_heads(cross_attn).astype(jnp.bfloat16)
    after_cross = after_self + project(cross_context, cross_output)
    normed_ff = rms_norm(after_cross, gain_ff).astype(jnp.bfloat16)
    before_act = project(normed_ff, feed_in)
    hidden = jax.nn.gelu(before_act).astype(jnp.bfloat16)
    output = (after_cross + project(hidden, feed_out)).astype(jnp.bfloat16)
    grad_feed_out = weight_grad(hidden, cotangent)
    grad_hidden = back_project(cotangent, feed_out)
    _, gelu_back = jax.vjp(jax.nn.gelu, before_act)
    grad_before = gelu_back(grad_hidden)[0].astype(jnp.bfloat16)
    grad_feed_in = weight_grad(normed_ff, grad_before)
    grad_cross_res, grad_gain_ff = norm_back(
        after_cross, gain_ff, back_project(grad_before, feed_in)
    )
    grad_cross_res = cotangent.astype(jnp.float32) + grad_cross_res
    cross_branch = grad_cross_res.astype(jnp.bfloat16)
    grad_cross_output = weight_grad(cross_context, cross_branch)
    grad_cross_ctx = back_project(cross_branch, cross_output).astype(jnp.bfloat16)
    cross_delta = head_delta(grad_cross_ctx, cross_attn)
    all_keys, all_values, all_docs = (
        lax.all_gather(cross_keys, "blk", axis=1, tiled=True),
        lax.all_gather(cross_values, "blk", axis=1, tiled=True),
        lax.all_gather(key_docs, "blk", axis=1, tiled=True),
    )

    def passage_step(running, block_index):
        offset = block_index * enc_shard
        piece_keys = lax.dynamic_slice_in_dim(all_keys, offset, enc_shard, 1)
        piece_values = lax.dynamic_slice_in_dim(all_values, offset, enc_shard, 1)
        piece_docs = lax.dynamic_slice_in_dim(all_docs, offset, enc_shard, 1)
        allowed = dec_seg[:, :, None] == piece_docs[:, None, :]
        grad_query, grad_kv = grad_pair(
            cross_queries, grad_cross_ctx, cross_lse, cross_delta, piece_keys, piece_values, allowed
        )
        return (running + grad_query, grad_kv)

    grad_cross_q, key_terms = lax.scan(
        passage_step, jnp.zeros((row_count, tok_shard, width), jnp.float32), block_ids
    )
    grad_cross_kv = lax.psum_scatter(
        key_terms.astype(jnp.bfloat16), "blk", scatter_dimension=0, tiled=True
    ).astype(jnp.float32)[0]
    low_cross_q = grad_cross_q.astype(jnp.bfloat16)
    low_cross_k = grad_cross_kv[..., :width].astype(jnp.bfloat16)
    low_cross_v = grad_cross_kv[..., width:].astype(jnp.bfloat16)
    grad_cross_query = weight_grad(normed_cross, low_cross_q)
    grad_cross_key = weight_grad(encoded, low_cross_k)
    grad_cross_value = weight_grad(encoded, low_cross_v)
    encoded_grad = back_project(low_cross_k, cross_key) + back_project(low_cross_v, cross_value)
    grad_self_res, grad_gain_cross = norm_back(
        after_self, gain_cross, back_project(low_cross_q, cross_query)
    )
    grad_self_res = grad_cross_res + grad_self_res
    self_branch = grad_self_res.astype(jnp.bfloat16)
    grad_self_output = weight_grad(self_context, self_branch)
    grad_self_ctx = back_project(self_branch, self_output).astype(jnp.bfloat16)
    self_delta = head_delta(grad_self_ctx, self_attn)
    all_self_keys, all_self_values, all_self_segs = (
        lax.all_gather(self_keys, "blk", axis=1, tiled=True),
        lax.all_gather(self_values, "blk", axis=1, tiled=True),
        lax.all_gather(dec_seg, "blk", axis=1, tiled=True),
    )

    def self_step(running, block_index):
        offset = block_index * tok_shard
        piece_keys = lax.dynamic_slice_in_dim(all_self_keys, offset, tok_shard, 1)
        piece_values = lax.dynamic_slice_in_dim(all_self_values, offset, tok_shard, 1)
        piece_segs = lax.dynamic_slice_in_dim(all_self_segs, offset, tok_shard, 1)
        key_places = offset + jnp.arange(tok_shard)
        allowed = (dec_seg[:, :, None] == piece_segs[:, None, :]) & (
            key_places[None, None, :] <= query_places[None, :, None]
        )
        grad_query, grad_kv = grad_pair(
            self_queries, grad_self_ctx, self_lse, self_delta, piece_keys, piece_values, allowed
        )
        return (running + grad_query, grad_kv)

    grad_self_q, self_terms = lax.scan(
        self_step, jnp.zeros((row_count, tok_shard, width), jnp.float32), block_ids
    )
    grad_self_kv = lax.psum_scatter(
        self_terms.astype(jnp.bfloat16), "blk", scatter_dimension=0, tiled=True
    ).astype(jnp.float32)[0]
    low_self_q = grad_self_q.astype(jnp.bfloat16)
    low_self_k = grad_self_kv[..., :width].astype(jnp.bfloat16)
    low_self_v = grad_self_kv[..., width:].astype(jnp.bfloat16)
    grad_self_query = weight_grad(normed_self, low_self_q)
    grad_self_key = weight_grad(normed_self, low_self_k)
    grad_self_value = weight_grad(normed_self, low_self_v)
    grad_normed = (
        back_project(low_self_q, self_query)
        + back_project(low_self_k, self_key)
        + back_project(low_self_v, self_value)
    )
    grad_first, grad_gain_self = norm_back(residual, gain_self, grad_normed)
    input_grad = grad_self_res + grad_first
    matrices = (
        grad_self_query,
        grad_self_key,
        grad_self_value,
        grad_self_output,
        grad_cross_query,
        grad_cross_key,
        grad_cross_value,
        grad_cross_output,
        grad_feed_in,
        grad_feed_out,
    )
    spread_mats = tuple((spread_matrix(matrix, row_split, block_count) for matrix in matrices))
    spread_gains = tuple(
        (
            spread_gain(vector, row_split, block_count)
            for vector in (grad_gain_self, grad_gain_cross, grad_gain_ff)
        )
    )
    summed = (
        lax.psum_scatter(spread_mats[0], ("rows", "blk"), scatter_dimension=0, tiled=True),
        lax.psum_scatter(spread_mats[1], ("rows", "blk"), scatter_dimension=0, tiled=True),
        lax.psum_scatter(spread_mats[2], ("rows", "blk"), scatter_dimension=0, tiled=True),
        lax.psum_scatter(spread_mats[3], ("rows", "blk"), scatter_dimension=0, tiled=True),
        lax.psum_scatter(spread_mats[4], ("rows", "blk"), scatter_dimension=0, tiled=True),
        lax.psum_scatter(spread_mats[5], ("rows", "blk"), scatter_dimension=0, tiled=True),
        lax.psum_scatter(spread_mats[6], ("rows", "blk"), scatter_dimension=0, tiled=True),
        lax.psum_scatter(spread_mats[7], ("rows", "blk"), scatter_dimension=0, tiled=True),
        lax.psum_scatter(spread_mats[8], ("rows", "blk"), scatter_dimension=0, tiled=True),
        lax.psum_scatter(spread_mats[9], ("rows", "blk"), scatter_dimension=0, tiled=True),
        lax.psum_scatter(spread_gains[0], ("rows", "blk"), scatter_dimension=0, tiled=True),
        lax.psum_scatter(spread_gains[1], ("rows", "blk"), scatter_dimension=0, tiled=True),
        lax.psum_scatter(spread_gains[2], ("rows", "blk"), scatter_dimension=0, tiled=True),
    )
    return (
        output,
        input_grad,
        encoded_grad,
        summed[0][0],
        summed[1][0],
        summed[2][0],
        summed[3][0],
        summed[4][0],
        summed[5][0],
        summed[6][0],
        summed[7][0],
        summed[8][0],
        summed[9][0],
        summed[10][0],
        summed[11][0],
        summed[12][0],
    )


BF16 = jnp.bfloat16
F32 = jnp.float32
LANES = 128
HALF = 2 * LANES + LANES
CORE_SWAP = ((0, 1), (1, 0), (2, 3), (3, 2))
CHIP_SWAP = ((0, 2), (2, 0), (1, 3), (3, 1))


def dot_nn(left, right):
    return jnp.dot(left, right, preferred_element_type=F32)


def dot_nt(left, right):
    return lax.dot_general(left, right, (((1,), (1,)), ((), ())), preferred_element_type=F32)


def dot_tn(left, right):
    return lax.dot_general(left, right, (((0,), (0,)), ((), ())), preferred_element_type=F32)


def whole(array):
    rank = len(array.shape)
    return pl.BlockSpec(array.shape, lambda *_: (0,) * rank)


def struct(shape, dtype):
    return jax.ShapeDtypeStruct(shape, dtype)


def run_kernel(name, body, scalars, args, in_specs, outs, out_specs, grid=(1,), scratch=(), flops=0, after=(), vmem=58):
    moved = sum(a.size * a.dtype.itemsize for a in args)
    if after:
        inner, given = (body, len(args))

        def body(s, *refs):
            inner(s, *refs[:given], *refs[given + len(after) :])

        args = (*args, *after)
        in_specs = [*in_specs, *([pl.BlockSpec(memory_space=pl.ANY)] * len(after))]
    moved += sum(o.size * o.dtype.itemsize for o in outs)
    return pl.pallas_call(
        body,
        grid_spec=pltpu.PrefetchScalarGridSpec(
            num_scalar_prefetch=1,
            grid=grid,
            in_specs=list(in_specs),
            out_specs=list(out_specs),
            scratch_shapes=list(scratch),
        ),
        out_shape=list(outs),
        compiler_params=pltpu.CompilerParams(vmem_limit_bytes=vmem << 20),
        name=name,
    )(scalars, *args)


def unit_norm(values):
    scale = lax.rsqrt(jnp.mean(values * values, axis=-1, keepdims=True) + 1e-06)
    return (values * scale, scale)


def norm_pull(values, gain_vec, grad_out):
    normal, scale = unit_norm(values)
    scaled = grad_out * gain_vec
    inner = jnp.mean(scaled * normal, axis=-1, keepdims=True)
    return (scale * (scaled - normal * inner), jnp.sum(grad_out * normal, axis=0, keepdims=True))


def head_lanes():
    lane = lax.broadcasted_iota(jnp.int32, (1, LANES), 1)
    return (lane, (lane < HEAD_DIM, lane >= HEAD_DIM))


def only(keep, values):
    return jnp.where(keep, values, jnp.zeros_like(values))


def soft_block(queries, marks, keys, values):
    lane, masks = head_lanes()
    attended, sums = ([], [])
    for keep in masks:
        scores = dot_nt(jnp.concatenate([only(keep, queries), marks], axis=1), keys)
        top = jnp.max(scores, axis=1, keepdims=True)
        weights = jnp.exp(scores - top)
        total = jnp.sum(weights, axis=1, keepdims=True)
        attended.append(dot_nn(weights.astype(BF16), values) / total)
        sums.append(top + jnp.log(total))
    return (jnp.where(masks[0], *attended), jnp.where(masks[0], *sums))


def causal_block(queries, marks, keys, values):
    lane, masks = head_lanes()
    rows, cols = queries.shape[0], keys.shape[0]
    flipped = values.T
    attended, sums = ([], [])
    for at, keep in enumerate(masks):
        scores = dot_nt(keys, jnp.concatenate([only(keep, queries), marks], axis=1))
        at_row = lax.broadcasted_iota(jnp.int32, (rows, rows), 0)
        at_col = lax.broadcasted_iota(jnp.int32, (rows, rows), 1)
        last = jnp.where(at_row <= at_col, scores[cols - rows :, :], NEG_FILL)
        scores = last if cols == rows else jnp.concatenate([scores[: cols - rows, :], last], axis=0)
        top = jnp.max(scores, axis=0, keepdims=True)
        weights = jnp.exp(scores - top)
        total = jnp.sum(weights, axis=0, keepdims=True)
        head = flipped[at * HEAD_DIM : (at + 1) * HEAD_DIM, :]
        attended.append(dot_nn(head, weights.astype(BF16)) / total)
        sums.append(jnp.broadcast_to(top + jnp.log(total), (HEAD_DIM, rows)))
    return (jnp.concatenate(attended, axis=0).T, jnp.concatenate(sums, axis=0).T)


def three_parts(lane, column, base):
    high = column.astype(BF16)
    rest = column - high.astype(F32)
    middle = rest.astype(BF16)
    low = (rest - middle.astype(F32)).astype(BF16)
    out = jnp.where(lane == 3, -high, base)
    out = jnp.where(lane == 4, -middle, out)
    return jnp.where(lane == 5, -low, out)


def pull_block(queries, marks, keys, key_marks, values, grads, attended, sums, causal):
    lane, masks = head_lanes()
    rows, cols = queries.shape[0], keys.shape[0]
    wide_keys = jnp.concatenate([keys, key_marks], axis=1)
    ones = jnp.where((lane >= 3) & (lane < 6), 1.0, 0.0).astype(BF16)
    wide_values = jnp.concatenate([values, jnp.broadcast_to(ones, (cols, LANES))], axis=1)
    product = grads.astype(F32) * attended
    flipped = keys.T
    grad_queries = []
    grad_keys = grad_values = None
    for at, keep in enumerate(masks):
        query, grad = (only(keep, queries), only(keep, grads))
        delta = jnp.sum(jnp.where(keep, product, 0.0), axis=1, keepdims=True)
        log_sum = sums[:, HEAD_DIM * at : HEAD_DIM * at + 1]
        wide_query = jnp.concatenate([query, three_parts(lane, log_sum, marks)], axis=1)
        wide_grad = jnp.concatenate([grad, three_parts(lane, delta, jnp.zeros_like(marks))], axis=1)
        probs = jnp.exp(dot_nt(wide_keys, wide_query))
        if causal:
            at_row = lax.broadcasted_iota(jnp.int32, (rows, rows), 0)
            at_col = lax.broadcasted_iota(jnp.int32, (rows, rows), 1)
            last = jnp.where(at_row <= at_col, probs[cols - rows :, :], 0.0)
            probs = last if cols == rows else jnp.concatenate([probs[: cols - rows, :], last], axis=0)
        grad_scores = (probs * dot_nt(wide_values, wide_grad)).astype(BF16)
        grad_queries.append(dot_nn(flipped, grad_scores))
        key_part = dot_nn(grad_scores, query)
        value_part = dot_nn(probs.astype(BF16), grad)
        grad_keys = key_part if at == 0 else grad_keys + key_part
        grad_values = value_part if at == 0 else grad_values + value_part
    sub = lax.broadcasted_iota(jnp.int32, (LANES, 1), 0)
    return (jnp.where(sub < HEAD_DIM, *grad_queries).T * SCALE, grad_keys, grad_values)


def pair_columns(array):
    return pl.BlockSpec((array.shape[0], LANES), lambda p, _: (0, p))


def query_marks(labels):
    lane = lax.broadcasted_iota(jnp.int32, (LANES, 1), 0)
    return jnp.where(labels == lane, 1.0, 0.0).T.astype(BF16)


def key_marks(labels):
    lane = lax.broadcasted_iota(jnp.int32, (LANES, 1), 0)
    closed = jnp.where(labels != lane, NEG_FILL, 0.0)
    return jnp.where(lane < 3, closed, jnp.where(lane < 6, 1.0, 0.0)).T.astype(BF16)


def doc_marks(label_ref, tok, enc):
    first = -(-tok // LANES) * LANES
    doc = label_ref[:, pl.ds(first + enc, LANES)][:, 0:1]
    return key_marks(jnp.where(label_ref[:, pl.ds(first, enc)] == 1, doc, -1))


def pair_lanes():
    return pl.ds(pl.multiple_of(pl.program_id(0) * LANES, LANES), LANES)


def column_block(array):
    return pl.BlockSpec((array.shape[0], HALF), lambda _, s: (0, s[0]))


def any_place(_):
    return pl.BlockSpec(memory_space=pl.ANY)


def copies(sources, targets, semaphores):
    return [pltpu.make_async_copy(src, dst, semaphores.at[at]) for at, (src, dst) in enumerate(zip(sources, targets))]


def find_passages(place, tok, enc, labels):
    spot = -(-tok // LANES) * LANES + enc

    def body(s, own_ref, *refs):
        label_refs, out_ref = refs[:4], refs[4]
        own = own_ref[:, pl.ds(0, tok)]
        used = [jnp.max(jnp.where(own == ref[0, spot], 1, 0)) for ref in label_refs]
        total = used[0] + used[1] + used[2] + used[3]
        out_ref[0] = s[0]
        out_ref[1] = s[1]
        out_ref[6] = total
        out_ref[7] = 0
        ahead, behind = (jnp.int32(0), total)
        for slot in range(4):
            out_ref[2 + jnp.where(used[slot] == 1, ahead, behind)] = jnp.int32(slot)
            ahead, behind = (ahead + used[slot], behind + 1 - used[slot])

    smem = pl.BlockSpec(memory_space=pltpu.SMEM)
    return run_kernel(
        "find_passages", body, place, (labels[0], *labels), [whole(labels[0])] + [smem] * 4, [struct((8,), jnp.int32)],
        [smem],
    )[0]


def write_projections(s, mine_ref, other_ref, gain, weight_refs, scales, normed_ref, out_refs):
    tok = mine_ref.shape[0]
    for source, part in ((mine_ref, s[0]), (other_ref, 1 - s[0])):
        rows = pl.ds(pl.multiple_of(part * tok, tok), tok)
        normed = (unit_norm(source[...].astype(F32))[0] * gain).astype(BF16)
        normed_ref[rows, :] = normed
        for weight_ref, out_ref, scale in zip(weight_refs, out_refs, scales):
            out_ref[rows, :] = (dot_nn(normed, weight_ref[...]) * scale).astype(BF16)


def near_part(place, mine, other, gain_vec, weights, labels, after=()):
    tok, width = mine.shape
    both = 2 * tok

    def body(
        s, mine_ref, other_ref, gain_ref, wq_ref, wk_ref, wv_ref, own_ref, core_ref,
        h_ref, q_ref, k_ref, v_ref, m_ref, km_ref, out_ref, sum_ref,
    ):
        @pl.when(pl.program_id(0) == 0)
        def _():
            for source, part in ((own_ref, s[0]), (core_ref, 1 - s[0])):
                rows = pl.ds(pl.multiple_of(part * tok, tok), tok)
                m_ref[rows, :] = query_marks(source[:, pl.ds(0, tok)])
                km_ref[rows, :] = key_marks(source[:, pl.ds(0, tok)])
            write_projections(
                s, mine_ref, other_ref, gain_ref[...].reshape(1, width), (wq_ref, wk_ref, wv_ref), (SCALE, 1.0, 1.0), h_ref,
                (q_ref, k_ref, v_ref),
            )

        pair = pair_lanes()
        for at in (0, 1):
            rows, seen = (pl.ds(at * tok, tok), pl.ds(0, (at + 1) * tok))
            wide = jnp.concatenate([k_ref[seen, pair], km_ref[seen, :]], axis=1)
            out_ref[rows, :], sum_ref[rows, :] = causal_block(
                q_ref[rows, pair], m_ref[rows, :], wide, v_ref[seen, pair]
            )

    args = (mine, other, gain_vec, *weights, *labels)
    specs = [whole(a) for a in args]
    specs[3:6] = [column_block(w) for w in weights]
    outs = [struct((both, width), BF16)] + [struct((both, HALF), BF16)] * 3 + [struct((both, LANES), BF16)] * 2
    outs += [struct((both, HALF), F32)] * 2
    return run_kernel(
        "near_part", body, place, args, specs, outs, [whole(o) for o in outs[:6]] + [pair_columns(o) for o in outs[6:]],
        grid=(HALF // LANES,), after=after, flops=both * both * 6 * 2 * HALF,
    )


def far_part(place, mine, other, gain_vec, weights, queries, marks, labels, near_out, near_sum, after=()):
    tok, width = mine.shape
    both = 2 * tok

    def body(
        s, mine_ref, other_ref, gain_ref, wk_ref, wv_ref, q_ref, m_ref, lx_ref, ld_ref, no_ref, ns_ref,
        h_ref, k_ref, v_ref, km_ref, out_ref, sum_ref, keep_ref, send_ref,
    ):
        pair = pair_lanes()

        @pl.when(pl.program_id(0) == 0)
        def _():
            for source, part in ((lx_ref, s[0]), (ld_ref, 1 - s[0])):
                rows = pl.ds(pl.multiple_of(part * tok, tok), tok)
                km_ref[rows, :] = key_marks(source[:, pl.ds(0, tok)])

        def write(at, out, log_sum):
            rows = pl.ds(at * tok, tok)
            out_ref[rows, :] = out
            sum_ref[rows, :] = log_sum

            @pl.when(s[0] == at)
            def _():
                keep_ref[...] = out.astype(BF16)

            @pl.when(s[0] != at)
            def _():
                send_ref[...] = out.astype(BF16)

        @pl.when(s[1] == 0)
        def _():
            for at in (0, 1):
                rows = pl.ds(at * tok, tok)
                write(at, no_ref[rows, :], ns_ref[rows, :])

            @pl.when(pl.program_id(0) == 0)
            def _():
                for ref in (h_ref, k_ref, v_ref):
                    ref[...] = jnp.zeros_like(ref)

        @pl.when(s[1] != 0)
        def _():
            @pl.when(pl.program_id(0) == 0)
            def _():
                write_projections(
                    s, mine_ref, other_ref, gain_ref[...].reshape(1, width), (wk_ref, wv_ref), (1.0, 1.0), h_ref, (k_ref, v_ref)
                )

            wide = jnp.concatenate([k_ref[:, pair], km_ref[...]], axis=1)
            for at in (0, 1):
                rows = pl.ds(at * tok, tok)
                out, log_sum = soft_block(q_ref[rows, :], m_ref[rows, :], wide, v_ref[:, pair])
                near_log = ns_ref[rows, :]
                top = jnp.maximum(near_log, log_sum)
                near_share, far_share = (jnp.exp(near_log - top), jnp.exp(log_sum - top))
                total = near_share + far_share
                write(at, (no_ref[rows, :] * near_share + out * far_share) / total, top + jnp.log(total))

    args = (mine, other, gain_vec, *weights, queries, marks, *labels, near_out, near_sum)
    specs = [whole(a) for a in args]
    specs[3:5] = [column_block(w) for w in weights]
    for at in (5, 9, 10):
        specs[at] = pair_columns(args[at])
    outs = [struct((both, width), BF16)] + [struct((both, HALF), BF16)] * 2 + [struct((both, LANES), BF16)]
    outs += [struct((both, HALF), F32)] * 2 + [struct((tok, HALF), BF16)] * 2
    return run_kernel(
        "far_part", body, place, args, specs, outs, [whole(o) for o in outs[:4]] + [pair_columns(o) for o in outs[4:]],
        grid=(HALF // LANES,), after=after, flops=both * both * 8 * 2 * HALF,
    )


def passage_pair(place, first, second, key_weight, value_weight, after=()):
    enc, width = first.shape

    def body(s, first_ref, second_ref, key_w_ref, value_w_ref, key_ref, value_ref):
        for at, source in enumerate((first_ref, second_ref)):
            rows = pl.ds(at * enc, enc)
            key_ref[rows, :] = dot_nn(source[...], key_w_ref[...]).astype(BF16)
            value_ref[rows, :] = dot_nn(source[...], value_w_ref[...]).astype(BF16)

    args = (first, second, key_weight, value_weight)
    outs = [struct((2 * enc, width), BF16)] * 2
    return run_kernel(
        "passage_pair", body, place, args, [whole(a) for a in args], outs, [whole(o) for o in outs],
        after=after, flops=8 * enc * width * width,
    )


def gather_slots(s, enc, target, first_ref, second_ref, lanes=slice(None)):
    for at in range(4):
        slot = s[2 + at]
        rows = pl.ds(at * enc, enc)

        @pl.when(slot < 2)
        def _():
            target[rows, :] = first_ref[pl.ds(pl.multiple_of(slot * enc, enc), enc), :]

        @pl.when(slot >= 2)
        def _():
            target[rows, :] = second_ref[pl.ds(pl.multiple_of((slot - 2) * enc, enc), enc), lanes]


def by_count(s, work):
    pl.when(s[6] <= 2)(lambda: work(2))
    pl.when(s[6] == 3)(lambda: work(3))
    pl.when(s[6] >= 4)(lambda: work(4))


def cross_part(
    place, inputs, ctx_keep, ctx_recv, out_weight, gain_vec, query_weight, first, second, key_weight, value_weight,
    keys, values, labels, after=(),
):
    tok, width = inputs.shape
    enc = first.shape[0]

    def body(
        s, in_ref, keep_ref, recv_ref, wa_ref, wb_ref, gain_ref, wq_ref, first_ref, second_ref, wk_ref, wv_ref, k0_ref, v0_ref,
        l0_ref, l1_ref, l2_ref, l3_ref,
        x_ref, h_ref, q_ref, ctx_ref, k1_ref, v1_ref, m_ref, km0_ref, km1_ref, cctx_ref, out_ref, sum_ref,
        all_k, all_v,
    ):
        keep = pl.ds(0, LANES)

        @pl.when(pl.program_id(0) == 0)
        def _():
            total = dot_nn(keep_ref[...], wa_ref[...]) + dot_nn(recv_ref[...], wb_ref[...])
            residual = in_ref[...].astype(F32) + total
            x_ref[...] = residual
            normed = (unit_norm(residual)[0] * gain_ref[...].reshape(1, width)).astype(BF16)
            h_ref[...] = normed
            q_ref[...] = (dot_nn(normed, wq_ref[...]) * SCALE).astype(BF16)
            ctx_ref[:, pl.ds(pl.multiple_of(s[0] * HALF, LANES), HALF)] = keep_ref[...]
            ctx_ref[:, pl.ds(pl.multiple_of((1 - s[0]) * HALF, LANES), HALF)] = recv_ref[...]
            for at, source in enumerate((first_ref, second_ref)):
                rows = pl.ds(at * enc, enc)
                k1_ref[rows, :] = dot_nn(source[...], wk_ref[...]).astype(BF16)
                v1_ref[rows, :] = dot_nn(source[...], wv_ref[...]).astype(BF16)
            m_ref[...] = query_marks(l0_ref[:, pl.ds(0, tok)])
            for target, low, high in ((km0_ref, l0_ref, l1_ref), (km1_ref, l2_ref, l3_ref)):
                target[pl.ds(0, enc), :] = doc_marks(low, tok, enc)
                target[pl.ds(enc, enc), :] = doc_marks(high, tok, enc)
            gather_slots(s, enc, all_k.at[:, pl.ds(LANES, LANES)], km0_ref, km1_ref)

        pair = pair_lanes()
        gather_slots(s, enc, all_k.at[:, keep], k0_ref, k1_ref, pair)
        gather_slots(s, enc, all_v, v0_ref, v1_ref, pair)

        def work(count):
            seen = pl.ds(0, count * enc)
            out, log_sum = soft_block(q_ref[:, pair], m_ref[...], all_k[seen, :], all_v[seen, :])
            cctx_ref[...] = out.astype(BF16)
            out_ref[...] = out
            sum_ref[...] = log_sum

        by_count(s, work)

    args = (
        inputs, ctx_keep, ctx_recv, out_weight, out_weight, gain_vec, query_weight, first, second, key_weight, value_weight,
        keys, values, *labels,
    )
    specs = [whole(a) for a in args]
    specs[3] = pl.BlockSpec((HALF, width), lambda _, s: (s[0], 0))
    specs[4] = pl.BlockSpec((HALF, width), lambda _, s: (1 - s[0], 0))
    specs[11], specs[12] = pair_columns(keys), pair_columns(values)
    outs = [struct((tok, width), F32)] + [struct((tok, width), BF16)] * 3 + [struct((2 * enc, width), BF16)] * 2
    outs += [struct((tok, LANES), BF16)] + [struct((2 * enc, LANES), BF16)] * 2
    outs += [struct((tok, width), BF16)] + [struct((tok, width), F32)] * 2
    return run_kernel(
        "cross_part", body, place, args, specs, outs, [whole(o) for o in outs[:9]] + [pair_columns(o) for o in outs[9:]],
        grid=(width // LANES,),
        scratch=[pltpu.VMEM((4 * enc, 2 * LANES), BF16), pltpu.VMEM((4 * enc, LANES), BF16)],
        after=after, flops=tok * 2.5 * enc * 8 * 2 * width + 12 * tok * width * width,
    )


def cross_back(place, queries, keys, values, marks, key_marks, grads, attended, sums, residual, grad_res, query_weight, gains, out_weight, after=()):
    tok, width = queries.shape
    enc = keys[0].shape[0] // 2
    last = width // LANES - 1

    def body(
        s, q_ref, k0_ref, k1_ref, v0_ref, v1_ref, m_ref, km0_ref, km1_ref, g_ref, at_ref, ls_ref, gain_ref,
        x_any, dx_any, wq_any, wo_any, dq_ref, dk_ref, dv_ref, dx1_ref, low_ref, gain_grad_ref, keep_ref, send_ref,
        all_k, all_v, all_m, x_ref, dx_ref, wq_ref, wo_ref, semaphores,
    ):
        later = copies((x_any, dx_any, wq_any, wo_any), (x_ref, dx_ref, wq_ref, wo_ref), semaphores)

        @pl.when(pl.program_id(0) == 0)
        def _():
            for copy in later:
                copy.start()
            gather_slots(s, enc, all_m, km0_ref, km1_ref)

        gather_slots(s, enc, all_k, k0_ref, k1_ref)
        gather_slots(s, enc, all_v, v0_ref, v1_ref)
        pair = pair_lanes()

        def work(count):
            seen = pl.ds(0, count * enc)
            grad_q, grad_k, grad_v = pull_block(
                q_ref[...], m_ref[...], all_k[seen, :], all_m[seen, :], all_v[seen, :], g_ref[...], at_ref[...],
                ls_ref[...], False,
            )
            dq_ref[:, pair] = grad_q.astype(BF16)
            low_k, low_v = (grad_k.astype(BF16), grad_v.astype(BF16))
            for at in range(4):
                rows = pl.ds(pl.multiple_of(s[2 + at] * enc, enc), enc)
                if at < count:
                    dk_ref[rows, :] = low_k[at * enc : (at + 1) * enc, :]
                    dv_ref[rows, :] = low_v[at * enc : (at + 1) * enc, :]
                else:
                    dk_ref[rows, :] = jnp.zeros((enc, LANES), BF16)
                    dv_ref[rows, :] = jnp.zeros((enc, LANES), BF16)

        by_count(s, work)

        @pl.when(pl.program_id(0) == last)
        def _():
            for copy in later:
                copy.wait()
            back, gain_grad_ref[...] = norm_pull(x_ref[...], gain_ref[...].reshape(1, width), dot_nt(dq_ref[...], wq_ref[...]))
            grad_x = dx_ref[...] + back
            dx1_ref[...] = grad_x
            low = grad_x.astype(BF16)
            low_ref[...] = low
            for target, half in ((keep_ref, s[0]), (send_ref, 1 - s[0])):
                rows = pl.ds(pl.multiple_of(half * HALF, HALF), HALF)
                target[...] = dot_nt(low, wo_ref[rows, :]).astype(BF16)

    late = (residual, grad_res, query_weight, out_weight)
    args = (queries, *keys, *values, marks, *key_marks, grads, attended, sums, gains, *late)
    specs = [pair_columns(a) for a in args]
    for at in (5, 6, 7, 11):
        specs[at] = whole(args[at])
    specs[12:] = [any_place(a) for a in late]
    outs = [struct((tok, width), BF16)] + [struct((4 * enc, width), BF16)] * 2
    outs += [struct((tok, width), F32), struct((tok, width), BF16), struct((1, width), F32)]
    outs += [struct((tok, HALF), BF16)] * 2
    out_specs = [whole(o) for o in outs]
    out_specs[1], out_specs[2] = pair_columns(outs[1]), pair_columns(outs[2])
    return run_kernel(
        "cross_back", body, place, args, specs, outs, out_specs,
        grid=(width // LANES,),
        scratch=[pltpu.VMEM((4 * enc, LANES), BF16)] * 3
        + [pltpu.VMEM(a.shape, a.dtype) for a in late]
        + [pltpu.SemaphoreType.DMA((len(late),))],
        after=after, flops=tok * 2.5 * enc * 20 * 2 * width,
    )


def write_normed_grads(s, tok, h_ref, gain, grad_refs, weight_refs, keep_ref, send_ref, gain_grad_ref):
    running = None
    for target, part in ((keep_ref, s[0]), (send_ref, 1 - s[0])):
        rows = pl.ds(pl.multiple_of(part * tok, tok), tok)
        value = None
        for grad_ref, weight_ref in zip(grad_refs, weight_refs):
            piece = dot_nt(grad_ref[rows, :], weight_ref[...])
            value = piece if value is None else value + piece
        target[...] = value.astype(BF16)
        inner = jnp.sum(value * h_ref[rows, :].astype(F32), axis=0, keepdims=True)
        running = inner if running is None else running + inner
    gain_grad_ref[...] = running / gain


def far_back(place, queries, keys, values, marks, key_marks, grad_keep, grad_recv, attended, sums, gains, normed, weights, after=()):
    both, width = normed.shape
    tok = both // 2
    last = HALF // LANES - 1

    def body(
        s, q_ref, k_ref, v_ref, m_ref, km_ref, gk_ref, gr_ref, at_ref, ls_ref, gain_ref, h_any, wk_any, wv_any,
        dq_ref, dk_ref, dv_ref, keep_ref, send_ref, gain_grad_ref, h_ref, wk_ref, wv_ref, semaphores,
    ):
        pair = pair_lanes()
        columns = pl.ds(pl.multiple_of(s[0] * HALF, LANES), HALF)
        later = copies((h_any, wk_any.at[:, columns], wv_any.at[:, columns]), (h_ref, wk_ref, wv_ref), semaphores)

        @pl.when(s[1] != 0)
        def _():
            @pl.when(pl.program_id(0) == 0)
            def _():
                for copy in later:
                    copy.start()

            sum_k = sum_v = None
            for at in (0, 1):
                rows = pl.ds(at * tok, tok)
                grads = jnp.where(s[0] == at, gk_ref[...], gr_ref[...])
                dq_ref[rows, :], grad_k, grad_v = pull_block(
                    q_ref[rows, :], m_ref[rows, :], k_ref[...], km_ref[...], v_ref[...], grads, at_ref[rows, :],
                    ls_ref[rows, :], False,
                )
                sum_k = grad_k if at == 0 else sum_k + grad_k
                sum_v = grad_v if at == 0 else sum_v + grad_v
            dk_ref[:, pair] = sum_k.astype(BF16)
            dv_ref[:, pair] = sum_v.astype(BF16)

            @pl.when(pl.program_id(0) == last)
            def _():
                for copy in later:
                    copy.wait()
                write_normed_grads(
                    s, tok, h_ref, gain_ref[...].reshape(1, width), (dk_ref, dv_ref), (wk_ref, wv_ref), keep_ref, send_ref, gain_grad_ref
                )

        @pl.when(s[1] == 0)
        def _():
            dq_ref[...] = jnp.zeros_like(dq_ref)
            for ref in (dk_ref, dv_ref, keep_ref, send_ref, gain_grad_ref):
                ref[...] = jnp.zeros_like(ref)

    args = (queries, keys, values, marks, key_marks, grad_keep, grad_recv, attended, sums, gains, normed, *weights)
    specs = [pair_columns(a) for a in args]
    specs[3], specs[4], specs[9] = whole(marks), whole(key_marks), whole(gains)
    specs[10:] = [any_place(a) for a in args[10:]]
    outs = [struct((both, HALF), F32)] + [struct((both, HALF), BF16)] * 2
    outs += [struct((tok, width), BF16)] * 2 + [struct((1, width), F32)]
    return run_kernel(
        "far_back", body, place, args, specs, outs, [pair_columns(outs[0])] + [whole(o) for o in outs[1:]],
        grid=(HALF // LANES,),
        scratch=[pltpu.VMEM((both, width), BF16)] + [pltpu.VMEM((width, HALF), BF16)] * 2 + [pltpu.SemaphoreType.DMA((3,))],
        after=after, flops=both * both * 20 * 2 * HALF,
    )


def write_square(s, value, keep, send, first, x_first=False):
    rows = value.shape[0] // 16
    side = HALF // 2

    def write(target, half):
        for at in range(8):
            high, low, far = (at // 4, (at // 2) % 2, at % 2)
            for chip in range(value.shape[1] // HALF):
                columns = slice(chip * HALF + half * side, chip * HALF + (half + 1) * side)
                place = (chip, far, low, high) if x_first else (far, chip, low, high)
                for part in range(2):
                    piece = value[(2 * at + part) * rows : (2 * at + part + 1) * rows, columns].astype(BF16)
                    target[*place, pl.ds(first, rows), pl.ds(part * side, side)] = piece

    @pl.when(s[0] == 0)
    def _():
        write(keep, 0)
        write(send, 1)

    @pl.when(s[0] != 0)
    def _():
        write(keep, 1)
        write(send, 0)


def near_back(
    place, queries, keys, values, marks, key_marks, grad_keep, grad_recv, attended, sums, carried, gains,
    normed, far_normed, weights, far_grads, after=(),
):
    both, width = normed.shape
    tok = both // 2
    last = HALF // LANES - 1
    late_shapes = [(both, width)] * 2 + [(width, HALF)] * 3 + [(both, HALF)] * 2

    def body(
        s, q_ref, k_ref, v_ref, m_ref, km_ref, gk_ref, gr_ref, at_ref, ls_ref, ca_ref, gain_ref,
        h_any, fh_any, wq_any, wk_any, wv_any, fk_any, fv_any,
        keep_ref, send_ref, gain_grad_ref, keep4, send4,
        dq, dk, dv, sum_k, sum_v, h_ref, fh_ref, wq_ref, wk_ref, wv_ref, fk_ref, fv_ref, semaphores,
    ):
        pair = pair_lanes()
        columns = pl.ds(pl.multiple_of(s[0] * HALF, LANES), HALF)
        later = copies(
            (h_any, fh_any, wq_any.at[:, columns], wk_any.at[:, columns], wv_any.at[:, columns], fk_any, fv_any),
            (h_ref, fh_ref, wq_ref, wk_ref, wv_ref, fk_ref, fv_ref),
            semaphores,
        )

        @pl.when(pl.program_id(0) == 0)
        def _():
            for copy in later:
                copy.start()

        for at in (0, 1):
            rows = pl.ds(at * tok, tok)
            count = (at + 1) * tok
            seen = pl.ds(0, count)
            grads = jnp.where(s[0] == at, gk_ref[...], gr_ref[...])
            grad_q, grad_k, grad_v = pull_block(
                q_ref[rows, :], m_ref[rows, :], k_ref[seen, :], km_ref[seen, :], v_ref[seen, :], grads,
                at_ref[rows, :], ls_ref[rows, :], True,
            )
            dq[rows, pair] = (grad_q + ca_ref[rows, :]).astype(BF16)
            if at == 0:
                sum_k[...] = grad_k
                sum_v[...] = grad_v
            else:
                dk[pl.ds(0, tok), pair] = (sum_k[...] + grad_k[:tok]).astype(BF16)
                dv[pl.ds(0, tok), pair] = (sum_v[...] + grad_v[:tok]).astype(BF16)
                dk[pl.ds(tok, tok), pair] = grad_k[tok:].astype(BF16)
                dv[pl.ds(tok, tok), pair] = grad_v[tok:].astype(BF16)

        @pl.when(pl.program_id(0) == last)
        def _():
            for copy in later:
                copy.wait()
            write_normed_grads(
                s, tok, h_ref, gain_ref[...].reshape(1, width), (dq, dk, dv), (wq_ref, wk_ref, wv_ref), keep_ref, send_ref, gain_grad_ref
            )
            rows = width // 16
            write_square(s, dot_tn(h_ref[...], dq[...]), keep4, send4, 0)
            value = dot_tn(h_ref[...], dk[...]) + dot_tn(fh_ref[...], fk_ref[...])
            write_square(s, value, keep4, send4, rows)
            value = dot_tn(h_ref[...], dv[...]) + dot_tn(fh_ref[...], fv_ref[...])
            write_square(s, value, keep4, send4, 2 * rows)

    late = (normed, far_normed, *weights, *far_grads)
    args = (queries, keys, values, marks, key_marks, grad_keep, grad_recv, attended, sums, carried, gains, *late)
    specs = [pair_columns(a) for a in args]
    specs[3], specs[4], specs[10] = whole(marks), whole(key_marks), whole(gains)
    specs[11:] = [any_place(a) for a in late]
    outs = [struct((tok, width), BF16)] * 2 + [struct((1, width), F32)]
    outs += [struct((2, 1, 2, 2, 3 * (width // 16), HALF), BF16)] * 2
    return run_kernel(
        "near_back", body, place, args, specs, outs, [whole(o) for o in outs],
        grid=(HALF // LANES,),
        scratch=[pltpu.VMEM((both, HALF), BF16)] * 3
        + [pltpu.VMEM((tok, LANES), F32)] * 2
        + [pltpu.VMEM(shape, BF16) for shape in late_shapes]
        + [pltpu.SemaphoreType.DMA((len(late),))],
        after=after, flops=both * both * 0.75 * 20 * 2 * HALF + 20 * both * width * HALF,
    )


def cross_grads(name, place, pairs, x_first, passages=None, after=()):
    width = pairs[0][0][0].shape[1]
    rows = width // 16
    count = len(pairs)
    order, spots, groups = ([], {}, [])
    for left, right in [*pairs, *([] if passages is None else [(passages[:2], passages[2:])])]:
        fresh = []
        for array in (*left, *right):
            if id(array) not in spots:
                spots[id(array)] = len(order)
                fresh.append(len(order))
                order.append(array)
        groups.append((fresh, [spots[id(array)] for array in left], [spots[id(array)] for array in right]))
    given = len(order)
    outs = [struct((2, 2, 2, 2, count * rows, HALF), BF16)] * 2
    if passages is not None:
        enc = passages[0].shape[0] // 4
        outs += [struct((2, enc, width), F32), struct((2, enc, width), BF16)]
    produced = len(outs)

    def body(s, *refs):
        sources, results = refs[:given], refs[given : given + produced]
        held, semaphores = refs[given + produced : -1], refs[-1]
        step = pl.program_id(0)
        moves = copies(sources, held, semaphores)

        @pl.when(step == 0)
        def _():
            for move in moves:
                move.start()

        for at, (fresh, left, right) in enumerate(groups):

            @pl.when(step == at)
            def _(at=at, fresh=fresh, left=left, right=right):
                for spot in fresh:
                    moves[spot].wait()
                if at < count:
                    value = None
                    for part, spot in enumerate(left):
                        tall = held[spot].shape[0]
                        piece = dot_tn(held[spot][...], held[right[0]][pl.ds(part * tall, tall), :])
                        value = piece if value is None else value + piece
                    write_square(s, value, results[0], results[1], 0, x_first)
                    return
                for slot in range(4):
                    slots = pl.ds(slot * enc, enc)
                    value = dot_nt(held[left[0]][slots, :], held[right[0]][...])
                    value = value + dot_nt(held[left[1]][slots, :], held[right[1]][...])
                    if slot % 2 == 0:
                        results[2][slot // 2] = value
                    else:
                        results[3][slot // 2] = value.astype(BF16)

    block = pl.BlockSpec((2, 2, 2, 2, rows, HALF), lambda m, _: (0, 0, 0, 0, jnp.minimum(m, count - 1), 0))
    return run_kernel(
        name, body, place, order, [any_place(a) for a in order], outs,
        [block, block, *(whole(o) for o in outs[2:])],
        grid=(len(groups),),
        scratch=[pltpu.VMEM(a.shape, a.dtype) for a in order]
        + [pltpu.SemaphoreType.DMA((given,))],
        after=after,
    )


def last_pull(place, inputs, gains, grad_res, parts, after=()):
    tok, width = inputs.shape
    steps = 2
    tile = tok // steps

    def body(s, in_ref, gain_ref, dx_ref, *refs):
        part_refs, out_ref = refs[:-1], refs[-1]
        total = part_refs[0][...].astype(F32)
        for ref in part_refs[1:]:
            total = total + ref[...].astype(F32)
        out_ref[...] = dx_ref[...] + norm_pull(in_ref[...].astype(F32), gain_ref[...].reshape(1, width), total)[0]

    args = (inputs, gains, grad_res, *parts)
    block = pl.BlockSpec((tile, width), lambda i, _: (i, 0))
    specs = [block for _ in args]
    specs[1] = whole(gains)
    return run_kernel(
        "last_pull", body, place, args, specs, [struct((tok, width), F32)], [block], grid=(steps,), after=after,
        flops=20 * tok * width,
    )[0]


def rounded(values):
    return lax.reduce_precision(values, 8, 7).astype(BF16)


def add_split(half, keep, recv):
    part = lambda array, at: lax.dynamic_index_in_dim(array, at, 0, False).astype(F32)
    kept = rounded(part(keep, half) + part(recv, half))
    return (kept, rounded(part(keep, 1 - half) + part(recv, 1 - half)))


class Halving:
    def __init__(self, keep, recv, steps):
        self.keep, self.recv, self.steps = (keep, recv, list(steps))

    def step(self, *after):
        half, axis, pairs = self.steps.pop(0)
        keep, recv = (self.keep.reshape(2, -1, HALF), self.recv.reshape(2, -1, HALF))
        if after:
            keep, recv, *_ = lax.optimization_barrier((keep, recv, *after))
        self.keep, send = add_split(half, keep, recv)
        self.recv = lax.ppermute(send, axis, pairs)
        return self.keep


def merge_split(place, step, sums, after=()):
    half, axis, pairs = step
    counts = [a.keep.shape[0] // 4 for a in sums]
    arrays = [array.reshape(2, 2, count, HALF) for a, count in zip(sums, counts) for array in (a.keep, a.recv)]
    starts = [sum(counts[:at]) for at in range(len(counts))]

    def body(s, *refs):
        given, (keep_ref, send_ref) = refs[: len(arrays)], refs[len(arrays) :]
        for target, side in ((keep_ref, s[0]), (send_ref, 1 - s[0])):
            for at, (first, count) in enumerate(zip(starts, counts)):
                for deep in range(2):
                    value = given[2 * at][side, deep].astype(F32) + given[2 * at + 1][side, deep].astype(F32)
                    target[deep, pl.ds(first, count), :] = value.astype(BF16)

    outs = [struct((2, sum(counts), HALF), BF16)] * 2
    keep, send = run_kernel(
        "merge_split", body, half.astype(jnp.int32).reshape(1), arrays, [whole(a) for a in arrays], outs,
        [whole(o) for o in outs], after=after,
    )
    merged = Halving(keep, lax.ppermute(send, axis, pairs), ())
    return merged


def self_start(place, keep4, recv4, gain_own, gain_other, after=()):
    cut = 80
    rest = keep4.shape[4] - cut
    width = gain_own.shape[1]
    piece = width // 8

    def body(s, keep_ref, recv_ref, own_ref, other_ref, ak_ref, as_ref, bk_ref, bs_ref, gains):
        for target, side in ((ak_ref, s[2]), (as_ref, 1 - s[2])):
            for slot, source in enumerate((keep_ref, recv_ref)):
                target[slot] = source[side, 0, :, :, pl.ds(0, cut), :]
        late = pl.ds(cut, rest)

        @pl.when(s[0] == s[1])
        def _():
            bk_ref[:, :, :, pl.ds(0, rest), :] = keep_ref[:, 0, :, :, late, :]
            bs_ref[:, :, :, pl.ds(0, rest), :] = recv_ref[:, 0, :, :, late, :]

        @pl.when(s[0] != s[1])
        def _():
            bk_ref[:, :, :, pl.ds(0, rest), :] = recv_ref[:, 0, :, :, late, :]
            bs_ref[:, :, :, pl.ds(0, rest), :] = keep_ref[:, 0, :, :, late, :]

        gains[...] = jnp.zeros_like(gains)
        gains[pl.ds(0, 3), :] = own_ref[...] + other_ref[...]
        low = gains[...].astype(BF16)
        at_row = lax.broadcasted_iota(jnp.int32, (width, HALF), 0)
        at_col = lax.broadcasted_iota(jnp.int32, (width, HALF), 1)
        for at in range(8):
            pick = jnp.where((at_row == at_col + at * piece) & (at_col < piece), 1.0, 0.0).astype(BF16)
            value = dot_nn(low, pick).astype(BF16)
            for target in (bk_ref, bs_ref):
                target[at % 2, (at // 2) % 2, at // 4, pl.ds(rest, 16), :] = value

    args = (keep4, recv4, gain_own, gain_other)
    outs = [struct((2, 2, 2, cut, HALF), BF16)] * 2 + [struct((2, 2, 2, rest + 16, HALF), BF16)] * 2
    return run_kernel(
        "self_start", body, place, args, [whole(a) for a in args], outs, [whole(o) for o in outs],
        after=after, scratch=[pltpu.VMEM((16, width), F32)],
    )


def finish_sums(name, keep, recv, count, tail=0, after=()):
    rows = (keep.shape[0] - tail) // count
    side = HALF // 2

    def body(s, keep_ref, recv_ref, *outs):
        for at in range(count):
            part = pl.ds(at * rows, rows)
            total = keep_ref[part, :].astype(F32) + recv_ref[part, :].astype(F32)
            outs[at][pl.ds(0, rows), :] = total[:, :side]
            outs[at][pl.ds(rows, rows), :] = total[:, side:]
        if tail:
            part = pl.ds(count * rows, tail)
            outs[count][...] = keep_ref[part, :].astype(F32) + recv_ref[part, :].astype(F32)

    outs = [struct((2 * rows, side), F32)] * count
    if tail:
        outs += [struct((tail, HALF), F32)]
    place = jnp.zeros((1,), jnp.int32)
    return run_kernel(
        name, body, place, (keep, recv), [whole(keep), whole(recv)], outs, [whole(o) for o in outs], after=after
    )


def feed_forward(place, residual, context, out_weight, gain_vec, feed_in, feed_out, cotangent, after=()):
    tok, width = residual.shape
    hidden_width = feed_in.shape[1]
    steps = 4
    chunk = hidden_width // steps
    rows_in = width // 8
    side = width // 4

    def body(
        s, x1_ref, ctx_ref, wo_ref, gain_ref, w1_ref, w2_ref, g_ref,
        out_ref, dx_ref, low_ref, dctx_ref, gain_grad_ref, spread,
        x2, normed, normed_flip, grad_flip, sum_out, sum_norm, block_in, block_out, semaphores,
    ):
        step = pl.program_id(0)

        @pl.when(step == 0)
        def _():
            x2[...] = x1_ref[...] + dot_nn(ctx_ref[...], wo_ref[...])
            normed[...] = (unit_norm(x2[...])[0] * gain_ref[...].reshape(1, width)).astype(BF16)
            normed_flip[...] = normed[...].T
            grad_flip[...] = g_ref[...].T
            sum_out[...] = jnp.zeros_like(sum_out)
            sum_norm[...] = jnp.zeros_like(sum_norm)

        w1, w2, grad = (w1_ref[...], w2_ref[...], g_ref[...])
        pre = dot_nn(normed[...], w1)
        root = 0.7978845608028654
        bend = 0.044715
        square = pre * pre
        swing = jnp.tanh(root * (pre + bend * pre * square))
        hidden = (0.5 * pre * (1.0 + swing)).astype(BF16)
        sum_out[...] += dot_nn(hidden, w2)
        slope = 0.5 * (1.0 + swing) + 0.5 * pre * (1.0 - swing * swing) * (root * (1.0 + 3.0 * bend * square))
        grad_pre = (dot_nt(grad, w2) * slope).astype(BF16)
        sum_norm[...] += dot_nt(grad_pre, w1)
        slot = step % 2

        def moves(at, slot):
            first = pltpu.make_async_copy(
                block_in.at[slot], spread.at[:, at, pl.ds(0, 2 * rows_in), :], semaphores.at[slot, 0]
            )
            second = pltpu.make_async_copy(
                block_out.at[slot], spread.at[pl.ds(2 * at, 2), :, pl.ds(2 * rows_in, side), :], semaphores.at[slot, 1]
            )
            return (first, second)

        @pl.when(step >= 2)
        def _():
            for move in moves(step - 2, slot):
                move.wait()

        grad_in = dot_nn(normed_flip[...], grad_pre).astype(BF16)
        for at in range(8):
            for unit in range(2):
                block_in[slot, at, pl.ds(unit * rows_in, rows_in), :] = grad_in[
                    at * rows_in : (at + 1) * rows_in, unit * HALF : (unit + 1) * HALF
                ]
        grad_out = dot_nn(grad_flip[...], hidden).astype(BF16)
        for at in range(2):
            for part in range(4):
                block_out[slot, at, part] = grad_out[part * side : (part + 1) * side, at * HALF : (at + 1) * HALF]
        for move in moves(step, slot):
            move.start()

        @pl.when(step == steps - 1)
        def _():
            for at in (steps - 2, steps - 1):
                for move in moves(at, at % 2):
                    move.wait()

        @pl.when(step == steps - 1)
        def _():
            out_ref[...] = (x2[...] + sum_out[...]).astype(BF16)
            back, gain_grad_ref[...] = norm_pull(x2[...], gain_ref[...].reshape(1, width), sum_norm[...])
            grad_x = grad.astype(F32) + back
            dx_ref[...] = grad_x
            low = grad_x.astype(BF16)
            low_ref[...] = low
            dctx_ref[...] = dot_nt(low, wo_ref[...]).astype(BF16)

    args = (residual, context, out_weight, gain_vec, feed_in, feed_out, cotangent)
    specs = [whole(a) for a in args]
    specs[4] = pl.BlockSpec((width, chunk), lambda c, _: (0, c))
    specs[5] = pl.BlockSpec((chunk, width), lambda c, _: (c, 0))
    outs = [
        struct((tok, width), BF16),
        struct((tok, width), F32),
        struct((tok, width), BF16),
        struct((tok, width), BF16),
        struct((1, width), F32),
        struct((8, 4, 2 * rows_in + side, HALF), BF16),
    ]
    out_specs = [whole(o) for o in outs]
    out_specs[5] = any_place(outs[5])
    return run_kernel(
        "feed_forward",
        body,
        place,
        args,
        specs,
        outs,
        out_specs,
        grid=(steps,),
        scratch=[
            pltpu.VMEM((tok, width), F32),
            pltpu.VMEM((tok, width), BF16),
            pltpu.VMEM((width, tok), BF16),
            pltpu.VMEM((width, tok), BF16),
            pltpu.VMEM((tok, width), F32),
            pltpu.VMEM((tok, width), F32),
            pltpu.VMEM((2, 8, 2 * rows_in, HALF), BF16),
            pltpu.VMEM((2, 2, 4, side, HALF), BF16),
            pltpu.SemaphoreType.DMA((2, 2)),
        ],
        after=after, flops=12 * tok * width * hidden_width + 4 * tok * width * width,
    )


def local_paired(
    inputs,
    encoded,
    cotangent,
    dec_seg,
    pass_doc,
    enc_mask,
    self_query,
    self_key,
    self_value,
    self_output,
    cross_query,
    cross_key,
    cross_value,
    cross_output,
    feed_in,
    feed_out,
    gain_self,
    gain_cross,
    gain_ff,
):
    inputs, encoded, cotangent = (inputs[0], encoded[0], cotangent[0])
    tok, width = inputs.shape
    enc = encoded.shape[0]
    blk, row = (lax.axis_index("blk"), lax.axis_index("rows"))
    core, chip = (blk % 2, blk // 2)
    y_at, z_low, z_high = (row % 2, (row // 2) % 2, row // 4)
    place = jnp.stack([core, chip, y_at]).astype(jnp.int32)
    gains = (gain_self, gain_cross, gain_ff)
    to_core = lambda array: lax.ppermute(array, "blk", CORE_SWAP)
    to_chip = lambda array: lax.ppermute(array, "blk", CHIP_SWAP)
    in_order = lambda mine, other: jnp.where(core == 0, jnp.concatenate([mine, other]), jnp.concatenate([other, mine]))

    def swap(distance):
        return tuple((at, at ^ distance) for at in range(8))

    over_x = (chip, "blk", CHIP_SWAP)
    over_y = (y_at, "rows", swap(1))
    over_z = ((z_low, "rows", swap(2)), (z_high, "rows", swap(4)))

    gap = -tok % LANES
    spare = jnp.zeros((8 * LANES - tok - gap - enc - 1,), jnp.int32)
    labels = jnp.concatenate([dec_seg[0], spare[:gap], enc_mask[0], pass_doc[0], spare[gap:]])
    labels = jnp.concatenate([labels, jnp.zeros((8 * LANES - labels.shape[0],), jnp.int32)]).reshape(1, 8 * LANES)
    labels_c = to_core(labels)
    inputs_c = to_core(inputs)
    inputs_x = to_chip(inputs)
    labels_x = to_chip(labels)
    encoded_x = to_chip(encoded)
    encoded_c = to_core(encoded)
    h1, sq, sk, sv, near_marks, near_keys_marks, near_out, near_sum = near_part(
        place, inputs, inputs_c, gain_self, (self_query, self_key, self_value), (labels, labels_c)
    )
    ck0, cv0 = passage_pair(place, encoded, encoded_c, cross_key, cross_value, after=(near_out,))
    inputs_x, encoded_x, labels_x, _ = lax.optimization_barrier((inputs_x, encoded_x, labels_x, ck0))
    labels_d = to_core(labels_x)
    inputs_d = to_core(inputs_x)
    encoded_d = to_core(encoded_x)
    spot = place
    place = find_passages(spot, tok, enc, (labels, labels_c, labels_x, labels_d))
    h1_far, fk, fv, far_keys_marks, self_out, self_sum, ctx_keep, ctx_send = far_part(
        spot, inputs_x, inputs_d, gain_self, (self_key, self_value), sq, near_marks, (labels_x, labels_d), near_out, near_sum
    )
    x1, h2, cq, self_context, ck1, cv1, own_marks, docs0, docs1, cross_context, cross_out, cross_sum = cross_part(
        place, inputs, ctx_keep, to_core(ctx_send), self_output, gain_cross, cross_query, encoded_x, encoded_d, cross_key,
        cross_value, ck0, cv0, (labels, labels_c, labels_x, labels_d),
    )
    docs = (docs0, docs1)
    output, dx2, e2, d_cross, grad_gain_ff, spread = feed_forward(
        place, x1, cross_context, cross_output, gain_ff, feed_in, feed_out, cotangent
    )
    total_ff = lax.psum_scatter(spread.reshape(32, *spread.shape[2:]), ("rows", "blk"), scatter_dimension=0, tiled=True)
    dcq, dck, dcv, dx1, e1, grad_gain_cross, ds_keep, ds_send = cross_back(
        place, cq, (ck0, ck1), (cv0, cv1), own_marks, docs, d_cross, cross_out, cross_sum, x1, dx2, cross_query,
        gain_cross, self_output,
    )
    ds_recv = to_core(ds_send)
    passages = (encoded, encoded_c, encoded_x, encoded_d)
    keep_p, send_p = cross_grads(
        "cross_grads", place, (((cross_context,), (e2,)), ((h2,), (dcq,)), (passages, (dck,))), True
    )
    keep_q, send_q, enc_keep, enc_send = cross_grads(
        "passage_grads", place, ((passages, (dcv,)), ((self_context,), (e1,))), False, (dck, dcv, cross_key, cross_value),
        after=(keep_p,),
    )
    recv_p = to_core(send_p)
    recv_p, ds_recv, send_q, enc_send = lax.optimization_barrier((recv_p, ds_recv, send_q, enc_send))
    sum_p = Halving(keep_p, recv_p, (over_x, over_y))
    sum_q = Halving(keep_q, to_core(send_q), (over_y, over_x))
    enc_recv = to_core(enc_send)
    held = (sum_p.step(), sum_q.step())
    dq_far, dk_far, dv_far, far_keep, far_send, gain_far = far_back(
        place, sq, fk, fv, near_marks, far_keys_marks, ds_keep, ds_recv, self_out, self_sum, gain_self, h1_far,
        (self_key, self_value), after=held,
    )
    sum_p.recv, sum_q.recv, far_send = lax.optimization_barrier((sum_p.recv, sum_q.recv, far_send))
    far_recv = to_core(far_send)
    held = (sum_p.step(), sum_q.step())
    far_keep, far_recv, *_ = lax.optimization_barrier((far_keep, far_recv, *held))
    far_here = (far_keep.astype(F32) + far_recv.astype(F32)).astype(BF16)
    from_far = to_chip(far_here)
    near_keep, near_send, gain_near, keep4, send4 = near_back(
        place, sq, sk, sv, near_marks, near_keys_marks, ds_keep, ds_recv, self_out, self_sum, dq_far, gain_self, h1, h1_far,
        (self_query, self_key, self_value), (dk_far, dv_far), after=(far_here, *held),
    )
    tied = lax.optimization_barrier((sum_p.recv, sum_q.recv, from_far, near_send, send4, gain_near))
    sum_p.recv, sum_q.recv, from_far, near_send, send4, gain_near = tied
    gain_grads = jnp.concatenate([gain_far + gain_near, grad_gain_cross, grad_gain_ff])
    gain_recv = to_core(gain_grads)
    recv4 = to_core(send4)
    near_recv = to_core(near_send)
    sum_cross = merge_split(place, over_z[0], (sum_p, sum_q))
    sum_cross.steps = [over_z[1]]
    first_keep, first_send, second_keep, second_send = self_start(
        spot, keep4, recv4, gain_grads, gain_recv, after=(sum_cross.keep,)
    )
    over_slot = (chip ^ core, "blk", CHIP_SWAP)
    sum_first = Halving(first_keep, lax.ppermute(first_send, "rows", swap(1)), (over_slot,))
    sum_second = Halving(second_keep, to_chip(second_send), (over_y,))
    input_grad = last_pull(
        place, inputs, gain_self, dx1, (near_keep, near_recv, from_far), after=(first_send, second_send)
    )
    enc_keep, enc_recv, _ = lax.optimization_barrier((enc_keep, enc_recv, input_grad))
    enc_sum = enc_keep + enc_recv.astype(F32)
    held = (sum_cross.step(input_grad), enc_sum)
    held = (sum_first.step(*held), sum_second.step(*held))
    enc_there, *_ = lax.optimization_barrier((enc_sum[1].astype(BF16), *held))
    from_chip = to_chip(enc_there)
    rows = width // 16
    total_ff, *_ = lax.optimization_barrier((total_ff[0], *held))
    total_ff = total_ff.astype(F32)
    grad_feed_in = jnp.concatenate([total_ff[: 2 * rows], total_ff[2 * rows : 4 * rows]], axis=1)
    feed_out_flip = total_ff[4 * rows :]
    cross_o, cross_q, cross_k, cross_v, self_o = finish_sums(
        "finish_cross", sum_cross.keep, sum_cross.recv, 5, after=held
    )
    sum_self = merge_split(place, over_z[0], (sum_first, sum_second), after=(self_o,))
    sum_self.steps = [over_z[1]]
    enc_last, from_chip, _ = lax.optimization_barrier((enc_sum[0], from_chip, sum_self.keep))
    encoded_grad = enc_last + from_chip.astype(F32)
    sum_self.step()
    self_q, self_k, self_v, gain_rows = finish_sums("finish_self", sum_self.keep, sum_self.recv, 3, 16)
    piece = width // 8
    return (
        output[None],
        input_grad[None],
        encoded_grad[None],
        self_q,
        self_k,
        self_v,
        self_o,
        cross_q,
        cross_k,
        cross_v,
        cross_o,
        grad_feed_in,
        feed_out_flip.T,
        gain_rows[0, :piece],
        gain_rows[1, :piece],
        gain_rows[2, :piece],
    )


def solution(mesh):
    paired = mesh.shape["blk"] == 4 and mesh.shape["rows"] == 8
    body = local_paired if paired else local_any
    in_specs = (
        P("rows", "blk", None),
        P("rows", "blk", None),
        P("rows", "blk", None),
        P("rows", "blk"),
        P("rows", "blk"),
        P("rows", "blk"),
        P(),
        P(),
        P(),
        P(),
        P(),
        P(),
        P(),
        P(),
        P(),
        P(),
        P(),
        P(),
        P(),
    )
    out_specs = (
        P("rows", "blk", None),
        P("rows", "blk", None),
        P("rows", "blk", None),
        P("rows", "blk"),
        P("rows", "blk"),
        P("rows", "blk"),
        P("rows", "blk"),
        P("rows", "blk"),
        P("rows", "blk"),
        P("rows", "blk"),
        P("rows", "blk"),
        P("rows", "blk"),
        P("rows", "blk"),
        P("rows"),
        P("rows"),
        P("rows"),
    )
    return jax.shard_map(body, mesh=mesh, in_specs=in_specs, out_specs=out_specs, check_vma=False)
```

```python
import jax
import jax.numpy as jnp
from jax import lax
from jax.experimental import pallas as pl
from jax.experimental.pallas import tpu as pltpu
from jax.sharding import PartitionSpec as P

HEADS = 12
HEAD_DIM = 64
PLEN = 384


NEG_FILL = -1e30
SCALE = 0.125


def split_heads(matrix):
    return matrix.reshape(matrix.shape[0], matrix.shape[1], HEADS, HEAD_DIM)


def join_heads(tensor):
    return jnp.transpose(tensor, (0, 2, 1, 3)).reshape(
        tensor.shape[0], tensor.shape[2], HEADS * HEAD_DIM
    )


def rms_norm(values, gain_vec):
    return values * lax.rsqrt(jnp.mean(values * values, axis=-1, keepdims=True) + 1e-06) * gain_vec


def norm_back(values, gain_vec, grad_out):
    _, pullback = jax.vjp(rms_norm, values, gain_vec)
    return pullback(grad_out)


def project(left, weight):
    return jnp.einsum("rqd,df->rqf", left, weight, preferred_element_type=jnp.float32)


def back_project(grad_out, weight):
    return jnp.einsum("rqf,df->rqd", grad_out, weight, preferred_element_type=jnp.float32)


def weight_grad(left, grad_out):
    return jnp.einsum("rqd,rqf->df", left, grad_out, preferred_element_type=jnp.float32)


def head_scores(queries, keys):
    return (
        jnp.einsum(
            "rqhe,rkhe->rhqk",
            split_heads(queries),
            split_heads(keys),
            preferred_element_type=jnp.float32,
        )
        * SCALE
    )


def empty_state(row_count, query_count):
    return (
        jnp.full((row_count, HEADS, query_count), NEG_FILL, jnp.float32),
        jnp.zeros((row_count, HEADS, query_count), jnp.float32),
        jnp.zeros((row_count, HEADS, query_count, HEAD_DIM), jnp.float32),
    )


def online_block(state, queries, keys, values, allowed):
    run_max, run_sum, run_acc = state
    scores = head_scores(queries, keys)
    allowed = allowed[:, None]
    new_max = jnp.maximum(run_max, jnp.max(jnp.where(allowed, scores, NEG_FILL), axis=-1))
    weights = jnp.where(allowed, jnp.exp(scores - new_max[..., None]), 0.0)
    new_sum = jnp.sum(weights, axis=-1)
    new_acc = jnp.einsum(
        "rhqk,rkhe->rhqe",
        weights.astype(jnp.bfloat16),
        split_heads(values),
        preferred_element_type=jnp.float32,
    )
    return (new_max, new_sum, new_acc)


def finish(state):
    run_max, run_sum, run_acc = state
    return (run_acc / run_sum[..., None], run_max + jnp.log(run_sum))


def grad_pair(queries, grad_ctx, log_sum, delta, keys, values, allowed):
    scores = head_scores(queries, keys)
    probs_now = jnp.where(allowed[:, None], jnp.exp(scores - log_sum[..., None]), 0.0)
    grad_probs = jnp.einsum(
        "rqhe,rkhe->rhqk",
        split_heads(grad_ctx),
        split_heads(values),
        preferred_element_type=jnp.float32,
    )
    grad_scores = (probs_now * (grad_probs - delta[..., None])).astype(jnp.bfloat16)
    grad_query = (
        jnp.einsum(
            "rhqk,rkhe->rqhe", grad_scores, split_heads(keys), preferred_element_type=jnp.float32
        )
        * SCALE
    )
    grad_key = (
        jnp.einsum(
            "rhqk,rqhe->rkhe", grad_scores, split_heads(queries), preferred_element_type=jnp.float32
        )
        * SCALE
    )
    grad_value = jnp.einsum(
        "rhqk,rqhe->rkhe",
        probs_now.astype(jnp.bfloat16),
        split_heads(grad_ctx),
        preferred_element_type=jnp.float32,
    )
    row_count = keys.shape[0]
    key_count = keys.shape[1]
    joined = jnp.concatenate(
        (grad_key.reshape(row_count, key_count, -1), grad_value.reshape(row_count, key_count, -1)),
        axis=-1,
    )
    return (grad_query.reshape(row_count, queries.shape[1], -1), joined)


def head_delta(grad_ctx, attended):
    return jnp.einsum("rqhe,rhqe->rhq", split_heads(grad_ctx).astype(jnp.float32), attended)


def spread_matrix(matrix, row_split, block_count):
    first, second = matrix.shape
    tiles = matrix.reshape(row_split, first // row_split, block_count, second // block_count)
    return jnp.transpose(tiles, (0, 2, 1, 3)).reshape(
        row_split * block_count, first // row_split, second // block_count
    )


def spread_gain(vector, row_split, block_count):
    tiles = vector.reshape(row_split, 1, vector.shape[0] // row_split)
    return jnp.broadcast_to(tiles, (row_split, block_count, vector.shape[0] // row_split)).reshape(
        row_split * block_count, vector.shape[0] // row_split
    )


def local_any(
    inputs,
    encoded,
    cotangent,
    dec_seg,
    pass_doc,
    enc_mask,
    self_query,
    self_key,
    self_value,
    self_output,
    cross_query,
    cross_key,
    cross_value,
    cross_output,
    feed_in,
    feed_out,
    gain_self,
    gain_cross,
    gain_ff,
):
    row_count, tok_shard, width = inputs.shape
    enc_shard = encoded.shape[1]
    block_count = lax.axis_size("blk")
    row_split = lax.axis_size("rows")
    block_ids = jnp.arange(block_count)
    query_places = lax.axis_index("blk") * tok_shard + jnp.arange(tok_shard)
    start_state = empty_state(row_count, tok_shard)
    residual = inputs.astype(jnp.float32)
    normed_self = rms_norm(residual, gain_self).astype(jnp.bfloat16)
    self_queries = project(normed_self, self_query).astype(jnp.bfloat16)
    self_keys = project(normed_self, self_key).astype(jnp.bfloat16)
    self_values = project(normed_self, self_value).astype(jnp.bfloat16)
    piece_keys = lax.all_gather(self_keys, "blk", axis=1, tiled=True)
    piece_values = lax.all_gather(self_values, "blk", axis=1, tiled=True)
    piece_segs = lax.all_gather(dec_seg, "blk", axis=1, tiled=True)
    key_places = jnp.arange(piece_keys.shape[1])
    allowed = (dec_seg[:, :, None] == piece_segs[:, None, :]) & (
        key_places[None, None, :] <= query_places[None, :, None]
    )
    self_attn, self_lse = finish(
        online_block(start_state, self_queries, piece_keys, piece_values, allowed)
    )
    self_context = join_heads(self_attn).astype(jnp.bfloat16)
    after_self = residual + project(self_context, self_output)
    normed_cross = rms_norm(after_self, gain_cross).astype(jnp.bfloat16)
    cross_queries = project(normed_cross, cross_query).astype(jnp.bfloat16)
    cross_keys = project(encoded, cross_key).astype(jnp.bfloat16)
    cross_values = project(encoded, cross_value).astype(jnp.bfloat16)
    key_docs = jnp.where(enc_mask == 1, jnp.repeat(pass_doc, PLEN, axis=1), -1)
    piece_keys = lax.all_gather(cross_keys, "blk", axis=1, tiled=True)
    piece_values = lax.all_gather(cross_values, "blk", axis=1, tiled=True)
    piece_docs = lax.all_gather(key_docs, "blk", axis=1, tiled=True)
    allowed = dec_seg[:, :, None] == piece_docs[:, None, :]
    cross_attn, cross_lse = finish(
        online_block(start_state, cross_queries, piece_keys, piece_values, allowed)
    )
    cross_context = join_heads(cross_attn).astype(jnp.bfloat16)
    after_cross = after_self + project(cross_context, cross_output)
    normed_ff = rms_norm(after_cross, gain_ff).astype(jnp.bfloat16)
    before_act = project(normed_ff, feed_in)
    hidden = jax.nn.gelu(before_act).astype(jnp.bfloat16)
    output = (after_cross + project(hidden, feed_out)).astype(jnp.bfloat16)
    grad_feed_out = weight_grad(hidden, cotangent)
    grad_hidden = back_project(cotangent, feed_out)
    _, gelu_back = jax.vjp(jax.nn.gelu, before_act)
    grad_before = gelu_back(grad_hidden)[0].astype(jnp.bfloat16)
    grad_feed_in = weight_grad(normed_ff, grad_before)
    grad_cross_res, grad_gain_ff = norm_back(
        after_cross, gain_ff, back_project(grad_before, feed_in)
    )
    grad_cross_res = cotangent.astype(jnp.float32) + grad_cross_res
    cross_branch = grad_cross_res.astype(jnp.bfloat16)
    grad_cross_output = weight_grad(cross_context, cross_branch)
    grad_cross_ctx = back_project(cross_branch, cross_output).astype(jnp.bfloat16)
    cross_delta = head_delta(grad_cross_ctx, cross_attn)
    all_keys, all_values, all_docs = (
        lax.all_gather(cross_keys, "blk", axis=1, tiled=True),
        lax.all_gather(cross_values, "blk", axis=1, tiled=True),
        lax.all_gather(key_docs, "blk", axis=1, tiled=True),
    )

    def passage_step(running, block_index):
        offset = block_index * enc_shard
        piece_keys = lax.dynamic_slice_in_dim(all_keys, offset, enc_shard, 1)
        piece_values = lax.dynamic_slice_in_dim(all_values, offset, enc_shard, 1)
        piece_docs = lax.dynamic_slice_in_dim(all_docs, offset, enc_shard, 1)
        allowed = dec_seg[:, :, None] == piece_docs[:, None, :]
        grad_query, grad_kv = grad_pair(
            cross_queries, grad_cross_ctx, cross_lse, cross_delta, piece_keys, piece_values, allowed
        )
        return (running + grad_query, grad_kv)

    grad_cross_q, key_terms = lax.scan(
        passage_step, jnp.zeros((row_count, tok_shard, width), jnp.float32), block_ids
    )
    grad_cross_kv = lax.psum_scatter(
        key_terms.astype(jnp.bfloat16), "blk", scatter_dimension=0, tiled=True
    ).astype(jnp.float32)[0]
    low_cross_q = grad_cross_q.astype(jnp.bfloat16)
    low_cross_k = grad_cross_kv[..., :width].astype(jnp.bfloat16)
    low_cross_v = grad_cross_kv[..., width:].astype(jnp.bfloat16)
    grad_cross_query = weight_grad(normed_cross, low_cross_q)
    grad_cross_key = weight_grad(encoded, low_cross_k)
    grad_cross_value = weight_grad(encoded, low_cross_v)
    encoded_grad = back_project(low_cross_k, cross_key) + back_project(low_cross_v, cross_value)
    grad_self_res, grad_gain_cross = norm_back(
        after_self, gain_cross, back_project(low_cross_q, cross_query)
    )
    grad_self_res = grad_cross_res + grad_self_res
    self_branch = grad_self_res.astype(jnp.bfloat16)
    grad_self_output = weight_grad(self_context, self_branch)
    grad_self_ctx = back_project(self_branch, self_output).astype(jnp.bfloat16)
    self_delta = head_delta(grad_self_ctx, self_attn)
    all_self_keys, all_self_values, all_self_segs = (
        lax.all_gather(self_keys, "blk", axis=1, tiled=True),
        lax.all_gather(self_values, "blk", axis=1, tiled=True),
        lax.all_gather(dec_seg, "blk", axis=1, tiled=True),
    )

    def self_step(running, block_index):
        offset = block_index * tok_shard
        piece_keys = lax.dynamic_slice_in_dim(all_self_keys, offset, tok_shard, 1)
        piece_values = lax.dynamic_slice_in_dim(all_self_values, offset, tok_shard, 1)
        piece_segs = lax.dynamic_slice_in_dim(all_self_segs, offset, tok_shard, 1)
        key_places = offset + jnp.arange(tok_shard)
        allowed = (dec_seg[:, :, None] == piece_segs[:, None, :]) & (
            key_places[None, None, :] <= query_places[None, :, None]
        )
        grad_query, grad_kv = grad_pair(
            self_queries, grad_self_ctx, self_lse, self_delta, piece_keys, piece_values, allowed
        )
        return (running + grad_query, grad_kv)

    grad_self_q, self_terms = lax.scan(
        self_step, jnp.zeros((row_count, tok_shard, width), jnp.float32), block_ids
    )
    grad_self_kv = lax.psum_scatter(
        self_terms.astype(jnp.bfloat16), "blk", scatter_dimension=0, tiled=True
    ).astype(jnp.float32)[0]
    low_self_q = grad_self_q.astype(jnp.bfloat16)
    low_self_k = grad_self_kv[..., :width].astype(jnp.bfloat16)
    low_self_v = grad_self_kv[..., width:].astype(jnp.bfloat16)
    grad_self_query = weight_grad(normed_self, low_self_q)
    grad_self_key = weight_grad(normed_self, low_self_k)
    grad_self_value = weight_grad(normed_self, low_self_v)
    grad_normed = (
        back_project(low_self_q, self_query)
        + back_project(low_self_k, self_key)
        + back_project(low_self_v, self_value)
    )
    grad_first, grad_gain_self = norm_back(residual, gain_self, grad_normed)
    input_grad = grad_self_res + grad_first
    matrices = (
        grad_self_query,
        grad_self_key,
        grad_self_value,
        grad_self_output,
        grad_cross_query,
        grad_cross_key,
        grad_cross_value,
        grad_cross_output,
        grad_feed_in,
        grad_feed_out,
    )
    spread_mats = tuple((spread_matrix(matrix, row_split, block_count) for matrix in matrices))
    spread_gains = tuple(
        (
            spread_gain(vector, row_split, block_count)
            for vector in (grad_gain_self, grad_gain_cross, grad_gain_ff)
        )
    )
    summed = (
        lax.psum_scatter(spread_mats[0], ("rows", "blk"), scatter_dimension=0, tiled=True),
        lax.psum_scatter(spread_mats[1], ("rows", "blk"), scatter_dimension=0, tiled=True),
        lax.psum_scatter(spread_mats[2], ("rows", "blk"), scatter_dimension=0, tiled=True),
        lax.psum_scatter(spread_mats[3], ("rows", "blk"), scatter_dimension=0, tiled=True),
        lax.psum_scatter(spread_mats[4], ("rows", "blk"), scatter_dimension=0, tiled=True),
        lax.psum_scatter(spread_mats[5], ("rows", "blk"), scatter_dimension=0, tiled=True),
        lax.psum_scatter(spread_mats[6], ("rows", "blk"), scatter_dimension=0, tiled=True),
        lax.psum_scatter(spread_mats[7], ("rows", "blk"), scatter_dimension=0, tiled=True),
        lax.psum_scatter(spread_mats[8], ("rows", "blk"), scatter_dimension=0, tiled=True),
        lax.psum_scatter(spread_mats[9], ("rows", "blk"), scatter_dimension=0, tiled=True),
        lax.psum_scatter(spread_gains[0], ("rows", "blk"), scatter_dimension=0, tiled=True),
        lax.psum_scatter(spread_gains[1], ("rows", "blk"), scatter_dimension=0, tiled=True),
        lax.psum_scatter(spread_gains[2], ("rows", "blk"), scatter_dimension=0, tiled=True),
    )
    return (
        output,
        input_grad,
        encoded_grad,
        summed[0][0],
        summed[1][0],
        summed[2][0],
        summed[3][0],
        summed[4][0],
        summed[5][0],
        summed[6][0],
        summed[7][0],
        summed[8][0],
        summed[9][0],
        summed[10][0],
        summed[11][0],
        summed[12][0],
    )


BF16 = jnp.bfloat16
F32 = jnp.float32
LANES = 128
HALF = 2 * LANES + LANES
CORE_SWAP = ((0, 1), (1, 0), (2, 3), (3, 2))
CHIP_SWAP = ((0, 2), (2, 0), (1, 3), (3, 1))


def dot_nn(left, right):
    return jnp.dot(left, right, preferred_element_type=F32)


def dot_nt(left, right):
    return lax.dot_general(left, right, (((1,), (1,)), ((), ())), preferred_element_type=F32)


def dot_tn(left, right):
    return lax.dot_general(left, right, (((0,), (0,)), ((), ())), preferred_element_type=F32)


def whole(array):
    rank = len(array.shape)
    return pl.BlockSpec(array.shape, lambda *_: (0,) * rank)


def struct(shape, dtype):
    return jax.ShapeDtypeStruct(shape, dtype)


def run_kernel(name, body, scalars, args, in_specs, outs, out_specs, grid=(1,), scratch=(), flops=0, after=(), vmem=58):
    moved = sum(a.size * a.dtype.itemsize for a in args)
    if after:
        inner, given = (body, len(args))

        def body(s, *refs):
            inner(s, *refs[:given], *refs[given + len(after) :])

        args = (*args, *after)
        in_specs = [*in_specs, *([pl.BlockSpec(memory_space=pl.ANY)] * len(after))]
    moved += sum(o.size * o.dtype.itemsize for o in outs)
    return pl.pallas_call(
        body,
        grid_spec=pltpu.PrefetchScalarGridSpec(
            num_scalar_prefetch=1,
            grid=grid,
            in_specs=list(in_specs),
            out_specs=list(out_specs),
            scratch_shapes=list(scratch),
        ),
        out_shape=list(outs),
        compiler_params=pltpu.CompilerParams(vmem_limit_bytes=vmem << 20),
        name=name,
    )(scalars, *args)


def unit_norm(values):
    scale = lax.rsqrt(jnp.mean(values * values, axis=-1, keepdims=True) + 1e-06)
    return (values * scale, scale)


def norm_pull(values, gain_vec, grad_out):
    normal, scale = unit_norm(values)
    scaled = grad_out * gain_vec
    inner = jnp.mean(scaled * normal, axis=-1, keepdims=True)
    return (scale * (scaled - normal * inner), jnp.sum(grad_out * normal, axis=0, keepdims=True))


def head_lanes():
    lane = lax.broadcasted_iota(jnp.int32, (1, LANES), 1)
    return (lane, (lane < HEAD_DIM, lane >= HEAD_DIM))


def only(keep, values):
    return jnp.where(keep, values, jnp.zeros_like(values))


def soft_block(queries, marks, keys, values):
    lane, masks = head_lanes()
    attended, sums = ([], [])
    for keep in masks:
        scores = dot_nt(jnp.concatenate([only(keep, queries), marks], axis=1), keys)
        top = jnp.max(scores, axis=1, keepdims=True)
        weights = jnp.exp(scores - top)
        total = jnp.sum(weights, axis=1, keepdims=True)
        attended.append(dot_nn(weights.astype(BF16), values) / total)
        sums.append(top + jnp.log(total))
    return (jnp.where(masks[0], *attended), jnp.where(masks[0], *sums))


def causal_block(queries, marks, keys, values):
    lane, masks = head_lanes()
    rows, cols = queries.shape[0], keys.shape[0]
    flipped = values.T
    attended, sums = ([], [])
    for at, keep in enumerate(masks):
        scores = dot_nt(keys, jnp.concatenate([only(keep, queries), marks], axis=1))
        at_row = lax.broadcasted_iota(jnp.int32, (rows, rows), 0)
        at_col = lax.broadcasted_iota(jnp.int32, (rows, rows), 1)
        last = jnp.where(at_row <= at_col, scores[cols - rows :, :], NEG_FILL)
        scores = last if cols == rows else jnp.concatenate([scores[: cols - rows, :], last], axis=0)
        top = jnp.max(scores, axis=0, keepdims=True)
        weights = jnp.exp(scores - top)
        total = jnp.sum(weights, axis=0, keepdims=True)
        head = flipped[at * HEAD_DIM : (at + 1) * HEAD_DIM, :]
        attended.append(dot_nn(head, weights.astype(BF16)) / total)
        sums.append(jnp.broadcast_to(top + jnp.log(total), (HEAD_DIM, rows)))
    return (jnp.concatenate(attended, axis=0).T, jnp.concatenate(sums, axis=0).T)


def three_parts(spread):
    high = spread.astype(BF16)
    rest = spread - high.astype(F32)
    middle = rest.astype(BF16)
    return (-high, -middle, -(rest - middle.astype(F32)).astype(BF16))


def put_parts(lane, head, parts, base):
    for at, part in enumerate(parts):
        base = jnp.where(lane == head * HEAD_DIM + 3 + at, part, base)
    return base


def ones_lanes(lane):
    place = lane % HEAD_DIM
    return (place >= 3) & (place < 6)


def head_totals(product):
    high = product.astype(BF16)
    low = (product - high.astype(F32)).astype(BF16)
    at_row = lax.broadcasted_iota(jnp.int32, (2 * LANES, LANES), 0) % LANES
    at_col = lax.broadcasted_iota(jnp.int32, (2 * LANES, LANES), 1)
    same = jnp.where((at_row < HEAD_DIM) == (at_col < HEAD_DIM), 1.0, 0.0).astype(BF16)
    return dot_nn(jnp.concatenate([high, low], axis=1), same)


def pull_block(queries, marks, keys, key_marks, values, grads, attended, sums, causal):
    lane, masks = head_lanes()
    rows, cols = queries.shape[0], keys.shape[0]
    wide_keys = jnp.concatenate([keys, key_marks], axis=1)
    ones = jnp.where(ones_lanes(lane), 1.0, 0.0).astype(BF16)
    wide_values = jnp.concatenate([values, jnp.broadcast_to(ones, (cols, LANES))], axis=1)
    delta_parts = three_parts(head_totals(grads.astype(F32) * attended))
    sum_parts = three_parts(sums)
    flipped = keys.T
    grad_queries = []
    grad_keys = grad_values = None
    for at, keep in enumerate(masks):
        query, grad = (only(keep, queries), only(keep, grads))
        wide_query = jnp.concatenate([query, put_parts(lane, at, sum_parts, marks)], axis=1)
        wide_grad = jnp.concatenate([grad, put_parts(lane, at, delta_parts, jnp.zeros_like(marks))], axis=1)
        probs = jnp.exp(dot_nt(wide_keys, wide_query))
        if causal:
            at_row = lax.broadcasted_iota(jnp.int32, (rows, rows), 0)
            at_col = lax.broadcasted_iota(jnp.int32, (rows, rows), 1)
            last = jnp.where(at_row <= at_col, probs[cols - rows :, :], 0.0)
            probs = last if cols == rows else jnp.concatenate([probs[: cols - rows, :], last], axis=0)
        grad_scores = (probs * dot_nt(wide_values, wide_grad)).astype(BF16)
        grad_queries.append(dot_nn(flipped, grad_scores))
        key_part = dot_nn(grad_scores, query)
        value_part = dot_nn(probs.astype(BF16), grad)
        grad_keys = key_part if at == 0 else grad_keys + key_part
        grad_values = value_part if at == 0 else grad_values + value_part
    sub = lax.broadcasted_iota(jnp.int32, (LANES, 1), 0)
    return (jnp.where(sub < HEAD_DIM, *grad_queries).T * SCALE, grad_keys, grad_values)


def pair_columns(array):
    return pl.BlockSpec((array.shape[0], LANES), lambda p, _: (0, p))


def query_marks(labels):
    lane = lax.broadcasted_iota(jnp.int32, (LANES, 1), 0)
    return jnp.where(labels == lane, 1.0, 0.0).T.astype(BF16)


def key_marks(labels):
    lane = lax.broadcasted_iota(jnp.int32, (LANES, 1), 0)
    closed = jnp.where(labels != lane, NEG_FILL, 0.0)
    return jnp.where(lane < 3, closed, jnp.where(ones_lanes(lane), 1.0, 0.0)).T.astype(BF16)


def doc_marks(label_ref, tok, enc):
    first = -(-tok // LANES) * LANES
    doc = label_ref[:, pl.ds(first + enc, LANES)][:, 0:1]
    return key_marks(jnp.where(label_ref[:, pl.ds(first, enc)] == 1, doc, -1))


def pair_lanes():
    return pl.ds(pl.multiple_of(pl.program_id(0) * LANES, LANES), LANES)


def column_block(array):
    return pl.BlockSpec((array.shape[0], HALF), lambda _, s: (0, s[0]))


def any_place(_):
    return pl.BlockSpec(memory_space=pl.ANY)


def copies(sources, targets, semaphores):
    return [pltpu.make_async_copy(src, dst, semaphores.at[at]) for at, (src, dst) in enumerate(zip(sources, targets))]


def find_passages(place, tok, enc, labels):
    spot = -(-tok // LANES) * LANES + enc

    def body(s, own_ref, *refs):
        label_refs, out_ref = refs[:4], refs[4]
        own = own_ref[:, pl.ds(0, tok)]
        used = [jnp.max(jnp.where(own == ref[0, spot], 1, 0)) for ref in label_refs]
        total = used[0] + used[1] + used[2] + used[3]
        out_ref[0] = s[0]
        out_ref[1] = s[1]
        out_ref[6] = total
        out_ref[7] = 0
        ahead, behind = (jnp.int32(0), total)
        for slot in range(4):
            out_ref[2 + jnp.where(used[slot] == 1, ahead, behind)] = jnp.int32(slot)
            ahead, behind = (ahead + used[slot], behind + 1 - used[slot])

    smem = pl.BlockSpec(memory_space=pltpu.SMEM)
    return run_kernel(
        "find_passages", body, place, (labels[0], *labels), [whole(labels[0])] + [smem] * 4, [struct((8,), jnp.int32)],
        [smem],
    )[0]


def write_projections(s, mine_ref, other_ref, gain, weight_refs, scales, normed_ref, out_refs):
    tok = mine_ref.shape[0]
    for source, part in ((mine_ref, s[0]), (other_ref, 1 - s[0])):
        rows = pl.ds(pl.multiple_of(part * tok, tok), tok)
        normed = (unit_norm(source[...].astype(F32))[0] * gain).astype(BF16)
        normed_ref[rows, :] = normed
        for weight_ref, out_ref, scale in zip(weight_refs, out_refs, scales):
            out_ref[rows, :] = (dot_nn(normed, weight_ref[...]) * scale).astype(BF16)


def near_part(place, mine, other, gain_vec, weights, labels, passages, passage_weights, after=()):
    tok, width = mine.shape
    both = 2 * tok
    enc = passages[0].shape[0]
    third = width // 3

    def body(
        s, mine_ref, other_ref, gain_ref, wq_ref, wk_ref, wv_ref, own_ref, core_ref, e0_ref, e1_ref, ck_ref, cv_ref,
        h_ref, q_ref, k_ref, v_ref, m_ref, km_ref, out_ref, sum_ref, pk_ref, pv_ref,
    ):
        @pl.when(pl.program_id(0) == 0)
        def _():
            for source, part in ((own_ref, s[0]), (core_ref, 1 - s[0])):
                rows = pl.ds(pl.multiple_of(part * tok, tok), tok)
                m_ref[rows, :] = query_marks(source[:, pl.ds(0, tok)])
                km_ref[rows, :] = key_marks(source[:, pl.ds(0, tok)])
            write_projections(
                s, mine_ref, other_ref, gain_ref[...].reshape(1, width), (wq_ref, wk_ref, wv_ref), (SCALE, 1.0, 1.0), h_ref,
                (q_ref, k_ref, v_ref),
            )

        pair = pair_lanes()
        for at in (0, 1):
            rows, seen = (pl.ds(at * tok, tok), pl.ds(0, (at + 1) * tok))
            wide = jnp.concatenate([k_ref[seen, pair], km_ref[seen, :]], axis=1)
            out_ref[rows, :], sum_ref[rows, :] = causal_block(
                q_ref[rows, pair], m_ref[rows, :], wide, v_ref[seen, pair]
            )
        for at, source in enumerate((e0_ref, e1_ref)):
            rows = pl.ds(at * enc, enc)
            pk_ref[rows, :] = dot_nn(source[...], ck_ref[...]).astype(BF16)
            pv_ref[rows, :] = dot_nn(source[...], cv_ref[...]).astype(BF16)

    args = (mine, other, gain_vec, *weights, *labels, *passages, *passage_weights)
    specs = [whole(a) for a in args]
    specs[3:6] = [column_block(w) for w in weights]
    specs[10:12] = [pl.BlockSpec((width, third), lambda p, _: (0, p))] * 2
    outs = [struct((both, width), BF16)] + [struct((both, HALF), BF16)] * 3 + [struct((both, LANES), BF16)] * 2
    outs += [struct((both, HALF), F32)] * 2 + [struct((2 * enc, width), BF16)] * 2
    return run_kernel(
        "near_part", body, place, args, specs, outs,
        [whole(o) for o in outs[:6]]
        + [pair_columns(o) for o in outs[6:8]]
        + [pl.BlockSpec((2 * enc, third), lambda p, _: (0, p))] * 2,
        grid=(HALF // LANES,), after=after, flops=both * both * 6 * 2 * HALF,
    )


def far_part(place, mine, other, gain_vec, weights, queries, marks, labels, near_out, near_sum, after=()):
    tok, width = mine.shape
    both = 2 * tok

    def body(
        s, mine_ref, other_ref, gain_ref, wk_ref, wv_ref, q_ref, m_ref, lx_ref, ld_ref, no_ref, ns_ref,
        h_ref, k_ref, v_ref, km_ref, out_ref, sum_ref, keep_ref, send_ref,
    ):
        pair = pair_lanes()

        @pl.when(pl.program_id(0) == 0)
        def _():
            for source, part in ((lx_ref, s[0]), (ld_ref, 1 - s[0])):
                rows = pl.ds(pl.multiple_of(part * tok, tok), tok)
                km_ref[rows, :] = key_marks(source[:, pl.ds(0, tok)])

        def write(at, out, log_sum):
            rows = pl.ds(at * tok, tok)
            out_ref[rows, :] = out
            sum_ref[rows, :] = log_sum

            @pl.when(s[0] == at)
            def _():
                keep_ref[...] = out.astype(BF16)

            @pl.when(s[0] != at)
            def _():
                send_ref[...] = out.astype(BF16)

        @pl.when(s[1] == 0)
        def _():
            for at in (0, 1):
                rows = pl.ds(at * tok, tok)
                write(at, no_ref[rows, :], ns_ref[rows, :])

            @pl.when(pl.program_id(0) == 0)
            def _():
                for ref in (h_ref, k_ref, v_ref):
                    ref[...] = jnp.zeros_like(ref)

        @pl.when(s[1] != 0)
        def _():
            @pl.when(pl.program_id(0) == 0)
            def _():
                write_projections(
                    s, mine_ref, other_ref, gain_ref[...].reshape(1, width), (wk_ref, wv_ref), (1.0, 1.0), h_ref, (k_ref, v_ref)
                )

            wide = jnp.concatenate([k_ref[:, pair], km_ref[...]], axis=1)
            for at in (0, 1):
                rows = pl.ds(at * tok, tok)
                out, log_sum = soft_block(q_ref[rows, :], m_ref[rows, :], wide, v_ref[:, pair])
                near_log = ns_ref[rows, :]
                top = jnp.maximum(near_log, log_sum)
                near_share, far_share = (jnp.exp(near_log - top), jnp.exp(log_sum - top))
                total = near_share + far_share
                write(at, (no_ref[rows, :] * near_share + out * far_share) / total, top + jnp.log(total))

    args = (mine, other, gain_vec, *weights, queries, marks, *labels, near_out, near_sum)
    specs = [whole(a) for a in args]
    specs[3:5] = [column_block(w) for w in weights]
    for at in (5, 9, 10):
        specs[at] = pair_columns(args[at])
    outs = [struct((both, width), BF16)] + [struct((both, HALF), BF16)] * 2 + [struct((both, LANES), BF16)]
    outs += [struct((both, HALF), F32)] * 2 + [struct((tok, HALF), BF16)] * 2
    return run_kernel(
        "far_part", body, place, args, specs, outs, [whole(o) for o in outs[:4]] + [pair_columns(o) for o in outs[4:]],
        grid=(HALF // LANES,), after=after, flops=both * both * 8 * 2 * HALF,
    )


def gather_slots(s, enc, target, first_ref, second_ref, lanes=slice(None)):
    for at in range(4):
        slot = s[2 + at]
        rows = pl.ds(at * enc, enc)

        @pl.when(slot < 2)
        def _():
            target[rows, :] = first_ref[pl.ds(pl.multiple_of(slot * enc, enc), enc), :]

        @pl.when(slot >= 2)
        def _():
            target[rows, :] = second_ref[pl.ds(pl.multiple_of((slot - 2) * enc, enc), enc), lanes]


def by_count(s, work):
    pl.when(s[6] <= 2)(lambda: work(2))
    pl.when(s[6] == 3)(lambda: work(3))
    pl.when(s[6] >= 4)(lambda: work(4))


def cross_part(
    place, inputs, ctx_keep, ctx_recv, out_weight, gain_vec, query_weight, first, second, key_weight, value_weight,
    keys, values, labels, after=(),
):
    tok, width = inputs.shape
    enc = first.shape[0]

    def body(
        s, in_ref, keep_ref, recv_ref, wa_ref, wb_ref, gain_ref, wq_ref, first_ref, second_ref, wk_ref, wv_ref, k0_ref, v0_ref,
        l0_ref, l1_ref, l2_ref, l3_ref,
        x_ref, h_ref, q_ref, ctx_ref, k1_ref, v1_ref, m_ref, km0_ref, km1_ref, cctx_ref, out_ref, sum_ref,
        all_k, all_v,
    ):
        keep = pl.ds(0, LANES)

        @pl.when(pl.program_id(0) == 0)
        def _():
            total = dot_nn(keep_ref[...], wa_ref[...]) + dot_nn(recv_ref[...], wb_ref[...])
            residual = in_ref[...].astype(F32) + total
            x_ref[...] = residual
            normed = (unit_norm(residual)[0] * gain_ref[...].reshape(1, width)).astype(BF16)
            h_ref[...] = normed
            q_ref[...] = (dot_nn(normed, wq_ref[...]) * SCALE).astype(BF16)
            ctx_ref[:, pl.ds(pl.multiple_of(s[0] * HALF, LANES), HALF)] = keep_ref[...]
            ctx_ref[:, pl.ds(pl.multiple_of((1 - s[0]) * HALF, LANES), HALF)] = recv_ref[...]
            for at, source in enumerate((first_ref, second_ref)):
                rows = pl.ds(at * enc, enc)
                k1_ref[rows, :] = dot_nn(source[...], wk_ref[...]).astype(BF16)
                v1_ref[rows, :] = dot_nn(source[...], wv_ref[...]).astype(BF16)
            m_ref[...] = query_marks(l0_ref[:, pl.ds(0, tok)])
            for target, low, high in ((km0_ref, l0_ref, l1_ref), (km1_ref, l2_ref, l3_ref)):
                target[pl.ds(0, enc), :] = doc_marks(low, tok, enc)
                target[pl.ds(enc, enc), :] = doc_marks(high, tok, enc)
            gather_slots(s, enc, all_k.at[:, pl.ds(LANES, LANES)], km0_ref, km1_ref)

        pair = pair_lanes()
        gather_slots(s, enc, all_k.at[:, keep], k0_ref, k1_ref, pair)
        gather_slots(s, enc, all_v, v0_ref, v1_ref, pair)

        def work(count):
            seen = pl.ds(0, count * enc)
            out, log_sum = soft_block(q_ref[:, pair], m_ref[...], all_k[seen, :], all_v[seen, :])
            cctx_ref[...] = out.astype(BF16)
            out_ref[...] = out
            sum_ref[...] = log_sum

        by_count(s, work)

    args = (
        inputs, ctx_keep, ctx_recv, out_weight, out_weight, gain_vec, query_weight, first, second, key_weight, value_weight,
        keys, values, *labels,
    )
    specs = [whole(a) for a in args]
    specs[3] = pl.BlockSpec((HALF, width), lambda _, s: (s[0], 0))
    specs[4] = pl.BlockSpec((HALF, width), lambda _, s: (1 - s[0], 0))
    specs[11], specs[12] = pair_columns(keys), pair_columns(values)
    outs = [struct((tok, width), F32)] + [struct((tok, width), BF16)] * 3 + [struct((2 * enc, width), BF16)] * 2
    outs += [struct((tok, LANES), BF16)] + [struct((2 * enc, LANES), BF16)] * 2
    outs += [struct((tok, width), BF16)] + [struct((tok, width), F32)] * 2
    return run_kernel(
        "cross_part", body, place, args, specs, outs, [whole(o) for o in outs[:9]] + [pair_columns(o) for o in outs[9:]],
        grid=(width // LANES,),
        scratch=[pltpu.VMEM((4 * enc, 2 * LANES), BF16), pltpu.VMEM((4 * enc, LANES), BF16)],
        after=after, flops=tok * 2.5 * enc * 8 * 2 * width + 12 * tok * width * width,
    )


def cross_back(place, queries, keys, values, marks, key_marks, grads, attended, sums, residual, grad_res, query_weight, gains, out_weight, after=()):
    tok, width = queries.shape
    enc = keys[0].shape[0] // 2
    last = width // LANES - 1

    def body(
        s, q_ref, k0_ref, k1_ref, v0_ref, v1_ref, m_ref, km0_ref, km1_ref, g_ref, at_ref, ls_ref, gain_ref,
        x_any, dx_any, wq_any, wo_any, dq_ref, dk_ref, dv_ref, dx1_ref, low_ref, gain_grad_ref, keep_ref, send_ref,
        all_k, all_v, all_m, x_ref, dx_ref, wq_ref, wo_ref, semaphores,
    ):
        later = copies((x_any, dx_any, wq_any, wo_any), (x_ref, dx_ref, wq_ref, wo_ref), semaphores)

        @pl.when(pl.program_id(0) == 0)
        def _():
            for copy in later:
                copy.start()
            gather_slots(s, enc, all_m, km0_ref, km1_ref)

        gather_slots(s, enc, all_k, k0_ref, k1_ref)
        gather_slots(s, enc, all_v, v0_ref, v1_ref)
        pair = pair_lanes()

        def work(count):
            seen = pl.ds(0, count * enc)
            grad_q, grad_k, grad_v = pull_block(
                q_ref[...], m_ref[...], all_k[seen, :], all_m[seen, :], all_v[seen, :], g_ref[...], at_ref[...],
                ls_ref[...], False,
            )
            dq_ref[:, pair] = grad_q.astype(BF16)
            low_k, low_v = (grad_k.astype(BF16), grad_v.astype(BF16))
            for at in range(4):
                rows = pl.ds(pl.multiple_of(s[2 + at] * enc, enc), enc)
                if at < count:
                    dk_ref[rows, :] = low_k[at * enc : (at + 1) * enc, :]
                    dv_ref[rows, :] = low_v[at * enc : (at + 1) * enc, :]
                else:
                    dk_ref[rows, :] = jnp.zeros((enc, LANES), BF16)
                    dv_ref[rows, :] = jnp.zeros((enc, LANES), BF16)

        by_count(s, work)

        @pl.when(pl.program_id(0) == last)
        def _():
            for copy in later:
                copy.wait()
            back, gain_grad_ref[...] = norm_pull(x_ref[...], gain_ref[...].reshape(1, width), dot_nt(dq_ref[...], wq_ref[...]))
            grad_x = dx_ref[...] + back
            dx1_ref[...] = grad_x
            low = grad_x.astype(BF16)
            low_ref[...] = low
            for target, half in ((keep_ref, s[0]), (send_ref, 1 - s[0])):
                rows = pl.ds(pl.multiple_of(half * HALF, HALF), HALF)
                target[...] = dot_nt(low, wo_ref[rows, :]).astype(BF16)

    late = (residual, grad_res, query_weight, out_weight)
    args = (queries, *keys, *values, marks, *key_marks, grads, attended, sums, gains, *late)
    specs = [pair_columns(a) for a in args]
    for at in (5, 6, 7, 11):
        specs[at] = whole(args[at])
    specs[12:] = [any_place(a) for a in late]
    outs = [struct((tok, width), BF16)] + [struct((4 * enc, width), BF16)] * 2
    outs += [struct((tok, width), F32), struct((tok, width), BF16), struct((1, width), F32)]
    outs += [struct((tok, HALF), BF16)] * 2
    out_specs = [whole(o) for o in outs]
    out_specs[1], out_specs[2] = pair_columns(outs[1]), pair_columns(outs[2])
    return run_kernel(
        "cross_back", body, place, args, specs, outs, out_specs,
        grid=(width // LANES,),
        scratch=[pltpu.VMEM((4 * enc, LANES), BF16)] * 3
        + [pltpu.VMEM(a.shape, a.dtype) for a in late]
        + [pltpu.SemaphoreType.DMA((len(late),))],
        after=after, flops=tok * 2.5 * enc * 20 * 2 * width,
    )


def write_normed_grads(s, tok, h_ref, gain, grad_refs, weight_refs, keep_ref, send_ref, gain_grad_ref):
    running = None
    for target, part in ((keep_ref, s[0]), (send_ref, 1 - s[0])):
        rows = pl.ds(pl.multiple_of(part * tok, tok), tok)
        value = None
        for grad_ref, weight_ref in zip(grad_refs, weight_refs):
            piece = dot_nt(grad_ref[rows, :], weight_ref[...])
            value = piece if value is None else value + piece
        target[...] = value.astype(BF16)
        inner = jnp.sum(value * h_ref[rows, :].astype(F32), axis=0, keepdims=True)
        running = inner if running is None else running + inner
    gain_grad_ref[...] = running / gain


def far_back(place, queries, keys, values, marks, key_marks, grad_keep, grad_recv, attended, sums, gains, normed, weights, after=()):
    both, width = normed.shape
    tok = both // 2
    last = HALF // LANES - 1

    def body(
        s, q_ref, k_ref, v_ref, m_ref, km_ref, gk_ref, gr_ref, at_ref, ls_ref, gain_ref, h_any, wk_any, wv_any,
        dq_ref, dk_ref, dv_ref, keep_ref, send_ref, gain_grad_ref, h_ref, wk_ref, wv_ref, semaphores,
    ):
        pair = pair_lanes()
        columns = pl.ds(pl.multiple_of(s[0] * HALF, LANES), HALF)
        later = copies((h_any, wk_any.at[:, columns], wv_any.at[:, columns]), (h_ref, wk_ref, wv_ref), semaphores)

        @pl.when(s[1] != 0)
        def _():
            @pl.when(pl.program_id(0) == 0)
            def _():
                for copy in later:
                    copy.start()

            sum_k = sum_v = None
            for at in (0, 1):
                rows = pl.ds(at * tok, tok)
                grads = jnp.where(s[0] == at, gk_ref[...], gr_ref[...])
                dq_ref[rows, :], grad_k, grad_v = pull_block(
                    q_ref[rows, :], m_ref[rows, :], k_ref[...], km_ref[...], v_ref[...], grads, at_ref[rows, :],
                    ls_ref[rows, :], False,
                )
                sum_k = grad_k if at == 0 else sum_k + grad_k
                sum_v = grad_v if at == 0 else sum_v + grad_v
            dk_ref[:, pair] = sum_k.astype(BF16)
            dv_ref[:, pair] = sum_v.astype(BF16)

            @pl.when(pl.program_id(0) == last)
            def _():
                for copy in later:
                    copy.wait()
                write_normed_grads(
                    s, tok, h_ref, gain_ref[...].reshape(1, width), (dk_ref, dv_ref), (wk_ref, wv_ref), keep_ref, send_ref, gain_grad_ref
                )

        @pl.when(s[1] == 0)
        def _():
            dq_ref[...] = jnp.zeros_like(dq_ref)
            for ref in (dk_ref, dv_ref, keep_ref, send_ref, gain_grad_ref):
                ref[...] = jnp.zeros_like(ref)

    args = (queries, keys, values, marks, key_marks, grad_keep, grad_recv, attended, sums, gains, normed, *weights)
    specs = [pair_columns(a) for a in args]
    specs[3], specs[4], specs[9] = whole(marks), whole(key_marks), whole(gains)
    specs[10:] = [any_place(a) for a in args[10:]]
    outs = [struct((both, HALF), F32)] + [struct((both, HALF), BF16)] * 2
    outs += [struct((tok, width), BF16)] * 2 + [struct((1, width), F32)]
    return run_kernel(
        "far_back", body, place, args, specs, outs, [pair_columns(outs[0])] + [whole(o) for o in outs[1:]],
        grid=(HALF // LANES,),
        scratch=[pltpu.VMEM((both, width), BF16)] + [pltpu.VMEM((width, HALF), BF16)] * 2 + [pltpu.SemaphoreType.DMA((3,))],
        after=after, flops=both * both * 20 * 2 * HALF,
    )


def write_square(s, value, keep, send, first, x_first=False):
    rows = value.shape[0] // 16
    side = HALF // 2

    def write(target, half):
        for at in range(8):
            high, low, far = (at // 4, (at // 2) % 2, at % 2)
            for chip in range(value.shape[1] // HALF):
                columns = slice(chip * HALF + half * side, chip * HALF + (half + 1) * side)
                place = (chip, far, low, high) if x_first else (far, chip, low, high)
                for part in range(2):
                    piece = value[(2 * at + part) * rows : (2 * at + part + 1) * rows, columns].astype(BF16)
                    target[*place, pl.ds(first, rows), pl.ds(part * side, side)] = piece

    @pl.when(s[0] == 0)
    def _():
        write(keep, 0)
        write(send, 1)

    @pl.when(s[0] != 0)
    def _():
        write(keep, 1)
        write(send, 0)


def near_back(
    place, queries, keys, values, marks, key_marks, grad_keep, grad_recv, attended, sums, carried, gains,
    normed, far_normed, weights, far_grads, gain_grads, after=(),
):
    both, width = normed.shape
    tok = both // 2
    last = HALF // LANES - 1
    late_shapes = [(both, width)] * 2 + [(width, HALF)] * 3 + [(both, HALF)] * 2

    def body(
        s, q_ref, k_ref, v_ref, m_ref, km_ref, gk_ref, gr_ref, at_ref, ls_ref, ca_ref, gain_ref,
        gs_ref, gc_ref, gf_ref, h_any, fh_any, wq_any, wk_any, wv_any, fk_any, fv_any,
        keep_ref, send_ref, keep4, send4,
        dq, dk, dv, sum_k, sum_v, gain_grad_ref, gain_rows, h_ref, fh_ref, wq_ref, wk_ref, wv_ref, fk_ref, fv_ref, semaphores,
    ):
        pair = pair_lanes()
        columns = pl.ds(pl.multiple_of(s[0] * HALF, LANES), HALF)
        later = copies(
            (h_any, fh_any, wq_any.at[:, columns], wk_any.at[:, columns], wv_any.at[:, columns], fk_any, fv_any),
            (h_ref, fh_ref, wq_ref, wk_ref, wv_ref, fk_ref, fv_ref),
            semaphores,
        )

        @pl.when(pl.program_id(0) == 0)
        def _():
            for copy in later:
                copy.start()

        for at in (0, 1):
            rows = pl.ds(at * tok, tok)
            count = (at + 1) * tok
            seen = pl.ds(0, count)
            grads = jnp.where(s[0] == at, gk_ref[...], gr_ref[...])
            grad_q, grad_k, grad_v = pull_block(
                q_ref[rows, :], m_ref[rows, :], k_ref[seen, :], km_ref[seen, :], v_ref[seen, :], grads,
                at_ref[rows, :], ls_ref[rows, :], True,
            )
            dq[rows, pair] = (grad_q + ca_ref[rows, :]).astype(BF16)
            if at == 0:
                sum_k[...] = grad_k
                sum_v[...] = grad_v
            else:
                dk[pl.ds(0, tok), pair] = (sum_k[...] + grad_k[:tok]).astype(BF16)
                dv[pl.ds(0, tok), pair] = (sum_v[...] + grad_v[:tok]).astype(BF16)
                dk[pl.ds(tok, tok), pair] = grad_k[tok:].astype(BF16)
                dv[pl.ds(tok, tok), pair] = grad_v[tok:].astype(BF16)

        @pl.when(pl.program_id(0) == last)
        def _():
            for copy in later:
                copy.wait()
            write_normed_grads(
                s, tok, h_ref, gain_ref[...].reshape(1, width), (dq, dk, dv), (wq_ref, wk_ref, wv_ref), keep_ref, send_ref, gain_grad_ref
            )
            rows = width // 16
            write_square(s, dot_tn(h_ref[...], dq[...]), keep4, send4, 0)
            value = dot_tn(h_ref[...], dk[...]) + dot_tn(fh_ref[...], fk_ref[...])
            write_square(s, value, keep4, send4, rows)
            value = dot_tn(h_ref[...], dv[...]) + dot_tn(fh_ref[...], fv_ref[...])
            write_square(s, value, keep4, send4, 2 * rows)
            gain_rows[...] = jnp.zeros_like(gain_rows)
            gain_rows[0:1, :] = gain_grad_ref[...] + gs_ref[...]
            gain_rows[1:2, :] = gc_ref[...]
            gain_rows[2:3, :] = gf_ref[...]
            low = gain_rows[...].astype(BF16)
            piece = width // 8
            at_row = lax.broadcasted_iota(jnp.int32, (width, HALF), 0)
            at_col = lax.broadcasted_iota(jnp.int32, (width, HALF), 1)
            for at in range(8):
                pick = jnp.where((at_row == at_col + at * piece) & (at_col < piece), 1.0, 0.0).astype(BF16)
                value = dot_nn(low, pick).astype(BF16)
                for target in (keep4, send4):
                    target[at % 2, 0, (at // 2) % 2, at // 4, pl.ds(3 * rows, 16), :] = value

    late = (normed, far_normed, *weights, *far_grads)
    args = (
        queries, keys, values, marks, key_marks, grad_keep, grad_recv, attended, sums, carried, gains, *gain_grads, *late
    )
    specs = [pair_columns(a) for a in args]
    specs[3], specs[4] = whole(marks), whole(key_marks)
    specs[10:14] = [whole(a) for a in args[10:14]]
    specs[14:] = [any_place(a) for a in late]
    outs = [struct((tok, width), BF16)] * 2
    outs += [struct((2, 1, 2, 2, 3 * (width // 16) + 16, HALF), BF16)] * 2
    return run_kernel(
        "near_back", body, place, args, specs, outs, [whole(o) for o in outs],
        grid=(HALF // LANES,),
        scratch=[pltpu.VMEM((both, HALF), BF16)] * 3
        + [pltpu.VMEM((tok, LANES), F32)] * 2
        + [pltpu.VMEM((1, width), F32), pltpu.VMEM((16, width), F32)]
        + [pltpu.VMEM(shape, BF16) for shape in late_shapes]
        + [pltpu.SemaphoreType.DMA((len(late),))],
        after=after, flops=both * both * 0.75 * 20 * 2 * HALF + 20 * both * width * HALF,
    )


def cross_grads(name, place, pairs, x_first, passages=None, after=()):
    width = pairs[0][0][0].shape[1]
    rows = width // 16
    count = len(pairs)
    order, spots, groups = ([], {}, [])
    for left, right in [*pairs, *([] if passages is None else [(passages[:2], passages[2:])])]:
        fresh = []
        for array in (*left, *right):
            if id(array) not in spots:
                spots[id(array)] = len(order)
                fresh.append(len(order))
                order.append(array)
        groups.append((fresh, [spots[id(array)] for array in left], [spots[id(array)] for array in right]))
    given = len(order)
    outs = [struct((2, 2, 2, 2, count * rows, HALF), BF16)] * 2
    if passages is not None:
        enc = passages[0].shape[0] // 4
        outs += [struct((2, enc, width), F32), struct((2, enc, width), BF16)]
    produced = len(outs)

    def body(s, *refs):
        sources, results = refs[:given], refs[given : given + produced]
        held, semaphores = refs[given + produced : -1], refs[-1]
        step = pl.program_id(0)
        moves = copies(sources, held, semaphores)

        @pl.when(step == 0)
        def _():
            for move in moves:
                move.start()

        for at, (fresh, left, right) in enumerate(groups):

            @pl.when(step == at)
            def _(at=at, fresh=fresh, left=left, right=right):
                for spot in fresh:
                    moves[spot].wait()
                if at < count:
                    value = None
                    for part, spot in enumerate(left):
                        tall = held[spot].shape[0]
                        piece = dot_tn(held[spot][...], held[right[0]][pl.ds(part * tall, tall), :])
                        value = piece if value is None else value + piece
                    write_square(s, value, results[0], results[1], 0, x_first)
                    return
                for slot in range(4):
                    slots = pl.ds(slot * enc, enc)
                    value = dot_nt(held[left[0]][slots, :], held[right[0]][...])
                    value = value + dot_nt(held[left[1]][slots, :], held[right[1]][...])
                    if slot % 2 == 0:
                        results[2][slot // 2] = value
                    else:
                        results[3][slot // 2] = value.astype(BF16)

    block = pl.BlockSpec((2, 2, 2, 2, rows, HALF), lambda m, _: (0, 0, 0, 0, jnp.minimum(m, count - 1), 0))
    return run_kernel(
        name, body, place, order, [any_place(a) for a in order], outs,
        [block, block, *(whole(o) for o in outs[2:])],
        grid=(len(groups),),
        scratch=[pltpu.VMEM(a.shape, a.dtype) for a in order]
        + [pltpu.SemaphoreType.DMA((given,))],
        after=after,
    )


def passage_grads(place, grad_keys, grad_values, key_weight, value_weight, after=()):
    keys4, width = grad_keys.shape
    enc = keys4 // 4

    def body(s, dk_ref, dv_ref, wk_ref, wv_ref, keep_ref, send_ref):
        value = dot_nt(dk_ref[...], wk_ref[...]) + dot_nt(dv_ref[...], wv_ref[...])

        @pl.when(pl.program_id(0) % 2 == 0)
        def _():
            keep_ref[0] = value

        @pl.when(pl.program_id(0) % 2 != 0)
        def _():
            send_ref[0] = value.astype(BF16)

    args = (grad_keys, grad_values, key_weight, value_weight)
    slot = pl.BlockSpec((enc, width), lambda i, _: (i, 0))
    result = pl.BlockSpec((1, enc, width), lambda i, _: (i // 2, 0, 0))
    outs = [struct((2, enc, width), F32), struct((2, enc, width), BF16)]
    return run_kernel(
        "passage_grads", body, place, args, [slot, slot, whole(key_weight), whole(value_weight)], outs, [result, result],
        grid=(4,), after=after,
    )


def last_pull(place, inputs, gains, grad_res, parts, after=()):
    tok, width = inputs.shape
    steps = 2
    tile = tok // steps

    def body(s, in_ref, gain_ref, dx_ref, *refs):
        part_refs, out_ref = refs[:-1], refs[-1]
        total = part_refs[0][...].astype(F32)
        for ref in part_refs[1:]:
            total = total + ref[...].astype(F32)
        out_ref[...] = dx_ref[...] + norm_pull(in_ref[...].astype(F32), gain_ref[...].reshape(1, width), total)[0]

    args = (inputs, gains, grad_res, *parts)
    block = pl.BlockSpec((tile, width), lambda i, _: (i, 0))
    specs = [block for _ in args]
    specs[1] = whole(gains)
    return run_kernel(
        "last_pull", body, place, args, specs, [struct((tok, width), F32)], [block], grid=(steps,), after=after,
        flops=20 * tok * width,
    )[0]


def rounded(values):
    return lax.reduce_precision(values, 8, 7).astype(BF16)


def add_split(half, keep, recv):
    part = lambda array, at: lax.dynamic_index_in_dim(array, at, 0, False).astype(F32)
    kept = rounded(part(keep, half) + part(recv, half))
    return (kept, rounded(part(keep, 1 - half) + part(recv, 1 - half)))


class Halving:
    def __init__(self, keep, recv, steps):
        self.keep, self.recv, self.steps = (keep, recv, list(steps))

    def step(self, *after):
        half, axis, pairs = self.steps.pop(0)
        keep, recv = (self.keep.reshape(2, -1, HALF), self.recv.reshape(2, -1, HALF))
        if after:
            keep, recv, *_ = lax.optimization_barrier((keep, recv, *after))
        self.keep, send = add_split(half, keep, recv)
        self.recv = lax.ppermute(send, axis, pairs)
        return self.keep


def merge_split(place, step, sums, after=()):
    half, axis, pairs = step
    counts = [a.keep.shape[0] // 4 for a in sums]
    arrays = [array.reshape(2, 2, count, HALF) for a, count in zip(sums, counts) for array in (a.keep, a.recv)]
    starts = [sum(counts[:at]) for at in range(len(counts))]

    def body(s, *refs):
        given, (keep_ref, send_ref) = refs[: len(arrays)], refs[len(arrays) :]
        for target, side in ((keep_ref, s[0]), (send_ref, 1 - s[0])):
            for at, (first, count) in enumerate(zip(starts, counts)):
                for deep in range(2):
                    value = given[2 * at][side, deep].astype(F32) + given[2 * at + 1][side, deep].astype(F32)
                    target[deep, pl.ds(first, count), :] = value.astype(BF16)

    outs = [struct((2, sum(counts), HALF), BF16)] * 2
    keep, send = run_kernel(
        "merge_split", body, half.astype(jnp.int32).reshape(1), arrays, [whole(a) for a in arrays], outs,
        [whole(o) for o in outs], after=after,
    )
    merged = Halving(keep, lax.ppermute(send, axis, pairs), ())
    return merged


def self_start(place, keep4, recv4, after=()):
    cut = 80
    rest = keep4.shape[4] - cut

    def body(s, keep_ref, recv_ref, ak_ref, as_ref, bk_ref, bs_ref):
        for target, side in ((ak_ref, s[2]), (as_ref, 1 - s[2])):
            for slot, source in enumerate((keep_ref, recv_ref)):
                target[slot] = source[side, 0, :, :, pl.ds(0, cut), :]
        late, front, tail = (pl.ds(cut, rest - 16), pl.ds(0, rest - 16), pl.ds(cut + rest - 16, 16))

        @pl.when(s[0] == s[1])
        def _():
            bk_ref[:, :, :, front, :] = keep_ref[:, 0, :, :, late, :]
            bs_ref[:, :, :, front, :] = recv_ref[:, 0, :, :, late, :]

        @pl.when(s[0] != s[1])
        def _():
            bk_ref[:, :, :, front, :] = recv_ref[:, 0, :, :, late, :]
            bs_ref[:, :, :, front, :] = keep_ref[:, 0, :, :, late, :]

        shared = keep_ref[:, 0, :, :, tail, :].astype(F32) + recv_ref[:, 0, :, :, tail, :].astype(F32)
        for target in (bk_ref, bs_ref):
            target[:, :, :, pl.ds(rest - 16, 16), :] = shared.astype(BF16)

    args = (keep4, recv4)
    outs = [struct((2, 2, 2, cut, HALF), BF16)] * 2 + [struct((2, 2, 2, rest, HALF), BF16)] * 2
    return run_kernel(
        "self_start", body, place, args, [whole(a) for a in args], outs, [whole(o) for o in outs], after=after
    )


def both_step(first, second, after=()):
    sums = (first, second)
    halves, axes, pairs = zip(*(a.steps.pop(0) for a in sums))
    arrays = [array.reshape(2, -1, HALF) for a in sums for array in (a.keep, a.recv)]

    def body(s, *refs):
        given, outs = refs[:4], refs[4:]
        for at in range(2):
            for target, side in ((outs[2 * at], s[at]), (outs[2 * at + 1], 1 - s[at])):
                target[...] = (given[2 * at][side].astype(F32) + given[2 * at + 1][side].astype(F32)).astype(BF16)

    outs = [struct(array.shape[1:], BF16) for array in arrays]
    results = run_kernel(
        "both_step", body, jnp.stack(halves).astype(jnp.int32), arrays, [whole(a) for a in arrays], outs,
        [whole(o) for o in outs], after=after,
    )
    for at, a in enumerate(sums):
        a.keep, a.recv = (results[2 * at], lax.ppermute(results[2 * at + 1], axes[at], pairs[at]))
    return results[0]


def finish_sums(name, keep, recv, count, tail=0, after=()):
    rows = (keep.shape[0] - tail) // count
    side = HALF // 2

    def body(s, keep_ref, recv_ref, *outs):
        for at in range(count):
            part = pl.ds(at * rows, rows)
            total = keep_ref[part, :].astype(F32) + recv_ref[part, :].astype(F32)
            outs[at][pl.ds(0, rows), :] = total[:, :side]
            outs[at][pl.ds(rows, rows), :] = total[:, side:]
        if tail:
            part = pl.ds(count * rows, tail)
            outs[count][...] = keep_ref[part, :].astype(F32) + recv_ref[part, :].astype(F32)

    outs = [struct((2 * rows, side), F32)] * count
    if tail:
        outs += [struct((tail, HALF), F32)]
    place = jnp.zeros((1,), jnp.int32)
    return run_kernel(
        name, body, place, (keep, recv), [whole(keep), whole(recv)], outs, [whole(o) for o in outs], after=after
    )


def feed_forward(place, residual, context, out_weight, gain_vec, feed_in, feed_out, cotangent, after=()):
    tok, width = residual.shape
    hidden_width = feed_in.shape[1]
    steps = 4
    chunk = hidden_width // steps
    rows_in = width // 8
    side = width // 4

    def body(
        s, x1_ref, ctx_ref, wo_ref, gain_ref, w1_ref, w2_ref, g_ref,
        out_ref, dx_ref, low_ref, dctx_ref, gain_grad_ref, spread,
        x2, normed, normed_flip, grad_flip, sum_out, sum_norm, block_in, block_out, semaphores,
    ):
        step = pl.program_id(0)

        @pl.when(step == 0)
        def _():
            x2[...] = x1_ref[...] + dot_nn(ctx_ref[...], wo_ref[...])
            normed[...] = (unit_norm(x2[...])[0] * gain_ref[...].reshape(1, width)).astype(BF16)
            normed_flip[...] = normed[...].T
            grad_flip[...] = g_ref[...].T
            sum_out[...] = jnp.zeros_like(sum_out)
            sum_norm[...] = jnp.zeros_like(sum_norm)

        w1, w2, grad = (w1_ref[...], w2_ref[...], g_ref[...])
        pre = dot_nn(normed[...], w1)
        root = 0.7978845608028654
        bend = 0.044715
        square = pre * pre
        swing = jnp.tanh(pre * (root + root * bend * square))
        half = 0.5 + 0.5 * swing
        active = pre * half
        hidden = active.astype(BF16)
        sum_out[...] += dot_nn(hidden, w2)
        slope = half + active * (1.0 - swing) * (root + 3.0 * root * bend * square)
        grad_pre = (dot_nt(grad, w2) * slope).astype(BF16)
        sum_norm[...] += dot_nt(grad_pre, w1)
        slot = step % 2

        def moves(at, slot):
            first = pltpu.make_async_copy(
                block_in.at[slot], spread.at[:, at, pl.ds(0, 2 * rows_in), :], semaphores.at[slot, 0]
            )
            second = pltpu.make_async_copy(
                block_out.at[slot], spread.at[pl.ds(2 * at, 2), :, pl.ds(2 * rows_in, side), :], semaphores.at[slot, 1]
            )
            return (first, second)

        @pl.when(step >= 2)
        def _():
            for move in moves(step - 2, slot):
                move.wait()

        grad_in = dot_nn(normed_flip[...], grad_pre).astype(BF16)
        for at in range(8):
            for unit in range(2):
                block_in[slot, at, pl.ds(unit * rows_in, rows_in), :] = grad_in[
                    at * rows_in : (at + 1) * rows_in, unit * HALF : (unit + 1) * HALF
                ]
        grad_out = dot_nn(grad_flip[...], hidden).astype(BF16)
        for at in range(2):
            for part in range(4):
                block_out[slot, at, part] = grad_out[part * side : (part + 1) * side, at * HALF : (at + 1) * HALF]
        for move in moves(step, slot):
            move.start()

        @pl.when(step == steps - 1)
        def _():
            for at in (steps - 2, steps - 1):
                for move in moves(at, at % 2):
                    move.wait()

        @pl.when(step == steps - 1)
        def _():
            out_ref[...] = (x2[...] + sum_out[...]).astype(BF16)
            back, gain_grad_ref[...] = norm_pull(x2[...], gain_ref[...].reshape(1, width), sum_norm[...])
            grad_x = grad.astype(F32) + back
            dx_ref[...] = grad_x
            low = grad_x.astype(BF16)
            low_ref[...] = low
            dctx_ref[...] = dot_nt(low, wo_ref[...]).astype(BF16)

    args = (residual, context, out_weight, gain_vec, feed_in, feed_out, cotangent)
    specs = [whole(a) for a in args]
    specs[4] = pl.BlockSpec((width, chunk), lambda c, _: (0, c))
    specs[5] = pl.BlockSpec((chunk, width), lambda c, _: (c, 0))
    outs = [
        struct((tok, width), BF16),
        struct((tok, width), F32),
        struct((tok, width), BF16),
        struct((tok, width), BF16),
        struct((1, width), F32),
        struct((8, 4, 2 * rows_in + side, HALF), BF16),
    ]
    out_specs = [whole(o) for o in outs]
    out_specs[5] = any_place(outs[5])
    return run_kernel(
        "feed_forward",
        body,
        place,
        args,
        specs,
        outs,
        out_specs,
        grid=(steps,),
        scratch=[
            pltpu.VMEM((tok, width), F32),
            pltpu.VMEM((tok, width), BF16),
            pltpu.VMEM((width, tok), BF16),
            pltpu.VMEM((width, tok), BF16),
            pltpu.VMEM((tok, width), F32),
            pltpu.VMEM((tok, width), F32),
            pltpu.VMEM((2, 8, 2 * rows_in, HALF), BF16),
            pltpu.VMEM((2, 2, 4, side, HALF), BF16),
            pltpu.SemaphoreType.DMA((2, 2)),
        ],
        after=after, flops=12 * tok * width * hidden_width + 4 * tok * width * width,
    )


def local_paired(
    inputs,
    encoded,
    cotangent,
    dec_seg,
    pass_doc,
    enc_mask,
    self_query,
    self_key,
    self_value,
    self_output,
    cross_query,
    cross_key,
    cross_value,
    cross_output,
    feed_in,
    feed_out,
    gain_self,
    gain_cross,
    gain_ff,
):
    inputs, encoded, cotangent = (inputs[0], encoded[0], cotangent[0])
    tok, width = inputs.shape
    enc = encoded.shape[0]
    blk, row = (lax.axis_index("blk"), lax.axis_index("rows"))
    core, chip = (blk % 2, blk // 2)
    y_at, z_low, z_high = (row % 2, (row // 2) % 2, row // 4)
    place = jnp.stack([core, chip, y_at]).astype(jnp.int32)
    gains = (gain_self, gain_cross, gain_ff)
    to_core = lambda array: lax.ppermute(array, "blk", CORE_SWAP)
    to_chip = lambda array: lax.ppermute(array, "blk", CHIP_SWAP)
    in_order = lambda mine, other: jnp.where(core == 0, jnp.concatenate([mine, other]), jnp.concatenate([other, mine]))

    def swap(distance):
        return tuple((at, at ^ distance) for at in range(8))

    over_x = (chip, "blk", CHIP_SWAP)
    over_y = (y_at, "rows", swap(1))
    over_z = ((z_low, "rows", swap(2)), (z_high, "rows", swap(4)))

    gap = -tok % LANES
    spare = jnp.zeros((8 * LANES - tok - gap - enc - 1,), jnp.int32)
    labels = jnp.concatenate([dec_seg[0], spare[:gap], enc_mask[0], pass_doc[0], spare[gap:]])
    labels = jnp.concatenate([labels, jnp.zeros((8 * LANES - labels.shape[0],), jnp.int32)]).reshape(1, 8 * LANES)
    labels_c = to_core(labels)
    inputs_c = to_core(inputs)
    inputs_x = to_chip(inputs)
    labels_x = to_chip(labels)
    encoded_c = to_core(encoded)
    h1, sq, sk, sv, near_marks, near_keys_marks, near_out, near_sum, ck0, cv0 = near_part(
        place, inputs, inputs_c, gain_self, (self_query, self_key, self_value), (labels, labels_c), (encoded, encoded_c),
        (cross_key, cross_value),
    )
    inputs_x, labels_x, encoded_late, _ = lax.optimization_barrier((inputs_x, labels_x, encoded, ck0))
    labels_d = to_core(labels_x)
    inputs_d = to_core(inputs_x)
    encoded_x = to_chip(encoded_late)
    spot = place
    place = find_passages(spot, tok, enc, (labels, labels_c, labels_x, labels_d))
    h1_far, fk, fv, far_keys_marks, self_out, self_sum, ctx_keep, ctx_send = far_part(
        place, inputs_x, inputs_d, gain_self, (self_key, self_value), sq, near_marks, (labels_x, labels_d), near_out, near_sum
    )
    encoded_x, _ = lax.optimization_barrier((encoded_x, self_out))
    encoded_d = to_core(encoded_x)
    x1, h2, cq, self_context, ck1, cv1, own_marks, docs0, docs1, cross_context, cross_out, cross_sum = cross_part(
        place, inputs, ctx_keep, to_core(ctx_send), self_output, gain_cross, cross_query, encoded_x, encoded_d, cross_key,
        cross_value, ck0, cv0, (labels, labels_c, labels_x, labels_d),
    )
    docs = (docs0, docs1)
    output, dx2, e2, d_cross, grad_gain_ff, spread = feed_forward(
        place, x1, cross_context, cross_output, gain_ff, feed_in, feed_out, cotangent
    )
    total_ff = lax.psum_scatter(spread.reshape(32, *spread.shape[2:]), ("rows", "blk"), scatter_dimension=0, tiled=True)
    dcq, dck, dcv, dx1, e1, grad_gain_cross, ds_keep, ds_send = cross_back(
        place, cq, (ck0, ck1), (cv0, cv1), own_marks, docs, d_cross, cross_out, cross_sum, x1, dx2, cross_query,
        gain_cross, self_output,
    )
    ds_recv = to_core(ds_send)
    passages = (encoded, encoded_c, encoded_x, encoded_d)
    keep_p, send_p = cross_grads(
        "cross_grads", place, (((cross_context,), (e2,)), ((h2,), (dcq,)), (passages, (dck,))), True
    )
    keep_q, send_q = cross_grads(
        "late_grads", place, ((passages, (dcv,)), ((self_context,), (e1,))), False, after=(keep_p,)
    )
    recv_p = to_core(send_p)
    recv_p, ds_recv, send_q = lax.optimization_barrier((recv_p, ds_recv, send_q))
    sum_p = Halving(keep_p, recv_p, (over_x, over_y))
    sum_q = Halving(keep_q, to_core(send_q), (over_y, over_x))
    held = (sum_p.step(), sum_q.step())
    dq_far, dk_far, dv_far, far_keep, far_send, gain_far = far_back(
        place, sq, fk, fv, near_marks, far_keys_marks, ds_keep, ds_recv, self_out, self_sum, gain_self, h1_far,
        (self_key, self_value), after=held,
    )
    sum_p.recv, sum_q.recv, far_send = lax.optimization_barrier((sum_p.recv, sum_q.recv, far_send))
    far_recv = to_core(far_send)
    held = (sum_p.step(), sum_q.step())
    far_keep, far_recv, *_ = lax.optimization_barrier((far_keep, far_recv, *held))
    far_here = (far_keep.astype(F32) + far_recv.astype(F32)).astype(BF16)
    from_far = to_chip(far_here)
    near_keep, near_send, keep4, send4 = near_back(
        place, sq, sk, sv, near_marks, near_keys_marks, ds_keep, ds_recv, self_out, self_sum, dq_far, gain_self, h1, h1_far,
        (self_query, self_key, self_value), (dk_far, dv_far), (gain_far, grad_gain_cross, grad_gain_ff),
        after=(far_here, *held),
    )
    tied = lax.optimization_barrier((sum_p.recv, sum_q.recv, from_far, near_send, send4))
    sum_p.recv, sum_q.recv, from_far, near_send, send4 = tied
    recv4 = to_core(send4)
    near_recv = to_core(near_send)
    sum_cross = merge_split(place, over_z[0], (sum_p, sum_q))
    sum_cross.steps = [over_z[1]]
    first_keep, first_send, second_keep, second_send = self_start(spot, keep4, recv4, after=(sum_cross.keep,))
    over_slot = (chip ^ core, "blk", CHIP_SWAP)
    sum_first = Halving(first_keep, lax.ppermute(first_send, "rows", swap(1)), (over_slot,))
    sum_second = Halving(second_keep, to_chip(second_send), (over_y,))
    input_grad = last_pull(
        place, inputs, gain_self, dx1, (near_keep, near_recv, from_far), after=(first_send, second_send)
    )
    enc_keep, enc_send = passage_grads(place, dck, dcv, cross_key, cross_value, after=(input_grad,))
    tied = lax.optimization_barrier((sum_first.recv, sum_second.recv, sum_cross.recv, enc_send))
    sum_first.recv, sum_second.recv, sum_cross.recv, enc_send = tied
    both_step(sum_first, sum_second, after=(enc_keep,))
    enc_recv = to_core(enc_send)
    enc_keep, enc_recv, _ = lax.optimization_barrier((enc_keep, enc_recv, sum_first.keep))
    enc_sum = enc_keep + enc_recv.astype(F32)
    from_chip = to_chip(enc_sum[1].astype(BF16))
    held = sum_cross.step(enc_sum)
    sum_self = merge_split(place, over_z[0], (sum_first, sum_second), after=(held,))
    sum_self.steps = [over_z[1]]
    rows = width // 16
    total_ff, _ = lax.optimization_barrier((total_ff[0], sum_self.keep))
    total_ff = total_ff.astype(F32)
    grad_feed_in = jnp.concatenate([total_ff[: 2 * rows], total_ff[2 * rows : 4 * rows]], axis=1)
    feed_out_flip = total_ff[4 * rows :]
    cross_o, cross_q, cross_k, cross_v, self_o = finish_sums(
        "finish_cross", sum_cross.keep, sum_cross.recv, 5, after=(sum_self.keep, grad_feed_in, feed_out_flip)
    )
    sum_self.step(cross_o)
    enc_last, from_chip, _ = lax.optimization_barrier((enc_sum[0], from_chip, sum_self.keep))
    encoded_grad = enc_last + from_chip.astype(F32)
    self_q, self_k, self_v, gain_rows = finish_sums(
        "finish_self", sum_self.keep, sum_self.recv, 3, 16, after=(encoded_grad,)
    )
    piece = width // 8
    return (
        output[None],
        input_grad[None],
        encoded_grad[None],
        self_q,
        self_k,
        self_v,
        self_o,
        cross_q,
        cross_k,
        cross_v,
        cross_o,
        grad_feed_in,
        feed_out_flip.T,
        gain_rows[0, :piece],
        gain_rows[1, :piece],
        gain_rows[2, :piece],
    )


def solution(mesh):
    paired = mesh.shape["blk"] == 4 and mesh.shape["rows"] == 8
    body = local_paired if paired else local_any
    in_specs = (
        P("rows", "blk", None),
        P("rows", "blk", None),
        P("rows", "blk", None),
        P("rows", "blk"),
        P("rows", "blk"),
        P("rows", "blk"),
        P(),
        P(),
        P(),
        P(),
        P(),
        P(),
        P(),
        P(),
        P(),
        P(),
        P(),
        P(),
        P(),
    )
    out_specs = (
        P("rows", "blk", None),
        P("rows", "blk", None),
        P("rows", "blk", None),
        P("rows", "blk"),
        P("rows", "blk"),
        P("rows", "blk"),
        P("rows", "blk"),
        P("rows", "blk"),
        P("rows", "blk"),
        P("rows", "blk"),
        P("rows", "blk"),
        P("rows", "blk"),
        P("rows", "blk"),
        P("rows"),
        P("rows"),
        P("rows"),
    )
    return jax.shard_map(body, mesh=mesh, in_specs=in_specs, out_specs=out_specs, check_vma=False)
```

```python
import jax
import jax.numpy as jnp
from jax import lax
from jax.experimental import pallas as pl
from jax.experimental.pallas import tpu as pltpu
from jax.sharding import PartitionSpec as P

HEADS = 12
HEAD_DIM = 64
PLEN = 384


NEG_FILL = -1e30
SCALE = 0.125


def split_heads(matrix):
    return matrix.reshape(matrix.shape[0], matrix.shape[1], HEADS, HEAD_DIM)


def join_heads(tensor):
    return jnp.transpose(tensor, (0, 2, 1, 3)).reshape(
        tensor.shape[0], tensor.shape[2], HEADS * HEAD_DIM
    )


def rms_norm(values, gain_vec):
    return values * lax.rsqrt(jnp.mean(values * values, axis=-1, keepdims=True) + 1e-06) * gain_vec


def norm_back(values, gain_vec, grad_out):
    _, pullback = jax.vjp(rms_norm, values, gain_vec)
    return pullback(grad_out)


def project(left, weight):
    return jnp.einsum("rqd,df->rqf", left, weight, preferred_element_type=jnp.float32)


def back_project(grad_out, weight):
    return jnp.einsum("rqf,df->rqd", grad_out, weight, preferred_element_type=jnp.float32)


def weight_grad(left, grad_out):
    return jnp.einsum("rqd,rqf->df", left, grad_out, preferred_element_type=jnp.float32)


def head_scores(queries, keys):
    return (
        jnp.einsum(
            "rqhe,rkhe->rhqk",
            split_heads(queries),
            split_heads(keys),
            preferred_element_type=jnp.float32,
        )
        * SCALE
    )


def empty_state(row_count, query_count):
    return (
        jnp.full((row_count, HEADS, query_count), NEG_FILL, jnp.float32),
        jnp.zeros((row_count, HEADS, query_count), jnp.float32),
        jnp.zeros((row_count, HEADS, query_count, HEAD_DIM), jnp.float32),
    )


def online_block(state, queries, keys, values, allowed):
    run_max, run_sum, run_acc = state
    scores = head_scores(queries, keys)
    allowed = allowed[:, None]
    new_max = jnp.maximum(run_max, jnp.max(jnp.where(allowed, scores, NEG_FILL), axis=-1))
    weights = jnp.where(allowed, jnp.exp(scores - new_max[..., None]), 0.0)
    new_sum = jnp.sum(weights, axis=-1)
    new_acc = jnp.einsum(
        "rhqk,rkhe->rhqe",
        weights.astype(jnp.bfloat16),
        split_heads(values),
        preferred_element_type=jnp.float32,
    )
    return (new_max, new_sum, new_acc)


def finish(state):
    run_max, run_sum, run_acc = state
    return (run_acc / run_sum[..., None], run_max + jnp.log(run_sum))


def grad_pair(queries, grad_ctx, log_sum, delta, keys, values, allowed):
    scores = head_scores(queries, keys)
    probs_now = jnp.where(allowed[:, None], jnp.exp(scores - log_sum[..., None]), 0.0)
    grad_probs = jnp.einsum(
        "rqhe,rkhe->rhqk",
        split_heads(grad_ctx),
        split_heads(values),
        preferred_element_type=jnp.float32,
    )
    grad_scores = (probs_now * (grad_probs - delta[..., None])).astype(jnp.bfloat16)
    grad_query = (
        jnp.einsum(
            "rhqk,rkhe->rqhe", grad_scores, split_heads(keys), preferred_element_type=jnp.float32
        )
        * SCALE
    )
    grad_key = (
        jnp.einsum(
            "rhqk,rqhe->rkhe", grad_scores, split_heads(queries), preferred_element_type=jnp.float32
        )
        * SCALE
    )
    grad_value = jnp.einsum(
        "rhqk,rqhe->rkhe",
        probs_now.astype(jnp.bfloat16),
        split_heads(grad_ctx),
        preferred_element_type=jnp.float32,
    )
    row_count = keys.shape[0]
    key_count = keys.shape[1]
    joined = jnp.concatenate(
        (grad_key.reshape(row_count, key_count, -1), grad_value.reshape(row_count, key_count, -1)),
        axis=-1,
    )
    return (grad_query.reshape(row_count, queries.shape[1], -1), joined)


def head_delta(grad_ctx, attended):
    return jnp.einsum("rqhe,rhqe->rhq", split_heads(grad_ctx).astype(jnp.float32), attended)


def spread_matrix(matrix, row_split, block_count):
    first, second = matrix.shape
    tiles = matrix.reshape(row_split, first // row_split, block_count, second // block_count)
    return jnp.transpose(tiles, (0, 2, 1, 3)).reshape(
        row_split * block_count, first // row_split, second // block_count
    )


def spread_gain(vector, row_split, block_count):
    tiles = vector.reshape(row_split, 1, vector.shape[0] // row_split)
    return jnp.broadcast_to(tiles, (row_split, block_count, vector.shape[0] // row_split)).reshape(
        row_split * block_count, vector.shape[0] // row_split
    )


def local_any(
    inputs,
    encoded,
    cotangent,
    dec_seg,
    pass_doc,
    enc_mask,
    self_query,
    self_key,
    self_value,
    self_output,
    cross_query,
    cross_key,
    cross_value,
    cross_output,
    feed_in,
    feed_out,
    gain_self,
    gain_cross,
    gain_ff,
):
    row_count, tok_shard, width = inputs.shape
    enc_shard = encoded.shape[1]
    block_count = lax.axis_size("blk")
    row_split = lax.axis_size("rows")
    block_ids = jnp.arange(block_count)
    query_places = lax.axis_index("blk") * tok_shard + jnp.arange(tok_shard)
    start_state = empty_state(row_count, tok_shard)
    residual = inputs.astype(jnp.float32)
    normed_self = rms_norm(residual, gain_self).astype(jnp.bfloat16)
    self_queries = project(normed_self, self_query).astype(jnp.bfloat16)
    self_keys = project(normed_self, self_key).astype(jnp.bfloat16)
    self_values = project(normed_self, self_value).astype(jnp.bfloat16)
    piece_keys = lax.all_gather(self_keys, "blk", axis=1, tiled=True)
    piece_values = lax.all_gather(self_values, "blk", axis=1, tiled=True)
    piece_segs = lax.all_gather(dec_seg, "blk", axis=1, tiled=True)
    key_places = jnp.arange(piece_keys.shape[1])
    allowed = (dec_seg[:, :, None] == piece_segs[:, None, :]) & (
        key_places[None, None, :] <= query_places[None, :, None]
    )
    self_attn, self_lse = finish(
        online_block(start_state, self_queries, piece_keys, piece_values, allowed)
    )
    self_context = join_heads(self_attn).astype(jnp.bfloat16)
    after_self = residual + project(self_context, self_output)
    normed_cross = rms_norm(after_self, gain_cross).astype(jnp.bfloat16)
    cross_queries = project(normed_cross, cross_query).astype(jnp.bfloat16)
    cross_keys = project(encoded, cross_key).astype(jnp.bfloat16)
    cross_values = project(encoded, cross_value).astype(jnp.bfloat16)
    key_docs = jnp.where(enc_mask == 1, jnp.repeat(pass_doc, PLEN, axis=1), -1)
    piece_keys = lax.all_gather(cross_keys, "blk", axis=1, tiled=True)
    piece_values = lax.all_gather(cross_values, "blk", axis=1, tiled=True)
    piece_docs = lax.all_gather(key_docs, "blk", axis=1, tiled=True)
    allowed = dec_seg[:, :, None] == piece_docs[:, None, :]
    cross_attn, cross_lse = finish(
        online_block(start_state, cross_queries, piece_keys, piece_values, allowed)
    )
    cross_context = join_heads(cross_attn).astype(jnp.bfloat16)
    after_cross = after_self + project(cross_context, cross_output)
    normed_ff = rms_norm(after_cross, gain_ff).astype(jnp.bfloat16)
    before_act = project(normed_ff, feed_in)
    hidden = jax.nn.gelu(before_act).astype(jnp.bfloat16)
    output = (after_cross + project(hidden, feed_out)).astype(jnp.bfloat16)
    grad_feed_out = weight_grad(hidden, cotangent)
    grad_hidden = back_project(cotangent, feed_out)
    _, gelu_back = jax.vjp(jax.nn.gelu, before_act)
    grad_before = gelu_back(grad_hidden)[0].astype(jnp.bfloat16)
    grad_feed_in = weight_grad(normed_ff, grad_before)
    grad_cross_res, grad_gain_ff = norm_back(
        after_cross, gain_ff, back_project(grad_before, feed_in)
    )
    grad_cross_res = cotangent.astype(jnp.float32) + grad_cross_res
    cross_branch = grad_cross_res.astype(jnp.bfloat16)
    grad_cross_output = weight_grad(cross_context, cross_branch)
    grad_cross_ctx = back_project(cross_branch, cross_output).astype(jnp.bfloat16)
    cross_delta = head_delta(grad_cross_ctx, cross_attn)
    all_keys, all_values, all_docs = (
        lax.all_gather(cross_keys, "blk", axis=1, tiled=True),
        lax.all_gather(cross_values, "blk", axis=1, tiled=True),
        lax.all_gather(key_docs, "blk", axis=1, tiled=True),
    )

    def passage_step(running, block_index):
        offset = block_index * enc_shard
        piece_keys = lax.dynamic_slice_in_dim(all_keys, offset, enc_shard, 1)
        piece_values = lax.dynamic_slice_in_dim(all_values, offset, enc_shard, 1)
        piece_docs = lax.dynamic_slice_in_dim(all_docs, offset, enc_shard, 1)
        allowed = dec_seg[:, :, None] == piece_docs[:, None, :]
        grad_query, grad_kv = grad_pair(
            cross_queries, grad_cross_ctx, cross_lse, cross_delta, piece_keys, piece_values, allowed
        )
        return (running + grad_query, grad_kv)

    grad_cross_q, key_terms = lax.scan(
        passage_step, jnp.zeros((row_count, tok_shard, width), jnp.float32), block_ids
    )
    grad_cross_kv = lax.psum_scatter(
        key_terms.astype(jnp.bfloat16), "blk", scatter_dimension=0, tiled=True
    ).astype(jnp.float32)[0]
    low_cross_q = grad_cross_q.astype(jnp.bfloat16)
    low_cross_k = grad_cross_kv[..., :width].astype(jnp.bfloat16)
    low_cross_v = grad_cross_kv[..., width:].astype(jnp.bfloat16)
    grad_cross_query = weight_grad(normed_cross, low_cross_q)
    grad_cross_key = weight_grad(encoded, low_cross_k)
    grad_cross_value = weight_grad(encoded, low_cross_v)
    encoded_grad = back_project(low_cross_k, cross_key) + back_project(low_cross_v, cross_value)
    grad_self_res, grad_gain_cross = norm_back(
        after_self, gain_cross, back_project(low_cross_q, cross_query)
    )
    grad_self_res = grad_cross_res + grad_self_res
    self_branch = grad_self_res.astype(jnp.bfloat16)
    grad_self_output = weight_grad(self_context, self_branch)
    grad_self_ctx = back_project(self_branch, self_output).astype(jnp.bfloat16)
    self_delta = head_delta(grad_self_ctx, self_attn)
    all_self_keys, all_self_values, all_self_segs = (
        lax.all_gather(self_keys, "blk", axis=1, tiled=True),
        lax.all_gather(self_values, "blk", axis=1, tiled=True),
        lax.all_gather(dec_seg, "blk", axis=1, tiled=True),
    )

    def self_step(running, block_index):
        offset = block_index * tok_shard
        piece_keys = lax.dynamic_slice_in_dim(all_self_keys, offset, tok_shard, 1)
        piece_values = lax.dynamic_slice_in_dim(all_self_values, offset, tok_shard, 1)
        piece_segs = lax.dynamic_slice_in_dim(all_self_segs, offset, tok_shard, 1)
        key_places = offset + jnp.arange(tok_shard)
        allowed = (dec_seg[:, :, None] == piece_segs[:, None, :]) & (
            key_places[None, None, :] <= query_places[None, :, None]
        )
        grad_query, grad_kv = grad_pair(
            self_queries, grad_self_ctx, self_lse, self_delta, piece_keys, piece_values, allowed
        )
        return (running + grad_query, grad_kv)

    grad_self_q, self_terms = lax.scan(
        self_step, jnp.zeros((row_count, tok_shard, width), jnp.float32), block_ids
    )
    grad_self_kv = lax.psum_scatter(
        self_terms.astype(jnp.bfloat16), "blk", scatter_dimension=0, tiled=True
    ).astype(jnp.float32)[0]
    low_self_q = grad_self_q.astype(jnp.bfloat16)
    low_self_k = grad_self_kv[..., :width].astype(jnp.bfloat16)
    low_self_v = grad_self_kv[..., width:].astype(jnp.bfloat16)
    grad_self_query = weight_grad(normed_self, low_self_q)
    grad_self_key = weight_grad(normed_self, low_self_k)
    grad_self_value = weight_grad(normed_self, low_self_v)
    grad_normed = (
        back_project(low_self_q, self_query)
        + back_project(low_self_k, self_key)
        + back_project(low_self_v, self_value)
    )
    grad_first, grad_gain_self = norm_back(residual, gain_self, grad_normed)
    input_grad = grad_self_res + grad_first
    matrices = (
        grad_self_query,
        grad_self_key,
        grad_self_value,
        grad_self_output,
        grad_cross_query,
        grad_cross_key,
        grad_cross_value,
        grad_cross_output,
        grad_feed_in,
        grad_feed_out,
    )
    spread_mats = tuple((spread_matrix(matrix, row_split, block_count) for matrix in matrices))
    spread_gains = tuple(
        (
            spread_gain(vector, row_split, block_count)
            for vector in (grad_gain_self, grad_gain_cross, grad_gain_ff)
        )
    )
    summed = (
        lax.psum_scatter(spread_mats[0], ("rows", "blk"), scatter_dimension=0, tiled=True),
        lax.psum_scatter(spread_mats[1], ("rows", "blk"), scatter_dimension=0, tiled=True),
        lax.psum_scatter(spread_mats[2], ("rows", "blk"), scatter_dimension=0, tiled=True),
        lax.psum_scatter(spread_mats[3], ("rows", "blk"), scatter_dimension=0, tiled=True),
        lax.psum_scatter(spread_mats[4], ("rows", "blk"), scatter_dimension=0, tiled=True),
        lax.psum_scatter(spread_mats[5], ("rows", "blk"), scatter_dimension=0, tiled=True),
        lax.psum_scatter(spread_mats[6], ("rows", "blk"), scatter_dimension=0, tiled=True),
        lax.psum_scatter(spread_mats[7], ("rows", "blk"), scatter_dimension=0, tiled=True),
        lax.psum_scatter(spread_mats[8], ("rows", "blk"), scatter_dimension=0, tiled=True),
        lax.psum_scatter(spread_mats[9], ("rows", "blk"), scatter_dimension=0, tiled=True),
        lax.psum_scatter(spread_gains[0], ("rows", "blk"), scatter_dimension=0, tiled=True),
        lax.psum_scatter(spread_gains[1], ("rows", "blk"), scatter_dimension=0, tiled=True),
        lax.psum_scatter(spread_gains[2], ("rows", "blk"), scatter_dimension=0, tiled=True),
    )
    return (
        output,
        input_grad,
        encoded_grad,
        summed[0][0],
        summed[1][0],
        summed[2][0],
        summed[3][0],
        summed[4][0],
        summed[5][0],
        summed[6][0],
        summed[7][0],
        summed[8][0],
        summed[9][0],
        summed[10][0],
        summed[11][0],
        summed[12][0],
    )


BF16 = jnp.bfloat16
F32 = jnp.float32
LANES = 128
HALF = 2 * LANES + LANES
CORE_SWAP = ((0, 1), (1, 0), (2, 3), (3, 2))
CHIP_SWAP = ((0, 2), (2, 0), (1, 3), (3, 1))


def dot_nn(left, right):
    return jnp.dot(left, right, preferred_element_type=F32)


def dot_nt(left, right):
    return lax.dot_general(left, right, (((1,), (1,)), ((), ())), preferred_element_type=F32)


def dot_tn(left, right):
    return lax.dot_general(left, right, (((0,), (0,)), ((), ())), preferred_element_type=F32)


def whole(array):
    rank = len(array.shape)
    return pl.BlockSpec(array.shape, lambda *_: (0,) * rank)


def struct(shape, dtype):
    return jax.ShapeDtypeStruct(shape, dtype)


def run_kernel(name, body, scalars, args, in_specs, outs, out_specs, grid=(1,), scratch=(), flops=0, after=(), vmem=58):
    moved = sum(a.size * a.dtype.itemsize for a in args)
    if after:
        inner, given = (body, len(args))

        def body(s, *refs):
            inner(s, *refs[:given], *refs[given + len(after) :])

        args = (*args, *after)
        in_specs = [*in_specs, *([pl.BlockSpec(memory_space=pl.ANY)] * len(after))]
    moved += sum(o.size * o.dtype.itemsize for o in outs)
    return pl.pallas_call(
        body,
        grid_spec=pltpu.PrefetchScalarGridSpec(
            num_scalar_prefetch=1,
            grid=grid,
            in_specs=list(in_specs),
            out_specs=list(out_specs),
            scratch_shapes=list(scratch),
        ),
        out_shape=list(outs),
        compiler_params=pltpu.CompilerParams(vmem_limit_bytes=vmem << 20),
        name=name,
    )(scalars, *args)


def unit_norm(values):
    scale = lax.rsqrt(jnp.mean(values * values, axis=-1, keepdims=True) + 1e-06)
    return (values * scale, scale)


def norm_pull(values, gain_vec, grad_out):
    normal, scale = unit_norm(values)
    scaled = grad_out * gain_vec
    inner = jnp.mean(scaled * normal, axis=-1, keepdims=True)
    return (scale * (scaled - normal * inner), jnp.sum(grad_out * normal, axis=0, keepdims=True))


def head_lanes():
    lane = lax.broadcasted_iota(jnp.int32, (1, LANES), 1)
    return (lane, (lane < HEAD_DIM, lane >= HEAD_DIM))


def only(keep, values):
    return jnp.where(keep, values, jnp.zeros_like(values))


def soft_block(queries, marks, keys, values):
    lane, masks = head_lanes()
    attended, sums = ([], [])
    for keep in masks:
        scores = dot_nt(jnp.concatenate([only(keep, queries), marks], axis=1), keys)
        top = jnp.max(scores, axis=1, keepdims=True)
        weights = jnp.exp(scores - top)
        total = jnp.sum(weights, axis=1, keepdims=True)
        attended.append(dot_nn(weights.astype(BF16), values) / total)
        sums.append(top + jnp.log(total))
    return (jnp.where(masks[0], *attended), jnp.where(masks[0], *sums))


def causal_block(queries, marks, keys, values):
    lane, masks = head_lanes()
    rows, cols = queries.shape[0], keys.shape[0]
    flipped = values.T
    attended, sums = ([], [])
    for at, keep in enumerate(masks):
        scores = dot_nt(keys, jnp.concatenate([only(keep, queries), marks], axis=1))
        at_row = lax.broadcasted_iota(jnp.int32, (rows, rows), 0)
        at_col = lax.broadcasted_iota(jnp.int32, (rows, rows), 1)
        last = jnp.where(at_row <= at_col, scores[cols - rows :, :], NEG_FILL)
        scores = last if cols == rows else jnp.concatenate([scores[: cols - rows, :], last], axis=0)
        top = jnp.max(scores, axis=0, keepdims=True)
        weights = jnp.exp(scores - top)
        total = jnp.sum(weights, axis=0, keepdims=True)
        head = flipped[at * HEAD_DIM : (at + 1) * HEAD_DIM, :]
        attended.append(dot_nn(head, weights.astype(BF16)) / total)
        sums.append(jnp.broadcast_to(top + jnp.log(total), (HEAD_DIM, rows)))
    return (jnp.concatenate(attended, axis=0).T, jnp.concatenate(sums, axis=0).T)


def three_parts(spread):
    high = spread.astype(BF16)
    rest = spread - high.astype(F32)
    middle = rest.astype(BF16)
    return (-high, -middle, -(rest - middle.astype(F32)).astype(BF16))


def put_parts(lane, head, parts, base):
    for at, part in enumerate(parts):
        base = jnp.where(lane == head * HEAD_DIM + 3 + at, part, base)
    return base


def ones_lanes(lane):
    place = lane % HEAD_DIM
    return (place >= 3) & (place < 6)


def head_totals(product):
    high = product.astype(BF16)
    low = (product - high.astype(F32)).astype(BF16)
    at_row = lax.broadcasted_iota(jnp.int32, (2 * LANES, LANES), 0) % LANES
    at_col = lax.broadcasted_iota(jnp.int32, (2 * LANES, LANES), 1)
    same = jnp.where((at_row < HEAD_DIM) == (at_col < HEAD_DIM), 1.0, 0.0).astype(BF16)
    return dot_nn(jnp.concatenate([high, low], axis=1), same)


def pull_block(queries, marks, keys, key_marks, values, grads, attended, sums, causal):
    lane, masks = head_lanes()
    rows, cols = queries.shape[0], keys.shape[0]
    wide_keys = jnp.concatenate([keys, key_marks], axis=1)
    ones = jnp.where(ones_lanes(lane), 1.0, 0.0).astype(BF16)
    wide_values = jnp.concatenate([values, jnp.broadcast_to(ones, (cols, LANES))], axis=1)
    delta_parts = three_parts(head_totals(grads.astype(F32) * attended))
    sum_parts = three_parts(sums)
    flipped = keys.T
    grad_queries = []
    grad_keys = grad_values = None
    for at, keep in enumerate(masks):
        query, grad = (only(keep, queries), only(keep, grads))
        wide_query = jnp.concatenate([query, put_parts(lane, at, sum_parts, marks)], axis=1)
        wide_grad = jnp.concatenate([grad, put_parts(lane, at, delta_parts, jnp.zeros_like(marks))], axis=1)
        probs = jnp.exp(dot_nt(wide_keys, wide_query))
        if causal:
            at_row = lax.broadcasted_iota(jnp.int32, (rows, rows), 0)
            at_col = lax.broadcasted_iota(jnp.int32, (rows, rows), 1)
            last = jnp.where(at_row <= at_col, probs[cols - rows :, :], 0.0)
            probs = last if cols == rows else jnp.concatenate([probs[: cols - rows, :], last], axis=0)
        grad_scores = (probs * dot_nt(wide_values, wide_grad)).astype(BF16)
        grad_queries.append(dot_nn(flipped, grad_scores))
        key_part = dot_nn(grad_scores, query)
        value_part = dot_nn(probs.astype(BF16), grad)
        grad_keys = key_part if at == 0 else grad_keys + key_part
        grad_values = value_part if at == 0 else grad_values + value_part
    sub = lax.broadcasted_iota(jnp.int32, (LANES, 1), 0)
    return (jnp.where(sub < HEAD_DIM, *grad_queries).T * SCALE, grad_keys, grad_values)


def pair_columns(array):
    return pl.BlockSpec((array.shape[0], LANES), lambda p, _: (0, p))


def query_marks(labels):
    lane = lax.broadcasted_iota(jnp.int32, (LANES, 1), 0)
    return jnp.where(labels == lane, 1.0, 0.0).T.astype(BF16)


def key_marks(labels):
    lane = lax.broadcasted_iota(jnp.int32, (LANES, 1), 0)
    closed = jnp.where(labels != lane, NEG_FILL, 0.0)
    return jnp.where(lane < 3, closed, jnp.where(ones_lanes(lane), 1.0, 0.0)).T.astype(BF16)


def doc_marks(label_ref, tok, enc):
    first = -(-tok // LANES) * LANES
    doc = label_ref[:, pl.ds(first + enc, LANES)][:, 0:1]
    return key_marks(jnp.where(label_ref[:, pl.ds(first, enc)] == 1, doc, -1))


def pair_lanes():
    return pl.ds(pl.multiple_of(pl.program_id(0) * LANES, LANES), LANES)


def column_block(array):
    return pl.BlockSpec((array.shape[0], HALF), lambda _, s: (0, s[0]))


def any_place(_):
    return pl.BlockSpec(memory_space=pl.ANY)


def copies(sources, targets, semaphores):
    return [pltpu.make_async_copy(src, dst, semaphores.at[at]) for at, (src, dst) in enumerate(zip(sources, targets))]


def find_passages(place, tok, enc, labels, after=()):
    spot = -(-tok // LANES) * LANES + enc

    def body(s, own_ref, *refs):
        label_refs, out_ref = refs[:4], refs[4]
        own = own_ref[:, pl.ds(0, tok)]
        used = [jnp.max(jnp.where(own == ref[0, spot], 1, 0)) for ref in label_refs]
        total = used[0] + used[1] + used[2] + used[3]
        out_ref[0] = s[0]
        out_ref[1] = s[1]
        out_ref[6] = total
        out_ref[7] = 0
        ahead, behind = (jnp.int32(0), total)
        for slot in range(4):
            out_ref[2 + jnp.where(used[slot] == 1, ahead, behind)] = jnp.int32(slot)
            ahead, behind = (ahead + used[slot], behind + 1 - used[slot])

    smem = pl.BlockSpec(memory_space=pltpu.SMEM)
    return run_kernel(
        "find_passages", body, place, (labels[0], *labels), [whole(labels[0])] + [smem] * 4, [struct((8,), jnp.int32)],
        [smem], after=after,
    )[0]


def write_projections(s, mine_ref, other_ref, gain, weight_refs, scales, normed_ref, out_refs):
    tok = mine_ref.shape[0]
    for source, part in ((mine_ref, s[0]), (other_ref, 1 - s[0])):
        rows = pl.ds(pl.multiple_of(part * tok, tok), tok)
        normed = (unit_norm(source[...].astype(F32))[0] * gain).astype(BF16)
        normed_ref[rows, :] = normed
        for weight_ref, out_ref, scale in zip(weight_refs, out_refs, scales):
            out_ref[rows, :] = (dot_nn(normed, weight_ref[...]) * scale).astype(BF16)


def near_part(place, mine, other, gain_vec, weights, labels, passages, passage_weights, after=()):
    tok, width = mine.shape
    both = 2 * tok
    enc = passages[0].shape[0]
    third = width // 3

    def body(
        s, mine_ref, other_ref, gain_ref, wq_ref, wk_ref, wv_ref, own_ref, core_ref, e0_ref, e1_ref, ck_ref, cv_ref,
        h_ref, q_ref, k_ref, v_ref, m_ref, km_ref, out_ref, sum_ref, pk_ref, pv_ref,
    ):
        @pl.when(pl.program_id(0) == 0)
        def _():
            for source, part in ((own_ref, s[0]), (core_ref, 1 - s[0])):
                rows = pl.ds(pl.multiple_of(part * tok, tok), tok)
                m_ref[rows, :] = query_marks(source[:, pl.ds(0, tok)])
                km_ref[rows, :] = key_marks(source[:, pl.ds(0, tok)])
            write_projections(
                s, mine_ref, other_ref, gain_ref[...].reshape(1, width), (wq_ref, wk_ref, wv_ref), (SCALE, 1.0, 1.0), h_ref,
                (q_ref, k_ref, v_ref),
            )

        pair = pair_lanes()
        for at in (0, 1):
            rows, seen = (pl.ds(at * tok, tok), pl.ds(0, (at + 1) * tok))
            wide = jnp.concatenate([k_ref[seen, pair], km_ref[seen, :]], axis=1)
            out_ref[rows, :], sum_ref[rows, :] = causal_block(
                q_ref[rows, pair], m_ref[rows, :], wide, v_ref[seen, pair]
            )
        for at, source in enumerate((e0_ref, e1_ref)):
            rows = pl.ds(at * enc, enc)
            pk_ref[rows, :] = dot_nn(source[...], ck_ref[...]).astype(BF16)
            pv_ref[rows, :] = dot_nn(source[...], cv_ref[...]).astype(BF16)

    args = (mine, other, gain_vec, *weights, *labels, *passages, *passage_weights)
    specs = [whole(a) for a in args]
    specs[3:6] = [column_block(w) for w in weights]
    specs[10:12] = [pl.BlockSpec((width, third), lambda p, _: (0, p))] * 2
    outs = [struct((both, width), BF16)] + [struct((both, HALF), BF16)] * 3 + [struct((both, LANES), BF16)] * 2
    outs += [struct((both, HALF), F32)] * 2 + [struct((2 * enc, width), BF16)] * 2
    return run_kernel(
        "near_part", body, place, args, specs, outs,
        [whole(o) for o in outs[:6]]
        + [pair_columns(o) for o in outs[6:8]]
        + [pl.BlockSpec((2 * enc, third), lambda p, _: (0, p))] * 2,
        grid=(HALF // LANES,), after=after, flops=both * both * 6 * 2 * HALF,
    )


def far_part(place, mine, other, gain_vec, weights, queries, marks, labels, near_out, near_sum, after=()):
    tok, width = mine.shape
    both = 2 * tok

    def body(
        s, mine_ref, other_ref, gain_ref, wk_ref, wv_ref, q_ref, m_ref, lx_ref, ld_ref, no_ref, ns_ref,
        h_ref, k_ref, v_ref, km_ref, out_ref, sum_ref, keep_ref, send_ref,
    ):
        pair = pair_lanes()

        @pl.when(pl.program_id(0) == 0)
        def _():
            for source, part in ((lx_ref, s[0]), (ld_ref, 1 - s[0])):
                rows = pl.ds(pl.multiple_of(part * tok, tok), tok)
                km_ref[rows, :] = key_marks(source[:, pl.ds(0, tok)])

        def write(at, out, log_sum):
            rows = pl.ds(at * tok, tok)
            out_ref[rows, :] = out
            sum_ref[rows, :] = log_sum

            @pl.when(s[0] == at)
            def _():
                keep_ref[...] = out.astype(BF16)

            @pl.when(s[0] != at)
            def _():
                send_ref[...] = out.astype(BF16)

        @pl.when(s[1] == 0)
        def _():
            for at in (0, 1):
                rows = pl.ds(at * tok, tok)
                write(at, no_ref[rows, :], ns_ref[rows, :])

            @pl.when(pl.program_id(0) == 0)
            def _():
                for ref in (h_ref, k_ref, v_ref):
                    ref[...] = jnp.zeros_like(ref)

        @pl.when(s[1] != 0)
        def _():
            @pl.when(pl.program_id(0) == 0)
            def _():
                write_projections(
                    s, mine_ref, other_ref, gain_ref[...].reshape(1, width), (wk_ref, wv_ref), (1.0, 1.0), h_ref, (k_ref, v_ref)
                )

            wide = jnp.concatenate([k_ref[:, pair], km_ref[...]], axis=1)
            for at in (0, 1):
                rows = pl.ds(at * tok, tok)
                out, log_sum = soft_block(q_ref[rows, :], m_ref[rows, :], wide, v_ref[:, pair])
                near_log = ns_ref[rows, :]
                top = jnp.maximum(near_log, log_sum)
                near_share, far_share = (jnp.exp(near_log - top), jnp.exp(log_sum - top))
                total = near_share + far_share
                write(at, (no_ref[rows, :] * near_share + out * far_share) / total, top + jnp.log(total))

    args = (mine, other, gain_vec, *weights, queries, marks, *labels, near_out, near_sum)
    specs = [whole(a) for a in args]
    specs[3:5] = [column_block(w) for w in weights]
    for at in (5, 9, 10):
        specs[at] = pair_columns(args[at])
    outs = [struct((both, width), BF16)] + [struct((both, HALF), BF16)] * 2 + [struct((both, LANES), BF16)]
    outs += [struct((both, HALF), F32)] * 2 + [struct((tok, HALF), BF16)] * 2
    return run_kernel(
        "far_part", body, place, args, specs, outs, [whole(o) for o in outs[:4]] + [pair_columns(o) for o in outs[4:]],
        grid=(HALF // LANES,), after=after, flops=both * both * 8 * 2 * HALF,
    )


def gather_slots(s, enc, target, first_ref, second_ref, lanes=slice(None)):
    for at in range(4):
        slot = s[2 + at]
        rows = pl.ds(at * enc, enc)

        @pl.when(slot < 2)
        def _():
            target[rows, :] = first_ref[pl.ds(pl.multiple_of(slot * enc, enc), enc), :]

        @pl.when(slot >= 2)
        def _():
            target[rows, :] = second_ref[pl.ds(pl.multiple_of((slot - 2) * enc, enc), enc), lanes]


def by_count(s, work):
    pl.when(s[6] <= 2)(lambda: work(2))
    pl.when(s[6] >= 3)(lambda: work(3))


def cross_part(
    place, inputs, ctx_keep, ctx_recv, out_weight, gain_vec, query_weight, first, second, key_weight, value_weight,
    keys, values, labels, after=(),
):
    tok, width = inputs.shape
    enc = first.shape[0]

    def body(
        s, in_ref, keep_ref, recv_ref, wa_ref, wb_ref, gain_ref, wq_any, first_any, second_any, wk_any, wv_any, k0_ref, v0_ref,
        l0_ref, l1_ref, l2_ref, l3_ref,
        x_ref, h_ref, q_ref, ctx_ref, k1_ref, v1_ref, m_ref, km0_ref, km1_ref, cctx_ref, out_ref, sum_ref,
        all_k, all_v, wq_ref, first_ref, second_ref, wk_ref, wv_ref, semaphores,
    ):
        keep = pl.ds(0, LANES)

        @pl.when(pl.program_id(0) == 0)
        def _():
            later = copies(
                (wq_any, first_any, wk_any, wv_any, second_any), (wq_ref, first_ref, wk_ref, wv_ref, second_ref), semaphores
            )
            for copy in later:
                copy.start()
            total = dot_nn(keep_ref[...], wa_ref[...]) + dot_nn(recv_ref[...], wb_ref[...])
            residual = in_ref[...].astype(F32) + total
            x_ref[...] = residual
            normed = (unit_norm(residual)[0] * gain_ref[...].reshape(1, width)).astype(BF16)
            h_ref[...] = normed
            later[0].wait()
            q_ref[...] = (dot_nn(normed, wq_ref[...]) * SCALE).astype(BF16)
            ctx_ref[:, pl.ds(pl.multiple_of(s[0] * HALF, LANES), HALF)] = keep_ref[...]
            ctx_ref[:, pl.ds(pl.multiple_of((1 - s[0]) * HALF, LANES), HALF)] = recv_ref[...]
            for copy in later[1:]:
                copy.wait()
            for at, source in enumerate((first_ref, second_ref)):
                rows = pl.ds(at * enc, enc)
                k1_ref[rows, :] = dot_nn(source[...], wk_ref[...]).astype(BF16)
                v1_ref[rows, :] = dot_nn(source[...], wv_ref[...]).astype(BF16)
            m_ref[...] = query_marks(l0_ref[:, pl.ds(0, tok)])
            for target, low, high in ((km0_ref, l0_ref, l1_ref), (km1_ref, l2_ref, l3_ref)):
                target[pl.ds(0, enc), :] = doc_marks(low, tok, enc)
                target[pl.ds(enc, enc), :] = doc_marks(high, tok, enc)
            gather_slots(s, enc, all_k.at[:, pl.ds(LANES, LANES)], km0_ref, km1_ref)

        pair = pair_lanes()
        gather_slots(s, enc, all_k.at[:, keep], k0_ref, k1_ref, pair)
        gather_slots(s, enc, all_v, v0_ref, v1_ref, pair)

        def work(count):
            seen = pl.ds(0, count * enc)
            out, log_sum = soft_block(q_ref[:, pair], m_ref[...], all_k[seen, :], all_v[seen, :])
            cctx_ref[...] = out.astype(BF16)
            out_ref[...] = out
            sum_ref[...] = log_sum

        by_count(s, work)

    args = (
        inputs, ctx_keep, ctx_recv, out_weight, out_weight, gain_vec, query_weight, first, second, key_weight, value_weight,
        keys, values, *labels,
    )
    specs = [whole(a) for a in args]
    specs[3] = pl.BlockSpec((HALF, width), lambda _, s: (s[0], 0))
    specs[4] = pl.BlockSpec((HALF, width), lambda _, s: (1 - s[0], 0))
    specs[6:11] = [any_place(a) for a in args[6:11]]
    specs[11], specs[12] = pair_columns(keys), pair_columns(values)
    outs = [struct((tok, width), F32)] + [struct((tok, width), BF16)] * 3 + [struct((2 * enc, width), BF16)] * 2
    outs += [struct((tok, LANES), BF16)] + [struct((2 * enc, LANES), BF16)] * 2
    outs += [struct((tok, width), BF16)] + [struct((tok, width), F32)] * 2
    return run_kernel(
        "cross_part", body, place, args, specs, outs, [whole(o) for o in outs[:9]] + [pair_columns(o) for o in outs[9:]],
        grid=(width // LANES,),
        scratch=[pltpu.VMEM((4 * enc, 2 * LANES), BF16), pltpu.VMEM((4 * enc, LANES), BF16)]
        + [pltpu.VMEM(a.shape, a.dtype) for a in args[6:11]]
        + [pltpu.SemaphoreType.DMA((5,))],
        after=after, flops=tok * 2.5 * enc * 8 * 2 * width + 12 * tok * width * width,
    )


def cross_back(place, queries, keys, values, marks, key_marks, grads, attended, sums, residual, grad_res, query_weight, gains, out_weight, after=()):
    tok, width = queries.shape
    enc = keys[0].shape[0] // 2
    last = width // LANES - 1

    def body(
        s, q_ref, k0_ref, k1_ref, v0_ref, v1_ref, m_ref, km0_ref, km1_ref, g_ref, at_ref, ls_ref, gain_ref,
        x_any, dx_any, wq_any, wo_any, dq_ref, dk_ref, dv_ref, dx1_ref, low_ref, gain_grad_ref, keep_ref, send_ref,
        all_k, all_v, all_m, x_ref, dx_ref, wq_ref, wo_ref, semaphores,
    ):
        later = copies((x_any, dx_any, wq_any, wo_any), (x_ref, dx_ref, wq_ref, wo_ref), semaphores)

        @pl.when(pl.program_id(0) == 0)
        def _():
            for copy in later:
                copy.start()
            gather_slots(s, enc, all_m, km0_ref, km1_ref)

        gather_slots(s, enc, all_k, k0_ref, k1_ref)
        gather_slots(s, enc, all_v, v0_ref, v1_ref)
        pair = pair_lanes()

        def work(count):
            seen = pl.ds(0, count * enc)
            grad_q, grad_k, grad_v = pull_block(
                q_ref[...], m_ref[...], all_k[seen, :], all_m[seen, :], all_v[seen, :], g_ref[...], at_ref[...],
                ls_ref[...], False,
            )
            dq_ref[:, pair] = grad_q.astype(BF16)
            low_k, low_v = (grad_k.astype(BF16), grad_v.astype(BF16))
            for at in range(4):
                rows = pl.ds(pl.multiple_of(s[2 + at] * enc, enc), enc)
                if at < count:
                    dk_ref[rows, :] = low_k[at * enc : (at + 1) * enc, :]
                    dv_ref[rows, :] = low_v[at * enc : (at + 1) * enc, :]
                else:
                    dk_ref[rows, :] = jnp.zeros((enc, LANES), BF16)
                    dv_ref[rows, :] = jnp.zeros((enc, LANES), BF16)

        by_count(s, work)

        @pl.when(pl.program_id(0) == last)
        def _():
            for copy in later:
                copy.wait()
            back, gain_grad_ref[...] = norm_pull(x_ref[...], gain_ref[...].reshape(1, width), dot_nt(dq_ref[...], wq_ref[...]))
            grad_x = dx_ref[...] + back
            dx1_ref[...] = grad_x
            low = grad_x.astype(BF16)
            low_ref[...] = low
            for target, half in ((keep_ref, s[0]), (send_ref, 1 - s[0])):
                rows = pl.ds(pl.multiple_of(half * HALF, HALF), HALF)
                target[...] = dot_nt(low, wo_ref[rows, :]).astype(BF16)

    late = (residual, grad_res, query_weight, out_weight)
    args = (queries, *keys, *values, marks, *key_marks, grads, attended, sums, gains, *late)
    specs = [pair_columns(a) for a in args]
    for at in (5, 6, 7, 11):
        specs[at] = whole(args[at])
    specs[12:] = [any_place(a) for a in late]
    outs = [struct((tok, width), BF16)] + [struct((4 * enc, width), BF16)] * 2
    outs += [struct((tok, width), F32), struct((tok, width), BF16), struct((1, width), F32)]
    outs += [struct((tok, HALF), BF16)] * 2
    out_specs = [whole(o) for o in outs]
    out_specs[1], out_specs[2] = pair_columns(outs[1]), pair_columns(outs[2])
    return run_kernel(
        "cross_back", body, place, args, specs, outs, out_specs,
        grid=(width // LANES,),
        scratch=[pltpu.VMEM((4 * enc, LANES), BF16)] * 3
        + [pltpu.VMEM(a.shape, a.dtype) for a in late]
        + [pltpu.SemaphoreType.DMA((len(late),))],
        after=after, flops=tok * 2.5 * enc * 20 * 2 * width,
    )


def write_normed_grads(s, tok, h_ref, gain, grad_refs, weight_refs, keep_ref, send_ref, gain_grad_ref):
    running = None
    for target, part in ((keep_ref, s[0]), (send_ref, 1 - s[0])):
        rows = pl.ds(pl.multiple_of(part * tok, tok), tok)
        value = None
        for grad_ref, weight_ref in zip(grad_refs, weight_refs):
            piece = dot_nt(grad_ref[rows, :], weight_ref[...])
            value = piece if value is None else value + piece
        target[...] = value.astype(BF16)
        inner = jnp.sum(value * h_ref[rows, :].astype(F32), axis=0, keepdims=True)
        running = inner if running is None else running + inner
    gain_grad_ref[...] = running / gain


def far_back(place, queries, keys, values, marks, key_marks, grad_keep, grad_recv, attended, sums, gains, normed, weights, after=()):
    both, width = normed.shape
    tok = both // 2
    last = HALF // LANES - 1

    def body(
        s, q_ref, k_ref, v_ref, m_ref, km_ref, gk_ref, gr_ref, at_ref, ls_ref, gain_ref, h_any, wk_any, wv_any,
        dq_ref, dk_ref, dv_ref, keep_ref, send_ref, gain_grad_ref, h_ref, wk_ref, wv_ref, semaphores,
    ):
        pair = pair_lanes()
        columns = pl.ds(pl.multiple_of(s[0] * HALF, LANES), HALF)
        later = copies((h_any, wk_any.at[:, columns], wv_any.at[:, columns]), (h_ref, wk_ref, wv_ref), semaphores)

        @pl.when(s[1] != 0)
        def _():
            @pl.when(pl.program_id(0) == 0)
            def _():
                for copy in later:
                    copy.start()

            sum_k = sum_v = None
            for at in (0, 1):
                rows = pl.ds(at * tok, tok)
                grads = jnp.where(s[0] == at, gk_ref[...], gr_ref[...])
                dq_ref[rows, :], grad_k, grad_v = pull_block(
                    q_ref[rows, :], m_ref[rows, :], k_ref[...], km_ref[...], v_ref[...], grads, at_ref[rows, :],
                    ls_ref[rows, :], False,
                )
                sum_k = grad_k if at == 0 else sum_k + grad_k
                sum_v = grad_v if at == 0 else sum_v + grad_v
            dk_ref[:, pair] = sum_k.astype(BF16)
            dv_ref[:, pair] = sum_v.astype(BF16)

            @pl.when(pl.program_id(0) == last)
            def _():
                for copy in later:
                    copy.wait()
                write_normed_grads(
                    s, tok, h_ref, gain_ref[...].reshape(1, width), (dk_ref, dv_ref), (wk_ref, wv_ref), keep_ref, send_ref, gain_grad_ref
                )

        @pl.when(s[1] == 0)
        def _():
            dq_ref[...] = jnp.zeros_like(dq_ref)
            for ref in (dk_ref, dv_ref, keep_ref, send_ref, gain_grad_ref):
                ref[...] = jnp.zeros_like(ref)

    args = (queries, keys, values, marks, key_marks, grad_keep, grad_recv, attended, sums, gains, normed, *weights)
    specs = [pair_columns(a) for a in args]
    specs[3], specs[4], specs[9] = whole(marks), whole(key_marks), whole(gains)
    specs[10:] = [any_place(a) for a in args[10:]]
    outs = [struct((both, HALF), F32)] + [struct((both, HALF), BF16)] * 2
    outs += [struct((tok, width), BF16)] * 2 + [struct((1, width), F32)]
    return run_kernel(
        "far_back", body, place, args, specs, outs, [pair_columns(outs[0])] + [whole(o) for o in outs[1:]],
        grid=(HALF // LANES,),
        scratch=[pltpu.VMEM((both, width), BF16)] + [pltpu.VMEM((width, HALF), BF16)] * 2 + [pltpu.SemaphoreType.DMA((3,))],
        after=after, flops=both * both * 20 * 2 * HALF,
    )


def write_square(s, value, keep, send, first, x_first=False):
    rows = value.shape[0] // 16
    side = HALF // 2

    def write(target, half):
        for at in range(8):
            high, low, far = (at // 4, (at // 2) % 2, at % 2)
            for chip in range(value.shape[1] // HALF):
                columns = slice(chip * HALF + half * side, chip * HALF + (half + 1) * side)
                place = (chip, far, low, high) if x_first else (far, chip, low, high)
                for part in range(2):
                    piece = value[(2 * at + part) * rows : (2 * at + part + 1) * rows, columns].astype(BF16)
                    target[*place, pl.ds(first, rows), pl.ds(part * side, side)] = piece

    @pl.when(s[0] == 0)
    def _():
        write(keep, 0)
        write(send, 1)

    @pl.when(s[0] != 0)
    def _():
        write(keep, 1)
        write(send, 0)


def near_back(
    place, queries, keys, values, marks, key_marks, grad_keep, grad_recv, attended, sums, carried, gains,
    normed, far_normed, weights, far_grads, gain_grads, after=(),
):
    both, width = normed.shape
    tok = both // 2
    last = HALF // LANES - 1
    late_shapes = [(both, width)] * 2 + [(width, HALF)] * 3 + [(both, HALF)] * 2

    def body(
        s, q_ref, k_ref, v_ref, m_ref, km_ref, gk_ref, gr_ref, at_ref, ls_ref, ca_ref, gain_ref,
        gs_ref, gc_ref, gf_ref, h_any, fh_any, wq_any, wk_any, wv_any, fk_any, fv_any,
        keep_ref, send_ref, keep4, send4,
        dq, dk, dv, sum_k, sum_v, gain_grad_ref, gain_rows, h_ref, fh_ref, wq_ref, wk_ref, wv_ref, fk_ref, fv_ref, semaphores,
    ):
        pair = pair_lanes()
        columns = pl.ds(pl.multiple_of(s[0] * HALF, LANES), HALF)
        later = copies(
            (h_any, fh_any, wq_any.at[:, columns], wk_any.at[:, columns], wv_any.at[:, columns], fk_any, fv_any),
            (h_ref, fh_ref, wq_ref, wk_ref, wv_ref, fk_ref, fv_ref),
            semaphores,
        )

        @pl.when(pl.program_id(0) == 0)
        def _():
            for copy in later:
                copy.start()

        for at in (0, 1):
            rows = pl.ds(at * tok, tok)
            count = (at + 1) * tok
            seen = pl.ds(0, count)
            grads = jnp.where(s[0] == at, gk_ref[...], gr_ref[...])
            grad_q, grad_k, grad_v = pull_block(
                q_ref[rows, :], m_ref[rows, :], k_ref[seen, :], km_ref[seen, :], v_ref[seen, :], grads,
                at_ref[rows, :], ls_ref[rows, :], True,
            )
            dq[rows, pair] = (grad_q + ca_ref[rows, :]).astype(BF16)
            if at == 0:
                sum_k[...] = grad_k
                sum_v[...] = grad_v
            else:
                dk[pl.ds(0, tok), pair] = (sum_k[...] + grad_k[:tok]).astype(BF16)
                dv[pl.ds(0, tok), pair] = (sum_v[...] + grad_v[:tok]).astype(BF16)
                dk[pl.ds(tok, tok), pair] = grad_k[tok:].astype(BF16)
                dv[pl.ds(tok, tok), pair] = grad_v[tok:].astype(BF16)

        @pl.when(pl.program_id(0) == last)
        def _():
            for copy in later:
                copy.wait()
            write_normed_grads(
                s, tok, h_ref, gain_ref[...].reshape(1, width), (dq, dk, dv), (wq_ref, wk_ref, wv_ref), keep_ref, send_ref, gain_grad_ref
            )
            rows = width // 16
            write_square(s, dot_tn(h_ref[...], dq[...]), keep4, send4, 0)
            value = dot_tn(h_ref[...], dk[...]) + dot_tn(fh_ref[...], fk_ref[...])
            write_square(s, value, keep4, send4, rows)
            value = dot_tn(h_ref[...], dv[...]) + dot_tn(fh_ref[...], fv_ref[...])
            write_square(s, value, keep4, send4, 2 * rows)
            gain_rows[...] = jnp.zeros_like(gain_rows)
            gain_rows[0:1, :] = gain_grad_ref[...] + gs_ref[...]
            gain_rows[1:2, :] = gc_ref[...]
            gain_rows[2:3, :] = gf_ref[...]
            low = gain_rows[...].astype(BF16)
            piece = width // 8
            at_row = lax.broadcasted_iota(jnp.int32, (width, HALF), 0)
            at_col = lax.broadcasted_iota(jnp.int32, (width, HALF), 1)
            for at in range(8):
                pick = jnp.where((at_row == at_col + at * piece) & (at_col < piece), 1.0, 0.0).astype(BF16)
                value = dot_nn(low, pick).astype(BF16)
                for target in (keep4, send4):
                    target[at % 2, 0, (at // 2) % 2, at // 4, pl.ds(3 * rows, 16), :] = value

    late = (normed, far_normed, *weights, *far_grads)
    args = (
        queries, keys, values, marks, key_marks, grad_keep, grad_recv, attended, sums, carried, gains, *gain_grads, *late
    )
    specs = [pair_columns(a) for a in args]
    specs[3], specs[4] = whole(marks), whole(key_marks)
    specs[10:14] = [whole(a) for a in args[10:14]]
    specs[14:] = [any_place(a) for a in late]
    outs = [struct((tok, width), BF16)] * 2
    outs += [struct((2, 1, 2, 2, 3 * (width // 16) + 16, HALF), BF16)] * 2
    return run_kernel(
        "near_back", body, place, args, specs, outs, [whole(o) for o in outs],
        grid=(HALF // LANES,),
        scratch=[pltpu.VMEM((both, HALF), BF16)] * 3
        + [pltpu.VMEM((tok, LANES), F32)] * 2
        + [pltpu.VMEM((1, width), F32), pltpu.VMEM((16, width), F32)]
        + [pltpu.VMEM(shape, BF16) for shape in late_shapes]
        + [pltpu.SemaphoreType.DMA((len(late),))],
        after=after, flops=both * both * 0.75 * 20 * 2 * HALF + 20 * both * width * HALF,
    )


def cross_grads(name, place, pairs, x_first, passages=None, after=()):
    width = pairs[0][0][0].shape[1]
    rows = width // 16
    count = len(pairs)
    order, spots, groups = ([], {}, [])
    for left, right in [*pairs, *([] if passages is None else [(passages[:2], passages[2:])])]:
        fresh = []
        for array in (*left, *right):
            if id(array) not in spots:
                spots[id(array)] = len(order)
                fresh.append(len(order))
                order.append(array)
        groups.append((fresh, [spots[id(array)] for array in left], [spots[id(array)] for array in right]))
    given = len(order)
    outs = [struct((2, 2, 2, 2, count * rows, HALF), BF16)] * 2
    if passages is not None:
        enc = passages[0].shape[0] // 4
        outs += [struct((2, enc, width), F32), struct((2, enc, width), BF16)]
    produced = len(outs)

    def body(s, *refs):
        sources, results = refs[:given], refs[given : given + produced]
        held, semaphores = refs[given + produced : -1], refs[-1]
        step = pl.program_id(0)
        moves = copies(sources, held, semaphores)

        @pl.when(step == 0)
        def _():
            for move in moves:
                move.start()

        for at, (fresh, left, right) in enumerate(groups):

            @pl.when(step == at)
            def _(at=at, fresh=fresh, left=left, right=right):
                for spot in fresh:
                    moves[spot].wait()
                if at < count:
                    value = None
                    for part, spot in enumerate(left):
                        tall = held[spot].shape[0]
                        piece = dot_tn(held[spot][...], held[right[0]][pl.ds(part * tall, tall), :])
                        value = piece if value is None else value + piece
                    write_square(s, value, results[0], results[1], 0, x_first)
                    return
                for slot in range(4):
                    slots = pl.ds(slot * enc, enc)
                    value = dot_nt(held[left[0]][slots, :], held[right[0]][...])
                    value = value + dot_nt(held[left[1]][slots, :], held[right[1]][...])
                    if slot % 2 == 0:
                        results[2][slot // 2] = value
                    else:
                        results[3][slot // 2] = value.astype(BF16)

    block = pl.BlockSpec((2, 2, 2, 2, rows, HALF), lambda m, _: (0, 0, 0, 0, jnp.minimum(m, count - 1), 0))
    return run_kernel(
        name, body, place, order, [any_place(a) for a in order], outs,
        [block, block, *(whole(o) for o in outs[2:])],
        grid=(len(groups),),
        scratch=[pltpu.VMEM(a.shape, a.dtype) for a in order]
        + [pltpu.SemaphoreType.DMA((given,))],
        after=after,
    )


def passage_grads(place, grad_keys, grad_values, key_weight, value_weight, after=()):
    keys4, width = grad_keys.shape
    enc = keys4 // 4

    def body(s, dk_ref, dv_ref, wk_ref, wv_ref, keep_ref, send_ref):
        value = dot_nt(dk_ref[...], wk_ref[...]) + dot_nt(dv_ref[...], wv_ref[...])

        @pl.when(pl.program_id(0) % 2 == 0)
        def _():
            keep_ref[0] = value

        @pl.when(pl.program_id(0) % 2 != 0)
        def _():
            send_ref[0] = value.astype(BF16)

    args = (grad_keys, grad_values, key_weight, value_weight)
    slot = pl.BlockSpec((enc, width), lambda i, _: (i, 0))
    result = pl.BlockSpec((1, enc, width), lambda i, _: (i // 2, 0, 0))
    outs = [struct((2, enc, width), F32), struct((2, enc, width), BF16)]
    return run_kernel(
        "passage_grads", body, place, args, [slot, slot, whole(key_weight), whole(value_weight)], outs, [result, result],
        grid=(4,), after=after,
    )


def last_pull(place, inputs, gains, grad_res, parts, after=()):
    tok, width = inputs.shape
    steps = 2
    tile = tok // steps

    def body(s, in_ref, gain_ref, dx_ref, *refs):
        part_refs, out_ref = refs[:-1], refs[-1]
        total = part_refs[0][...].astype(F32)
        for ref in part_refs[1:]:
            total = total + ref[...].astype(F32)
        out_ref[...] = dx_ref[...] + norm_pull(in_ref[...].astype(F32), gain_ref[...].reshape(1, width), total)[0]

    args = (inputs, gains, grad_res, *parts)
    block = pl.BlockSpec((tile, width), lambda i, _: (i, 0))
    specs = [block for _ in args]
    specs[1] = whole(gains)
    return run_kernel(
        "last_pull", body, place, args, specs, [struct((tok, width), F32)], [block], grid=(steps,), after=after,
        flops=20 * tok * width,
    )[0]


def rounded(values):
    return lax.reduce_precision(values, 8, 7).astype(BF16)


def add_split(half, keep, recv):
    part = lambda array, at: lax.dynamic_index_in_dim(array, at, 0, False).astype(F32)
    kept = rounded(part(keep, half) + part(recv, half))
    return (kept, rounded(part(keep, 1 - half) + part(recv, 1 - half)))


class Halving:
    def __init__(self, keep, recv, steps):
        self.keep, self.recv, self.steps = (keep, recv, list(steps))

    def step(self, *after):
        half, axis, pairs = self.steps.pop(0)
        keep, recv = (self.keep.reshape(2, -1, HALF), self.recv.reshape(2, -1, HALF))
        if after:
            keep, recv, *_ = lax.optimization_barrier((keep, recv, *after))
        self.keep, send = add_split(half, keep, recv)
        self.recv = lax.ppermute(send, axis, pairs)
        return self.keep


def merge_split(place, step, sums, after=()):
    half, axis, pairs = step
    counts = [a.keep.shape[0] // 4 for a in sums]
    arrays = [array.reshape(2, 2, count, HALF) for a, count in zip(sums, counts) for array in (a.keep, a.recv)]
    starts = [sum(counts[:at]) for at in range(len(counts))]

    def body(s, *refs):
        given, (keep_ref, send_ref) = refs[: len(arrays)], refs[len(arrays) :]
        for target, side in ((keep_ref, s[0]), (send_ref, 1 - s[0])):
            for at, (first, count) in enumerate(zip(starts, counts)):
                for deep in range(2):
                    value = given[2 * at][side, deep].astype(F32) + given[2 * at + 1][side, deep].astype(F32)
                    target[deep, pl.ds(first, count), :] = value.astype(BF16)

    outs = [struct((2, sum(counts), HALF), BF16)] * 2
    keep, send = run_kernel(
        "merge_split", body, half.astype(jnp.int32).reshape(1), arrays, [whole(a) for a in arrays], outs,
        [whole(o) for o in outs], after=after,
    )
    merged = Halving(keep, lax.ppermute(send, axis, pairs), ())
    return merged


def self_start(place, keep4, recv4, after=()):
    cut = 80
    rest = keep4.shape[4] - cut

    def body(s, keep_ref, recv_ref, ak_ref, as_ref, bk_ref, bs_ref):
        for target, side in ((ak_ref, s[2]), (as_ref, 1 - s[2])):
            for slot, source in enumerate((keep_ref, recv_ref)):
                target[slot] = source[side, 0, :, :, pl.ds(0, cut), :]
        late, front, tail = (pl.ds(cut, rest - 16), pl.ds(0, rest - 16), pl.ds(cut + rest - 16, 16))

        @pl.when(s[0] == s[1])
        def _():
            bk_ref[:, :, :, front, :] = keep_ref[:, 0, :, :, late, :]
            bs_ref[:, :, :, front, :] = recv_ref[:, 0, :, :, late, :]

        @pl.when(s[0] != s[1])
        def _():
            bk_ref[:, :, :, front, :] = recv_ref[:, 0, :, :, late, :]
            bs_ref[:, :, :, front, :] = keep_ref[:, 0, :, :, late, :]

        shared = keep_ref[:, 0, :, :, tail, :].astype(F32) + recv_ref[:, 0, :, :, tail, :].astype(F32)
        for target in (bk_ref, bs_ref):
            target[:, :, :, pl.ds(rest - 16, 16), :] = shared.astype(BF16)

    args = (keep4, recv4)
    outs = [struct((2, 2, 2, cut, HALF), BF16)] * 2 + [struct((2, 2, 2, rest, HALF), BF16)] * 2
    return run_kernel(
        "self_start", body, place, args, [whole(a) for a in args], outs, [whole(o) for o in outs], after=after
    )


def both_step(place, first, second, after=()):
    sums = (first, second)
    spots, axes, pairs = zip(*(a.steps.pop(0) for a in sums))
    arrays = [array.reshape(2, -1, HALF) for a in sums for array in (a.keep, a.recv)]

    def body(s, *refs):
        given, outs = refs[:4], refs[4:]
        for at in range(2):
            side = s[spots[at]]
            for target, side in ((outs[2 * at], side), (outs[2 * at + 1], 1 - side)):
                target[...] = (given[2 * at][side].astype(F32) + given[2 * at + 1][side].astype(F32)).astype(BF16)

    outs = [struct(array.shape[1:], BF16) for array in arrays]
    results = run_kernel(
        "both_step", body, place, arrays, [whole(a) for a in arrays], outs,
        [whole(o) for o in outs], after=after,
    )
    for at, a in enumerate(sums):
        a.keep, a.recv = (results[2 * at], lax.ppermute(results[2 * at + 1], axes[at], pairs[at]))
    return results[0]


def finish_sums(name, keep, recv, count, tail=0, after=()):
    rows = keep.shape[0] // 16 // count * 16
    side = HALF // 2

    def body(s, keep_ref, recv_ref, *outs):
        for at in range(count):
            part = pl.ds(at * rows, rows)
            total = keep_ref[part, :].astype(F32) + recv_ref[part, :].astype(F32)
            outs[at][pl.ds(0, rows), :] = total[:, :side]
            outs[at][pl.ds(rows, rows), :] = total[:, side:]
        if tail:
            part = pl.ds(count * rows, 16)
            total = keep_ref[part, :].astype(F32) + recv_ref[part, :].astype(F32)
            for at in range(tail):
                outs[count + at][...] = total[at, : 2 * rows]

    outs = [struct((2 * rows, side), F32)] * count + [struct((2 * rows,), F32)] * tail
    place = jnp.zeros((1,), jnp.int32)
    return run_kernel(
        name, body, place, (keep, recv), [whole(keep), whole(recv)], outs, [whole(o) for o in outs], after=after
    )


def feed_forward(place, residual, context, out_weight, gain_vec, feed_in, feed_out, cotangent, after=()):
    tok, width = residual.shape
    hidden_width = feed_in.shape[1]
    steps = 4
    chunk = hidden_width // steps
    rows_in = width // 8
    side = width // 4

    def body(
        s, x1_ref, ctx_ref, wo_ref, gain_ref, w1_ref, w2_ref, g_ref,
        out_ref, dx_ref, low_ref, dctx_ref, gain_grad_ref, spread,
        x2, normed, normed_flip, grad_flip, sum_out, sum_norm, block_in, block_out, semaphores,
    ):
        step = pl.program_id(0)

        @pl.when(step == 0)
        def _():
            x2[...] = x1_ref[...] + dot_nn(ctx_ref[...], wo_ref[...])
            normed[...] = (unit_norm(x2[...])[0] * gain_ref[...].reshape(1, width)).astype(BF16)
            normed_flip[...] = normed[...].T
            grad_flip[...] = g_ref[...].T
            sum_out[...] = jnp.zeros_like(sum_out)
            sum_norm[...] = jnp.zeros_like(sum_norm)

        w1, w2, grad = (w1_ref[...], w2_ref[...], g_ref[...])
        pre = dot_nn(normed[...], w1)
        root = 0.7978845608028654
        bend = 0.044715
        square = pre * pre
        swing = jnp.tanh(pre * (root + root * bend * square))
        half = 0.5 + 0.5 * swing
        active = pre * half
        hidden = active.astype(BF16)
        sum_out[...] += dot_nn(hidden, w2)
        slope = half + active * (1.0 - swing) * (root + 3.0 * root * bend * square)
        grad_pre = (dot_nt(grad, w2) * slope).astype(BF16)
        sum_norm[...] += dot_nt(grad_pre, w1)
        slot = step % 2

        def moves(at, slot):
            first = pltpu.make_async_copy(
                block_in.at[slot], spread.at[:, at, pl.ds(0, 2 * rows_in), :], semaphores.at[slot, 0]
            )
            second = pltpu.make_async_copy(
                block_out.at[slot], spread.at[pl.ds(2 * at, 2), :, pl.ds(2 * rows_in, side), :], semaphores.at[slot, 1]
            )
            return (first, second)

        @pl.when(step >= 2)
        def _():
            for move in moves(step - 2, slot):
                move.wait()

        grad_in = dot_nn(normed_flip[...], grad_pre).astype(BF16)
        for at in range(8):
            for unit in range(2):
                block_in[slot, at, pl.ds(unit * rows_in, rows_in), :] = grad_in[
                    at * rows_in : (at + 1) * rows_in, unit * HALF : (unit + 1) * HALF
                ]
        grad_out = dot_nn(grad_flip[...], hidden).astype(BF16)
        for at in range(2):
            for part in range(4):
                block_out[slot, at, part] = grad_out[part * side : (part + 1) * side, at * HALF : (at + 1) * HALF]
        for move in moves(step, slot):
            move.start()

        @pl.when(step == steps - 1)
        def _():
            for at in (steps - 2, steps - 1):
                for move in moves(at, at % 2):
                    move.wait()

        @pl.when(step == steps - 1)
        def _():
            out_ref[...] = (x2[...] + sum_out[...]).astype(BF16)
            back, gain_grad_ref[...] = norm_pull(x2[...], gain_ref[...].reshape(1, width), sum_norm[...])
            grad_x = grad.astype(F32) + back
            dx_ref[...] = grad_x
            low = grad_x.astype(BF16)
            low_ref[...] = low
            dctx_ref[...] = dot_nt(low, wo_ref[...]).astype(BF16)

    args = (residual, context, out_weight, gain_vec, feed_in, feed_out, cotangent)
    specs = [whole(a) for a in args]
    specs[4] = pl.BlockSpec((width, chunk), lambda c, _: (0, c))
    specs[5] = pl.BlockSpec((chunk, width), lambda c, _: (c, 0))
    outs = [
        struct((tok, width), BF16),
        struct((tok, width), F32),
        struct((tok, width), BF16),
        struct((tok, width), BF16),
        struct((1, width), F32),
        struct((8, 4, 2 * rows_in + side, HALF), BF16),
    ]
    out_specs = [whole(o) for o in outs]
    out_specs[5] = any_place(outs[5])
    return run_kernel(
        "feed_forward",
        body,
        place,
        args,
        specs,
        outs,
        out_specs,
        grid=(steps,),
        scratch=[
            pltpu.VMEM((tok, width), F32),
            pltpu.VMEM((tok, width), BF16),
            pltpu.VMEM((width, tok), BF16),
            pltpu.VMEM((width, tok), BF16),
            pltpu.VMEM((tok, width), F32),
            pltpu.VMEM((tok, width), F32),
            pltpu.VMEM((2, 8, 2 * rows_in, HALF), BF16),
            pltpu.VMEM((2, 2, 4, side, HALF), BF16),
            pltpu.SemaphoreType.DMA((2, 2)),
        ],
        after=after, flops=12 * tok * width * hidden_width + 4 * tok * width * width,
    )


def local_paired(
    inputs,
    encoded,
    cotangent,
    dec_seg,
    pass_doc,
    enc_mask,
    self_query,
    self_key,
    self_value,
    self_output,
    cross_query,
    cross_key,
    cross_value,
    cross_output,
    feed_in,
    feed_out,
    gain_self,
    gain_cross,
    gain_ff,
):
    inputs, encoded, cotangent = (inputs[0], encoded[0], cotangent[0])
    tok, width = inputs.shape
    enc = encoded.shape[0]
    blk, row = (lax.axis_index("blk"), lax.axis_index("rows"))
    core, chip = (blk % 2, blk // 2)
    y_at, z_low, z_high = (row % 2, (row // 2) % 2, row // 4)
    place = jnp.stack([core, chip, y_at, chip ^ core]).astype(jnp.int32)
    gains = (gain_self, gain_cross, gain_ff)
    to_core = lambda array: lax.ppermute(array, "blk", CORE_SWAP)
    to_chip = lambda array: lax.ppermute(array, "blk", CHIP_SWAP)
    in_order = lambda mine, other: jnp.where(core == 0, jnp.concatenate([mine, other]), jnp.concatenate([other, mine]))

    def swap(distance):
        return tuple((at, at ^ distance) for at in range(8))

    over_x = (chip, "blk", CHIP_SWAP)
    over_y = (y_at, "rows", swap(1))
    over_z = ((z_low, "rows", swap(2)), (z_high, "rows", swap(4)))

    gap = -tok % LANES
    spare = jnp.zeros((8 * LANES - tok - gap - enc - 1,), jnp.int32)
    labels = jnp.concatenate([dec_seg[0], spare[:gap], enc_mask[0], pass_doc[0], spare[gap:]])
    labels = jnp.concatenate([labels, jnp.zeros((8 * LANES - labels.shape[0],), jnp.int32)]).reshape(1, 8 * LANES)
    seg_c = to_core(dec_seg)
    labels_c = to_core(labels)
    inputs_c = to_core(inputs)
    inputs_x = to_chip(inputs)
    labels_x = to_chip(labels)
    encoded_c = to_core(encoded)
    h1, sq, sk, sv, near_marks, near_keys_marks, near_out, near_sum, ck0, cv0 = near_part(
        place, inputs, inputs_c, gain_self, (self_query, self_key, self_value), (dec_seg, seg_c), (encoded, encoded_c),
        (cross_key, cross_value),
    )
    inputs_x, labels_x, encoded_late, _ = lax.optimization_barrier((inputs_x, labels_x, encoded, ck0))
    labels_d = to_core(labels_x)
    inputs_d = to_core(inputs_x)
    encoded_x = to_chip(encoded_late)
    spot = place
    h1_far, fk, fv, far_keys_marks, self_out, self_sum, ctx_keep, ctx_send = far_part(
        spot, inputs_x, inputs_d, gain_self, (self_key, self_value), sq, near_marks, (labels_x, labels_d), near_out, near_sum
    )
    place = find_passages(spot, tok, enc, (labels, labels_c, labels_x, labels_d), after=(ctx_send,))
    encoded_x, _ = lax.optimization_barrier((encoded_x, self_out))
    encoded_d = to_core(encoded_x)
    x1, h2, cq, self_context, ck1, cv1, own_marks, docs0, docs1, cross_context, cross_out, cross_sum = cross_part(
        place, inputs, ctx_keep, to_core(ctx_send), self_output, gain_cross, cross_query, encoded_x, encoded_d, cross_key,
        cross_value, ck0, cv0, (labels, labels_c, labels_x, labels_d),
    )
    docs = (docs0, docs1)
    output, dx2, e2, d_cross, grad_gain_ff, spread = feed_forward(
        place, x1, cross_context, cross_output, gain_ff, feed_in, feed_out, cotangent
    )
    total_ff = lax.psum_scatter(spread.reshape(32, *spread.shape[2:]), ("rows", "blk"), scatter_dimension=0, tiled=True)
    dcq, dck, dcv, dx1, e1, grad_gain_cross, ds_keep, ds_send = cross_back(
        place, cq, (ck0, ck1), (cv0, cv1), own_marks, docs, d_cross, cross_out, cross_sum, x1, dx2, cross_query,
        gain_cross, self_output,
    )
    ds_recv = to_core(ds_send)
    passages = (encoded, encoded_c, encoded_x, encoded_d)
    keep_p, send_p = cross_grads(
        "cross_grads", place, (((cross_context,), (e2,)), ((h2,), (dcq,)), (passages, (dck,))), True
    )
    keep_q, send_q = cross_grads(
        "late_grads", place, ((passages, (dcv,)), ((self_context,), (e1,))), False, after=(keep_p,)
    )
    recv_p = to_core(send_p)
    recv_p, ds_recv, send_q = lax.optimization_barrier((recv_p, ds_recv, send_q))
    sum_p = Halving(keep_p, recv_p, (over_x, over_y))
    sum_q = Halving(keep_q, to_core(send_q), (over_y, over_x))
    held = (sum_p.step(), sum_q.step())
    dq_far, dk_far, dv_far, far_keep, far_send, gain_far = far_back(
        place, sq, fk, fv, near_marks, far_keys_marks, ds_keep, ds_recv, self_out, self_sum, gain_self, h1_far,
        (self_key, self_value), after=held,
    )
    sum_p.recv, sum_q.recv, far_send = lax.optimization_barrier((sum_p.recv, sum_q.recv, far_send))
    far_recv = to_core(far_send)
    held = (sum_p.step(), sum_q.step())
    far_keep, far_recv, *_ = lax.optimization_barrier((far_keep, far_recv, *held))
    far_here = (far_keep.astype(F32) + far_recv.astype(F32)).astype(BF16)
    from_far = to_chip(far_here)
    near_keep, near_send, keep4, send4 = near_back(
        place, sq, sk, sv, near_marks, near_keys_marks, ds_keep, ds_recv, self_out, self_sum, dq_far, gain_self, h1, h1_far,
        (self_query, self_key, self_value), (dk_far, dv_far), (gain_far, grad_gain_cross, grad_gain_ff),
        after=(far_here, *held),
    )
    tied = lax.optimization_barrier((sum_p.recv, sum_q.recv, from_far, near_send, send4))
    sum_p.recv, sum_q.recv, from_far, near_send, send4 = tied
    recv4 = to_core(send4)
    near_recv = to_core(near_send)
    sum_cross = merge_split(place, over_z[0], (sum_p, sum_q))
    sum_cross.steps = [over_z[1]]
    first_keep, first_send, second_keep, second_send = self_start(spot, keep4, recv4, after=(sum_cross.keep,))
    sum_first = Halving(first_keep, lax.ppermute(first_send, "rows", swap(1)), ((3, "blk", CHIP_SWAP),))
    sum_second = Halving(second_keep, to_chip(second_send), ((2, "rows", swap(1)),))
    input_grad = last_pull(
        place, inputs, gain_self, dx1, (near_keep, near_recv, from_far), after=(first_send, second_send)
    )
    enc_keep, enc_send = passage_grads(place, dck, dcv, cross_key, cross_value, after=(input_grad,))
    tied = lax.optimization_barrier((sum_first.recv, sum_second.recv, sum_cross.recv, enc_send))
    sum_first.recv, sum_second.recv, sum_cross.recv, enc_send = tied
    both_step(spot, sum_first, sum_second, after=(enc_keep,))
    enc_recv = to_core(enc_send)
    enc_keep, enc_recv, _ = lax.optimization_barrier((enc_keep, enc_recv, sum_first.keep))
    enc_sum = enc_keep + enc_recv.astype(F32)
    from_chip = to_chip(enc_sum[1].astype(BF16))
    held = sum_cross.step(enc_sum)
    sum_self = merge_split(place, over_z[0], (sum_first, sum_second), after=(held,))
    sum_self.steps = [over_z[1]]
    rows = width // 16
    total_ff, _ = lax.optimization_barrier((total_ff[0], sum_self.keep))
    total_ff = total_ff.astype(F32)
    grad_feed_in = jnp.concatenate([total_ff[: 2 * rows], total_ff[2 * rows : 4 * rows]], axis=1)
    feed_out_flip = total_ff[4 * rows :]
    cross_o, cross_q, cross_k, cross_v, self_o = finish_sums(
        "finish_cross", sum_cross.keep, sum_cross.recv, 5, after=(sum_self.keep, grad_feed_in, feed_out_flip)
    )
    sum_self.step(cross_o)
    enc_last, from_chip, _ = lax.optimization_barrier((enc_sum[0], from_chip, sum_self.keep))
    encoded_grad = enc_last + from_chip.astype(F32)
    self_q, self_k, self_v, *gain_grads = finish_sums(
        "finish_self", sum_self.keep, sum_self.recv, 3, 3, after=(encoded_grad,)
    )
    return (
        output[None],
        input_grad[None],
        encoded_grad[None],
        self_q,
        self_k,
        self_v,
        self_o,
        cross_q,
        cross_k,
        cross_v,
        cross_o,
        grad_feed_in,
        feed_out_flip.T,
        *gain_grads,
    )


def solution(mesh):
    paired = mesh.shape["blk"] == 4 and mesh.shape["rows"] == 8
    body = local_paired if paired else local_any
    in_specs = (
        P("rows", "blk", None),
        P("rows", "blk", None),
        P("rows", "blk", None),
        P("rows", "blk"),
        P("rows", "blk"),
        P("rows", "blk"),
        P(),
        P(),
        P(),
        P(),
        P(),
        P(),
        P(),
        P(),
        P(),
        P(),
        P(),
        P(),
        P(),
    )
    out_specs = (
        P("rows", "blk", None),
        P("rows", "blk", None),
        P("rows", "blk", None),
        P("rows", "blk"),
        P("rows", "blk"),
        P("rows", "blk"),
        P("rows", "blk"),
        P("rows", "blk"),
        P("rows", "blk"),
        P("rows", "blk"),
        P("rows", "blk"),
        P("rows", "blk"),
        P("rows", "blk"),
        P("rows"),
        P("rows"),
        P("rows"),
    )
    return jax.shard_map(body, mesh=mesh, in_specs=in_specs, out_specs=out_specs, check_vma=False)
```

```python
import jax
import jax.numpy as jnp
from jax import lax
from jax.experimental import pallas as pl
from jax.experimental.pallas import tpu as pltpu
from jax.sharding import PartitionSpec as P

HEADS = 12
HEAD_DIM = 64
PLEN = 384


NEG_FILL = -1e30
SCALE = 0.125


def split_heads(matrix):
    return matrix.reshape(matrix.shape[0], matrix.shape[1], HEADS, HEAD_DIM)


def join_heads(tensor):
    return jnp.transpose(tensor, (0, 2, 1, 3)).reshape(
        tensor.shape[0], tensor.shape[2], HEADS * HEAD_DIM
    )


def rms_norm(values, gain_vec):
    return values * lax.rsqrt(jnp.mean(values * values, axis=-1, keepdims=True) + 1e-06) * gain_vec


def norm_back(values, gain_vec, grad_out):
    _, pullback = jax.vjp(rms_norm, values, gain_vec)
    return pullback(grad_out)


def project(left, weight):
    return jnp.einsum("rqd,df->rqf", left, weight, preferred_element_type=jnp.float32)


def back_project(grad_out, weight):
    return jnp.einsum("rqf,df->rqd", grad_out, weight, preferred_element_type=jnp.float32)


def weight_grad(left, grad_out):
    return jnp.einsum("rqd,rqf->df", left, grad_out, preferred_element_type=jnp.float32)


def head_scores(queries, keys):
    return (
        jnp.einsum(
            "rqhe,rkhe->rhqk",
            split_heads(queries),
            split_heads(keys),
            preferred_element_type=jnp.float32,
        )
        * SCALE
    )


def empty_state(row_count, query_count):
    return (
        jnp.full((row_count, HEADS, query_count), NEG_FILL, jnp.float32),
        jnp.zeros((row_count, HEADS, query_count), jnp.float32),
        jnp.zeros((row_count, HEADS, query_count, HEAD_DIM), jnp.float32),
    )


def online_block(state, queries, keys, values, allowed):
    run_max, run_sum, run_acc = state
    scores = head_scores(queries, keys)
    allowed = allowed[:, None]
    new_max = jnp.maximum(run_max, jnp.max(jnp.where(allowed, scores, NEG_FILL), axis=-1))
    weights = jnp.where(allowed, jnp.exp(scores - new_max[..., None]), 0.0)
    new_sum = jnp.sum(weights, axis=-1)
    new_acc = jnp.einsum(
        "rhqk,rkhe->rhqe",
        weights.astype(jnp.bfloat16),
        split_heads(values),
        preferred_element_type=jnp.float32,
    )
    return (new_max, new_sum, new_acc)


def finish(state):
    run_max, run_sum, run_acc = state
    return (run_acc / run_sum[..., None], run_max + jnp.log(run_sum))


def grad_pair(queries, grad_ctx, log_sum, delta, keys, values, allowed):
    scores = head_scores(queries, keys)
    probs_now = jnp.where(allowed[:, None], jnp.exp(scores - log_sum[..., None]), 0.0)
    grad_probs = jnp.einsum(
        "rqhe,rkhe->rhqk",
        split_heads(grad_ctx),
        split_heads(values),
        preferred_element_type=jnp.float32,
    )
    grad_scores = (probs_now * (grad_probs - delta[..., None])).astype(jnp.bfloat16)
    grad_query = (
        jnp.einsum(
            "rhqk,rkhe->rqhe", grad_scores, split_heads(keys), preferred_element_type=jnp.float32
        )
        * SCALE
    )
    grad_key = (
        jnp.einsum(
            "rhqk,rqhe->rkhe", grad_scores, split_heads(queries), preferred_element_type=jnp.float32
        )
        * SCALE
    )
    grad_value = jnp.einsum(
        "rhqk,rqhe->rkhe",
        probs_now.astype(jnp.bfloat16),
        split_heads(grad_ctx),
        preferred_element_type=jnp.float32,
    )
    row_count = keys.shape[0]
    key_count = keys.shape[1]
    joined = jnp.concatenate(
        (grad_key.reshape(row_count, key_count, -1), grad_value.reshape(row_count, key_count, -1)),
        axis=-1,
    )
    return (grad_query.reshape(row_count, queries.shape[1], -1), joined)


def head_delta(grad_ctx, attended):
    return jnp.einsum("rqhe,rhqe->rhq", split_heads(grad_ctx).astype(jnp.float32), attended)


def spread_matrix(matrix, row_split, block_count):
    first, second = matrix.shape
    tiles = matrix.reshape(row_split, first // row_split, block_count, second // block_count)
    return jnp.transpose(tiles, (0, 2, 1, 3)).reshape(
        row_split * block_count, first // row_split, second // block_count
    )


def spread_gain(vector, row_split, block_count):
    tiles = vector.reshape(row_split, 1, vector.shape[0] // row_split)
    return jnp.broadcast_to(tiles, (row_split, block_count, vector.shape[0] // row_split)).reshape(
        row_split * block_count, vector.shape[0] // row_split
    )


def local_any(
    inputs,
    encoded,
    cotangent,
    dec_seg,
    pass_doc,
    enc_mask,
    self_query,
    self_key,
    self_value,
    self_output,
    cross_query,
    cross_key,
    cross_value,
    cross_output,
    feed_in,
    feed_out,
    gain_self,
    gain_cross,
    gain_ff,
):
    row_count, tok_shard, width = inputs.shape
    enc_shard = encoded.shape[1]
    block_count = lax.axis_size("blk")
    row_split = lax.axis_size("rows")
    block_ids = jnp.arange(block_count)
    query_places = lax.axis_index("blk") * tok_shard + jnp.arange(tok_shard)
    start_state = empty_state(row_count, tok_shard)
    residual = inputs.astype(jnp.float32)
    normed_self = rms_norm(residual, gain_self).astype(jnp.bfloat16)
    self_queries = project(normed_self, self_query).astype(jnp.bfloat16)
    self_keys = project(normed_self, self_key).astype(jnp.bfloat16)
    self_values = project(normed_self, self_value).astype(jnp.bfloat16)
    piece_keys = lax.all_gather(self_keys, "blk", axis=1, tiled=True)
    piece_values = lax.all_gather(self_values, "blk", axis=1, tiled=True)
    piece_segs = lax.all_gather(dec_seg, "blk", axis=1, tiled=True)
    key_places = jnp.arange(piece_keys.shape[1])
    allowed = (dec_seg[:, :, None] == piece_segs[:, None, :]) & (
        key_places[None, None, :] <= query_places[None, :, None]
    )
    self_attn, self_lse = finish(
        online_block(start_state, self_queries, piece_keys, piece_values, allowed)
    )
    self_context = join_heads(self_attn).astype(jnp.bfloat16)
    after_self = residual + project(self_context, self_output)
    normed_cross = rms_norm(after_self, gain_cross).astype(jnp.bfloat16)
    cross_queries = project(normed_cross, cross_query).astype(jnp.bfloat16)
    cross_keys = project(encoded, cross_key).astype(jnp.bfloat16)
    cross_values = project(encoded, cross_value).astype(jnp.bfloat16)
    key_docs = jnp.where(enc_mask == 1, jnp.repeat(pass_doc, PLEN, axis=1), -1)
    piece_keys = lax.all_gather(cross_keys, "blk", axis=1, tiled=True)
    piece_values = lax.all_gather(cross_values, "blk", axis=1, tiled=True)
    piece_docs = lax.all_gather(key_docs, "blk", axis=1, tiled=True)
    allowed = dec_seg[:, :, None] == piece_docs[:, None, :]
    cross_attn, cross_lse = finish(
        online_block(start_state, cross_queries, piece_keys, piece_values, allowed)
    )
    cross_context = join_heads(cross_attn).astype(jnp.bfloat16)
    after_cross = after_self + project(cross_context, cross_output)
    normed_ff = rms_norm(after_cross, gain_ff).astype(jnp.bfloat16)
    before_act = project(normed_ff, feed_in)
    hidden = jax.nn.gelu(before_act).astype(jnp.bfloat16)
    output = (after_cross + project(hidden, feed_out)).astype(jnp.bfloat16)
    grad_feed_out = weight_grad(hidden, cotangent)
    grad_hidden = back_project(cotangent, feed_out)
    _, gelu_back = jax.vjp(jax.nn.gelu, before_act)
    grad_before = gelu_back(grad_hidden)[0].astype(jnp.bfloat16)
    grad_feed_in = weight_grad(normed_ff, grad_before)
    grad_cross_res, grad_gain_ff = norm_back(
        after_cross, gain_ff, back_project(grad_before, feed_in)
    )
    grad_cross_res = cotangent.astype(jnp.float32) + grad_cross_res
    cross_branch = grad_cross_res.astype(jnp.bfloat16)
    grad_cross_output = weight_grad(cross_context, cross_branch)
    grad_cross_ctx = back_project(cross_branch, cross_output).astype(jnp.bfloat16)
    cross_delta = head_delta(grad_cross_ctx, cross_attn)
    all_keys, all_values, all_docs = (
        lax.all_gather(cross_keys, "blk", axis=1, tiled=True),
        lax.all_gather(cross_values, "blk", axis=1, tiled=True),
        lax.all_gather(key_docs, "blk", axis=1, tiled=True),
    )

    def passage_step(running, block_index):
        offset = block_index * enc_shard
        piece_keys = lax.dynamic_slice_in_dim(all_keys, offset, enc_shard, 1)
        piece_values = lax.dynamic_slice_in_dim(all_values, offset, enc_shard, 1)
        piece_docs = lax.dynamic_slice_in_dim(all_docs, offset, enc_shard, 1)
        allowed = dec_seg[:, :, None] == piece_docs[:, None, :]
        grad_query, grad_kv = grad_pair(
            cross_queries, grad_cross_ctx, cross_lse, cross_delta, piece_keys, piece_values, allowed
        )
        return (running + grad_query, grad_kv)

    grad_cross_q, key_terms = lax.scan(
        passage_step, jnp.zeros((row_count, tok_shard, width), jnp.float32), block_ids
    )
    grad_cross_kv = lax.psum_scatter(
        key_terms.astype(jnp.bfloat16), "blk", scatter_dimension=0, tiled=True
    ).astype(jnp.float32)[0]
    low_cross_q = grad_cross_q.astype(jnp.bfloat16)
    low_cross_k = grad_cross_kv[..., :width].astype(jnp.bfloat16)
    low_cross_v = grad_cross_kv[..., width:].astype(jnp.bfloat16)
    grad_cross_query = weight_grad(normed_cross, low_cross_q)
    grad_cross_key = weight_grad(encoded, low_cross_k)
    grad_cross_value = weight_grad(encoded, low_cross_v)
    encoded_grad = back_project(low_cross_k, cross_key) + back_project(low_cross_v, cross_value)
    grad_self_res, grad_gain_cross = norm_back(
        after_self, gain_cross, back_project(low_cross_q, cross_query)
    )
    grad_self_res = grad_cross_res + grad_self_res
    self_branch = grad_self_res.astype(jnp.bfloat16)
    grad_self_output = weight_grad(self_context, self_branch)
    grad_self_ctx = back_project(self_branch, self_output).astype(jnp.bfloat16)
    self_delta = head_delta(grad_self_ctx, self_attn)
    all_self_keys, all_self_values, all_self_segs = (
        lax.all_gather(self_keys, "blk", axis=1, tiled=True),
        lax.all_gather(self_values, "blk", axis=1, tiled=True),
        lax.all_gather(dec_seg, "blk", axis=1, tiled=True),
    )

    def self_step(running, block_index):
        offset = block_index * tok_shard
        piece_keys = lax.dynamic_slice_in_dim(all_self_keys, offset, tok_shard, 1)
        piece_values = lax.dynamic_slice_in_dim(all_self_values, offset, tok_shard, 1)
        piece_segs = lax.dynamic_slice_in_dim(all_self_segs, offset, tok_shard, 1)
        key_places = offset + jnp.arange(tok_shard)
        allowed = (dec_seg[:, :, None] == piece_segs[:, None, :]) & (
            key_places[None, None, :] <= query_places[None, :, None]
        )
        grad_query, grad_kv = grad_pair(
            self_queries, grad_self_ctx, self_lse, self_delta, piece_keys, piece_values, allowed
        )
        return (running + grad_query, grad_kv)

    grad_self_q, self_terms = lax.scan(
        self_step, jnp.zeros((row_count, tok_shard, width), jnp.float32), block_ids
    )
    grad_self_kv = lax.psum_scatter(
        self_terms.astype(jnp.bfloat16), "blk", scatter_dimension=0, tiled=True
    ).astype(jnp.float32)[0]
    low_self_q = grad_self_q.astype(jnp.bfloat16)
    low_self_k = grad_self_kv[..., :width].astype(jnp.bfloat16)
    low_self_v = grad_self_kv[..., width:].astype(jnp.bfloat16)
    grad_self_query = weight_grad(normed_self, low_self_q)
    grad_self_key = weight_grad(normed_self, low_self_k)
    grad_self_value = weight_grad(normed_self, low_self_v)
    grad_normed = (
        back_project(low_self_q, self_query)
        + back_project(low_self_k, self_key)
        + back_project(low_self_v, self_value)
    )
    grad_first, grad_gain_self = norm_back(residual, gain_self, grad_normed)
    input_grad = grad_self_res + grad_first
    matrices = (
        grad_self_query,
        grad_self_key,
        grad_self_value,
        grad_self_output,
        grad_cross_query,
        grad_cross_key,
        grad_cross_value,
        grad_cross_output,
        grad_feed_in,
        grad_feed_out,
    )
    spread_mats = tuple((spread_matrix(matrix, row_split, block_count) for matrix in matrices))
    spread_gains = tuple(
        (
            spread_gain(vector, row_split, block_count)
            for vector in (grad_gain_self, grad_gain_cross, grad_gain_ff)
        )
    )
    summed = (
        lax.psum_scatter(spread_mats[0], ("rows", "blk"), scatter_dimension=0, tiled=True),
        lax.psum_scatter(spread_mats[1], ("rows", "blk"), scatter_dimension=0, tiled=True),
        lax.psum_scatter(spread_mats[2], ("rows", "blk"), scatter_dimension=0, tiled=True),
        lax.psum_scatter(spread_mats[3], ("rows", "blk"), scatter_dimension=0, tiled=True),
        lax.psum_scatter(spread_mats[4], ("rows", "blk"), scatter_dimension=0, tiled=True),
        lax.psum_scatter(spread_mats[5], ("rows", "blk"), scatter_dimension=0, tiled=True),
        lax.psum_scatter(spread_mats[6], ("rows", "blk"), scatter_dimension=0, tiled=True),
        lax.psum_scatter(spread_mats[7], ("rows", "blk"), scatter_dimension=0, tiled=True),
        lax.psum_scatter(spread_mats[8], ("rows", "blk"), scatter_dimension=0, tiled=True),
        lax.psum_scatter(spread_mats[9], ("rows", "blk"), scatter_dimension=0, tiled=True),
        lax.psum_scatter(spread_gains[0], ("rows", "blk"), scatter_dimension=0, tiled=True),
        lax.psum_scatter(spread_gains[1], ("rows", "blk"), scatter_dimension=0, tiled=True),
        lax.psum_scatter(spread_gains[2], ("rows", "blk"), scatter_dimension=0, tiled=True),
    )
    return (
        output,
        input_grad,
        encoded_grad,
        summed[0][0],
        summed[1][0],
        summed[2][0],
        summed[3][0],
        summed[4][0],
        summed[5][0],
        summed[6][0],
        summed[7][0],
        summed[8][0],
        summed[9][0],
        summed[10][0],
        summed[11][0],
        summed[12][0],
    )


BF16 = jnp.bfloat16
F32 = jnp.float32
LANES = 128
HALF = 2 * LANES + LANES
CORE_SWAP = ((0, 1), (1, 0), (2, 3), (3, 2))
CHIP_SWAP = ((0, 2), (2, 0), (1, 3), (3, 1))


def dot_nn(left, right):
    return jnp.dot(left, right, preferred_element_type=F32)


def dot_nt(left, right):
    return lax.dot_general(left, right, (((1,), (1,)), ((), ())), preferred_element_type=F32)


def dot_tn(left, right):
    return lax.dot_general(left, right, (((0,), (0,)), ((), ())), preferred_element_type=F32)


def whole(array):
    rank = len(array.shape)
    return pl.BlockSpec(array.shape, lambda *_: (0,) * rank)


def struct(shape, dtype):
    return jax.ShapeDtypeStruct(shape, dtype)


def run_kernel(name, body, scalars, args, in_specs, outs, out_specs, grid=(1,), scratch=(), flops=0, after=(), vmem=58):
    moved = sum(a.size * a.dtype.itemsize for a in args)
    if after:
        inner, given = (body, len(args))

        def body(s, *refs):
            inner(s, *refs[:given], *refs[given + len(after) :])

        args = (*args, *after)
        in_specs = [*in_specs, *([pl.BlockSpec(memory_space=pl.ANY)] * len(after))]
    moved += sum(o.size * o.dtype.itemsize for o in outs)
    return pl.pallas_call(
        body,
        grid_spec=pltpu.PrefetchScalarGridSpec(
            num_scalar_prefetch=1,
            grid=grid,
            in_specs=list(in_specs),
            out_specs=list(out_specs),
            scratch_shapes=list(scratch),
        ),
        out_shape=list(outs),
        compiler_params=pltpu.CompilerParams(vmem_limit_bytes=vmem << 20),
        name=name,
    )(scalars, *args)


def unit_norm(values):
    scale = lax.rsqrt(jnp.mean(values * values, axis=-1, keepdims=True) + 1e-06)
    return (values * scale, scale)


def norm_pull(values, gain_vec, grad_out):
    normal, scale = unit_norm(values)
    scaled = grad_out * gain_vec
    inner = jnp.mean(scaled * normal, axis=-1, keepdims=True)
    return (scale * (scaled - normal * inner), jnp.sum(grad_out * normal, axis=0, keepdims=True))


def head_lanes():
    lane = lax.broadcasted_iota(jnp.int32, (1, LANES), 1)
    return (lane, (lane < HEAD_DIM, lane >= HEAD_DIM))


def only(keep, values):
    return jnp.where(keep, values, jnp.zeros_like(values))


def soft_block(queries, marks, keys, values):
    lane, masks = head_lanes()
    attended, sums = ([], [])
    for keep in masks:
        scores = dot_nt(jnp.concatenate([only(keep, queries), marks], axis=1), keys)
        top = jnp.max(scores, axis=1, keepdims=True)
        weights = jnp.exp(scores - top)
        total = jnp.sum(weights, axis=1, keepdims=True)
        attended.append(dot_nn(weights.astype(BF16), values) / total)
        sums.append(top + jnp.log(total))
    return (jnp.where(masks[0], *attended), jnp.where(masks[0], *sums))


def causal_block(queries, marks, keys, values):
    lane, masks = head_lanes()
    rows, cols = queries.shape[0], keys.shape[0]
    flipped = values.T
    attended, sums = ([], [])
    for at, keep in enumerate(masks):
        scores = dot_nt(keys, jnp.concatenate([only(keep, queries), marks], axis=1))
        at_row = lax.broadcasted_iota(jnp.int32, (rows, rows), 0)
        at_col = lax.broadcasted_iota(jnp.int32, (rows, rows), 1)
        last = jnp.where(at_row <= at_col, scores[cols - rows :, :], NEG_FILL)
        scores = last if cols == rows else jnp.concatenate([scores[: cols - rows, :], last], axis=0)
        top = jnp.max(scores, axis=0, keepdims=True)
        weights = jnp.exp(scores - top)
        total = jnp.sum(weights, axis=0, keepdims=True)
        head = flipped[at * HEAD_DIM : (at + 1) * HEAD_DIM, :]
        attended.append(dot_nn(head, weights.astype(BF16)) / total)
        sums.append(jnp.broadcast_to(top + jnp.log(total), (HEAD_DIM, rows)))
    return (jnp.concatenate(attended, axis=0).T, jnp.concatenate(sums, axis=0).T)


def three_parts(spread):
    high = spread.astype(BF16)
    rest = spread - high.astype(F32)
    middle = rest.astype(BF16)
    return (-high, -middle, -(rest - middle.astype(F32)).astype(BF16))


def put_parts(lane, head, parts, base):
    for at, part in enumerate(parts):
        base = jnp.where(lane == head * HEAD_DIM + 3 + at, part, base)
    return base


def ones_lanes(lane):
    place = lane % HEAD_DIM
    return (place >= 3) & (place < 6)


def head_totals(product):
    high = product.astype(BF16)
    low = (product - high.astype(F32)).astype(BF16)
    at_row = lax.broadcasted_iota(jnp.int32, (2 * LANES, LANES), 0) % LANES
    at_col = lax.broadcasted_iota(jnp.int32, (2 * LANES, LANES), 1)
    same = jnp.where((at_row < HEAD_DIM) == (at_col < HEAD_DIM), 1.0, 0.0).astype(BF16)
    return dot_nn(jnp.concatenate([high, low], axis=1), same)


def pull_block(queries, marks, keys, key_marks, values, grads, attended, sums, causal):
    lane, masks = head_lanes()
    rows, cols = queries.shape[0], keys.shape[0]
    wide_keys = jnp.concatenate([keys, key_marks], axis=1)
    ones = jnp.where(ones_lanes(lane), 1.0, 0.0).astype(BF16)
    wide_values = jnp.concatenate([values, jnp.broadcast_to(ones, (cols, LANES))], axis=1)
    delta_parts = three_parts(head_totals(grads.astype(F32) * attended))
    sum_parts = three_parts(sums)
    flipped = keys.T
    grad_queries = []
    grad_keys = grad_values = None
    for at, keep in enumerate(masks):
        query, grad = (only(keep, queries), only(keep, grads))
        wide_query = jnp.concatenate([query, put_parts(lane, at, sum_parts, marks)], axis=1)
        wide_grad = jnp.concatenate([grad, put_parts(lane, at, delta_parts, jnp.zeros_like(marks))], axis=1)
        probs = jnp.exp(dot_nt(wide_keys, wide_query))
        if causal:
            at_row = lax.broadcasted_iota(jnp.int32, (rows, rows), 0)
            at_col = lax.broadcasted_iota(jnp.int32, (rows, rows), 1)
            last = jnp.where(at_row <= at_col, probs[cols - rows :, :], 0.0)
            probs = last if cols == rows else jnp.concatenate([probs[: cols - rows, :], last], axis=0)
        grad_scores = (probs * dot_nt(wide_values, wide_grad)).astype(BF16)
        grad_queries.append(dot_nn(flipped, grad_scores))
        key_part = dot_nn(grad_scores, query)
        value_part = dot_nn(probs.astype(BF16), grad)
        grad_keys = key_part if at == 0 else grad_keys + key_part
        grad_values = value_part if at == 0 else grad_values + value_part
    sub = lax.broadcasted_iota(jnp.int32, (LANES, 1), 0)
    return (jnp.where(sub < HEAD_DIM, *grad_queries).T * SCALE, grad_keys, grad_values)


def pair_columns(array, group=0):
    first = group * (HALF // LANES)
    return pl.BlockSpec((array.shape[0], LANES), lambda p, _: (0, p + first))


def query_marks(labels):
    lane = lax.broadcasted_iota(jnp.int32, (LANES, 1), 0)
    return jnp.where(labels == lane, 1.0, 0.0).T.astype(BF16)


def key_marks(labels):
    lane = lax.broadcasted_iota(jnp.int32, (LANES, 1), 0)
    closed = jnp.where(labels != lane, NEG_FILL, 0.0)
    return jnp.where(lane < 3, closed, jnp.where(ones_lanes(lane), 1.0, 0.0)).T.astype(BF16)


def doc_marks(label_ref, tok, enc):
    first = -(-tok // LANES) * LANES
    doc = label_ref[:, pl.ds(first + enc, LANES)][:, 0:1]
    return key_marks(jnp.where(label_ref[:, pl.ds(first, enc)] == 1, doc, -1))


def pair_lanes(group=0):
    return pl.ds(pl.multiple_of(pl.program_id(0) * LANES + group * HALF, LANES), LANES)


def side_by_side(s, sources, target):
    columns = pl.ds(pl.multiple_of(s[0] * HALF, LANES), HALF)
    return (
        [source.at[:, columns] for source in sources],
        [target.at[:, pl.ds(at * HALF, HALF)] for at in range(len(sources))],
    )


def column_block(array):
    return pl.BlockSpec((array.shape[0], HALF), lambda _, s: (0, s[0]))


def any_place(_):
    return pl.BlockSpec(memory_space=pl.ANY)


def copies(sources, targets, semaphores):
    return [pltpu.make_async_copy(src, dst, semaphores.at[at]) for at, (src, dst) in enumerate(zip(sources, targets))]


def find_passages(place, tok, enc, labels, after=()):
    spot = -(-tok // LANES) * LANES + enc

    def body(s, own_ref, *refs):
        label_refs, out_ref = refs[:4], refs[4]
        own = own_ref[:, pl.ds(0, tok)]
        used = [jnp.max(jnp.where(own == ref[0, spot], 1, 0)) for ref in label_refs]
        total = used[0] + used[1] + used[2] + used[3]
        out_ref[0] = s[0]
        out_ref[1] = s[1]
        out_ref[6] = total
        out_ref[7] = 0
        ahead, behind = (jnp.int32(0), total)
        for slot in range(4):
            out_ref[2 + jnp.where(used[slot] == 1, ahead, behind)] = jnp.int32(slot)
            ahead, behind = (ahead + used[slot], behind + 1 - used[slot])

    smem = pl.BlockSpec(memory_space=pltpu.SMEM)
    return run_kernel(
        "find_passages", body, place, (labels[0], *labels), [whole(labels[0])] + [smem] * 4, [struct((8,), jnp.int32)],
        [smem], after=after,
    )[0]


def write_projections(s, mine_ref, other_ref, gain, weight_refs, normed_ref, out_ref, scaled):
    tok = mine_ref.shape[0]
    parts = ((mine_ref, s[0]), (other_ref, 1 - s[0]))
    for source, part in parts:
        rows = pl.ds(pl.multiple_of(part * tok, tok), tok)
        normed_ref[rows, :] = (unit_norm(source[...].astype(F32))[0] * gain).astype(BF16)
    weight = jnp.concatenate([ref[...] for ref in weight_refs], axis=1)
    for _, part in parts:
        rows = pl.ds(pl.multiple_of(part * tok, tok), tok)
        result = dot_nn(normed_ref[rows, :], weight)
        if scaled:
            out_ref[rows, pl.ds(0, scaled)] = (result[:, :scaled] * SCALE).astype(BF16)
        out_ref[rows, pl.ds(scaled, result.shape[1] - scaled)] = result[:, scaled:].astype(BF16)


def near_part(place, mine, other, gain_vec, weights, labels, passages, passage_weights, after=()):
    tok, width = mine.shape
    both = 2 * tok
    enc = passages[0].shape[0]
    third = width // 3

    def body(
        s, mine_ref, other_ref, gain_ref, wq_ref, wk_ref, wv_ref, own_ref, core_ref, e0_ref, e1_ref, ck_ref, cv_ref,
        h_ref, qkv_ref, m_ref, km_ref, out_ref, sum_ref, pk_ref, pv_ref,
    ):
        @pl.when(pl.program_id(0) == 0)
        def _():
            for source, part in ((own_ref, s[0]), (core_ref, 1 - s[0])):
                rows = pl.ds(pl.multiple_of(part * tok, tok), tok)
                m_ref[rows, :] = query_marks(source[:, pl.ds(0, tok)])
                km_ref[rows, :] = key_marks(source[:, pl.ds(0, tok)])
            write_projections(
                s, mine_ref, other_ref, gain_ref[...].reshape(1, width), (wq_ref, wk_ref, wv_ref), h_ref, qkv_ref, HALF
            )

        query_pair, key_pair, value_pair = (pair_lanes(group) for group in range(3))
        for at in (0, 1):
            rows, seen = (pl.ds(at * tok, tok), pl.ds(0, (at + 1) * tok))
            wide = jnp.concatenate([qkv_ref[seen, key_pair], km_ref[seen, :]], axis=1)
            out_ref[rows, :], sum_ref[rows, :] = causal_block(
                qkv_ref[rows, query_pair], m_ref[rows, :], wide, qkv_ref[seen, value_pair]
            )
        for at, source in enumerate((e0_ref, e1_ref)):
            rows = pl.ds(at * enc, enc)
            pk_ref[rows, :] = dot_nn(source[...], ck_ref[...]).astype(BF16)
            pv_ref[rows, :] = dot_nn(source[...], cv_ref[...]).astype(BF16)

    args = (mine, other, gain_vec, *weights, *labels, *passages, *passage_weights)
    specs = [whole(a) for a in args]
    specs[3:6] = [column_block(w) for w in weights]
    specs[10:12] = [pl.BlockSpec((width, third), lambda p, _: (0, p))] * 2
    outs = [struct((both, width), BF16), struct((both, 3 * HALF), BF16)] + [struct((both, LANES), BF16)] * 2
    outs += [struct((both, HALF), F32)] * 2 + [struct((2 * enc, width), BF16)] * 2
    return run_kernel(
        "near_part", body, place, args, specs, outs,
        [whole(o) for o in outs[:4]]
        + [pair_columns(o) for o in outs[4:6]]
        + [pl.BlockSpec((2 * enc, third), lambda p, _: (0, p))] * 2,
        grid=(HALF // LANES,), after=after, flops=both * both * 6 * 2 * HALF,
    )


def far_part(place, mine, other, gain_vec, weights, queries, marks, labels, near_out, near_sum, after=()):
    tok, width = mine.shape
    both = 2 * tok

    def body(
        s, mine_ref, other_ref, gain_ref, wk_ref, wv_ref, q_ref, m_ref, lx_ref, ld_ref, no_ref, ns_ref,
        h_ref, kv_ref, km_ref, out_ref, sum_ref, keep_ref, send_ref,
    ):
        @pl.when(pl.program_id(0) == 0)
        def _():
            for source, part in ((lx_ref, s[0]), (ld_ref, 1 - s[0])):
                rows = pl.ds(pl.multiple_of(part * tok, tok), tok)
                km_ref[rows, :] = key_marks(source[:, pl.ds(0, tok)])

        def write(at, out, log_sum):
            rows = pl.ds(at * tok, tok)
            out_ref[rows, :] = out
            sum_ref[rows, :] = log_sum

            @pl.when(s[0] == at)
            def _():
                keep_ref[...] = out.astype(BF16)

            @pl.when(s[0] != at)
            def _():
                send_ref[...] = out.astype(BF16)

        @pl.when(s[1] == 0)
        def _():
            for at in (0, 1):
                rows = pl.ds(at * tok, tok)
                write(at, no_ref[rows, :], ns_ref[rows, :])

            @pl.when(pl.program_id(0) == 0)
            def _():
                for ref in (h_ref, kv_ref):
                    ref[...] = jnp.zeros_like(ref)

        @pl.when(s[1] != 0)
        def _():
            @pl.when(pl.program_id(0) == 0)
            def _():
                write_projections(
                    s, mine_ref, other_ref, gain_ref[...].reshape(1, width), (wk_ref, wv_ref), h_ref, kv_ref, 0
                )

            wide = jnp.concatenate([kv_ref[:, pair_lanes()], km_ref[...]], axis=1)
            for at in (0, 1):
                rows = pl.ds(at * tok, tok)
                out, log_sum = soft_block(q_ref[rows, :], m_ref[rows, :], wide, kv_ref[:, pair_lanes(1)])
                near_log = ns_ref[rows, :]
                top = jnp.maximum(near_log, log_sum)
                near_share, far_share = (jnp.exp(near_log - top), jnp.exp(log_sum - top))
                total = near_share + far_share
                write(at, (no_ref[rows, :] * near_share + out * far_share) / total, top + jnp.log(total))

    args = (mine, other, gain_vec, *weights, queries, marks, *labels, near_out, near_sum)
    specs = [whole(a) for a in args]
    specs[3:5] = [column_block(w) for w in weights]
    for at in (5, 9, 10):
        specs[at] = pair_columns(args[at])
    outs = [struct((both, width), BF16), struct((both, 2 * HALF), BF16), struct((both, LANES), BF16)]
    outs += [struct((both, HALF), F32)] * 2 + [struct((tok, HALF), BF16)] * 2
    return run_kernel(
        "far_part", body, place, args, specs, outs, [whole(o) for o in outs[:3]] + [pair_columns(o) for o in outs[3:]],
        grid=(HALF // LANES,), after=after, flops=both * both * 8 * 2 * HALF,
    )


def gather_slots(s, enc, target, first_ref, second_ref, lanes=slice(None)):
    for at in range(4):
        slot = s[2 + at]
        rows = pl.ds(at * enc, enc)

        @pl.when(slot < 2)
        def _():
            target[rows, :] = first_ref[pl.ds(pl.multiple_of(slot * enc, enc), enc), :]

        @pl.when(slot >= 2)
        def _():
            target[rows, :] = second_ref[pl.ds(pl.multiple_of((slot - 2) * enc, enc), enc), lanes]


def by_count(s, work):
    pl.when(s[6] <= 2)(lambda: work(2))
    pl.when(s[6] >= 3)(lambda: work(3))


def cross_part(
    place, inputs, ctx_keep, ctx_recv, out_weight, gain_vec, query_weight, first, second, key_weight, value_weight,
    keys, values, labels, after=(),
):
    tok, width = inputs.shape
    enc = first.shape[0]

    def body(
        s, in_ref, keep_ref, recv_ref, wa_ref, wb_ref, gain_ref, wq_any, first_any, second_any, wk_any, wv_any, k0_ref, v0_ref,
        l0_ref, l1_ref, l2_ref, l3_ref,
        x_ref, h_ref, q_ref, ctx_ref, k1_ref, v1_ref, m_ref, km0_ref, km1_ref, cctx_ref, out_ref, sum_ref,
        all_k, all_v, wq_ref, first_ref, second_ref, wk_ref, wv_ref, semaphores,
    ):
        keep = pl.ds(0, LANES)

        @pl.when(pl.program_id(0) == 0)
        def _():
            later = copies(
                (wq_any, first_any, wk_any, wv_any, second_any), (wq_ref, first_ref, wk_ref, wv_ref, second_ref), semaphores
            )
            for copy in later:
                copy.start()
            total = dot_nn(keep_ref[...], wa_ref[...]) + dot_nn(recv_ref[...], wb_ref[...])
            residual = in_ref[...].astype(F32) + total
            x_ref[...] = residual
            normed = (unit_norm(residual)[0] * gain_ref[...].reshape(1, width)).astype(BF16)
            h_ref[...] = normed
            later[0].wait()
            q_ref[...] = (dot_nn(normed, wq_ref[...]) * SCALE).astype(BF16)
            ctx_ref[:, pl.ds(pl.multiple_of(s[0] * HALF, LANES), HALF)] = keep_ref[...]
            ctx_ref[:, pl.ds(pl.multiple_of((1 - s[0]) * HALF, LANES), HALF)] = recv_ref[...]
            for copy in later[1:]:
                copy.wait()
            for at, source in enumerate((first_ref, second_ref)):
                rows = pl.ds(at * enc, enc)
                k1_ref[rows, :] = dot_nn(source[...], wk_ref[...]).astype(BF16)
                v1_ref[rows, :] = dot_nn(source[...], wv_ref[...]).astype(BF16)
            m_ref[...] = query_marks(l0_ref[:, pl.ds(0, tok)])
            for target, low, high in ((km0_ref, l0_ref, l1_ref), (km1_ref, l2_ref, l3_ref)):
                target[pl.ds(0, enc), :] = doc_marks(low, tok, enc)
                target[pl.ds(enc, enc), :] = doc_marks(high, tok, enc)
            gather_slots(s, enc, all_k.at[:, pl.ds(LANES, LANES)], km0_ref, km1_ref)

        pair = pair_lanes()
        gather_slots(s, enc, all_k.at[:, keep], k0_ref, k1_ref, pair)
        gather_slots(s, enc, all_v, v0_ref, v1_ref, pair)

        def work(count):
            seen = pl.ds(0, count * enc)
            out, log_sum = soft_block(q_ref[:, pair], m_ref[...], all_k[seen, :], all_v[seen, :])
            cctx_ref[...] = out.astype(BF16)
            out_ref[...] = out
            sum_ref[...] = log_sum

        by_count(s, work)

    args = (
        inputs, ctx_keep, ctx_recv, out_weight, out_weight, gain_vec, query_weight, first, second, key_weight, value_weight,
        keys, values, *labels,
    )
    specs = [whole(a) for a in args]
    specs[3] = pl.BlockSpec((HALF, width), lambda _, s: (s[0], 0))
    specs[4] = pl.BlockSpec((HALF, width), lambda _, s: (1 - s[0], 0))
    specs[6:11] = [any_place(a) for a in args[6:11]]
    specs[11], specs[12] = pair_columns(keys), pair_columns(values)
    outs = [struct((tok, width), F32)] + [struct((tok, width), BF16)] * 3 + [struct((2 * enc, width), BF16)] * 2
    outs += [struct((tok, LANES), BF16)] + [struct((2 * enc, LANES), BF16)] * 2
    outs += [struct((tok, width), BF16)] + [struct((tok, width), F32)] * 2
    return run_kernel(
        "cross_part", body, place, args, specs, outs, [whole(o) for o in outs[:9]] + [pair_columns(o) for o in outs[9:]],
        grid=(width // LANES,),
        scratch=[pltpu.VMEM((4 * enc, 2 * LANES), BF16), pltpu.VMEM((4 * enc, LANES), BF16)]
        + [pltpu.VMEM(a.shape, a.dtype) for a in args[6:11]]
        + [pltpu.SemaphoreType.DMA((5,))],
        after=after, flops=tok * 2.5 * enc * 8 * 2 * width + 12 * tok * width * width,
    )


def cross_back(place, queries, keys, values, marks, key_marks, grads, attended, sums, residual, grad_res, query_weight, gains, out_weight, after=()):
    tok, width = queries.shape
    enc = keys[0].shape[0] // 2
    last = width // LANES - 1

    def body(
        s, q_ref, k0_ref, k1_ref, v0_ref, v1_ref, m_ref, km0_ref, km1_ref, g_ref, at_ref, ls_ref, gain_ref,
        x_any, dx_any, wq_any, wo_any, dq_ref, dk_ref, dv_ref, dx1_ref, low_ref, gain_grad_ref, keep_ref, send_ref,
        all_k, all_v, all_m, x_ref, dx_ref, wq_ref, wo_ref, semaphores,
    ):
        later = copies((x_any, dx_any, wq_any, wo_any), (x_ref, dx_ref, wq_ref, wo_ref), semaphores)

        @pl.when(pl.program_id(0) == 0)
        def _():
            for copy in later:
                copy.start()
            gather_slots(s, enc, all_m, km0_ref, km1_ref)

        gather_slots(s, enc, all_k, k0_ref, k1_ref)
        gather_slots(s, enc, all_v, v0_ref, v1_ref)
        pair = pair_lanes()

        def work(count):
            seen = pl.ds(0, count * enc)
            grad_q, grad_k, grad_v = pull_block(
                q_ref[...], m_ref[...], all_k[seen, :], all_m[seen, :], all_v[seen, :], g_ref[...], at_ref[...],
                ls_ref[...], False,
            )
            dq_ref[:, pair] = grad_q.astype(BF16)
            low_k, low_v = (grad_k.astype(BF16), grad_v.astype(BF16))
            for at in range(4):
                rows = pl.ds(pl.multiple_of(s[2 + at] * enc, enc), enc)
                if at < count:
                    dk_ref[rows, :] = low_k[at * enc : (at + 1) * enc, :]
                    dv_ref[rows, :] = low_v[at * enc : (at + 1) * enc, :]
                else:
                    dk_ref[rows, :] = jnp.zeros((enc, LANES), BF16)
                    dv_ref[rows, :] = jnp.zeros((enc, LANES), BF16)

        by_count(s, work)

        @pl.when(pl.program_id(0) == last)
        def _():
            for copy in later:
                copy.wait()
            back, gain_grad_ref[...] = norm_pull(x_ref[...], gain_ref[...].reshape(1, width), dot_nt(dq_ref[...], wq_ref[...]))
            grad_x = dx_ref[...] + back
            dx1_ref[...] = grad_x
            low = grad_x.astype(BF16)
            low_ref[...] = low
            for target, half in ((keep_ref, s[0]), (send_ref, 1 - s[0])):
                rows = pl.ds(pl.multiple_of(half * HALF, HALF), HALF)
                target[...] = dot_nt(low, wo_ref[rows, :]).astype(BF16)

    late = (residual, grad_res, query_weight, out_weight)
    args = (queries, *keys, *values, marks, *key_marks, grads, attended, sums, gains, *late)
    specs = [pair_columns(a) for a in args]
    for at in (5, 6, 7, 11):
        specs[at] = whole(args[at])
    specs[12:] = [any_place(a) for a in late]
    outs = [struct((tok, width), BF16)] + [struct((4 * enc, width), BF16)] * 2
    outs += [struct((tok, width), F32), struct((tok, width), BF16), struct((1, width), F32)]
    outs += [struct((tok, HALF), BF16)] * 2
    out_specs = [whole(o) for o in outs]
    out_specs[1], out_specs[2] = pair_columns(outs[1]), pair_columns(outs[2])
    return run_kernel(
        "cross_back", body, place, args, specs, outs, out_specs,
        grid=(width // LANES,),
        scratch=[pltpu.VMEM((4 * enc, LANES), BF16)] * 3
        + [pltpu.VMEM(a.shape, a.dtype) for a in late]
        + [pltpu.SemaphoreType.DMA((len(late),))],
        after=after, flops=tok * 2.5 * enc * 20 * 2 * width,
    )


def write_normed_grads(s, tok, h_ref, gain, grad_ref, weight_ref, keep_ref, send_ref, gain_grad_ref):
    running = None
    for target, part in ((keep_ref, s[0]), (send_ref, 1 - s[0])):
        rows = pl.ds(pl.multiple_of(part * tok, tok), tok)
        value = dot_nt(grad_ref[rows, :], weight_ref[...])
        target[...] = value.astype(BF16)
        inner = jnp.sum(value * h_ref[rows, :].astype(F32), axis=0, keepdims=True)
        running = inner if running is None else running + inner
    gain_grad_ref[...] = running / gain


def far_back(place, qkv, far_kv, marks, key_marks, grad_keep, grad_recv, attended, sums, gains, normed, weights, after=()):
    both, width = normed.shape
    tok = both // 2
    last = HALF // LANES - 1

    def body(
        s, q_ref, k_ref, v_ref, m_ref, km_ref, gk_ref, gr_ref, at_ref, ls_ref, gain_ref, h_any, wk_any, wv_any,
        dq_ref, dkv_ref, keep_ref, send_ref, gain_grad_ref, h_ref, weight_ref, semaphores,
    ):
        sources, targets = side_by_side(s, (wk_any, wv_any), weight_ref)
        later = copies((h_any, *sources), (h_ref, *targets), semaphores)

        @pl.when(s[1] != 0)
        def _():
            @pl.when(pl.program_id(0) == 0)
            def _():
                for copy in later:
                    copy.start()

            sum_k = sum_v = None
            for at in (0, 1):
                rows = pl.ds(at * tok, tok)
                grads = jnp.where(s[0] == at, gk_ref[...], gr_ref[...])
                dq_ref[rows, :], grad_k, grad_v = pull_block(
                    q_ref[rows, :], m_ref[rows, :], k_ref[...], km_ref[...], v_ref[...], grads, at_ref[rows, :],
                    ls_ref[rows, :], False,
                )
                sum_k = grad_k if at == 0 else sum_k + grad_k
                sum_v = grad_v if at == 0 else sum_v + grad_v
            dkv_ref[:, pair_lanes()] = sum_k.astype(BF16)
            dkv_ref[:, pair_lanes(1)] = sum_v.astype(BF16)

            @pl.when(pl.program_id(0) == last)
            def _():
                for copy in later:
                    copy.wait()
                write_normed_grads(
                    s, tok, h_ref, gain_ref[...].reshape(1, width), dkv_ref, weight_ref, keep_ref, send_ref, gain_grad_ref
                )

        @pl.when(s[1] == 0)
        def _():
            dq_ref[...] = jnp.zeros_like(dq_ref)
            for ref in (dkv_ref, keep_ref, send_ref, gain_grad_ref):
                ref[...] = jnp.zeros_like(ref)

    args = (qkv, far_kv, far_kv, marks, key_marks, grad_keep, grad_recv, attended, sums, gains, normed, *weights)
    specs = [pair_columns(a) for a in args]
    specs[2] = pair_columns(far_kv, 1)
    specs[3], specs[4], specs[9] = whole(marks), whole(key_marks), whole(gains)
    specs[10:] = [any_place(a) for a in args[10:]]
    outs = [struct((both, HALF), F32), struct((both, 2 * HALF), BF16)]
    outs += [struct((tok, width), BF16)] * 2 + [struct((1, width), F32)]
    return run_kernel(
        "far_back", body, place, args, specs, outs, [pair_columns(outs[0])] + [whole(o) for o in outs[1:]],
        grid=(HALF // LANES,),
        scratch=[pltpu.VMEM((both, width), BF16), pltpu.VMEM((width, 2 * HALF), BF16), pltpu.SemaphoreType.DMA((3,))],
        after=after, flops=both * both * 20 * 2 * HALF,
    )


def write_square(s, value, keep, send, first, x_first=False):
    rows = value.shape[0] // 16
    side = HALF // 2

    def write(target, half):
        for at in range(8):
            high, low, far = (at // 4, (at // 2) % 2, at % 2)
            for chip in range(value.shape[1] // HALF):
                columns = slice(chip * HALF + half * side, chip * HALF + (half + 1) * side)
                place = (chip, far, low, high) if x_first else (far, chip, low, high)
                for part in range(2):
                    piece = value[(2 * at + part) * rows : (2 * at + part + 1) * rows, columns].astype(BF16)
                    target[*place, pl.ds(first, rows), pl.ds(part * side, side)] = piece

    @pl.when(s[0] == 0)
    def _():
        write(keep, 0)
        write(send, 1)

    @pl.when(s[0] != 0)
    def _():
        write(keep, 1)
        write(send, 0)


def near_back(
    place, qkv, marks, key_marks, grad_keep, grad_recv, attended, sums, carried, gains,
    normed, far_normed, weights, far_grads, gain_grads, after=(),
):
    both, width = normed.shape
    tok = both // 2
    last = HALF // LANES - 1
    late_shapes = [(both, width)] * 2 + [(width, 3 * HALF), (both, 2 * HALF)]

    def body(
        s, q_ref, k_ref, v_ref, m_ref, km_ref, gk_ref, gr_ref, at_ref, ls_ref, ca_ref, gain_ref,
        gs_ref, gc_ref, gf_ref, h_any, fh_any, wq_any, wk_any, wv_any, fkv_any,
        keep_ref, send_ref, keep4, send4,
        dqkv, sum_k, sum_v, gain_grad_ref, gain_rows, h_ref, fh_ref, weight_ref, fkv_ref, semaphores,
    ):
        query_pair, key_pair, value_pair = (pair_lanes(group) for group in range(3))
        sources, targets = side_by_side(s, (wq_any, wk_any, wv_any), weight_ref)
        later = copies((h_any, fh_any, *sources, fkv_any), (h_ref, fh_ref, *targets, fkv_ref), semaphores)

        @pl.when(pl.program_id(0) == 0)
        def _():
            for copy in later:
                copy.start()

        for at in (0, 1):
            rows = pl.ds(at * tok, tok)
            count = (at + 1) * tok
            seen = pl.ds(0, count)
            grads = jnp.where(s[0] == at, gk_ref[...], gr_ref[...])
            grad_q, grad_k, grad_v = pull_block(
                q_ref[rows, :], m_ref[rows, :], k_ref[seen, :], km_ref[seen, :], v_ref[seen, :], grads,
                at_ref[rows, :], ls_ref[rows, :], True,
            )
            dqkv[rows, query_pair] = (grad_q + ca_ref[rows, :]).astype(BF16)
            if at == 0:
                sum_k[...] = grad_k
                sum_v[...] = grad_v
            else:
                dqkv[pl.ds(0, tok), key_pair] = (sum_k[...] + grad_k[:tok]).astype(BF16)
                dqkv[pl.ds(0, tok), value_pair] = (sum_v[...] + grad_v[:tok]).astype(BF16)
                dqkv[pl.ds(tok, tok), key_pair] = grad_k[tok:].astype(BF16)
                dqkv[pl.ds(tok, tok), value_pair] = grad_v[tok:].astype(BF16)

        @pl.when(pl.program_id(0) == last)
        def _():
            for copy in later:
                copy.wait()
            write_normed_grads(
                s, tok, h_ref, gain_ref[...].reshape(1, width), dqkv, weight_ref, keep_ref, send_ref, gain_grad_ref
            )
            rows = width // 16
            near_value = dot_tn(h_ref[...], dqkv[...])
            far_value = dot_tn(fh_ref[...], fkv_ref[...])
            write_square(s, near_value[:, :HALF], keep4, send4, 0)
            for at in (1, 2):
                value = near_value[:, at * HALF : (at + 1) * HALF] + far_value[:, (at - 1) * HALF : at * HALF]
                write_square(s, value, keep4, send4, at * rows)
            gain_rows[...] = jnp.zeros_like(gain_rows)
            gain_rows[0:1, :] = gain_grad_ref[...] + gs_ref[...]
            gain_rows[1:2, :] = gc_ref[...]
            gain_rows[2:3, :] = gf_ref[...]
            low = gain_rows[...].astype(BF16)
            piece = width // 8
            at_row = lax.broadcasted_iota(jnp.int32, (width, HALF), 0)
            at_col = lax.broadcasted_iota(jnp.int32, (width, HALF), 1)
            for at in range(8):
                pick = jnp.where((at_row == at_col + at * piece) & (at_col < piece), 1.0, 0.0).astype(BF16)
                value = dot_nn(low, pick).astype(BF16)
                for target in (keep4, send4):
                    target[at % 2, 0, (at // 2) % 2, at // 4, pl.ds(3 * rows, 16), :] = value

    late = (normed, far_normed, *weights, far_grads)
    args = (
        qkv, qkv, qkv, marks, key_marks, grad_keep, grad_recv, attended, sums, carried, gains, *gain_grads, *late
    )
    specs = [pair_columns(a) for a in args]
    specs[3], specs[4] = whole(marks), whole(key_marks)
    specs[1], specs[2] = pair_columns(qkv, 1), pair_columns(qkv, 2)
    specs[10:14] = [whole(a) for a in args[10:14]]
    specs[14:] = [any_place(a) for a in late]
    outs = [struct((tok, width), BF16)] * 2
    outs += [struct((2, 1, 2, 2, 3 * (width // 16) + 16, HALF), BF16)] * 2
    return run_kernel(
        "near_back", body, place, args, specs, outs, [whole(o) for o in outs],
        grid=(HALF // LANES,),
        scratch=[pltpu.VMEM((both, 3 * HALF), BF16)]
        + [pltpu.VMEM((tok, LANES), F32)] * 2
        + [pltpu.VMEM((1, width), F32), pltpu.VMEM((16, width), F32)]
        + [pltpu.VMEM(shape, BF16) for shape in late_shapes]
        + [pltpu.SemaphoreType.DMA((len(late),))],
        after=after, flops=both * both * 0.75 * 20 * 2 * HALF + 20 * both * width * HALF,
    )


def cross_grads(name, place, pairs, x_first, passages=None, after=()):
    width = pairs[0][0][0].shape[1]
    rows = width // 16
    count = len(pairs)
    order, spots, groups = ([], {}, [])
    for left, right in [*pairs, *([] if passages is None else [(passages[:2], passages[2:])])]:
        fresh = []
        for array in (*left, *right):
            if id(array) not in spots:
                spots[id(array)] = len(order)
                fresh.append(len(order))
                order.append(array)
        groups.append((fresh, [spots[id(array)] for array in left], [spots[id(array)] for array in right]))
    given = len(order)
    outs = [struct((2, 2, 2, 2, count * rows, HALF), BF16)] * 2
    if passages is not None:
        enc = passages[0].shape[0] // 4
        outs += [struct((2, enc, width), F32), struct((2, enc, width), BF16)]
    produced = len(outs)

    def body(s, *refs):
        sources, results = refs[:given], refs[given : given + produced]
        held, semaphores = refs[given + produced : -1], refs[-1]
        step = pl.program_id(0)
        moves = copies(sources, held, semaphores)

        @pl.when(step == 0)
        def _():
            for move in moves:
                move.start()

        for at, (fresh, left, right) in enumerate(groups):

            @pl.when(step == at)
            def _(at=at, fresh=fresh, left=left, right=right):
                for spot in fresh:
                    moves[spot].wait()
                if at < count:
                    value = None
                    for part, spot in enumerate(left):
                        tall = held[spot].shape[0]
                        piece = dot_tn(held[spot][...], held[right[0]][pl.ds(part * tall, tall), :])
                        value = piece if value is None else value + piece
                    write_square(s, value, results[0], results[1], 0, x_first)
                    return
                for slot in range(4):
                    slots = pl.ds(slot * enc, enc)
                    value = dot_nt(held[left[0]][slots, :], held[right[0]][...])
                    value = value + dot_nt(held[left[1]][slots, :], held[right[1]][...])
                    if slot % 2 == 0:
                        results[2][slot // 2] = value
                    else:
                        results[3][slot // 2] = value.astype(BF16)

    block = pl.BlockSpec((2, 2, 2, 2, rows, HALF), lambda m, _: (0, 0, 0, 0, jnp.minimum(m, count - 1), 0))
    return run_kernel(
        name, body, place, order, [any_place(a) for a in order], outs,
        [block, block, *(whole(o) for o in outs[2:])],
        grid=(len(groups),),
        scratch=[pltpu.VMEM(a.shape, a.dtype) for a in order]
        + [pltpu.SemaphoreType.DMA((given,))],
        after=after,
    )


def passage_grads(place, grad_keys, grad_values, key_weight, value_weight, after=()):
    keys4, width = grad_keys.shape
    enc = keys4 // 4

    def body(s, dk_ref, dv_ref, wk_ref, wv_ref, keep_ref, send_ref):
        value = dot_nt(dk_ref[...], wk_ref[...]) + dot_nt(dv_ref[...], wv_ref[...])

        @pl.when(pl.program_id(0) % 2 == 0)
        def _():
            keep_ref[0] = value

        @pl.when(pl.program_id(0) % 2 != 0)
        def _():
            send_ref[0] = value.astype(BF16)

    args = (grad_keys, grad_values, key_weight, value_weight)
    slot = pl.BlockSpec((enc, width), lambda i, _: (i, 0))
    result = pl.BlockSpec((1, enc, width), lambda i, _: (i // 2, 0, 0))
    outs = [struct((2, enc, width), F32), struct((2, enc, width), BF16)]
    return run_kernel(
        "passage_grads", body, place, args, [slot, slot, whole(key_weight), whole(value_weight)], outs, [result, result],
        grid=(4,), after=after,
    )


def last_pull(place, inputs, gains, grad_res, parts, after=()):
    tok, width = inputs.shape
    steps = 2
    tile = tok // steps

    def body(s, in_ref, gain_ref, dx_ref, *refs):
        part_refs, out_ref = refs[:-1], refs[-1]
        total = part_refs[0][...].astype(F32)
        for ref in part_refs[1:]:
            total = total + ref[...].astype(F32)
        out_ref[...] = dx_ref[...] + norm_pull(in_ref[...].astype(F32), gain_ref[...].reshape(1, width), total)[0]

    args = (inputs, gains, grad_res, *parts)
    block = pl.BlockSpec((tile, width), lambda i, _: (i, 0))
    specs = [block for _ in args]
    specs[1] = whole(gains)
    return run_kernel(
        "last_pull", body, place, args, specs, [struct((tok, width), F32)], [block], grid=(steps,), after=after,
        flops=20 * tok * width,
    )[0]


def rounded(values):
    return lax.reduce_precision(values, 8, 7).astype(BF16)


def add_split(half, keep, recv):
    part = lambda array, at: lax.dynamic_index_in_dim(array, at, 0, False).astype(F32)
    kept = rounded(part(keep, half) + part(recv, half))
    return (kept, rounded(part(keep, 1 - half) + part(recv, 1 - half)))


class Halving:
    def __init__(self, keep, recv, steps):
        self.keep, self.recv, self.steps = (keep, recv, list(steps))

    def step(self, *after):
        half, axis, pairs = self.steps.pop(0)
        keep, recv = (self.keep.reshape(2, -1, HALF), self.recv.reshape(2, -1, HALF))
        if after:
            keep, recv, *_ = lax.optimization_barrier((keep, recv, *after))
        self.keep, send = add_split(half, keep, recv)
        self.recv = lax.ppermute(send, axis, pairs)
        return self.keep


def merge_split(place, step, sums, after=()):
    half, axis, pairs = step
    counts = [a.keep.shape[0] // 4 for a in sums]
    arrays = [array.reshape(2, 2, count, HALF) for a, count in zip(sums, counts) for array in (a.keep, a.recv)]
    starts = [sum(counts[:at]) for at in range(len(counts))]

    def body(s, *refs):
        given, (keep_ref, send_ref) = refs[: len(arrays)], refs[len(arrays) :]
        for target, side in ((keep_ref, s[0]), (send_ref, 1 - s[0])):
            for at, (first, count) in enumerate(zip(starts, counts)):
                for deep in range(2):
                    value = given[2 * at][side, deep].astype(F32) + given[2 * at + 1][side, deep].astype(F32)
                    target[deep, pl.ds(first, count), :] = value.astype(BF16)

    outs = [struct((2, sum(counts), HALF), BF16)] * 2
    keep, send = run_kernel(
        "merge_split", body, half.astype(jnp.int32).reshape(1), arrays, [whole(a) for a in arrays], outs,
        [whole(o) for o in outs], after=after,
    )
    merged = Halving(keep, lax.ppermute(send, axis, pairs), ())
    return merged


def self_start(place, keep4, recv4, after=()):
    cut = 80
    rest = keep4.shape[4] - cut

    def body(s, keep_ref, recv_ref, ak_ref, as_ref, bk_ref, bs_ref):
        for target, side in ((ak_ref, s[2]), (as_ref, 1 - s[2])):
            for slot, source in enumerate((keep_ref, recv_ref)):
                target[slot] = source[side, 0, :, :, pl.ds(0, cut), :]
        late, front, tail = (pl.ds(cut, rest - 16), pl.ds(0, rest - 16), pl.ds(cut + rest - 16, 16))

        @pl.when(s[0] == s[1])
        def _():
            bk_ref[:, :, :, front, :] = keep_ref[:, 0, :, :, late, :]
            bs_ref[:, :, :, front, :] = recv_ref[:, 0, :, :, late, :]

        @pl.when(s[0] != s[1])
        def _():
            bk_ref[:, :, :, front, :] = recv_ref[:, 0, :, :, late, :]
            bs_ref[:, :, :, front, :] = keep_ref[:, 0, :, :, late, :]

        shared = keep_ref[:, 0, :, :, tail, :].astype(F32) + recv_ref[:, 0, :, :, tail, :].astype(F32)
        for target in (bk_ref, bs_ref):
            target[:, :, :, pl.ds(rest - 16, 16), :] = shared.astype(BF16)

    args = (keep4, recv4)
    outs = [struct((2, 2, 2, cut, HALF), BF16)] * 2 + [struct((2, 2, 2, rest, HALF), BF16)] * 2
    return run_kernel(
        "self_start", body, place, args, [whole(a) for a in args], outs, [whole(o) for o in outs], after=after
    )


def both_step(place, first, second, after=()):
    sums = (first, second)
    spots, axes, pairs = zip(*(a.steps.pop(0) for a in sums))
    arrays = [array.reshape(2, -1, HALF) for a in sums for array in (a.keep, a.recv)]

    def body(s, *refs):
        given, outs = refs[:4], refs[4:]
        for at in range(2):
            side = s[spots[at]]
            for target, side in ((outs[2 * at], side), (outs[2 * at + 1], 1 - side)):
                target[...] = (given[2 * at][side].astype(F32) + given[2 * at + 1][side].astype(F32)).astype(BF16)

    outs = [struct(array.shape[1:], BF16) for array in arrays]
    results = run_kernel(
        "both_step", body, place, arrays, [whole(a) for a in arrays], outs,
        [whole(o) for o in outs], after=after,
    )
    for at, a in enumerate(sums):
        a.keep, a.recv = (results[2 * at], lax.ppermute(results[2 * at + 1], axes[at], pairs[at]))
    return results[0]


def finish_sums(name, keep, recv, count, tail=0, after=()):
    rows = keep.shape[0] // 16 // count * 16
    side = HALF // 2

    def body(s, keep_ref, recv_ref, *outs):
        for at in range(count):
            part = pl.ds(at * rows, rows)
            total = keep_ref[part, :].astype(F32) + recv_ref[part, :].astype(F32)
            outs[at][pl.ds(0, rows), :] = total[:, :side]
            outs[at][pl.ds(rows, rows), :] = total[:, side:]
        if tail:
            part = pl.ds(count * rows, 16)
            total = keep_ref[part, :].astype(F32) + recv_ref[part, :].astype(F32)
            for at in range(tail):
                outs[count + at][...] = total[at, : 2 * rows]

    outs = [struct((2 * rows, side), F32)] * count + [struct((2 * rows,), F32)] * tail
    place = jnp.zeros((1,), jnp.int32)
    return run_kernel(
        name, body, place, (keep, recv), [whole(keep), whole(recv)], outs, [whole(o) for o in outs], after=after
    )


def feed_forward(place, residual, context, out_weight, gain_vec, feed_in, feed_out, cotangent, after=()):
    tok, width = residual.shape
    hidden_width = feed_in.shape[1]
    steps = 4
    chunk = hidden_width // steps
    rows_in = width // 8
    side = width // 4

    def body(
        s, x1_ref, ctx_ref, wo_ref, gain_ref, w1_ref, w2_ref, g_ref,
        out_ref, dx_ref, low_ref, dctx_ref, gain_grad_ref, keep, send,
        x2, normed, normed_flip, grad_flip, sum_out, sum_norm, block_in, block_out, semaphores,
    ):
        step = pl.program_id(0)

        @pl.when(step == 0)
        def _():
            x2[...] = x1_ref[...] + dot_nn(ctx_ref[...], wo_ref[...])
            normed[...] = (unit_norm(x2[...])[0] * gain_ref[...].reshape(1, width)).astype(BF16)
            normed_flip[...] = normed[...].T
            grad_flip[...] = g_ref[...].T
            sum_out[...] = jnp.zeros_like(sum_out)
            sum_norm[...] = jnp.zeros_like(sum_norm)

        w1, w2, grad = (w1_ref[...], w2_ref[...], g_ref[...])
        pre = dot_nn(normed[...], w1)
        root = 0.7978845608028654
        bend = 0.044715
        square = pre * pre
        swing = jnp.tanh(pre * (root + root * bend * square))
        half = 0.5 + 0.5 * swing
        active = pre * half
        hidden = active.astype(BF16)
        sum_out[...] += dot_nn(hidden, w2)
        slope = half + active * (1.0 - swing) * (root + 3.0 * root * bend * square)
        grad_pre = (dot_nt(grad, w2) * slope).astype(BF16)
        sum_norm[...] += dot_nt(grad_pre, w1)
        slot = step % 2

        def moves(at, slot):
            columns = (pl.ds(0, 2 * rows_in), pl.ds(2 * rows_in, side))
            inner = [
                pltpu.make_async_copy(block_in.at[slot], target.at[:, at // 2, columns[0], :], semaphores.at[slot, 0])
                for target in (keep, send)
            ]
            outer = [
                pltpu.make_async_copy(
                    block_out.at[slot, half], target.at[pl.ds(2 * at, 2), :, columns[1], :], semaphores.at[slot, 1 + kind]
                )
                for kind, (target, half) in enumerate(((keep, s[0]), (send, 1 - s[0])))
            ]
            return (inner, outer)

        def start(at, slot):
            inner, outer = moves(at, slot)
            pl.when(at % 2 == s[0])(inner[0].start)
            pl.when(at % 2 != s[0])(inner[1].start)
            for move in outer:
                move.start()

        def wait(at, slot):
            inner, outer = moves(at, slot)
            pl.when(at % 2 == s[0])(inner[0].wait)
            pl.when(at % 2 != s[0])(inner[1].wait)
            for move in outer:
                move.wait()

        @pl.when(step >= 2)
        def _():
            wait(step - 2, slot)

        grad_in = dot_nn(normed_flip[...], grad_pre).astype(BF16)
        for at in range(8):
            for unit in range(2):
                block_in[slot, at, pl.ds(unit * rows_in, rows_in), :] = grad_in[
                    at * rows_in : (at + 1) * rows_in, unit * HALF : (unit + 1) * HALF
                ]
        grad_out = dot_nn(grad_flip[...], hidden).astype(BF16)
        for at in range(2):
            for part in range(4):
                block_out[slot, part % 2, at, part // 2] = grad_out[part * side : (part + 1) * side, at * HALF : (at + 1) * HALF]
        start(step, slot)

        @pl.when(step == steps - 1)
        def _():
            for at in (steps - 2, steps - 1):
                wait(at, at % 2)

        @pl.when(step == steps - 1)
        def _():
            out_ref[...] = (x2[...] + sum_out[...]).astype(BF16)
            back, gain_grad_ref[...] = norm_pull(x2[...], gain_ref[...].reshape(1, width), sum_norm[...])
            grad_x = grad.astype(F32) + back
            dx_ref[...] = grad_x
            low = grad_x.astype(BF16)
            low_ref[...] = low
            dctx_ref[...] = dot_nt(low, wo_ref[...]).astype(BF16)

    args = (residual, context, out_weight, gain_vec, feed_in, feed_out, cotangent)
    specs = [whole(a) for a in args]
    specs[4] = pl.BlockSpec((width, chunk), lambda c, _: (0, c))
    specs[5] = pl.BlockSpec((chunk, width), lambda c, _: (c, 0))
    outs = [
        struct((tok, width), BF16),
        struct((tok, width), F32),
        struct((tok, width), BF16),
        struct((tok, width), BF16),
        struct((1, width), F32),
        struct((8, 2, 2 * rows_in + side, HALF), BF16),
        struct((8, 2, 2 * rows_in + side, HALF), BF16),
    ]
    out_specs = [whole(o) for o in outs]
    out_specs[5] = out_specs[6] = any_place(outs[5])
    return run_kernel(
        "feed_forward",
        body,
        place,
        args,
        specs,
        outs,
        out_specs,
        grid=(steps,),
        scratch=[
            pltpu.VMEM((tok, width), F32),
            pltpu.VMEM((tok, width), BF16),
            pltpu.VMEM((width, tok), BF16),
            pltpu.VMEM((width, tok), BF16),
            pltpu.VMEM((tok, width), F32),
            pltpu.VMEM((tok, width), F32),
            pltpu.VMEM((2, 8, 2 * rows_in, HALF), BF16),
            pltpu.VMEM((2, 2, 2, 2, side, HALF), BF16),
            pltpu.SemaphoreType.DMA((2, 3)),
        ],
        after=after, flops=12 * tok * width * hidden_width + 4 * tok * width * width,
    )


def local_paired(
    inputs,
    encoded,
    cotangent,
    dec_seg,
    pass_doc,
    enc_mask,
    self_query,
    self_key,
    self_value,
    self_output,
    cross_query,
    cross_key,
    cross_value,
    cross_output,
    feed_in,
    feed_out,
    gain_self,
    gain_cross,
    gain_ff,
):
    inputs, encoded, cotangent = (inputs[0], encoded[0], cotangent[0])
    tok, width = inputs.shape
    enc = encoded.shape[0]
    blk, row = (lax.axis_index("blk"), lax.axis_index("rows"))
    core, chip = (blk % 2, blk // 2)
    y_at, z_low, z_high = (row % 2, (row // 2) % 2, row // 4)
    place = jnp.stack([core, chip, y_at, chip ^ core]).astype(jnp.int32)
    gains = (gain_self, gain_cross, gain_ff)
    to_core = lambda array: lax.ppermute(array, "blk", CORE_SWAP)
    to_chip = lambda array: lax.ppermute(array, "blk", CHIP_SWAP)
    in_order = lambda mine, other: jnp.where(core == 0, jnp.concatenate([mine, other]), jnp.concatenate([other, mine]))

    def swap(distance):
        return tuple((at, at ^ distance) for at in range(8))

    over_x = (chip, "blk", CHIP_SWAP)
    over_y = (y_at, "rows", swap(1))
    over_z = ((z_low, "rows", swap(2)), (z_high, "rows", swap(4)))

    gap = -tok % LANES
    spare = jnp.zeros((8 * LANES - tok - gap - enc - 1,), jnp.int32)
    labels = jnp.concatenate([dec_seg[0], spare[:gap], enc_mask[0], pass_doc[0], spare[gap:]])
    labels = jnp.concatenate([labels, jnp.zeros((8 * LANES - labels.shape[0],), jnp.int32)]).reshape(1, 8 * LANES)
    seg_c = to_core(dec_seg)
    labels_c = to_core(labels)
    inputs_c = to_core(inputs)
    inputs_x = to_chip(inputs)
    labels_x = to_chip(labels)
    encoded_c = to_core(encoded)
    h1, qkv, near_marks, near_keys_marks, near_out, near_sum, ck0, cv0 = near_part(
        place, inputs, inputs_c, gain_self, (self_query, self_key, self_value), (dec_seg, seg_c), (encoded, encoded_c),
        (cross_key, cross_value),
    )
    inputs_x, labels_x, encoded_late, _ = lax.optimization_barrier((inputs_x, labels_x, encoded, ck0))
    labels_d = to_core(labels_x)
    inputs_d = to_core(inputs_x)
    encoded_x = to_chip(encoded_late)
    spot = place
    h1_far, far_kv, far_keys_marks, self_out, self_sum, ctx_keep, ctx_send = far_part(
        spot, inputs_x, inputs_d, gain_self, (self_key, self_value), qkv, near_marks, (labels_x, labels_d), near_out, near_sum
    )
    place = find_passages(spot, tok, enc, (labels, labels_c, labels_x, labels_d), after=(ctx_send,))
    encoded_x, _ = lax.optimization_barrier((encoded_x, self_out))
    encoded_d = to_core(encoded_x)
    x1, h2, cq, self_context, ck1, cv1, own_marks, docs0, docs1, cross_context, cross_out, cross_sum = cross_part(
        place, inputs, ctx_keep, to_core(ctx_send), self_output, gain_cross, cross_query, encoded_x, encoded_d, cross_key,
        cross_value, ck0, cv0, (labels, labels_c, labels_x, labels_d),
    )
    docs = (docs0, docs1)
    output, dx2, e2, d_cross, grad_gain_ff, keep_ff, send_ff = feed_forward(
        place, x1, cross_context, cross_output, gain_ff, feed_in, feed_out, cotangent
    )
    recv_ff = to_core(send_ff)
    dcq, dck, dcv, dx1, e1, grad_gain_cross, ds_keep, ds_send = cross_back(
        place, cq, (ck0, ck1), (cv0, cv1), own_marks, docs, d_cross, cross_out, cross_sum, x1, dx2, cross_query,
        gain_cross, self_output,
    )
    ds_recv = to_core(ds_send)
    keep_ff, recv_ff, _ = lax.optimization_barrier((keep_ff, recv_ff, dcq))
    chip_ff = (keep_ff.astype(F32) + recv_ff.astype(F32)).astype(BF16)
    row_ff = lax.psum_scatter(chip_ff, "rows", scatter_dimension=0, tiled=True)
    passages = (encoded, encoded_c, encoded_x, encoded_d)
    keep_p, send_p = cross_grads(
        "cross_grads", place, (((cross_context,), (e2,)), ((h2,), (dcq,)), ((self_context,), (e1,))), True,
        after=(chip_ff,),
    )
    keep_q, send_q = cross_grads(
        "late_grads", place, ((passages, (dck,)), (passages, (dcv,))), False, after=(keep_p,)
    )
    recv_p = to_core(send_p)
    recv_p, ds_recv, send_q = lax.optimization_barrier((recv_p, ds_recv, send_q))
    sum_p = Halving(keep_p, recv_p, (over_x, over_y))
    sum_q = Halving(keep_q, to_core(send_q), (over_y, over_x))
    held = (sum_p.step(), sum_q.step())
    dq_far, dkv_far, far_keep, far_send, gain_far = far_back(
        place, qkv, far_kv, near_marks, far_keys_marks, ds_keep, ds_recv, self_out, self_sum, gain_self, h1_far,
        (self_key, self_value), after=held,
    )
    sum_p.recv, sum_q.recv, far_send = lax.optimization_barrier((sum_p.recv, sum_q.recv, far_send))
    far_recv = to_core(far_send)
    held = (sum_p.step(), sum_q.step())
    far_keep, far_recv, *_ = lax.optimization_barrier((far_keep, far_recv, *held))
    far_here = (far_keep.astype(F32) + far_recv.astype(F32)).astype(BF16)
    from_far = to_chip(far_here)
    near_keep, near_send, keep4, send4 = near_back(
        place, qkv, near_marks, near_keys_marks, ds_keep, ds_recv, self_out, self_sum, dq_far, gain_self, h1, h1_far,
        (self_query, self_key, self_value), dkv_far, (gain_far, grad_gain_cross, grad_gain_ff),
        after=(far_here, *held),
    )
    tied = lax.optimization_barrier((sum_p.recv, sum_q.recv, from_far, near_send, send4))
    sum_p.recv, sum_q.recv, from_far, near_send, send4 = tied
    recv4 = to_core(send4)
    near_recv = to_core(near_send)
    first_keep, first_send, second_keep, second_send = self_start(spot, keep4, recv4)
    sum_first = Halving(first_keep, lax.ppermute(first_send, "rows", swap(1)), ((3, "blk", CHIP_SWAP),))
    sum_second = Halving(second_keep, to_chip(second_send), ((2, "rows", swap(1)),))
    input_grad = last_pull(
        place, inputs, gain_self, dx1, (near_keep, near_recv, from_far), after=(first_send, second_send)
    )
    enc_keep, enc_send = passage_grads(place, dck, dcv, cross_key, cross_value, after=(input_grad,))
    sum_first.recv, sum_second.recv, enc_send = lax.optimization_barrier((sum_first.recv, sum_second.recv, enc_send))
    both_step(spot, sum_first, sum_second, after=(enc_keep,))
    sum_cross = merge_split(place, over_z[0], (sum_p, sum_q), after=(sum_first.keep,))
    sum_cross.steps = [over_z[1]]
    enc_send, _ = lax.optimization_barrier((enc_send, sum_first.keep))
    enc_recv = to_core(enc_send)
    row_ff, enc_keep, enc_recv, _ = lax.optimization_barrier((row_ff, enc_keep, enc_recv, sum_cross.keep))
    ff_keep = lax.dynamic_index_in_dim(row_ff[0], chip, 0, False)
    ff_recv = to_chip(lax.dynamic_index_in_dim(row_ff[0], 1 - chip, 0, False))
    enc_sum = enc_keep + enc_recv.astype(F32)
    from_chip = to_chip(enc_sum[1].astype(BF16))
    sum_self = merge_split(place, over_z[0], (sum_first, sum_second), after=(enc_sum,))
    sum_self.steps = [over_z[1]]
    rows = width // 16
    ff_keep, ff_recv, _ = lax.optimization_barrier((ff_keep, ff_recv, sum_self.keep))
    total_ff = ff_keep.astype(F32) + ff_recv.astype(F32)
    grad_feed_in = jnp.concatenate([total_ff[: 2 * rows], total_ff[2 * rows : 4 * rows]], axis=1)
    feed_out_flip = total_ff[4 * rows :]
    held = sum_cross.step(grad_feed_in, feed_out_flip)
    held = sum_self.step(held)
    enc_last, from_chip, _ = lax.optimization_barrier((enc_sum[0], from_chip, held))
    encoded_grad = enc_last + from_chip.astype(F32)
    self_q, self_k, self_v, *gain_grads = finish_sums("finish_self", sum_self.keep, sum_self.recv, 3, 3, after=(held,))
    cross_o, cross_q, self_o, cross_k, cross_v = finish_sums(
        "finish_cross", sum_cross.keep, sum_cross.recv, 5, after=(self_q,)
    )
    return (
        output[None],
        input_grad[None],
        encoded_grad[None],
        self_q,
        self_k,
        self_v,
        self_o,
        cross_q,
        cross_k,
        cross_v,
        cross_o,
        grad_feed_in,
        feed_out_flip.T,
        *gain_grads,
    )


def solution(mesh):
    paired = mesh.shape["blk"] == 4 and mesh.shape["rows"] == 8
    body = local_paired if paired else local_any
    in_specs = (
        P("rows", "blk", None),
        P("rows", "blk", None),
        P("rows", "blk", None),
        P("rows", "blk"),
        P("rows", "blk"),
        P("rows", "blk"),
        P(),
        P(),
        P(),
        P(),
        P(),
        P(),
        P(),
        P(),
        P(),
        P(),
        P(),
        P(),
        P(),
    )
    out_specs = (
        P("rows", "blk", None),
        P("rows", "blk", None),
        P("rows", "blk", None),
        P("rows", "blk"),
        P("rows", "blk"),
        P("rows", "blk"),
        P("rows", "blk"),
        P("rows", "blk"),
        P("rows", "blk"),
        P("rows", "blk"),
        P("rows", "blk"),
        P("rows", "blk"),
        P("rows", "blk"),
        P("rows"),
        P("rows"),
        P("rows"),
    )
    return jax.shard_map(body, mesh=mesh, in_specs=in_specs, out_specs=out_specs, check_vma=False)
```

```python
import jax
import jax.numpy as jnp
from jax import lax
from jax.experimental import pallas as pl
from jax.experimental.pallas import tpu as pltpu
from jax.sharding import PartitionSpec as P

HEADS = 12
HEAD_DIM = 64
PLEN = 384


NEG_FILL = -1e30
SCALE = 0.125


def split_heads(matrix):
    return matrix.reshape(matrix.shape[0], matrix.shape[1], HEADS, HEAD_DIM)


def join_heads(tensor):
    return jnp.transpose(tensor, (0, 2, 1, 3)).reshape(
        tensor.shape[0], tensor.shape[2], HEADS * HEAD_DIM
    )


def rms_norm(values, gain_vec):
    return values * lax.rsqrt(jnp.mean(values * values, axis=-1, keepdims=True) + 1e-06) * gain_vec


def norm_back(values, gain_vec, grad_out):
    _, pullback = jax.vjp(rms_norm, values, gain_vec)
    return pullback(grad_out)


def project(left, weight):
    return jnp.einsum("rqd,df->rqf", left, weight, preferred_element_type=jnp.float32)


def back_project(grad_out, weight):
    return jnp.einsum("rqf,df->rqd", grad_out, weight, preferred_element_type=jnp.float32)


def weight_grad(left, grad_out):
    return jnp.einsum("rqd,rqf->df", left, grad_out, preferred_element_type=jnp.float32)


def head_scores(queries, keys):
    return (
        jnp.einsum(
            "rqhe,rkhe->rhqk",
            split_heads(queries),
            split_heads(keys),
            preferred_element_type=jnp.float32,
        )
        * SCALE
    )


def empty_state(row_count, query_count):
    return (
        jnp.full((row_count, HEADS, query_count), NEG_FILL, jnp.float32),
        jnp.zeros((row_count, HEADS, query_count), jnp.float32),
        jnp.zeros((row_count, HEADS, query_count, HEAD_DIM), jnp.float32),
    )


def online_block(state, queries, keys, values, allowed):
    run_max, run_sum, run_acc = state
    scores = head_scores(queries, keys)
    allowed = allowed[:, None]
    new_max = jnp.maximum(run_max, jnp.max(jnp.where(allowed, scores, NEG_FILL), axis=-1))
    weights = jnp.where(allowed, jnp.exp(scores - new_max[..., None]), 0.0)
    new_sum = jnp.sum(weights, axis=-1)
    new_acc = jnp.einsum(
        "rhqk,rkhe->rhqe",
        weights.astype(jnp.bfloat16),
        split_heads(values),
        preferred_element_type=jnp.float32,
    )
    return (new_max, new_sum, new_acc)


def finish(state):
    run_max, run_sum, run_acc = state
    return (run_acc / run_sum[..., None], run_max + jnp.log(run_sum))


def grad_pair(queries, grad_ctx, log_sum, delta, keys, values, allowed):
    scores = head_scores(queries, keys)
    probs_now = jnp.where(allowed[:, None], jnp.exp(scores - log_sum[..., None]), 0.0)
    grad_probs = jnp.einsum(
        "rqhe,rkhe->rhqk",
        split_heads(grad_ctx),
        split_heads(values),
        preferred_element_type=jnp.float32,
    )
    grad_scores = (probs_now * (grad_probs - delta[..., None])).astype(jnp.bfloat16)
    grad_query = (
        jnp.einsum(
            "rhqk,rkhe->rqhe", grad_scores, split_heads(keys), preferred_element_type=jnp.float32
        )
        * SCALE
    )
    grad_key = (
        jnp.einsum(
            "rhqk,rqhe->rkhe", grad_scores, split_heads(queries), preferred_element_type=jnp.float32
        )
        * SCALE
    )
    grad_value = jnp.einsum(
        "rhqk,rqhe->rkhe",
        probs_now.astype(jnp.bfloat16),
        split_heads(grad_ctx),
        preferred_element_type=jnp.float32,
    )
    row_count = keys.shape[0]
    key_count = keys.shape[1]
    joined = jnp.concatenate(
        (grad_key.reshape(row_count, key_count, -1), grad_value.reshape(row_count, key_count, -1)),
        axis=-1,
    )
    return (grad_query.reshape(row_count, queries.shape[1], -1), joined)


def head_delta(grad_ctx, attended):
    return jnp.einsum("rqhe,rhqe->rhq", split_heads(grad_ctx).astype(jnp.float32), attended)


def spread_matrix(matrix, row_split, block_count):
    first, second = matrix.shape
    tiles = matrix.reshape(row_split, first // row_split, block_count, second // block_count)
    return jnp.transpose(tiles, (0, 2, 1, 3)).reshape(
        row_split * block_count, first // row_split, second // block_count
    )


def spread_gain(vector, row_split, block_count):
    tiles = vector.reshape(row_split, 1, vector.shape[0] // row_split)
    return jnp.broadcast_to(tiles, (row_split, block_count, vector.shape[0] // row_split)).reshape(
        row_split * block_count, vector.shape[0] // row_split
    )


def local_any(
    inputs,
    encoded,
    cotangent,
    dec_seg,
    pass_doc,
    enc_mask,
    self_query,
    self_key,
    self_value,
    self_output,
    cross_query,
    cross_key,
    cross_value,
    cross_output,
    feed_in,
    feed_out,
    gain_self,
    gain_cross,
    gain_ff,
):
    row_count, tok_shard, width = inputs.shape
    enc_shard = encoded.shape[1]
    block_count = lax.axis_size("blk")
    row_split = lax.axis_size("rows")
    block_ids = jnp.arange(block_count)
    query_places = lax.axis_index("blk") * tok_shard + jnp.arange(tok_shard)
    start_state = empty_state(row_count, tok_shard)
    residual = inputs.astype(jnp.float32)
    normed_self = rms_norm(residual, gain_self).astype(jnp.bfloat16)
    self_queries = project(normed_self, self_query).astype(jnp.bfloat16)
    self_keys = project(normed_self, self_key).astype(jnp.bfloat16)
    self_values = project(normed_self, self_value).astype(jnp.bfloat16)
    piece_keys = lax.all_gather(self_keys, "blk", axis=1, tiled=True)
    piece_values = lax.all_gather(self_values, "blk", axis=1, tiled=True)
    piece_segs = lax.all_gather(dec_seg, "blk", axis=1, tiled=True)
    key_places = jnp.arange(piece_keys.shape[1])
    allowed = (dec_seg[:, :, None] == piece_segs[:, None, :]) & (
        key_places[None, None, :] <= query_places[None, :, None]
    )
    self_attn, self_lse = finish(
        online_block(start_state, self_queries, piece_keys, piece_values, allowed)
    )
    self_context = join_heads(self_attn).astype(jnp.bfloat16)
    after_self = residual + project(self_context, self_output)
    normed_cross = rms_norm(after_self, gain_cross).astype(jnp.bfloat16)
    cross_queries = project(normed_cross, cross_query).astype(jnp.bfloat16)
    cross_keys = project(encoded, cross_key).astype(jnp.bfloat16)
    cross_values = project(encoded, cross_value).astype(jnp.bfloat16)
    key_docs = jnp.where(enc_mask == 1, jnp.repeat(pass_doc, PLEN, axis=1), -1)
    piece_keys = lax.all_gather(cross_keys, "blk", axis=1, tiled=True)
    piece_values = lax.all_gather(cross_values, "blk", axis=1, tiled=True)
    piece_docs = lax.all_gather(key_docs, "blk", axis=1, tiled=True)
    allowed = dec_seg[:, :, None] == piece_docs[:, None, :]
    cross_attn, cross_lse = finish(
        online_block(start_state, cross_queries, piece_keys, piece_values, allowed)
    )
    cross_context = join_heads(cross_attn).astype(jnp.bfloat16)
    after_cross = after_self + project(cross_context, cross_output)
    normed_ff = rms_norm(after_cross, gain_ff).astype(jnp.bfloat16)
    before_act = project(normed_ff, feed_in)
    hidden = jax.nn.gelu(before_act).astype(jnp.bfloat16)
    output = (after_cross + project(hidden, feed_out)).astype(jnp.bfloat16)
    grad_feed_out = weight_grad(hidden, cotangent)
    grad_hidden = back_project(cotangent, feed_out)
    _, gelu_back = jax.vjp(jax.nn.gelu, before_act)
    grad_before = gelu_back(grad_hidden)[0].astype(jnp.bfloat16)
    grad_feed_in = weight_grad(normed_ff, grad_before)
    grad_cross_res, grad_gain_ff = norm_back(
        after_cross, gain_ff, back_project(grad_before, feed_in)
    )
    grad_cross_res = cotangent.astype(jnp.float32) + grad_cross_res
    cross_branch = grad_cross_res.astype(jnp.bfloat16)
    grad_cross_output = weight_grad(cross_context, cross_branch)
    grad_cross_ctx = back_project(cross_branch, cross_output).astype(jnp.bfloat16)
    cross_delta = head_delta(grad_cross_ctx, cross_attn)
    all_keys, all_values, all_docs = (
        lax.all_gather(cross_keys, "blk", axis=1, tiled=True),
        lax.all_gather(cross_values, "blk", axis=1, tiled=True),
        lax.all_gather(key_docs, "blk", axis=1, tiled=True),
    )

    def passage_step(running, block_index):
        offset = block_index * enc_shard
        piece_keys = lax.dynamic_slice_in_dim(all_keys, offset, enc_shard, 1)
        piece_values = lax.dynamic_slice_in_dim(all_values, offset, enc_shard, 1)
        piece_docs = lax.dynamic_slice_in_dim(all_docs, offset, enc_shard, 1)
        allowed = dec_seg[:, :, None] == piece_docs[:, None, :]
        grad_query, grad_kv = grad_pair(
            cross_queries, grad_cross_ctx, cross_lse, cross_delta, piece_keys, piece_values, allowed
        )
        return (running + grad_query, grad_kv)

    grad_cross_q, key_terms = lax.scan(
        passage_step, jnp.zeros((row_count, tok_shard, width), jnp.float32), block_ids
    )
    grad_cross_kv = lax.psum_scatter(
        key_terms.astype(jnp.bfloat16), "blk", scatter_dimension=0, tiled=True
    ).astype(jnp.float32)[0]
    low_cross_q = grad_cross_q.astype(jnp.bfloat16)
    low_cross_k = grad_cross_kv[..., :width].astype(jnp.bfloat16)
    low_cross_v = grad_cross_kv[..., width:].astype(jnp.bfloat16)
    grad_cross_query = weight_grad(normed_cross, low_cross_q)
    grad_cross_key = weight_grad(encoded, low_cross_k)
    grad_cross_value = weight_grad(encoded, low_cross_v)
    encoded_grad = back_project(low_cross_k, cross_key) + back_project(low_cross_v, cross_value)
    grad_self_res, grad_gain_cross = norm_back(
        after_self, gain_cross, back_project(low_cross_q, cross_query)
    )
    grad_self_res = grad_cross_res + grad_self_res
    self_branch = grad_self_res.astype(jnp.bfloat16)
    grad_self_output = weight_grad(self_context, self_branch)
    grad_self_ctx = back_project(self_branch, self_output).astype(jnp.bfloat16)
    self_delta = head_delta(grad_self_ctx, self_attn)
    all_self_keys, all_self_values, all_self_segs = (
        lax.all_gather(self_keys, "blk", axis=1, tiled=True),
        lax.all_gather(self_values, "blk", axis=1, tiled=True),
        lax.all_gather(dec_seg, "blk", axis=1, tiled=True),
    )

    def self_step(running, block_index):
        offset = block_index * tok_shard
        piece_keys = lax.dynamic_slice_in_dim(all_self_keys, offset, tok_shard, 1)
        piece_values = lax.dynamic_slice_in_dim(all_self_values, offset, tok_shard, 1)
        piece_segs = lax.dynamic_slice_in_dim(all_self_segs, offset, tok_shard, 1)
        key_places = offset + jnp.arange(tok_shard)
        allowed = (dec_seg[:, :, None] == piece_segs[:, None, :]) & (
            key_places[None, None, :] <= query_places[None, :, None]
        )
        grad_query, grad_kv = grad_pair(
            self_queries, grad_self_ctx, self_lse, self_delta, piece_keys, piece_values, allowed
        )
        return (running + grad_query, grad_kv)

    grad_self_q, self_terms = lax.scan(
        self_step, jnp.zeros((row_count, tok_shard, width), jnp.float32), block_ids
    )
    grad_self_kv = lax.psum_scatter(
        self_terms.astype(jnp.bfloat16), "blk", scatter_dimension=0, tiled=True
    ).astype(jnp.float32)[0]
    low_self_q = grad_self_q.astype(jnp.bfloat16)
    low_self_k = grad_self_kv[..., :width].astype(jnp.bfloat16)
    low_self_v = grad_self_kv[..., width:].astype(jnp.bfloat16)
    grad_self_query = weight_grad(normed_self, low_self_q)
    grad_self_key = weight_grad(normed_self, low_self_k)
    grad_self_value = weight_grad(normed_self, low_self_v)
    grad_normed = (
        back_project(low_self_q, self_query)
        + back_project(low_self_k, self_key)
        + back_project(low_self_v, self_value)
    )
    grad_first, grad_gain_self = norm_back(residual, gain_self, grad_normed)
    input_grad = grad_self_res + grad_first
    matrices = (
        grad_self_query,
        grad_self_key,
        grad_self_value,
        grad_self_output,
        grad_cross_query,
        grad_cross_key,
        grad_cross_value,
        grad_cross_output,
        grad_feed_in,
        grad_feed_out,
    )
    spread_mats = tuple((spread_matrix(matrix, row_split, block_count) for matrix in matrices))
    spread_gains = tuple(
        (
            spread_gain(vector, row_split, block_count)
            for vector in (grad_gain_self, grad_gain_cross, grad_gain_ff)
        )
    )
    summed = (
        lax.psum_scatter(spread_mats[0], ("rows", "blk"), scatter_dimension=0, tiled=True),
        lax.psum_scatter(spread_mats[1], ("rows", "blk"), scatter_dimension=0, tiled=True),
        lax.psum_scatter(spread_mats[2], ("rows", "blk"), scatter_dimension=0, tiled=True),
        lax.psum_scatter(spread_mats[3], ("rows", "blk"), scatter_dimension=0, tiled=True),
        lax.psum_scatter(spread_mats[4], ("rows", "blk"), scatter_dimension=0, tiled=True),
        lax.psum_scatter(spread_mats[5], ("rows", "blk"), scatter_dimension=0, tiled=True),
        lax.psum_scatter(spread_mats[6], ("rows", "blk"), scatter_dimension=0, tiled=True),
        lax.psum_scatter(spread_mats[7], ("rows", "blk"), scatter_dimension=0, tiled=True),
        lax.psum_scatter(spread_mats[8], ("rows", "blk"), scatter_dimension=0, tiled=True),
        lax.psum_scatter(spread_mats[9], ("rows", "blk"), scatter_dimension=0, tiled=True),
        lax.psum_scatter(spread_gains[0], ("rows", "blk"), scatter_dimension=0, tiled=True),
        lax.psum_scatter(spread_gains[1], ("rows", "blk"), scatter_dimension=0, tiled=True),
        lax.psum_scatter(spread_gains[2], ("rows", "blk"), scatter_dimension=0, tiled=True),
    )
    return (
        output,
        input_grad,
        encoded_grad,
        summed[0][0],
        summed[1][0],
        summed[2][0],
        summed[3][0],
        summed[4][0],
        summed[5][0],
        summed[6][0],
        summed[7][0],
        summed[8][0],
        summed[9][0],
        summed[10][0],
        summed[11][0],
        summed[12][0],
    )


BF16 = jnp.bfloat16
F32 = jnp.float32
LANES = 128
HALF = 2 * LANES + LANES
CORE_SWAP = ((0, 1), (1, 0), (2, 3), (3, 2))
CHIP_SWAP = ((0, 2), (2, 0), (1, 3), (3, 1))


def dot_nn(left, right):
    return jnp.dot(left, right, preferred_element_type=F32)


def dot_nt(left, right):
    return lax.dot_general(left, right, (((1,), (1,)), ((), ())), preferred_element_type=F32)


def dot_tn(left, right):
    return lax.dot_general(left, right, (((0,), (0,)), ((), ())), preferred_element_type=F32)


def whole(array):
    rank = len(array.shape)
    return pl.BlockSpec(array.shape, lambda *_: (0,) * rank)


def struct(shape, dtype):
    return jax.ShapeDtypeStruct(shape, dtype)


def run_kernel(name, body, scalars, args, in_specs, outs, out_specs, grid=(1,), scratch=(), flops=0, after=(), vmem=58):
    moved = sum(a.size * a.dtype.itemsize for a in args)
    if after:
        inner, given = (body, len(args))

        def body(s, *refs):
            inner(s, *refs[:given], *refs[given + len(after) :])

        args = (*args, *after)
        in_specs = [*in_specs, *([pl.BlockSpec(memory_space=pl.ANY)] * len(after))]
    moved += sum(o.size * o.dtype.itemsize for o in outs)
    return pl.pallas_call(
        body,
        grid_spec=pltpu.PrefetchScalarGridSpec(
            num_scalar_prefetch=1,
            grid=grid,
            in_specs=list(in_specs),
            out_specs=list(out_specs),
            scratch_shapes=list(scratch),
        ),
        out_shape=list(outs),
        compiler_params=pltpu.CompilerParams(vmem_limit_bytes=vmem << 20),
        name=name,
    )(scalars, *args)


def unit_norm(values):
    scale = lax.rsqrt(jnp.mean(values * values, axis=-1, keepdims=True) + 1e-06)
    return (values * scale, scale)


def norm_pull(values, gain_vec, grad_out):
    normal, scale = unit_norm(values)
    scaled = grad_out * gain_vec
    inner = jnp.mean(scaled * normal, axis=-1, keepdims=True)
    return (scale * (scaled - normal * inner), jnp.sum(grad_out * normal, axis=0, keepdims=True))


def head_lanes():
    lane = lax.broadcasted_iota(jnp.int32, (1, LANES), 1)
    return (lane, (lane < HEAD_DIM, lane >= HEAD_DIM))


def only(keep, values):
    return jnp.where(keep, values, jnp.zeros_like(values))


def soft_block(queries, marks, keys, values):
    lane, masks = head_lanes()
    attended, sums = ([], [])
    for keep in masks:
        scores = dot_nt(jnp.concatenate([only(keep, queries), marks], axis=1), keys)
        top = jnp.max(scores, axis=1, keepdims=True)
        weights = jnp.exp(scores - top)
        total = jnp.sum(weights, axis=1, keepdims=True)
        attended.append(dot_nn(weights.astype(BF16), values) / total)
        sums.append(top + jnp.log(total))
    return (jnp.where(masks[0], *attended), jnp.where(masks[0], *sums))


def causal_block(queries, marks, keys, values):
    lane, masks = head_lanes()
    rows, cols = queries.shape[0], keys.shape[0]
    flipped = values.T
    attended, sums = ([], [])
    for at, keep in enumerate(masks):
        scores = dot_nt(keys, jnp.concatenate([only(keep, queries), marks], axis=1))
        at_row = lax.broadcasted_iota(jnp.int32, (rows, rows), 0)
        at_col = lax.broadcasted_iota(jnp.int32, (rows, rows), 1)
        last = jnp.where(at_row <= at_col, scores[cols - rows :, :], NEG_FILL)
        scores = last if cols == rows else jnp.concatenate([scores[: cols - rows, :], last], axis=0)
        top = jnp.max(scores, axis=0, keepdims=True)
        weights = jnp.exp(scores - top)
        total = jnp.sum(weights, axis=0, keepdims=True)
        head = flipped[at * HEAD_DIM : (at + 1) * HEAD_DIM, :]
        attended.append(dot_nn(head, weights.astype(BF16)) / total)
        sums.append(jnp.broadcast_to(top + jnp.log(total), (HEAD_DIM, rows)))
    return (jnp.concatenate(attended, axis=0).T, jnp.concatenate(sums, axis=0).T)


def three_parts(spread):
    high = spread.astype(BF16)
    rest = spread - high.astype(F32)
    middle = rest.astype(BF16)
    return (-high, -middle, -(rest - middle.astype(F32)).astype(BF16))


def put_parts(lane, head, parts, base):
    for at, part in enumerate(parts):
        base = jnp.where(lane == head * HEAD_DIM + 3 + at, part, base)
    return base


def ones_lanes(lane):
    place = lane % HEAD_DIM
    return (place >= 3) & (place < 6)


def head_totals(product):
    high = product.astype(BF16)
    low = (product - high.astype(F32)).astype(BF16)
    at_row = lax.broadcasted_iota(jnp.int32, (2 * LANES, LANES), 0) % LANES
    at_col = lax.broadcasted_iota(jnp.int32, (2 * LANES, LANES), 1)
    same = jnp.where((at_row < HEAD_DIM) == (at_col < HEAD_DIM), 1.0, 0.0).astype(BF16)
    return dot_nn(jnp.concatenate([high, low], axis=1), same)


def pull_block(queries, marks, keys, key_marks, values, grads, attended, sums, causal):
    lane, masks = head_lanes()
    rows, cols = queries.shape[0], keys.shape[0]
    wide_keys = jnp.concatenate([keys, key_marks], axis=1)
    ones = jnp.where(ones_lanes(lane), 1.0, 0.0).astype(BF16)
    wide_values = jnp.concatenate([values, jnp.broadcast_to(ones, (cols, LANES))], axis=1)
    delta_parts = three_parts(head_totals(grads.astype(F32) * attended))
    sum_parts = three_parts(sums)
    flipped = keys.T
    grad_queries = []
    grad_keys = grad_values = None
    for at, keep in enumerate(masks):
        query, grad = (only(keep, queries), only(keep, grads))
        wide_query = jnp.concatenate([query, put_parts(lane, at, sum_parts, marks)], axis=1)
        wide_grad = jnp.concatenate([grad, put_parts(lane, at, delta_parts, jnp.zeros_like(marks))], axis=1)
        probs = jnp.exp(dot_nt(wide_keys, wide_query))
        if causal:
            at_row = lax.broadcasted_iota(jnp.int32, (rows, rows), 0)
            at_col = lax.broadcasted_iota(jnp.int32, (rows, rows), 1)
            last = jnp.where(at_row <= at_col, probs[cols - rows :, :], 0.0)
            probs = last if cols == rows else jnp.concatenate([probs[: cols - rows, :], last], axis=0)
        grad_scores = (probs * dot_nt(wide_values, wide_grad)).astype(BF16)
        grad_queries.append(dot_nn(flipped, grad_scores))
        key_part = dot_nn(grad_scores, query)
        value_part = dot_nn(probs.astype(BF16), grad)
        grad_keys = key_part if at == 0 else grad_keys + key_part
        grad_values = value_part if at == 0 else grad_values + value_part
    sub = lax.broadcasted_iota(jnp.int32, (LANES, 1), 0)
    return (jnp.where(sub < HEAD_DIM, *grad_queries).T * SCALE, grad_keys, grad_values)


def pair_columns(array, group=0):
    first = group * (HALF // LANES)
    return pl.BlockSpec((array.shape[0], LANES), lambda p, _: (0, p + first))


def query_marks(labels):
    lane = lax.broadcasted_iota(jnp.int32, (LANES, 1), 0)
    return jnp.where(labels == lane, 1.0, 0.0).T.astype(BF16)


def key_marks(labels):
    lane = lax.broadcasted_iota(jnp.int32, (LANES, 1), 0)
    closed = jnp.where(labels != lane, NEG_FILL, 0.0)
    return jnp.where(lane < 3, closed, jnp.where(ones_lanes(lane), 1.0, 0.0)).T.astype(BF16)


def doc_marks(label_ref, tok, enc):
    first = -(-tok // LANES) * LANES
    doc = label_ref[:, pl.ds(first + enc, LANES)][:, 0:1]
    return key_marks(jnp.where(label_ref[:, pl.ds(first, enc)] == 1, doc, -1))


def pair_lanes(group=0):
    return pl.ds(pl.multiple_of(pl.program_id(0) * LANES + group * HALF, LANES), LANES)


def side_by_side(s, sources, target):
    columns = pl.ds(pl.multiple_of(s[0] * HALF, LANES), HALF)
    return (
        [source.at[:, columns] for source in sources],
        [target.at[:, pl.ds(at * HALF, HALF)] for at in range(len(sources))],
    )


def column_block(array):
    return pl.BlockSpec((array.shape[0], HALF), lambda _, s: (0, s[0]))


def any_place(_):
    return pl.BlockSpec(memory_space=pl.ANY)


def copies(sources, targets, semaphores):
    return [pltpu.make_async_copy(src, dst, semaphores.at[at]) for at, (src, dst) in enumerate(zip(sources, targets))]


def find_passages(place, tok, enc, labels, after=()):
    spot = -(-tok // LANES) * LANES + enc

    def body(s, own_ref, *refs):
        label_refs, out_ref = refs[:4], refs[4]
        own = own_ref[:, pl.ds(0, tok)]
        used = [jnp.max(jnp.where(own == ref[0, spot], 1, 0)) for ref in label_refs]
        total = used[0] + used[1] + used[2] + used[3]
        out_ref[0] = s[0]
        out_ref[1] = s[1]
        out_ref[6] = total
        out_ref[7] = 0
        ahead, behind = (jnp.int32(0), total)
        for slot in range(4):
            out_ref[2 + jnp.where(used[slot] == 1, ahead, behind)] = jnp.int32(slot)
            ahead, behind = (ahead + used[slot], behind + 1 - used[slot])

    smem = pl.BlockSpec(memory_space=pltpu.SMEM)
    return run_kernel(
        "find_passages", body, place, (labels[0], *labels), [whole(labels[0])] + [smem] * 4, [struct((8,), jnp.int32)],
        [smem], after=after,
    )[0]


def write_projections(s, mine_ref, other_ref, gain, weight_refs, normed_ref, out_ref, scaled):
    tok = mine_ref.shape[0]
    parts = ((mine_ref, s[0]), (other_ref, 1 - s[0]))
    for source, part in parts:
        rows = pl.ds(pl.multiple_of(part * tok, tok), tok)
        normed_ref[rows, :] = (unit_norm(source[...].astype(F32))[0] * gain).astype(BF16)
    weight = jnp.concatenate([ref[...] for ref in weight_refs], axis=1)
    for _, part in parts:
        rows = pl.ds(pl.multiple_of(part * tok, tok), tok)
        result = dot_nn(normed_ref[rows, :], weight)
        if scaled:
            out_ref[rows, pl.ds(0, scaled)] = (result[:, :scaled] * SCALE).astype(BF16)
        out_ref[rows, pl.ds(scaled, result.shape[1] - scaled)] = result[:, scaled:].astype(BF16)


def near_part(place, mine, other, gain_vec, weights, labels, passages, passage_weights, after=()):
    tok, width = mine.shape
    both = 2 * tok
    enc = passages[0].shape[0]
    third = width // 3

    def body(
        s, mine_ref, other_ref, gain_ref, wq_ref, wk_ref, wv_ref, own_ref, core_ref, e0_ref, e1_ref, ck_ref, cv_ref,
        h_ref, qkv_ref, m_ref, km_ref, out_ref, sum_ref, pk_ref, pv_ref,
    ):
        @pl.when(pl.program_id(0) == 0)
        def _():
            for source, part in ((own_ref, s[0]), (core_ref, 1 - s[0])):
                rows = pl.ds(pl.multiple_of(part * tok, tok), tok)
                m_ref[rows, :] = query_marks(source[:, pl.ds(0, tok)])
                km_ref[rows, :] = key_marks(source[:, pl.ds(0, tok)])
            write_projections(
                s, mine_ref, other_ref, gain_ref[...].reshape(1, width), (wq_ref, wk_ref, wv_ref), h_ref, qkv_ref, HALF
            )

        query_pair, key_pair, value_pair = (pair_lanes(group) for group in range(3))
        for at in (0, 1):
            rows, seen = (pl.ds(at * tok, tok), pl.ds(0, (at + 1) * tok))
            wide = jnp.concatenate([qkv_ref[seen, key_pair], km_ref[seen, :]], axis=1)
            out_ref[rows, :], sum_ref[rows, :] = causal_block(
                qkv_ref[rows, query_pair], m_ref[rows, :], wide, qkv_ref[seen, value_pair]
            )
        for at, source in enumerate((e0_ref, e1_ref)):
            rows = pl.ds(at * enc, enc)
            pk_ref[rows, :] = dot_nn(source[...], ck_ref[...]).astype(BF16)
            pv_ref[rows, :] = dot_nn(source[...], cv_ref[...]).astype(BF16)

    args = (mine, other, gain_vec, *weights, *labels, *passages, *passage_weights)
    specs = [whole(a) for a in args]
    specs[3:6] = [column_block(w) for w in weights]
    specs[10:12] = [pl.BlockSpec((width, third), lambda p, _: (0, p))] * 2
    outs = [struct((both, width), BF16), struct((both, 3 * HALF), BF16)] + [struct((both, LANES), BF16)] * 2
    outs += [struct((both, HALF), F32)] * 2 + [struct((2 * enc, width), BF16)] * 2
    return run_kernel(
        "near_part", body, place, args, specs, outs,
        [whole(o) for o in outs[:4]]
        + [pair_columns(o) for o in outs[4:6]]
        + [pl.BlockSpec((2 * enc, third), lambda p, _: (0, p))] * 2,
        grid=(HALF // LANES,), after=after, flops=both * both * 6 * 2 * HALF,
    )


def far_part(place, mine, other, gain_vec, weights, queries, marks, labels, near_out, near_sum, after=()):
    tok, width = mine.shape
    both = 2 * tok

    def body(
        s, mine_ref, other_ref, gain_ref, wk_ref, wv_ref, q_ref, m_ref, lx_ref, ld_ref, no_ref, ns_ref,
        h_ref, kv_ref, km_ref, out_ref, sum_ref, keep_ref, send_ref,
    ):
        @pl.when(pl.program_id(0) == 0)
        def _():
            for source, part in ((lx_ref, s[0]), (ld_ref, 1 - s[0])):
                rows = pl.ds(pl.multiple_of(part * tok, tok), tok)
                km_ref[rows, :] = key_marks(source[:, pl.ds(0, tok)])

        def write(at, out, log_sum):
            rows = pl.ds(at * tok, tok)
            out_ref[rows, :] = out
            sum_ref[rows, :] = log_sum

            @pl.when(s[0] == at)
            def _():
                keep_ref[...] = out.astype(BF16)

            @pl.when(s[0] != at)
            def _():
                send_ref[...] = out.astype(BF16)

        @pl.when(s[1] == 0)
        def _():
            for at in (0, 1):
                rows = pl.ds(at * tok, tok)
                write(at, no_ref[rows, :], ns_ref[rows, :])

            @pl.when(pl.program_id(0) == 0)
            def _():
                for ref in (h_ref, kv_ref):
                    ref[...] = jnp.zeros_like(ref)

        @pl.when(s[1] != 0)
        def _():
            @pl.when(pl.program_id(0) == 0)
            def _():
                write_projections(
                    s, mine_ref, other_ref, gain_ref[...].reshape(1, width), (wk_ref, wv_ref), h_ref, kv_ref, 0
                )

            wide = jnp.concatenate([kv_ref[:, pair_lanes()], km_ref[...]], axis=1)
            for at in (0, 1):
                rows = pl.ds(at * tok, tok)
                out, log_sum = soft_block(q_ref[rows, :], m_ref[rows, :], wide, kv_ref[:, pair_lanes(1)])
                near_log = ns_ref[rows, :]
                top = jnp.maximum(near_log, log_sum)
                near_share, far_share = (jnp.exp(near_log - top), jnp.exp(log_sum - top))
                total = near_share + far_share
                write(at, (no_ref[rows, :] * near_share + out * far_share) / total, top + jnp.log(total))

    args = (mine, other, gain_vec, *weights, queries, marks, *labels, near_out, near_sum)
    specs = [whole(a) for a in args]
    specs[3:5] = [column_block(w) for w in weights]
    for at in (5, 9, 10):
        specs[at] = pair_columns(args[at])
    outs = [struct((both, width), BF16), struct((both, 2 * HALF), BF16), struct((both, LANES), BF16)]
    outs += [struct((both, HALF), F32)] * 2 + [struct((tok, HALF), BF16)] * 2
    return run_kernel(
        "far_part", body, place, args, specs, outs, [whole(o) for o in outs[:3]] + [pair_columns(o) for o in outs[3:]],
        grid=(HALF // LANES,), after=after, flops=both * both * 8 * 2 * HALF,
    )


def gather_slots(s, enc, target, first_ref, second_ref, lanes=slice(None)):
    for at in range(4):
        slot = s[2 + at]
        rows = pl.ds(at * enc, enc)

        @pl.when(slot < 2)
        def _():
            target[rows, :] = first_ref[pl.ds(pl.multiple_of(slot * enc, enc), enc), :]

        @pl.when(slot >= 2)
        def _():
            target[rows, :] = second_ref[pl.ds(pl.multiple_of((slot - 2) * enc, enc), enc), lanes]


def by_count(s, work):
    pl.when(s[6] <= 2)(lambda: work(2))
    pl.when(s[6] >= 3)(lambda: work(3))


def cross_part(
    place, inputs, ctx_keep, ctx_recv, out_weight, gain_vec, query_weight, first, second, key_weight, value_weight,
    keys, values, labels, after=(),
):
    tok, width = inputs.shape
    enc = first.shape[0]

    def body(
        s, in_ref, keep_ref, recv_ref, wa_ref, wb_ref, gain_ref, wq_any, first_any, second_any, wk_any, wv_any, k0_ref, v0_ref,
        l0_ref, l1_ref, l2_ref, l3_ref,
        x_ref, h_ref, q_ref, ctx_ref, k1_ref, v1_ref, m_ref, km0_ref, km1_ref, cctx_ref, out_ref, sum_ref,
        all_k, all_v, wq_ref, first_ref, second_ref, wk_ref, wv_ref, semaphores,
    ):
        keep = pl.ds(0, LANES)

        @pl.when(pl.program_id(0) == 0)
        def _():
            later = copies(
                (wq_any, first_any, wk_any, wv_any, second_any), (wq_ref, first_ref, wk_ref, wv_ref, second_ref), semaphores
            )
            for copy in later:
                copy.start()
            total = dot_nn(keep_ref[...], wa_ref[...]) + dot_nn(recv_ref[...], wb_ref[...])
            residual = in_ref[...].astype(F32) + total
            x_ref[...] = residual
            normed = (unit_norm(residual)[0] * gain_ref[...].reshape(1, width)).astype(BF16)
            h_ref[...] = normed
            later[0].wait()
            q_ref[...] = (dot_nn(normed, wq_ref[...]) * SCALE).astype(BF16)
            ctx_ref[:, pl.ds(pl.multiple_of(s[0] * HALF, LANES), HALF)] = keep_ref[...]
            ctx_ref[:, pl.ds(pl.multiple_of((1 - s[0]) * HALF, LANES), HALF)] = recv_ref[...]
            for copy in later[1:]:
                copy.wait()
            for at, source in enumerate((first_ref, second_ref)):
                rows = pl.ds(at * enc, enc)
                k1_ref[rows, :] = dot_nn(source[...], wk_ref[...]).astype(BF16)
                v1_ref[rows, :] = dot_nn(source[...], wv_ref[...]).astype(BF16)
            m_ref[...] = query_marks(l0_ref[:, pl.ds(0, tok)])
            for target, low, high in ((km0_ref, l0_ref, l1_ref), (km1_ref, l2_ref, l3_ref)):
                target[pl.ds(0, enc), :] = doc_marks(low, tok, enc)
                target[pl.ds(enc, enc), :] = doc_marks(high, tok, enc)
            gather_slots(s, enc, all_k.at[:, pl.ds(LANES, LANES)], km0_ref, km1_ref)

        pair = pair_lanes()
        gather_slots(s, enc, all_k.at[:, keep], k0_ref, k1_ref, pair)
        gather_slots(s, enc, all_v, v0_ref, v1_ref, pair)

        def work(count):
            seen = pl.ds(0, count * enc)
            out, log_sum = soft_block(q_ref[:, pair], m_ref[...], all_k[seen, :], all_v[seen, :])
            cctx_ref[...] = out.astype(BF16)
            out_ref[...] = out
            sum_ref[...] = log_sum

        by_count(s, work)

    args = (
        inputs, ctx_keep, ctx_recv, out_weight, out_weight, gain_vec, query_weight, first, second, key_weight, value_weight,
        keys, values, *labels,
    )
    specs = [whole(a) for a in args]
    specs[3] = pl.BlockSpec((HALF, width), lambda _, s: (s[0], 0))
    specs[4] = pl.BlockSpec((HALF, width), lambda _, s: (1 - s[0], 0))
    specs[6:11] = [any_place(a) for a in args[6:11]]
    specs[11], specs[12] = pair_columns(keys), pair_columns(values)
    outs = [struct((tok, width), F32)] + [struct((tok, width), BF16)] * 3 + [struct((2 * enc, width), BF16)] * 2
    outs += [struct((tok, LANES), BF16)] + [struct((2 * enc, LANES), BF16)] * 2
    outs += [struct((tok, width), BF16)] + [struct((tok, width), F32)] * 2
    return run_kernel(
        "cross_part", body, place, args, specs, outs, [whole(o) for o in outs[:9]] + [pair_columns(o) for o in outs[9:]],
        grid=(width // LANES,),
        scratch=[pltpu.VMEM((4 * enc, 2 * LANES), BF16), pltpu.VMEM((4 * enc, LANES), BF16)]
        + [pltpu.VMEM(a.shape, a.dtype) for a in args[6:11]]
        + [pltpu.SemaphoreType.DMA((5,))],
        after=after, flops=tok * 2.5 * enc * 8 * 2 * width + 12 * tok * width * width,
    )


def cross_back(place, queries, keys, values, marks, key_marks, grads, attended, sums, residual, grad_res, query_weight, gains, out_weight, after=()):
    tok, width = queries.shape
    enc = keys[0].shape[0] // 2
    last = width // LANES - 1

    def body(
        s, q_ref, k0_ref, k1_ref, v0_ref, v1_ref, m_ref, km0_ref, km1_ref, g_ref, at_ref, ls_ref, gain_ref,
        x_any, dx_any, wq_any, wo_any, dq_ref, dk_ref, dv_ref, dx1_ref, low_ref, gain_grad_ref, keep_ref, send_ref,
        all_k, all_v, all_m, x_ref, dx_ref, wq_ref, wo_ref, semaphores,
    ):
        later = copies((x_any, dx_any, wq_any, wo_any), (x_ref, dx_ref, wq_ref, wo_ref), semaphores)

        @pl.when(pl.program_id(0) == 0)
        def _():
            for copy in later:
                copy.start()
            gather_slots(s, enc, all_m, km0_ref, km1_ref)

        gather_slots(s, enc, all_k, k0_ref, k1_ref)
        gather_slots(s, enc, all_v, v0_ref, v1_ref)
        pair = pair_lanes()

        def work(count):
            seen = pl.ds(0, count * enc)
            grad_q, grad_k, grad_v = pull_block(
                q_ref[...], m_ref[...], all_k[seen, :], all_m[seen, :], all_v[seen, :], g_ref[...], at_ref[...],
                ls_ref[...], False,
            )
            dq_ref[:, pair] = grad_q.astype(BF16)
            low_k, low_v = (grad_k.astype(BF16), grad_v.astype(BF16))
            for at in range(4):
                rows = pl.ds(pl.multiple_of(s[2 + at] * enc, enc), enc)
                if at < count:
                    dk_ref[rows, :] = low_k[at * enc : (at + 1) * enc, :]
                    dv_ref[rows, :] = low_v[at * enc : (at + 1) * enc, :]
                else:
                    dk_ref[rows, :] = jnp.zeros((enc, LANES), BF16)
                    dv_ref[rows, :] = jnp.zeros((enc, LANES), BF16)

        by_count(s, work)

        @pl.when(pl.program_id(0) == last)
        def _():
            for copy in later:
                copy.wait()
            back, gain_grad_ref[...] = norm_pull(x_ref[...], gain_ref[...].reshape(1, width), dot_nt(dq_ref[...], wq_ref[...]))
            grad_x = dx_ref[...] + back
            dx1_ref[...] = grad_x
            low = grad_x.astype(BF16)
            low_ref[...] = low
            for target, half in ((keep_ref, s[0]), (send_ref, 1 - s[0])):
                rows = pl.ds(pl.multiple_of(half * HALF, HALF), HALF)
                target[...] = dot_nt(low, wo_ref[rows, :]).astype(BF16)

    late = (residual, grad_res, query_weight, out_weight)
    args = (queries, *keys, *values, marks, *key_marks, grads, attended, sums, gains, *late)
    specs = [pair_columns(a) for a in args]
    for at in (5, 6, 7, 11):
        specs[at] = whole(args[at])
    specs[12:] = [any_place(a) for a in late]
    outs = [struct((tok, width), BF16)] + [struct((4 * enc, width), BF16)] * 2
    outs += [struct((tok, width), F32), struct((tok, width), BF16), struct((1, width), F32)]
    outs += [struct((tok, HALF), BF16)] * 2
    out_specs = [whole(o) for o in outs]
    out_specs[1], out_specs[2] = pair_columns(outs[1]), pair_columns(outs[2])
    return run_kernel(
        "cross_back", body, place, args, specs, outs, out_specs,
        grid=(width // LANES,),
        scratch=[pltpu.VMEM((4 * enc, LANES), BF16)] * 3
        + [pltpu.VMEM(a.shape, a.dtype) for a in late]
        + [pltpu.SemaphoreType.DMA((len(late),))],
        after=after, flops=tok * 2.5 * enc * 20 * 2 * width,
    )


def write_normed_grads(s, tok, h_ref, gain, grad_ref, weight_ref, keep_ref, send_ref, gain_grad_ref):
    running = None
    for target, part in ((keep_ref, s[0]), (send_ref, 1 - s[0])):
        rows = pl.ds(pl.multiple_of(part * tok, tok), tok)
        value = dot_nt(grad_ref[rows, :], weight_ref[...])
        target[...] = value.astype(BF16)
        inner = jnp.sum(value * h_ref[rows, :].astype(F32), axis=0, keepdims=True)
        running = inner if running is None else running + inner
    gain_grad_ref[...] = running / gain


def far_back(place, qkv, far_kv, marks, key_marks, grad_keep, grad_recv, attended, sums, gains, normed, weights, after=()):
    both, width = normed.shape
    tok = both // 2
    last = HALF // LANES - 1

    def body(
        s, q_ref, k_ref, v_ref, m_ref, km_ref, gk_ref, gr_ref, at_ref, ls_ref, gain_ref, h_any, wk_any, wv_any,
        dq_ref, dkv_ref, keep_ref, send_ref, gain_grad_ref, h_ref, weight_ref, semaphores,
    ):
        sources, targets = side_by_side(s, (wk_any, wv_any), weight_ref)
        later = copies((h_any, *sources), (h_ref, *targets), semaphores)

        @pl.when(s[1] != 0)
        def _():
            @pl.when(pl.program_id(0) == 0)
            def _():
                for copy in later:
                    copy.start()

            sum_k = sum_v = None
            for at in (0, 1):
                rows = pl.ds(at * tok, tok)
                grads = jnp.where(s[0] == at, gk_ref[...], gr_ref[...])
                dq_ref[rows, :], grad_k, grad_v = pull_block(
                    q_ref[rows, :], m_ref[rows, :], k_ref[...], km_ref[...], v_ref[...], grads, at_ref[rows, :],
                    ls_ref[rows, :], False,
                )
                sum_k = grad_k if at == 0 else sum_k + grad_k
                sum_v = grad_v if at == 0 else sum_v + grad_v
            dkv_ref[:, pair_lanes()] = sum_k.astype(BF16)
            dkv_ref[:, pair_lanes(1)] = sum_v.astype(BF16)

            @pl.when(pl.program_id(0) == last)
            def _():
                for copy in later:
                    copy.wait()
                write_normed_grads(
                    s, tok, h_ref, gain_ref[...].reshape(1, width), dkv_ref, weight_ref, keep_ref, send_ref, gain_grad_ref
                )

        @pl.when(s[1] == 0)
        def _():
            dq_ref[...] = jnp.zeros_like(dq_ref)
            for ref in (dkv_ref, keep_ref, send_ref, gain_grad_ref):
                ref[...] = jnp.zeros_like(ref)

    args = (qkv, far_kv, far_kv, marks, key_marks, grad_keep, grad_recv, attended, sums, gains, normed, *weights)
    specs = [pair_columns(a) for a in args]
    specs[2] = pair_columns(far_kv, 1)
    specs[3], specs[4], specs[9] = whole(marks), whole(key_marks), whole(gains)
    specs[10:] = [any_place(a) for a in args[10:]]
    outs = [struct((both, HALF), F32), struct((both, 2 * HALF), BF16)]
    outs += [struct((tok, width), BF16)] * 2 + [struct((1, width), F32)]
    return run_kernel(
        "far_back", body, place, args, specs, outs, [pair_columns(outs[0])] + [whole(o) for o in outs[1:]],
        grid=(HALF // LANES,),
        scratch=[pltpu.VMEM((both, width), BF16), pltpu.VMEM((width, 2 * HALF), BF16), pltpu.SemaphoreType.DMA((3,))],
        after=after, flops=both * both * 20 * 2 * HALF,
    )


def write_square(s, value, keep, send, first, order=0):
    rows = value.shape[0] // 16
    side = HALF // 2

    def write(target, half):
        for at in range(8):
            high, low, far = (at // 4, (at // 2) % 2, at % 2)
            for chip in range(value.shape[1] // HALF):
                columns = slice(chip * HALF + half * side, chip * HALF + (half + 1) * side)
                place = ((far, chip, low, high), (low, far, chip, high), (far, low, chip, high))[order]
                for part in range(2):
                    piece = value[(2 * at + part) * rows : (2 * at + part + 1) * rows, columns].astype(BF16)
                    target[*place, pl.ds(first, rows), pl.ds(part * side, side)] = piece

    @pl.when(s[0] == 0)
    def _():
        write(keep, 0)
        write(send, 1)

    @pl.when(s[0] != 0)
    def _():
        write(keep, 1)
        write(send, 0)


def near_back(
    place, qkv, marks, key_marks, grad_keep, grad_recv, attended, sums, carried, gains,
    normed, far_normed, weights, far_grads, gain_grads, after=(),
):
    both, width = normed.shape
    tok = both // 2
    last = HALF // LANES - 1
    late_shapes = [(both, width)] * 2 + [(width, 3 * HALF), (both, 2 * HALF)]

    def body(
        s, q_ref, k_ref, v_ref, m_ref, km_ref, gk_ref, gr_ref, at_ref, ls_ref, ca_ref, gain_ref,
        gs_ref, gc_ref, gf_ref, h_any, fh_any, wq_any, wk_any, wv_any, fkv_any,
        keep_ref, send_ref, keep4, send4,
        dqkv, sum_k, sum_v, gain_grad_ref, gain_rows, h_ref, fh_ref, weight_ref, fkv_ref, semaphores,
    ):
        query_pair, key_pair, value_pair = (pair_lanes(group) for group in range(3))
        sources, targets = side_by_side(s, (wq_any, wk_any, wv_any), weight_ref)
        later = copies((h_any, fh_any, *sources, fkv_any), (h_ref, fh_ref, *targets, fkv_ref), semaphores)

        @pl.when(pl.program_id(0) == 0)
        def _():
            for copy in later:
                copy.start()

        for at in (0, 1):
            rows = pl.ds(at * tok, tok)
            count = (at + 1) * tok
            seen = pl.ds(0, count)
            grads = jnp.where(s[0] == at, gk_ref[...], gr_ref[...])
            grad_q, grad_k, grad_v = pull_block(
                q_ref[rows, :], m_ref[rows, :], k_ref[seen, :], km_ref[seen, :], v_ref[seen, :], grads,
                at_ref[rows, :], ls_ref[rows, :], True,
            )
            dqkv[rows, query_pair] = (grad_q + ca_ref[rows, :]).astype(BF16)
            if at == 0:
                sum_k[...] = grad_k
                sum_v[...] = grad_v
            else:
                dqkv[pl.ds(0, tok), key_pair] = (sum_k[...] + grad_k[:tok]).astype(BF16)
                dqkv[pl.ds(0, tok), value_pair] = (sum_v[...] + grad_v[:tok]).astype(BF16)
                dqkv[pl.ds(tok, tok), key_pair] = grad_k[tok:].astype(BF16)
                dqkv[pl.ds(tok, tok), value_pair] = grad_v[tok:].astype(BF16)

        @pl.when(pl.program_id(0) == last)
        def _():
            for copy in later:
                copy.wait()
            write_normed_grads(
                s, tok, h_ref, gain_ref[...].reshape(1, width), dqkv, weight_ref, keep_ref, send_ref, gain_grad_ref
            )
            rows = width // 16
            near_value = dot_tn(h_ref[...], dqkv[...])
            far_value = dot_tn(fh_ref[...], fkv_ref[...])
            write_square(s, near_value[:, :HALF], keep4, send4, 0)
            for at in (1, 2):
                value = near_value[:, at * HALF : (at + 1) * HALF] + far_value[:, (at - 1) * HALF : at * HALF]
                write_square(s, value, keep4, send4, at * rows)
            gain_rows[...] = jnp.zeros_like(gain_rows)
            gain_rows[0:1, :] = gain_grad_ref[...] + gs_ref[...]
            gain_rows[1:2, :] = gc_ref[...]
            gain_rows[2:3, :] = gf_ref[...]
            low = gain_rows[...].astype(BF16)
            piece = width // 8
            at_row = lax.broadcasted_iota(jnp.int32, (width, HALF), 0)
            at_col = lax.broadcasted_iota(jnp.int32, (width, HALF), 1)
            for at in range(8):
                pick = jnp.where((at_row == at_col + at * piece) & (at_col < piece), 1.0, 0.0).astype(BF16)
                value = dot_nn(low, pick).astype(BF16)
                for target in (keep4, send4):
                    target[at % 2, 0, (at // 2) % 2, at // 4, pl.ds(3 * rows, 16), :] = value

    late = (normed, far_normed, *weights, far_grads)
    args = (
        qkv, qkv, qkv, marks, key_marks, grad_keep, grad_recv, attended, sums, carried, gains, *gain_grads, *late
    )
    specs = [pair_columns(a) for a in args]
    specs[3], specs[4] = whole(marks), whole(key_marks)
    specs[1], specs[2] = pair_columns(qkv, 1), pair_columns(qkv, 2)
    specs[10:14] = [whole(a) for a in args[10:14]]
    specs[14:] = [any_place(a) for a in late]
    outs = [struct((tok, width), BF16)] * 2
    outs += [struct((2, 1, 2, 2, 3 * (width // 16) + 16, HALF), BF16)] * 2
    return run_kernel(
        "near_back", body, place, args, specs, outs, [whole(o) for o in outs],
        grid=(HALF // LANES,),
        scratch=[pltpu.VMEM((both, 3 * HALF), BF16)]
        + [pltpu.VMEM((tok, LANES), F32)] * 2
        + [pltpu.VMEM((1, width), F32), pltpu.VMEM((16, width), F32)]
        + [pltpu.VMEM(shape, BF16) for shape in late_shapes]
        + [pltpu.SemaphoreType.DMA((len(late),))],
        after=after, flops=both * both * 0.75 * 20 * 2 * HALF + 20 * both * width * HALF,
    )


def cross_grads(name, place, pairs, layout, passages=None, after=()):
    width = pairs[0][0][0].shape[1]
    rows = width // 16
    count = len(pairs)
    order, spots, groups = ([], {}, [])
    for left, right in [*pairs, *([] if passages is None else [(passages[:2], passages[2:])])]:
        fresh = []
        for array in (*left, *right):
            if id(array) not in spots:
                spots[id(array)] = len(order)
                fresh.append(len(order))
                order.append(array)
        groups.append((fresh, [spots[id(array)] for array in left], [spots[id(array)] for array in right]))
    given = len(order)
    outs = [struct((2, 2, 2, 2, count * rows, HALF), BF16)] * 2
    if passages is not None:
        enc = passages[0].shape[0] // 4
        outs += [struct((2, enc, width), F32), struct((2, enc, width), BF16)]
    produced = len(outs)

    def body(s, *refs):
        sources, results = refs[:given], refs[given : given + produced]
        held, semaphores = refs[given + produced : -1], refs[-1]
        step = pl.program_id(0)
        moves = copies(sources, held, semaphores)

        @pl.when(step == 0)
        def _():
            for move in moves:
                move.start()

        for at, (fresh, left, right) in enumerate(groups):

            @pl.when(step == at)
            def _(at=at, fresh=fresh, left=left, right=right):
                for spot in fresh:
                    moves[spot].wait()
                if at < count:
                    value = None
                    for part, spot in enumerate(left):
                        tall = held[spot].shape[0]
                        piece = dot_tn(held[spot][...], held[right[0]][pl.ds(part * tall, tall), :])
                        value = piece if value is None else value + piece
                    write_square(s, value, results[0], results[1], 0, layout)
                    return
                for slot in range(4):
                    slots = pl.ds(slot * enc, enc)
                    value = dot_nt(held[left[0]][slots, :], held[right[0]][...])
                    value = value + dot_nt(held[left[1]][slots, :], held[right[1]][...])
                    if slot % 2 == 0:
                        results[2][slot // 2] = value
                    else:
                        results[3][slot // 2] = value.astype(BF16)

    block = pl.BlockSpec((2, 2, 2, 2, rows, HALF), lambda m, _: (0, 0, 0, 0, jnp.minimum(m, count - 1), 0))
    return run_kernel(
        name, body, place, order, [any_place(a) for a in order], outs,
        [block, block, *(whole(o) for o in outs[2:])],
        grid=(len(groups),),
        scratch=[pltpu.VMEM(a.shape, a.dtype) for a in order]
        + [pltpu.SemaphoreType.DMA((given,))],
        after=after,
    )


def passage_grads(place, grad_keys, grad_values, key_weight, value_weight, after=()):
    keys4, width = grad_keys.shape
    enc = keys4 // 4

    def body(s, dk_ref, dv_ref, wk_ref, wv_ref, keep_ref, send_ref):
        value = dot_nt(dk_ref[...], wk_ref[...]) + dot_nt(dv_ref[...], wv_ref[...])

        @pl.when(pl.program_id(0) % 2 == 0)
        def _():
            keep_ref[0] = value

        @pl.when(pl.program_id(0) % 2 != 0)
        def _():
            send_ref[0] = value.astype(BF16)

    args = (grad_keys, grad_values, key_weight, value_weight)
    slot = pl.BlockSpec((enc, width), lambda i, _: (i, 0))
    result = pl.BlockSpec((1, enc, width), lambda i, _: (i // 2, 0, 0))
    outs = [struct((2, enc, width), F32), struct((2, enc, width), BF16)]
    return run_kernel(
        "passage_grads", body, place, args, [slot, slot, whole(key_weight), whole(value_weight)], outs, [result, result],
        grid=(4,), after=after,
    )


def last_pull(place, inputs, gains, grad_res, parts, after=()):
    tok, width = inputs.shape
    steps = 2
    tile = tok // steps

    def body(s, in_ref, gain_ref, dx_ref, *refs):
        part_refs, out_ref = refs[:-1], refs[-1]
        total = part_refs[0][...].astype(F32)
        for ref in part_refs[1:]:
            total = total + ref[...].astype(F32)
        out_ref[...] = dx_ref[...] + norm_pull(in_ref[...].astype(F32), gain_ref[...].reshape(1, width), total)[0]

    args = (inputs, gains, grad_res, *parts)
    block = pl.BlockSpec((tile, width), lambda i, _: (i, 0))
    specs = [block for _ in args]
    specs[1] = whole(gains)
    return run_kernel(
        "last_pull", body, place, args, specs, [struct((tok, width), F32)], [block], grid=(steps,), after=after,
        flops=20 * tok * width,
    )[0]


def rounded(values):
    return lax.reduce_precision(values, 8, 7).astype(BF16)


def add_split(half, keep, recv):
    part = lambda array, at: lax.dynamic_index_in_dim(array, at, 0, False).astype(F32)
    kept = rounded(part(keep, half) + part(recv, half))
    return (kept, rounded(part(keep, 1 - half) + part(recv, 1 - half)))


class Halving:
    def __init__(self, keep, recv, steps):
        self.keep, self.recv, self.steps = (keep, recv, list(steps))

    def step(self, *after):
        half, axis, pairs = self.steps.pop(0)
        keep, recv = (self.keep.reshape(2, -1, HALF), self.recv.reshape(2, -1, HALF))
        if after:
            keep, recv, *_ = lax.optimization_barrier((keep, recv, *after))
        self.keep, send = add_split(half, keep, recv)
        self.recv = lax.ppermute(send, axis, pairs)
        return self.keep


def merge_split(place, step, sums, after=()):
    half, axis, pairs = step
    counts = [a.keep.shape[0] // 4 for a in sums]
    arrays = [array.reshape(2, 2, count, HALF) for a, count in zip(sums, counts) for array in (a.keep, a.recv)]
    starts = [sum(counts[:at]) for at in range(len(counts))]

    def body(s, *refs):
        given, (keep_ref, send_ref) = refs[: len(arrays)], refs[len(arrays) :]
        for target, side in ((keep_ref, s[0]), (send_ref, 1 - s[0])):
            for at, (first, count) in enumerate(zip(starts, counts)):
                for deep in range(2):
                    value = given[2 * at][side, deep].astype(F32) + given[2 * at + 1][side, deep].astype(F32)
                    target[deep, pl.ds(first, count), :] = value.astype(BF16)

    outs = [struct((2, sum(counts), HALF), BF16)] * 2
    keep, send = run_kernel(
        "merge_split", body, half.astype(jnp.int32).reshape(1), arrays, [whole(a) for a in arrays], outs,
        [whole(o) for o in outs], after=after,
    )
    merged = Halving(keep, lax.ppermute(send, axis, pairs), ())
    return merged


def self_start(place, keep4, recv4, after=()):
    cut = 80
    rest = keep4.shape[4] - cut

    def body(s, keep_ref, recv_ref, ak_ref, as_ref, bk_ref, bs_ref):
        for target, side in ((ak_ref, s[2]), (as_ref, 1 - s[2])):
            for slot, source in enumerate((keep_ref, recv_ref)):
                target[slot] = source[side, 0, :, :, pl.ds(0, cut), :]
        late, front, tail = (pl.ds(cut, rest - 16), pl.ds(0, rest - 16), pl.ds(cut + rest - 16, 16))

        @pl.when(s[0] == s[1])
        def _():
            bk_ref[:, :, :, front, :] = keep_ref[:, 0, :, :, late, :]
            bs_ref[:, :, :, front, :] = recv_ref[:, 0, :, :, late, :]

        @pl.when(s[0] != s[1])
        def _():
            bk_ref[:, :, :, front, :] = recv_ref[:, 0, :, :, late, :]
            bs_ref[:, :, :, front, :] = keep_ref[:, 0, :, :, late, :]

        shared = keep_ref[:, 0, :, :, tail, :].astype(F32) + recv_ref[:, 0, :, :, tail, :].astype(F32)
        for target in (bk_ref, bs_ref):
            target[:, :, :, pl.ds(rest - 16, 16), :] = shared.astype(BF16)

    args = (keep4, recv4)
    outs = [struct((2, 2, 2, cut, HALF), BF16)] * 2 + [struct((2, 2, 2, rest, HALF), BF16)] * 2
    return run_kernel(
        "self_start", body, place, args, [whole(a) for a in args], outs, [whole(o) for o in outs], after=after
    )


def both_step(place, first, second, after=()):
    sums = (first, second)
    spots, axes, pairs = zip(*(a.steps.pop(0) for a in sums))
    arrays = [array.reshape(2, -1, HALF) for a in sums for array in (a.keep, a.recv)]

    def body(s, *refs):
        given, outs = refs[:4], refs[4:]
        for at in range(2):
            side = s[spots[at]]
            for target, side in ((outs[2 * at], side), (outs[2 * at + 1], 1 - side)):
                target[...] = (given[2 * at][side].astype(F32) + given[2 * at + 1][side].astype(F32)).astype(BF16)

    outs = [struct(array.shape[1:], BF16) for array in arrays]
    results = run_kernel(
        "both_step", body, place, arrays, [whole(a) for a in arrays], outs,
        [whole(o) for o in outs], after=after,
    )
    for at, a in enumerate(sums):
        a.keep, a.recv = (results[2 * at], lax.ppermute(results[2 * at + 1], axes[at], pairs[at]))
    return results[0]


def finish_sums(name, keep, recv, count, tail=0, after=()):
    rows = keep.shape[0] // 16 // count * 16
    side = HALF // 2

    def body(s, keep_ref, recv_ref, *outs):
        for at in range(count):
            part = pl.ds(at * rows, rows)
            total = keep_ref[part, :].astype(F32) + recv_ref[part, :].astype(F32)
            outs[at][pl.ds(0, rows), :] = total[:, :side]
            outs[at][pl.ds(rows, rows), :] = total[:, side:]
        if tail:
            part = pl.ds(count * rows, 16)
            total = keep_ref[part, :].astype(F32) + recv_ref[part, :].astype(F32)
            for at in range(tail):
                outs[count + at][...] = total[at, : 2 * rows]

    outs = [struct((2 * rows, side), F32)] * count + [struct((2 * rows,), F32)] * tail
    place = jnp.zeros((1,), jnp.int32)
    return run_kernel(
        name, body, place, (keep, recv), [whole(keep), whole(recv)], outs, [whole(o) for o in outs], after=after
    )


def feed_forward(place, residual, context, out_weight, gain_vec, feed_in, feed_out, cotangent, after=()):
    tok, width = residual.shape
    hidden_width = feed_in.shape[1]
    steps = 4
    chunk = hidden_width // steps
    rows_in = width // 8
    side = width // 4

    def body(
        s, x1_ref, ctx_ref, wo_ref, gain_ref, w1_ref, w2_ref, g_ref,
        out_ref, dx_ref, low_ref, dctx_ref, gain_grad_ref, keep_in, send_in, keep_out, send_out,
        x2, normed, normed_flip, grad_flip, sum_out, sum_norm, block_in, block_out, semaphores,
    ):
        step = pl.program_id(0)

        @pl.when(step == 0)
        def _():
            x2[...] = x1_ref[...] + dot_nn(ctx_ref[...], wo_ref[...])
            normed[...] = (unit_norm(x2[...])[0] * gain_ref[...].reshape(1, width)).astype(BF16)
            normed_flip[...] = normed[...].T
            grad_flip[...] = g_ref[...].T
            sum_out[...] = jnp.zeros_like(sum_out)
            sum_norm[...] = jnp.zeros_like(sum_norm)

        w1, w2, grad = (w1_ref[...], w2_ref[...], g_ref[...])
        pre = dot_nn(normed[...], w1)
        root = 0.7978845608028654
        bend = 0.044715
        square = pre * pre
        swing = jnp.tanh(pre * (root + root * bend * square))
        half = 0.5 + 0.5 * swing
        active = pre * half
        hidden = active.astype(BF16)
        sum_out[...] += dot_nn(hidden, w2)
        slope = half + active * (1.0 - swing) * (root + 3.0 * root * bend * square)
        grad_pre = (dot_nt(grad, w2) * slope).astype(BF16)
        sum_norm[...] += dot_nt(grad_pre, w1)
        slot = step % 2

        def moves(at, slot):
            inner = [
                pltpu.make_async_copy(block_in.at[slot], target.at[at // 2], semaphores.at[slot, 0])
                for target in (keep_in, send_in)
            ]
            outer = [
                pltpu.make_async_copy(
                    block_out.at[slot, half], target.at[:, at % 2, :, at // 2], semaphores.at[slot, 1 + kind]
                )
                for kind, (target, half) in enumerate(((keep_out, s[0]), (send_out, 1 - s[0])))
            ]
            return (inner, outer)

        def start(at, slot):
            inner, outer = moves(at, slot)
            pl.when(at % 2 == s[0])(inner[0].start)
            pl.when(at % 2 != s[0])(inner[1].start)
            for move in outer:
                move.start()

        def wait(at, slot):
            inner, outer = moves(at, slot)
            pl.when(at % 2 == s[0])(inner[0].wait)
            pl.when(at % 2 != s[0])(inner[1].wait)
            for move in outer:
                move.wait()

        @pl.when(step >= 2)
        def _():
            wait(step - 2, slot)

        grad_in = dot_nn(normed_flip[...], grad_pre).astype(BF16)
        for at in range(8):
            for unit in range(2):
                block_in[slot, (at // 2) % 2, at % 2, at // 4, pl.ds(unit * rows_in, rows_in), :] = grad_in[
                    at * rows_in : (at + 1) * rows_in, unit * HALF : (unit + 1) * HALF
                ]
        grad_out = dot_nn(grad_flip[...], hidden).astype(BF16)
        for at in range(2):
            for part in range(4):
                block_out[slot, part % 2, at, part // 2] = grad_out[part * side : (part + 1) * side, at * HALF : (at + 1) * HALF]
        start(step, slot)

        @pl.when(step == steps - 1)
        def _():
            for at in (steps - 2, steps - 1):
                wait(at, at % 2)

        @pl.when(step == steps - 1)
        def _():
            out_ref[...] = (x2[...] + sum_out[...]).astype(BF16)
            back, gain_grad_ref[...] = norm_pull(x2[...], gain_ref[...].reshape(1, width), sum_norm[...])
            grad_x = grad.astype(F32) + back
            dx_ref[...] = grad_x
            low = grad_x.astype(BF16)
            low_ref[...] = low
            dctx_ref[...] = dot_nt(low, wo_ref[...]).astype(BF16)

    args = (residual, context, out_weight, gain_vec, feed_in, feed_out, cotangent)
    specs = [whole(a) for a in args]
    specs[4] = pl.BlockSpec((width, chunk), lambda c, _: (0, c))
    specs[5] = pl.BlockSpec((chunk, width), lambda c, _: (c, 0))
    outs = [
        struct((tok, width), BF16),
        struct((tok, width), F32),
        struct((tok, width), BF16),
        struct((tok, width), BF16),
        struct((1, width), F32),
        struct((2, 2, 2, 2, 2 * rows_in, HALF), BF16),
        struct((2, 2, 2, 2, 2 * rows_in, HALF), BF16),
        struct((2, 2, 2, 2, side, HALF), BF16),
        struct((2, 2, 2, 2, side, HALF), BF16),
    ]
    out_specs = [whole(o) for o in outs]
    out_specs[5:] = [any_place(o) for o in outs[5:]]
    return run_kernel(
        "feed_forward",
        body,
        place,
        args,
        specs,
        outs,
        out_specs,
        grid=(steps,),
        scratch=[
            pltpu.VMEM((tok, width), F32),
            pltpu.VMEM((tok, width), BF16),
            pltpu.VMEM((width, tok), BF16),
            pltpu.VMEM((width, tok), BF16),
            pltpu.VMEM((tok, width), F32),
            pltpu.VMEM((tok, width), F32),
            pltpu.VMEM((2, 2, 2, 2, 2 * rows_in, HALF), BF16),
            pltpu.VMEM((2, 2, 2, 2, side, HALF), BF16),
            pltpu.SemaphoreType.DMA((2, 3)),
        ],
        after=after, flops=12 * tok * width * hidden_width + 4 * tok * width * width,
    )


def local_paired(
    inputs,
    encoded,
    cotangent,
    dec_seg,
    pass_doc,
    enc_mask,
    self_query,
    self_key,
    self_value,
    self_output,
    cross_query,
    cross_key,
    cross_value,
    cross_output,
    feed_in,
    feed_out,
    gain_self,
    gain_cross,
    gain_ff,
):
    inputs, encoded, cotangent = (inputs[0], encoded[0], cotangent[0])
    tok, width = inputs.shape
    enc = encoded.shape[0]
    blk, row = (lax.axis_index("blk"), lax.axis_index("rows"))
    core, chip = (blk % 2, blk // 2)
    y_at, z_low, z_high = (row % 2, (row // 2) % 2, row // 4)
    place = jnp.stack([core, chip, y_at, chip ^ core]).astype(jnp.int32)
    gains = (gain_self, gain_cross, gain_ff)
    to_core = lambda array: lax.ppermute(array, "blk", CORE_SWAP)
    to_chip = lambda array: lax.ppermute(array, "blk", CHIP_SWAP)
    in_order = lambda mine, other: jnp.where(core == 0, jnp.concatenate([mine, other]), jnp.concatenate([other, mine]))

    def swap(distance):
        return tuple((at, at ^ distance) for at in range(8))

    over_x = (chip, "blk", CHIP_SWAP)
    over_y = (y_at, "rows", swap(1))
    over_z = ((z_low, "rows", swap(2)), (z_high, "rows", swap(4)))

    gap = -tok % LANES
    spare = jnp.zeros((8 * LANES - tok - gap - enc - 1,), jnp.int32)
    labels = jnp.concatenate([dec_seg[0], spare[:gap], enc_mask[0], pass_doc[0], spare[gap:]])
    labels = jnp.concatenate([labels, jnp.zeros((8 * LANES - labels.shape[0],), jnp.int32)]).reshape(1, 8 * LANES)
    seg_c = to_core(dec_seg)
    labels_c = to_core(labels)
    inputs_c = to_core(inputs)
    inputs_x = to_chip(inputs)
    labels_x = to_chip(labels)
    encoded_c = to_core(encoded)
    h1, qkv, near_marks, near_keys_marks, near_out, near_sum, ck0, cv0 = near_part(
        place, inputs, inputs_c, gain_self, (self_query, self_key, self_value), (dec_seg, seg_c), (encoded, encoded_c),
        (cross_key, cross_value),
    )
    inputs_x, labels_x, encoded_late, _ = lax.optimization_barrier((inputs_x, labels_x, encoded, ck0))
    labels_d = to_core(labels_x)
    inputs_d = to_core(inputs_x)
    encoded_x = to_chip(encoded_late)
    spot = place
    h1_far, far_kv, far_keys_marks, self_out, self_sum, ctx_keep, ctx_send = far_part(
        spot, inputs_x, inputs_d, gain_self, (self_key, self_value), qkv, near_marks, (labels_x, labels_d), near_out, near_sum
    )
    place = find_passages(spot, tok, enc, (labels, labels_c, labels_x, labels_d), after=(ctx_send,))
    encoded_x, _ = lax.optimization_barrier((encoded_x, self_out))
    encoded_d = to_core(encoded_x)
    x1, h2, cq, self_context, ck1, cv1, own_marks, docs0, docs1, cross_context, cross_out, cross_sum = cross_part(
        place, inputs, ctx_keep, to_core(ctx_send), self_output, gain_cross, cross_query, encoded_x, encoded_d, cross_key,
        cross_value, ck0, cv0, (labels, labels_c, labels_x, labels_d),
    )
    docs = (docs0, docs1)
    output, dx2, e2, d_cross, grad_gain_ff, keep_in, send_in, keep_out, send_out = feed_forward(
        place, x1, cross_context, cross_output, gain_ff, feed_in, feed_out, cotangent
    )
    sum_in = Halving(keep_in, to_core(send_in), (over_x, over_z[0], over_y))
    sum_out = Halving(keep_out, to_core(send_out), (over_y, over_z[0], over_x))
    dcq, dck, dcv, dx1, e1, grad_gain_cross, ds_keep, ds_send = cross_back(
        place, cq, (ck0, ck1), (cv0, cv1), own_marks, docs, d_cross, cross_out, cross_sum, x1, dx2, cross_query,
        gain_cross, self_output,
    )
    ds_recv = to_core(ds_send)
    held = (sum_in.step(dcq), sum_out.step(dcq))
    passages = (encoded, encoded_c, encoded_x, encoded_d)
    keep_p, send_p = cross_grads(
        "cross_grads", place, (((cross_context,), (e2,)), ((h2,), (dcq,)), ((self_context,), (e1,))), 1,
        after=held,
    )
    keep_q, send_q = cross_grads(
        "late_grads", place, ((passages, (dck,)), (passages, (dcv,))), 2, after=(keep_p,)
    )
    recv_p = to_core(send_p)
    recv_p, ds_recv, send_q = lax.optimization_barrier((recv_p, ds_recv, send_q))
    sum_p = Halving(keep_p, recv_p, (over_z[0], over_y))
    sum_q = Halving(keep_q, to_core(send_q), (over_y, over_z[0]))
    held = (sum_p.step(),)
    dq_far, dkv_far, far_keep, far_send, gain_far = far_back(
        place, qkv, far_kv, near_marks, far_keys_marks, ds_keep, ds_recv, self_out, self_sum, gain_self, h1_far,
        (self_key, self_value), after=held,
    )
    tied = lax.optimization_barrier((sum_in.recv, sum_out.recv, sum_p.recv, far_send))
    sum_in.recv, sum_out.recv, sum_p.recv, far_send = tied
    far_recv = to_core(far_send)
    held = (sum_in.step(far_keep), sum_out.step(far_keep), sum_p.step(), sum_q.step())
    far_keep, far_recv, *_ = lax.optimization_barrier((far_keep, far_recv, *held))
    far_here = (far_keep.astype(F32) + far_recv.astype(F32)).astype(BF16)
    from_far = to_chip(far_here)
    near_keep, near_send, keep4, send4 = near_back(
        place, qkv, near_marks, near_keys_marks, ds_keep, ds_recv, self_out, self_sum, dq_far, gain_self, h1, h1_far,
        (self_query, self_key, self_value), dkv_far, (gain_far, grad_gain_cross, grad_gain_ff),
        after=(far_here, *held),
    )
    tied = lax.optimization_barrier((sum_in.recv, sum_out.recv, sum_p.recv, sum_q.recv, from_far, near_send, send4))
    sum_in.recv, sum_out.recv, sum_p.recv, sum_q.recv, from_far, near_send, send4 = tied
    recv4 = to_core(send4)
    near_recv = to_core(near_send)
    held = (sum_in.step(), sum_out.step())
    first_keep, first_send, second_keep, second_send = self_start(spot, keep4, recv4, after=held)
    sum_first = Halving(first_keep, lax.ppermute(first_send, "rows", swap(1)), ((3, "blk", CHIP_SWAP),))
    sum_second = Halving(second_keep, to_chip(second_send), ((2, "rows", swap(1)),))
    input_grad = last_pull(
        place, inputs, gain_self, dx1, (near_keep, near_recv, from_far), after=(first_send, second_send)
    )
    held = sum_q.step(input_grad)
    enc_keep, enc_send = passage_grads(place, dck, dcv, cross_key, cross_value, after=(held,))
    sums = (sum_first, sum_second, sum_in, sum_out, sum_q)
    *tied, enc_send = lax.optimization_barrier((*(a.recv for a in sums), enc_send))
    for a, array in zip(sums, tied):
        a.recv = array
    both_step(spot, sum_first, sum_second, after=(enc_keep,))
    sum_cross = merge_split(place, over_x, (sum_p, sum_q), after=(sum_first.keep,))
    sum_cross.steps = [over_z[1]]
    enc_send, _ = lax.optimization_barrier((enc_send, sum_first.keep))
    enc_recv = to_core(enc_send)
    enc_keep, enc_recv, _ = lax.optimization_barrier((enc_keep, enc_recv, sum_cross.keep))
    sum_ff = merge_split(place, over_z[1], (sum_in, sum_out), after=(sum_cross.keep,))
    held = (sum_ff.keep,)
    enc_sum = enc_keep + enc_recv.astype(F32)
    from_chip = to_chip(enc_sum[1].astype(BF16))
    sum_self = merge_split(place, over_z[0], (sum_first, sum_second), after=(enc_sum, *held))
    sum_self.steps = [over_z[1]]
    rows = width // 16
    held = sum_cross.step(sum_self.keep)
    held = sum_self.step(held)
    sum_ff.recv, _ = lax.optimization_barrier((sum_ff.recv, held))
    total_ff = (sum_ff.keep.astype(F32) + sum_ff.recv.astype(F32)).reshape(2, -1, HALF)
    total_in, feed_out_flip = (total_ff[:, part].reshape(4 * rows, HALF) for part in (slice(0, 2 * rows), slice(2 * rows, None)))
    grad_feed_in = jnp.concatenate([total_in[: 2 * rows], total_in[2 * rows :]], axis=1)
    enc_last, from_chip, _ = lax.optimization_barrier((enc_sum[0], from_chip, held))
    encoded_grad = enc_last + from_chip.astype(F32)
    self_q, self_k, self_v, *gain_grads = finish_sums("finish_self", sum_self.keep, sum_self.recv, 3, 3, after=(held,))
    cross_o, cross_q, self_o, cross_k, cross_v = finish_sums(
        "finish_cross", sum_cross.keep, sum_cross.recv, 5, after=(self_q,)
    )
    return (
        output[None],
        input_grad[None],
        encoded_grad[None],
        self_q,
        self_k,
        self_v,
        self_o,
        cross_q,
        cross_k,
        cross_v,
        cross_o,
        grad_feed_in,
        feed_out_flip.T,
        *gain_grads,
    )


def solution(mesh):
    paired = mesh.shape["blk"] == 4 and mesh.shape["rows"] == 8
    body = local_paired if paired else local_any
    in_specs = (
        P("rows", "blk", None),
        P("rows", "blk", None),
        P("rows", "blk", None),
        P("rows", "blk"),
        P("rows", "blk"),
        P("rows", "blk"),
        P(),
        P(),
        P(),
        P(),
        P(),
        P(),
        P(),
        P(),
        P(),
        P(),
        P(),
        P(),
        P(),
    )
    out_specs = (
        P("rows", "blk", None),
        P("rows", "blk", None),
        P("rows", "blk", None),
        P("rows", "blk"),
        P("rows", "blk"),
        P("rows", "blk"),
        P("rows", "blk"),
        P("rows", "blk"),
        P("rows", "blk"),
        P("rows", "blk"),
        P("rows", "blk"),
        P("rows", "blk"),
        P("rows", "blk"),
        P("rows"),
        P("rows"),
        P("rows"),
    )
    return jax.shard_map(body, mesh=mesh, in_specs=in_specs, out_specs=out_specs, check_vma=False)
```
